32 devices in a mesh: section: 16 (over z, y, core), coil: 2 (over x).
Axes of the slice: x: 2, y: 2, z: 4, core: 2. Of those that a mesh axis runs over, the one named last changes fastest.
Arguments:
- kspace: bfloat16 [16, 16, 16, 640], P('coil', None, 'section'), may hold values from -6 to 6
- coil_maps: bfloat16 [16, 16, 16, 640], P('coil', 'section'), may hold values from -1.5 to 1.5
- sampling: int32 [2, 8, 320], replicated, may hold values 0 or 1
- dc_weight: float32 [2], replicated, may hold values from 0.5 to 2.5
- kernel_in: float32 [2, 9, 18, 2], replicated, may hold values from -1.5 to 1.5
- bias_in: float32 [2, 18], replicated, may hold values from -0.5 to 0.5
- kernel_out: float32 [2, 9, 2, 18], replicated, may hold values from -0.5 to 0.5
- bias_out: float32 [2, 2], replicated, may hold values from -0.5 to 0.5
- cotangent: bfloat16 [16, 16, 640], P('section'), may hold values from -6 to 6
Outputs:
- image_out: float32 [16, 16, 640], P('section')
- grad_kspace: float32 [16, 16, 16, 640], P('coil', None, 'section')
The draws below stay inside these ranges and needn't reach their ends.
All inputs are finite; a program needn't handle non-finite values.
Results may differ from the reference program's by a relative error of at most 0.035.
Values may be sent and summed in bfloat16 or wider, within the bound.
No kernel may reach another device: no remote copies, remote signals or barrier semaphores. Data moves between devices by JAX's collectives and lax.ppermute only.
A program may use at most 64 MiB of HBM per device.

```python
import math
import jax
import jax.numpy as jnp
from jax import lax

COILS = 16
LINES = 320
CHANNELS = 18
CASCADES = 2
VOLUMES = 2
ROWS = 16
SLOTS = 16
DEPTH = 8


def plant(drawn, stream_key, low, high):
    longest = drawn.shape.index(max(drawn.shape))
    spots = []
    for shift in (0, 1):
        where = [jax.random.randint(jax.random.fold_in(stream_key, axis), (), 0, length) for axis, length in enumerate(drawn.shape)]
        where[longest] = (where[longest] + shift) % drawn.shape[longest]
        spots.append(tuple(where))
    return drawn.at[spots[0]].set(low).at[spots[1]].set(high)


def block_levels(own_key, dims, shards, least, high):
    loudness = 1.0
    for axis_at, parts in shards:
        steps = jax.random.uniform(jax.random.fold_in(jax.random.fold_in(own_key, 6), axis_at), (parts,), jnp.float32, least / len(shards), high / len(shards))
        loudness = loudness * jnp.repeat(jnp.exp(steps), dims[axis_at] // parts).reshape((-1,) + (1,) * (len(dims) - 1 - axis_at))
    return loudness


def normal_values(key, shape, width, reach, split=(), kind=jnp.bfloat16):
    level = block_levels(key, shape, split, -0.22, 0.18) if split else 1.0
    entries = jax.random.normal(key, shape, jnp.float32) * width * level
    return jnp.minimum(jnp.maximum(entries, -reach), reach).astype(kind)


def setup_inputs(seed: int = 0) -> dict:
    splits = jax.random.split(jax.random.key(seed), 10)
    return {
        "kspace": normal_values(splits[0], (COILS, SLOTS, ROWS, 2 * LINES), 1.0, 6.0, ((0, 2), (2, 16))),
        "coil_maps": normal_values(splits[1], (COILS, SLOTS, ROWS, 2 * LINES), COILS ** -0.5, 1.5, ((0, 2), (1, 16))),
        "sampling": plant((jax.random.randint(splits[2], (VOLUMES, DEPTH, LINES), 0, 3) < 1).astype(jnp.int32), jax.random.fold_in(splits[2], 1), 0, 1),
        "dc_weight": jnp.clip(jax.random.uniform(splits[3], (CASCADES,), jnp.float32, 0.5, 2.5), 0.5, 2.5),
        "kernel_in": normal_values(splits[4], (CASCADES, 9, CHANNELS, 2), 18 ** -0.5, 1.5, (), jnp.float32),
        "bias_in": jnp.clip(jax.random.uniform(splits[5], (CASCADES, CHANNELS), jnp.float32, -0.5, 0.5), -0.5, 0.5),
        "kernel_out": normal_values(splits[6], (CASCADES, 9, 2, CHANNELS), (9 * CHANNELS) ** -0.5, 0.5, (), jnp.float32),
        "bias_out": jnp.clip(jax.random.uniform(splits[7], (CASCADES, 2), jnp.float32, -0.5, 0.5), -0.5, 0.5),
        "cotangent": normal_values(splits[8], (SLOTS, ROWS, 2 * LINES), 1.0, 6.0, ((0, 16),)),
    }


PRECISE = lax.Precision.HIGHEST

def line_table(count, exponent_sign):
    indices = jnp.arange(count, dtype=jnp.int32)
    product = indices[:, None] * indices[None, :] % count
    angles = product.astype(jnp.float32) * (2.0 * math.pi / count)
    factor = 1.0 / math.sqrt(count)
    return (jnp.cos(angles) * factor, exponent_sign * jnp.sin(angles) * factor)

def to_bf(values):
    return lax.optimization_barrier(values.astype(jnp.bfloat16)).astype(jnp.float32)

def line_matrix(count, exponent_sign):
    real_part, imag_part = line_table(count, exponent_sign)
    upper_rows = jnp.concatenate([real_part, imag_part], axis=1)
    lower_rows = jnp.concatenate([-imag_part, real_part], axis=1)
    return to_bf(jnp.concatenate([upper_rows, lower_rows], axis=0))

def line_transform(values, matrix):
    return jnp.dot(to_bf(values), matrix, precision=PRECISE, preferred_element_type=jnp.float32)

def depth_transform(values, volumes, exponent_sign):
    layout_shape = values.shape
    width_two = layout_shape[-1]
    half_width = width_two // 2
    depth_count = layout_shape[1] // volumes
    real_part, imag_part = line_table(depth_count, exponent_sign)
    blocks = to_bf(values).reshape(layout_shape[0], volumes, depth_count, layout_shape[2], width_two)
    straight = jnp.einsum('kz,cvzrw->cvkrw', to_bf(real_part), blocks, precision=PRECISE)
    crossed = jnp.einsum('kz,cvzrw->cvkrw', to_bf(imag_part), blocks, precision=PRECISE)
    turned = jnp.concatenate([-crossed[..., half_width:], crossed[..., :half_width]], axis=-1)
    return (straight + turned).reshape(layout_shape)

def spread(coil_maps, picture):
    half_width = coil_maps.shape[-1] // 2
    maps_real = coil_maps[..., :half_width].astype(jnp.float32)
    maps_imag = coil_maps[..., half_width:].astype(jnp.float32)
    pic_real = picture[..., :half_width].astype(jnp.float32)
    pic_imag = picture[..., half_width:].astype(jnp.float32)
    return jnp.concatenate([maps_real * pic_real - maps_imag * pic_imag, maps_real * pic_imag + maps_imag * pic_real], axis=-1)

def collect(coil_maps, coil_images):
    half_width = coil_maps.shape[-1] // 2
    maps_real = coil_maps[..., :half_width].astype(jnp.float32)
    maps_imag = coil_maps[..., half_width:].astype(jnp.float32)
    img_real = coil_images[..., :half_width]
    img_imag = coil_images[..., half_width:]
    summed = jnp.concatenate([maps_real * img_real + maps_imag * img_imag, maps_real * img_imag - maps_imag * img_real], axis=-1)
    return lax.optimization_barrier(jnp.sum(summed, axis=0))

def shifted_windows(planes):
    row_count, col_count = (planes.shape[-2], planes.shape[-1])
    padded = jnp.pad(planes, ((0, 0), (1, 1), (1, 1)))
    return jnp.stack([padded[:, row_shift:row_shift + row_count, col_shift:col_shift + col_count] for row_shift in range(3) for col_shift in range(3)], axis=0)

def conv_out(hidden, kernel, bias):
    row_count, col_count = (hidden.shape[-2], hidden.shape[-1])
    projected = jnp.einsum('toc,cxy->toxy', kernel, hidden, precision=PRECISE)
    padded = jnp.pad(projected, ((0, 0), (0, 0), (1, 1), (1, 1)))
    summed = jnp.zeros((kernel.shape[1], row_count, col_count), jnp.float32) + bias[:, None, None]
    for tap_index in range(9):
        row_shift = tap_index // 3
        col_shift = tap_index % 3
        summed = summed + padded[tap_index, :, row_shift:row_shift + row_count, col_shift:col_shift + col_count]
    return summed

def refine(picture, kernel_in, bias_in, kernel_out, bias_out):
    half_width = picture.shape[-1] // 2
    planes = jnp.stack([picture[:, :half_width], picture[:, half_width:]], axis=0)
    hidden = jnp.einsum('toc,tcxy->oxy', kernel_in, shifted_windows(planes), precision=PRECISE) + bias_in[:, None, None]
    hidden = jax.nn.silu(hidden)
    output = conv_out(hidden, kernel_out, bias_out)
    return jnp.concatenate([output[0], output[1]], axis=1)

def reference(kspace, coil_maps, sampling, dc_weight, kernel_in, bias_in, kernel_out, bias_out, cotangent):
    lines_used = sampling.astype(jnp.float32).reshape(SLOTS, LINES)
    sampled = jnp.concatenate([lines_used, lines_used], axis=1)[None, :, None, :]
    measured = sampled * kspace.astype(jnp.float32)
    forward_line = line_matrix(LINES, -1.0)
    inverse_line = line_matrix(LINES, 1.0)

    def expand(picture):
        return depth_transform(line_transform(spread(coil_maps, picture[None]), forward_line), VOLUMES, -1.0)

    def combine(kstate):
        return collect(coil_maps, line_transform(depth_transform(kstate, VOLUMES, 1.0), inverse_line))
    refine_all = jax.vmap(refine, in_axes=(0, None, None, None, None))
    kstate = measured
    stored = []
    for cascade in range(CASCADES):
        picture = combine(kstate).astype(jnp.bfloat16).astype(jnp.float32)
        stored.append(picture)
        model = refine_all(picture, kernel_in[cascade], bias_in[cascade], kernel_out[cascade], bias_out[cascade])
        update = expand(model.astype(jnp.bfloat16))
        kstate = kstate - dc_weight[cascade] * sampled * (kstate - measured) + update
    image_out = combine(kstate)
    adjoint = expand(cotangent)
    grad_measured = jnp.zeros(measured.shape, jnp.float32)
    for cascade in reversed(range(CASCADES)):
        weighted = dc_weight[cascade] * sampled
        grad_measured = grad_measured + weighted * adjoint
        model_bar = combine(adjoint).astype(jnp.bfloat16).astype(jnp.float32)
        adjoint = adjoint - weighted * adjoint

        def local_model(flat, index=cascade):
            return refine_all(flat, kernel_in[index], bias_in[index], kernel_out[index], bias_out[index])
        unused, pull_back = jax.vjp(local_model, stored[cascade])
        picture_bar = pull_back(model_bar)[0]
        adjoint = adjoint + expand(picture_bar.astype(jnp.bfloat16))
    grad_measured = grad_measured + adjoint
    return (image_out, sampled * grad_measured)
```

```python
import functools
import math

import jax
import jax.numpy as jnp
import ml_dtypes
import numpy as np
from jax import lax
from jax.experimental import pallas as pl
from jax.experimental.pallas import tpu as pltpu
from jax.sharding import PartitionSpec as P

CASCADES = 2
VOLUMES = 2
LANES = 128
VMEM_BYTES = 48 * 1024 * 1024

F32 = jnp.float32
BF16 = jnp.bfloat16


def padded(size, unit):
    return -(-size // unit) * unit


def dft_parts(count):
    indices = np.arange(count)
    angles = (indices[:, None] * indices[None, :] % count) * (2.0 * math.pi / count)
    factor = 1.0 / math.sqrt(count)
    return np.cos(angles) * factor, np.sin(angles) * factor


def line_constant(lines):
    width = padded(lines, LANES)
    cosine, sine = dft_parts(lines)
    table = np.zeros((width, 2 * width), np.float32)
    table[:lines, :lines] = cosine
    table[:lines, width : width + lines] = sine
    return table.astype(ml_dtypes.bfloat16)


def depth_constant(coils, slots, volumes, sign):
    cosine, sine = dft_parts(slots // volumes)
    spread_over = np.eye(coils * volumes)
    real, imag = np.kron(spread_over, cosine), sign * np.kron(spread_over, sine)
    return np.block([[real, -imag], [imag, real]]).astype(np.float32).astype(ml_dtypes.bfloat16)


def conv_constants(rows, channels):
    groups = 6
    width = padded(groups * rows, LANES)
    repeat = np.kron(np.eye(channels), np.ones((rows, 1))).astype(np.float32)
    taps = CASCADES * 3
    place = np.zeros((padded(2 * taps * groups + CASCADES, LANES), 2 * taps * width), np.float32)
    for kind in range(2):
        for tap in range(taps):
            for group in range(groups):
                start = (kind * taps + tap) * width + group * rows
                place[(kind * taps + tap) * groups + group, start : start + rows] = 1.0
    offset = np.full((channels * rows, width), -9.0, np.float32)
    row = np.arange(rows)
    offset[:, : groups * rows] = np.tile(row[None, :] - row[:, None] + 1.0, (channels, groups))
    offset = np.clip(offset, -9.0, 9.0)
    return repeat, place.astype(ml_dtypes.bfloat16), offset


def lane_index(shape):
    return lax.broadcasted_iota(jnp.int32, shape, len(shape) - 1)


def split_complex(chunks, lines):
    whole, rest = divmod(lines, LANES)
    count = padded(lines, LANES) // LANES
    if rest == 0:
        return jnp.concatenate(chunks[:count], 1), jnp.concatenate(chunks[count:], 1)
    lane = lane_index(chunks[0].shape)
    real = chunks[:whole] + [jnp.where(lane < rest, chunks[whole], 0.0)]
    turned = [pltpu.roll(chunk, LANES - rest, 1) for chunk in chunks[whole:]]
    turned.append(jnp.zeros_like(turned[0]))
    imag = [jnp.where(lane < LANES - rest, turned[k], turned[k + 1]) for k in range(count)]
    imag[-1] = jnp.where(lane < rest, imag[-1], 0.0)
    return jnp.concatenate(real, 1), jnp.concatenate(imag, 1)


def lane_chunks(value):
    return [value[:, start : start + LANES] for start in range(0, value.shape[1], LANES)]


def join_complex(real, imag, lines):
    whole, rest = divmod(lines, LANES)
    real, imag = lane_chunks(real), lane_chunks(imag)
    if rest == 0:
        return real + imag
    lane = lane_index(real[0].shape)
    turned = [real[whole]] + [pltpu.roll(chunk, rest, 1) for chunk in imag]
    mixed = [jnp.where(lane < rest, turned[k], turned[k + 1]) for k in range(len(imag))]
    return (real[:whole] + mixed)[: 2 * lines // LANES]


def halves(stacked):
    half = stacked.shape[0] // 2
    return stacked[:half], stacked[half:]


def line_apply(stacked, table_ref, sign):
    mixed = jnp.dot(stacked.astype(BF16), table_ref[...], preferred_element_type=F32)
    width = table_ref.shape[1] // 2
    top, bottom = halves(mixed)
    return jnp.concatenate(
        [
            top[:, :width] - sign * bottom[:, width:],
            bottom[:, :width] + sign * top[:, width:],
        ],
        axis=0,
    )


def depth_apply(stacked, depth_ref):
    return jnp.dot(depth_ref[...], stacked.astype(BF16), preferred_element_type=F32)


def over_coils(value, coils):
    return jnp.concatenate([value] * coils, axis=0)


def coil_sum(value, coils):
    slots = value.shape[0] // coils
    total = value[:slots]
    for coil in range(1, coils):
        total = total + value[coil * slots : (coil + 1) * slots]
    return total


def spread(maps_real, maps_imag, real, imag, coils):
    real, imag = over_coils(real, coils), over_coils(imag, coils)
    return jnp.concatenate(
        [maps_real * real - maps_imag * imag, maps_real * imag + maps_imag * real], axis=0
    )


def collect(maps_real, maps_imag, images, coils):
    real, imag = halves(images)
    return (
        coil_sum(maps_real * real + maps_imag * imag, coils),
        coil_sum(maps_real * imag - maps_imag * real, coils),
    )


def masked_normal(images, table_ref, minus_ref, plus_ref, mask):
    spectrum = depth_apply(line_apply(images, table_ref, -1.0), minus_ref)
    return line_apply(depth_apply(spectrum * mask, plus_ref), table_ref, 1.0)


def write_rows(scratch, pitch, values, first=0):
    for index, value in enumerate(values):
        scratch[pl.ds(first + index, value.shape[0], stride=pitch), :] = value


def read_rows(scratch, pitch, first, count, rows):
    return [scratch[pl.ds(first + index, rows, stride=pitch), :] for index in range(count)]


def shifted(value, step):
    if step == 0:
        return value
    width = value.shape[1]
    return pltpu.roll(value, (-step) % width, 1)


def stack_shifted(value, order):
    return jnp.concatenate([shifted(value, step) for step in order], axis=0).astype(BF16)


def add_shifted(value, order, rows):
    total = None
    for index, step in enumerate(order):
        part = shifted(value[index * rows : (index + 1) * rows], step)
        total = part if total is None else total + part
    return total


def hidden_state(image, first_ref, bias_column):
    stack = stack_shifted(image, (-1, 0, 1))
    return (
        jnp.dot(first_ref[:, : stack.shape[0]], stack, preferred_element_type=F32) + bias_column
    )


def second_conv(hidden, second_ref, bias, rows, valid):
    mixed = jnp.dot(
        second_ref[...], jnp.where(valid, hidden, 0.0).astype(BF16), preferred_element_type=F32
    )
    total = add_shifted(mixed, (-1, 0, 1), 2 * rows)
    row = lax.broadcasted_iota(jnp.int32, total.shape, 0)
    total = total + jnp.where(row < rows, bias[0], bias[1])
    return jnp.where(valid[: 2 * rows], total, 0.0)


def pull_back(cotangent, slope, first_t_ref, second_t_ref, rows, valid):
    stack = stack_shifted(cotangent, (1, 0, -1))
    back = jnp.dot(second_t_ref[:, : stack.shape[0]], stack, preferred_element_type=F32)
    back = jnp.where(valid, back * slope, 0.0).astype(BF16)
    mixed = jnp.dot(first_t_ref[...], back, preferred_element_type=F32)
    total = add_shifted(mixed, (1, 0, -1), 2 * rows)
    return jnp.where(valid[: 2 * rows], total, 0.0)


def valid_lanes(rows, width, lines):
    return lane_index((rows, width)) < lines


def round_bf(value):
    return value.astype(BF16).astype(F32)


def pack_kernel(coils, rows, pitch, maps_ref, image_ref, out_ref, scratch):
    scratch[...] = jnp.zeros_like(scratch)
    count = maps_ref.shape[1] // LANES
    for coil in range(coils):
        value = maps_ref[coil * rows : (coil + 1) * rows, :].astype(F32)
        write_rows(scratch, pitch, lane_chunks(value), coil * count)
    write_rows(scratch, pitch, lane_chunks(image_ref[...].astype(F32)), coils * count)
    out_ref[...] = scratch[...].astype(BF16).reshape(out_ref.shape)


def begin_kernel(
    coils,
    lines,
    rows,
    kspace_ref,
    mask_ref,
    table_ref,
    plus_ref,
    taps_ref,
    repeat_ref,
    place_ref,
    offset_ref,
    images_ref,
    first_ref,
    first_t_ref,
    second_ref,
    second_t_ref,
    bias_ref,
):
    real, imag = split_complex(lane_chunks(kspace_ref[...].astype(F32)), lines)
    mask = over_coils(mask_ref[...], coils)
    measured = jnp.concatenate([real * mask, imag * mask], axis=0)
    images = line_apply(depth_apply(measured, plus_ref), table_ref, 1.0)
    images_ref[...] = images.astype(BF16)

    tall = jnp.dot(
        repeat_ref[...],
        taps_ref[...],
        precision=lax.Precision.HIGHEST,
        preferred_element_type=F32,
    )
    bias_ref[...] = tall
    wide = jnp.dot(tall.astype(BF16), place_ref[...], preferred_element_type=F32)
    offset = offset_ref[...]
    width = offset.shape[1]
    for cascade in range(CASCADES):
        for kind, straight, turned in ((0, first_ref, first_t_ref), (1, second_t_ref, second_ref)):
            total = jnp.zeros_like(offset)
            for tap in range(3):
                start = ((kind * CASCADES + cascade) * 3 + tap) * width
                wanted = float(tap if kind == 0 else 2 - tap)
                total = total + jnp.where(offset == wanted, wide[:, start : start + width], 0.0)
            straight[cascade] = total.astype(BF16)
            turned[cascade] = total.T[: 6 * rows].astype(BF16)


def rows_kernel(
    coils,
    slots,
    lines,
    pitch,
    sent_ref,
    images_ref,
    mask_ref,
    table_ref,
    minus_ref,
    plus_ref,
    out_ref,
    maps_ref,
    arrived,
    leaving,
):
    arrived[...] = sent_ref[...].astype(F32).reshape(arrived.shape)
    count = 2 * lines // LANES
    parts = [
        split_complex(read_rows(arrived, pitch, coil * count, count, slots), lines)
        for coil in range(coils)
    ]
    maps_real = jnp.concatenate([part[0] for part in parts], axis=0)
    maps_imag = jnp.concatenate([part[1] for part in parts], axis=0)
    maps_ref[...] = jnp.concatenate([maps_real, maps_imag], axis=0).astype(BF16)
    real, imag = split_complex(read_rows(arrived, pitch, coils * count, count, slots), lines)
    mask = over_coils(mask_ref[...], 2 * coils)
    images = spread(maps_real, maps_imag, real, imag, coils)
    images = masked_normal(images, table_ref, minus_ref, plus_ref, mask)
    turned = collect(maps_real, maps_imag, images, coils)
    begun = collect(maps_real, maps_imag, images_ref[...].astype(F32), coils)
    power = coil_sum(maps_real * maps_real + maps_imag * maps_imag, coils)
    leaving[...] = jnp.zeros_like(leaving)
    values = []
    for value in (*begun, *turned, power):
        values += lane_chunks(value)
    write_rows(leaving, out_ref.shape[2], values)
    message = leaving[...].astype(BF16).reshape(slots, *out_ref.shape[2:])
    for device in range(out_ref.shape[1]):
        out_ref[:, device] = message


def unpack_sum(sent_ref, scratch):
    total = sent_ref[:, 0].astype(F32)
    for device in range(1, sent_ref.shape[1]):
        total = total + sent_ref[:, device].astype(F32)
    scratch[...] = total.reshape(scratch.shape)


def read_pair(scratch, pitch, first, count, rows):
    real = jnp.concatenate(read_rows(scratch, pitch, first, count, rows), axis=1)
    imag = jnp.concatenate(read_rows(scratch, pitch, first + count, count, rows), axis=1)
    return jnp.concatenate([real, imag], axis=0)


def first_refine_kernel(
    lines, rows, bias_out_ref, sent_ref, first_ref, second_ref, bias_ref, out_ref, model_ref, arrived, leaving
):
    unpack_sum(sent_ref, arrived)
    width = padded(lines, LANES)
    count = width // LANES
    picture = round_bf(read_pair(arrived, sent_ref.shape[2], 0, count, rows))
    bias_at = 4 * 9 * CASCADES
    hidden = hidden_state(picture, first_ref.at[0], bias_ref[:, bias_at : bias_at + 1])
    valid = valid_lanes(hidden.shape[0], width, lines)
    hidden = hidden * jax.nn.sigmoid(hidden)
    bias = (bias_out_ref[0, 0], bias_out_ref[0, 1])
    model = second_conv(hidden, second_ref.at[0], bias, rows, valid)
    model_ref[...] = model.astype(BF16)
    leaving[...] = jnp.zeros_like(leaving)
    real, imag = halves(model)
    write_rows(leaving, out_ref.shape[1], lane_chunks(real) + lane_chunks(imag))
    out_ref[...] = leaving[...].astype(BF16).reshape(out_ref.shape)


def slots_kernel(
    lines,
    rows,
    weight_ref,
    bias_out_ref,
    sent_ref,
    model_ref,
    cotangent_ref,
    first_ref,
    first_t_ref,
    second_ref,
    second_t_ref,
    bias_ref,
    image_ref,
    spread_ref,
    arrived,
):
    unpack_sum(sent_ref, arrived)
    width = padded(lines, LANES)
    count = width // LANES
    pitch = sent_ref.shape[2]
    begun = read_pair(arrived, pitch, 0, count, rows)
    turned = read_pair(arrived, pitch, 2 * count, count, rows)
    power = jnp.concatenate(read_rows(arrived, pitch, 4 * count, count, rows), axis=1)
    power = jnp.concatenate([power, power], axis=0)
    cotangent = jnp.concatenate(
        split_complex(lane_chunks(cotangent_ref[...].astype(F32)), lines), axis=0
    )
    model = model_ref[...].astype(F32)
    bias_at = 4 * 9 * CASCADES
    weight = (weight_ref[0], weight_ref[1])

    share = [jnp.float32(1.0)]
    for cascade in range(CASCADES):
        share.append(share[cascade] - weight[cascade] * (share[cascade] - 1.0))

    def slopes(hidden):
        gate = jax.nn.sigmoid(hidden)
        return hidden * gate, gate * (1.0 + hidden * (1.0 - gate))

    hidden = hidden_state(round_bf(begun), first_ref.at[0], bias_ref[:, bias_at : bias_at + 1])
    valid = valid_lanes(hidden.shape[0], width, lines)
    unused, slope_first = slopes(hidden)
    picture = round_bf(share[1] * begun + power * model)
    hidden = hidden_state(picture, first_ref.at[1], bias_ref[:, bias_at + 1 : bias_at + 2])
    active, slope_second = slopes(hidden)
    bias = (bias_out_ref[1, 0], bias_out_ref[1, 1])
    later = round_bf(second_conv(active, second_ref.at[1], bias, rows, valid))
    image_ref[...] = share[2] * begun + power * (model + later)

    through = power * cotangent
    back_second = round_bf(
        pull_back(through, slope_second, first_t_ref.at[1], second_t_ref.at[1], rows, valid)
    )
    through = through - weight[1] * turned + power * back_second
    back_first = round_bf(
        pull_back(through, slope_first, first_t_ref.at[0], second_t_ref.at[0], rows, valid)
    )
    kept = (1.0 - weight[0], 1.0 - weight[1])
    of_cotangent = weight[1] + weight[0] * kept[1] + kept[0] * kept[1]
    of_second = weight[0] + kept[0]
    spread_ref[...] = of_cotangent * cotangent + of_second * back_second + back_first


def normal_kernel(
    coils,
    slots,
    sent_ref,
    maps_ref,
    spread_ref,
    mask_ref,
    table_ref,
    minus_ref,
    plus_ref,
    out_ref,
    arrived,
    leaving,
):
    arrived[...] = sent_ref[...].astype(F32).reshape(arrived.shape)
    count = maps_ref.shape[1] // LANES
    real, imag = halves(read_pair(arrived, sent_ref.shape[1], 0, count, slots))
    maps_real, maps_imag = halves(maps_ref[...].astype(F32))
    mask = over_coils(mask_ref[...], 2 * coils)
    images = spread(maps_real, maps_imag, real, imag, coils)
    images = masked_normal(images, table_ref, minus_ref, plus_ref, mask)
    leaving[...] = jnp.zeros_like(leaving)
    values = []
    for value in (*collect(maps_real, maps_imag, images, coils), *halves(spread_ref[...])):
        values += lane_chunks(value)
    write_rows(leaving, out_ref.shape[2], values)
    message = leaving[...].astype(BF16).reshape(slots, *out_ref.shape[2:])
    for device in range(out_ref.shape[1]):
        out_ref[:, device] = message


def end_kernel(
    coils,
    slots,
    lines,
    weight_ref,
    sent_ref,
    image_ref,
    maps_ref,
    mask_ref,
    table_ref,
    minus_ref,
    picture_ref,
    grad_ref,
    arrived,
):
    count = maps_ref.shape[1] // LANES
    pitch = sent_ref.shape[2]
    arrived[...] = sent_ref[:, 0].astype(F32).reshape(arrived.shape)
    real, imag = halves(read_pair(arrived, pitch, 2 * count, count, slots))
    maps_real, maps_imag = halves(maps_ref[...].astype(F32))
    images = spread(maps_real, maps_imag, real, imag, coils)
    spectrum = depth_apply(line_apply(images, table_ref, -1.0), minus_ref)
    spectrum = spectrum * over_coils(mask_ref[...], 2 * coils)
    for index, chunk in enumerate(join_complex(*halves(spectrum), lines)):
        grad_ref[:, index * LANES : (index + 1) * LANES] = chunk

    unpack_sum(sent_ref, arrived)
    turned = read_pair(arrived, pitch, 0, count, slots)
    picture = image_ref[...] - weight_ref[1] * turned
    for index, chunk in enumerate(join_complex(*halves(picture), lines)):
        picture_ref[:, index * LANES : (index + 1) * LANES] = chunk


def call(kernel, name, operands, scalars, outs, scratch, flops):
    spaces = [pltpu.SMEM] * scalars + [pltpu.VMEM] * (len(operands) - scalars)
    moved = sum(math.prod(item.shape) * item.dtype.itemsize for item in (*operands, *outs))
    return pl.pallas_call(
        kernel,
        name=name,
        out_shape=tuple(outs),
        in_specs=[pl.BlockSpec(memory_space=space) for space in spaces],
        out_specs=tuple(pl.BlockSpec(memory_space=pltpu.VMEM) for item in outs),
        scratch_shapes=[pltpu.VMEM(shape, F32) for shape in scratch],
        compiler_params=pltpu.CompilerParams(vmem_limit_bytes=VMEM_BYTES),
        cost_estimate=pl.CostEstimate(flops=flops, bytes_accessed=moved, transcendentals=0),
    )(*operands)


def body(
    kspace, coil_maps, sampling, dc_weight, kernel_in, bias_in, kernel_out, bias_out, cotangent
):
    coils, slots = kspace.shape[:2]
    rows, two_lines = coil_maps.shape[2:]
    lines = two_lines // 2
    channels = bias_in.shape[1]
    coil_devices = lax.axis_size("coil")
    width = padded(lines, LANES)
    count = width // LANES
    planes = coils * slots
    both = ("section", "coil")

    table = jnp.asarray(line_constant(lines))
    minus = jnp.asarray(depth_constant(coils, slots, VOLUMES, -1.0))
    plus = jnp.asarray(depth_constant(coils, slots, VOLUMES, 1.0))
    repeat, place, offset = (jnp.asarray(item) for item in conv_constants(rows, channels))
    mask = sampling.astype(F32).reshape(slots, lines)
    mask = jnp.pad(mask, ((0, 0), (0, width - lines)))
    taps = jnp.concatenate(
        [
            kernel_in.transpose(2, 0, 1, 3).reshape(channels, -1),
            kernel_out.transpose(3, 0, 1, 2).reshape(channels, -1),
            bias_in.T,
        ],
        axis=1,
    )
    taps = jnp.pad(taps, ((0, 0), (0, place.shape[0] - taps.shape[1])))

    def shape(*dims, kind=F32):
        return jax.ShapeDtypeStruct(dims, kind)

    line_flops = 2 * (2 * planes) * width * (2 * width)

    pitch = padded((coils + 1) * (two_lines // LANES), 16)
    (packed,) = call(
        functools.partial(pack_kernel, coils, rows, pitch),
        "pack_maps",
        (coil_maps.reshape(coils * rows, two_lines), cotangent.reshape(rows, two_lines)),
        0,
        [shape(rows, pitch, LANES, kind=BF16)],
        [(rows * pitch, LANES)],
        1000,
    )
    arrived = lax.all_to_all(packed, "section", 0, 0, tiled=True)

    tall, wide = channels * rows, offset.shape[1]
    images, first, first_t, second, second_t, bias = call(
        functools.partial(begin_kernel, coils, lines, rows),
        "measured_images",
        (kspace.reshape(planes, two_lines), mask, table, plus, taps, repeat, place, offset),
        0,
        [
            shape(2 * planes, width, kind=BF16),
            shape(CASCADES, tall, wide, kind=BF16),
            shape(CASCADES, 6 * rows, tall, kind=BF16),
            shape(CASCADES, 6 * rows, tall, kind=BF16),
            shape(CASCADES, tall, wide, kind=BF16),
            shape(tall, place.shape[0]),
        ],
        [],
        2 * line_flops,
    )

    depth_pitch = padded(5 * count, 16)
    partial, maps = call(
        functools.partial(rows_kernel, coils, slots, lines, pitch),
        "combine_rows",
        (arrived, images, mask, table, minus, plus),
        0,
        [
            shape(slots, coil_devices, depth_pitch, LANES, kind=BF16),
            shape(2 * planes, width, kind=BF16),
        ],
        [(slots * pitch, LANES), (slots * depth_pitch, LANES)],
        3 * line_flops,
    )
    partial = partial.reshape(slots * coil_devices, depth_pitch, LANES)
    partial = lax.all_to_all(partial, both, 0, 0, tiled=True)
    partial = partial.reshape(rows, coil_devices, depth_pitch, LANES)

    model_pitch = padded(2 * count, 8)
    moved, model = call(
        functools.partial(first_refine_kernel, lines, rows),
        "refine_first",
        (bias_out, partial, first, second, bias),
        1,
        [shape(rows, model_pitch, LANES, kind=BF16), shape(2 * rows, width, kind=BF16)],
        [(rows * depth_pitch, LANES), (rows * model_pitch, LANES)],
        4 * tall * wide * width,
    )
    moved = lax.all_to_all(moved, "section", 0, 0, tiled=True)

    image, pulled = call(
        functools.partial(slots_kernel, lines, rows),
        "refine_and_back",
        (
            dc_weight,
            bias_out,
            partial,
            model,
            cotangent.reshape(rows, two_lines),
            first,
            first_t,
            second,
            second_t,
            bias,
        ),
        2,
        [shape(2 * rows, width), shape(2 * rows, width)],
        [(rows * depth_pitch, LANES)],
        14 * tall * wide * width,
    )

    end_pitch = padded(4 * count, 16)
    (partial,) = call(
        functools.partial(normal_kernel, coils, slots),
        "masked_normal",
        (moved, maps, pulled, mask, table, minus, plus),
        0,
        [shape(slots, coil_devices, end_pitch, LANES, kind=BF16)],
        [(slots * model_pitch, LANES), (slots * end_pitch, LANES)],
        3 * line_flops,
    )
    partial = partial.reshape(slots * coil_devices, end_pitch, LANES)
    partial = lax.all_to_all(partial, both, 0, 0, tiled=True)
    partial = partial.reshape(rows, coil_devices, end_pitch, LANES)

    image, grad = call(
        functools.partial(end_kernel, coils, slots, lines),
        "outputs",
        (dc_weight, partial, image, maps, mask, table, minus),
        1,
        [shape(rows, two_lines), shape(planes, two_lines)],
        [(rows * end_pitch, LANES)],
        2 * line_flops,
    )
    return image.reshape(1, rows, two_lines), grad.reshape(coils, slots, 1, two_lines)


def solution(mesh):
    return jax.shard_map(
        body,
        mesh=mesh,
        in_specs=(
            P("coil", None, "section", None),
            P("coil", "section", None, None),
            P(),
            P(),
            P(),
            P(),
            P(),
            P(),
            P("section", None, None),
        ),
        out_specs=(P("section", None, None), P("coil", None, "section", None)),
        check_vma=False,
    )
```

```python
import functools
import math

import jax
import jax.numpy as jnp
import ml_dtypes
import numpy as np
from jax import lax
from jax.experimental import pallas as pl
from jax.experimental.pallas import tpu as pltpu
from jax.sharding import PartitionSpec as P

CASCADES = 2
VOLUMES = 2
LANES = 128
VMEM_BYTES = 48 * 1024 * 1024
PACK_VMEM_BYTES = 60 * 1024 * 1024

F32 = jnp.float32
BF16 = jnp.bfloat16


def padded(size, unit):
    return -(-size // unit) * unit


def dft_parts(count):
    indices = np.arange(count)
    angles = (indices[:, None] * indices[None, :] % count) * (2.0 * math.pi / count)
    factor = 1.0 / math.sqrt(count)
    return np.cos(angles) * factor, np.sin(angles) * factor


def line_constant(lines):
    width = padded(lines, LANES)
    cosine, sine = dft_parts(lines)
    table = np.zeros((width, 2 * width), np.float32)
    table[:lines, :lines] = cosine
    table[:lines, width : width + lines] = sine
    return table.astype(ml_dtypes.bfloat16)


def depth_constant(coils, slots, volumes, sign):
    cosine, sine = dft_parts(slots // volumes)
    spread_over = np.eye(coils * volumes)
    real, imag = np.kron(spread_over, cosine), sign * np.kron(spread_over, sine)
    return np.block([[real, -imag], [imag, real]]).astype(np.float32).astype(ml_dtypes.bfloat16)


def conv_constants(rows, channels):
    groups = 6
    width = padded(groups * rows, LANES)
    repeat = np.kron(np.eye(channels), np.ones((rows, 1))).astype(np.float32)
    taps = CASCADES * 3
    place = np.zeros((padded(2 * taps * groups + 3 * CASCADES, LANES), 2 * taps * width), np.float32)
    for kind in range(2):
        for tap in range(taps):
            for group in range(groups):
                start = (kind * taps + tap) * width + group * rows
                place[(kind * taps + tap) * groups + group, start : start + rows] = 1.0
    offset = np.full((channels * rows, width), -9.0, np.float32)
    row = np.arange(rows)
    offset[:, : groups * rows] = np.tile(row[None, :] - row[:, None] + 1.0, (channels, groups))
    offset = np.clip(offset, -9.0, 9.0)
    return repeat, place.astype(ml_dtypes.bfloat16), offset


def lane_index(shape):
    return lax.broadcasted_iota(jnp.int32, shape, len(shape) - 1)


def split_complex(chunks, lines):
    whole, rest = divmod(lines, LANES)
    count = padded(lines, LANES) // LANES
    if rest == 0:
        return jnp.concatenate(chunks[:count], 1), jnp.concatenate(chunks[count:], 1)
    lane = lane_index(chunks[0].shape)
    real = chunks[:whole] + [jnp.where(lane < rest, chunks[whole], 0.0)]
    turned = [pltpu.roll(chunk, LANES - rest, 1) for chunk in chunks[whole:]]
    turned.append(jnp.zeros_like(turned[0]))
    imag = [jnp.where(lane < LANES - rest, turned[k], turned[k + 1]) for k in range(count)]
    imag[-1] = jnp.where(lane < rest, imag[-1], 0.0)
    return jnp.concatenate(real, 1), jnp.concatenate(imag, 1)


def lane_chunks(value):
    return [value[:, start : start + LANES] for start in range(0, value.shape[1], LANES)]


def join_complex(real, imag, lines):
    whole, rest = divmod(lines, LANES)
    real, imag = lane_chunks(real), lane_chunks(imag)
    if rest == 0:
        return real + imag
    lane = lane_index(real[0].shape)
    turned = [real[whole]] + [pltpu.roll(chunk, rest, 1) for chunk in imag]
    mixed = [jnp.where(lane < rest, turned[k], turned[k + 1]) for k in range(len(imag))]
    return (real[:whole] + mixed)[: 2 * lines // LANES]


def halves(stacked):
    half = stacked.shape[0] // 2
    return stacked[:half], stacked[half:]


def line_apply(stacked, table_ref, sign):
    mixed = jnp.dot(stacked.astype(BF16), table_ref[...], preferred_element_type=F32)
    width = table_ref.shape[1] // 2
    top, bottom = halves(mixed)
    return jnp.concatenate(
        [
            top[:, :width] - sign * bottom[:, width:],
            bottom[:, :width] + sign * top[:, width:],
        ],
        axis=0,
    )


def depth_apply(stacked, depth_ref):
    return jnp.dot(depth_ref[...], stacked.astype(BF16), preferred_element_type=F32)


def over_coils(value, coils):
    return jnp.concatenate([value] * coils, axis=0)


def coil_sum(value, coils):
    slots = value.shape[0] // coils
    total = value[:slots]
    for coil in range(1, coils):
        total = total + value[coil * slots : (coil + 1) * slots]
    return total


def spread(maps_real, maps_imag, real, imag, coils):
    real, imag = over_coils(real, coils), over_coils(imag, coils)
    return jnp.concatenate(
        [maps_real * real - maps_imag * imag, maps_real * imag + maps_imag * real], axis=0
    )


def collect(maps_real, maps_imag, images, coils):
    real, imag = halves(images)
    return (
        coil_sum(maps_real * real + maps_imag * imag, coils),
        coil_sum(maps_real * imag - maps_imag * real, coils),
    )


def masked_normal(images, table_ref, minus_ref, plus_ref, mask):
    spectrum = depth_apply(line_apply(images, table_ref, -1.0), minus_ref)
    return line_apply(depth_apply(spectrum * mask, plus_ref), table_ref, 1.0)


def write_rows(scratch, pitch, values, first=0):
    for index, value in enumerate(values):
        scratch[pl.ds(first + index, value.shape[0], stride=pitch), :] = value


def read_rows(scratch, pitch, first, count, rows):
    return [scratch[pl.ds(first + index, rows, stride=pitch), :] for index in range(count)]


def shifted(value, step):
    if step == 0:
        return value
    width = value.shape[1]
    return pltpu.roll(value, (-step) % width, 1)


def stack_shifted(value, order):
    return jnp.concatenate([shifted(value, step) for step in order], axis=0).astype(BF16)


def add_shifted(value, order, rows):
    total = None
    for index, step in enumerate(order):
        part = shifted(value[index * rows : (index + 1) * rows], step)
        total = part if total is None else total + part
    return total


def hidden_state(image, first_ref, bias_column):
    stack = stack_shifted(image, (-1, 0, 1))
    return (
        jnp.dot(first_ref[:, : stack.shape[0]], stack, preferred_element_type=F32) + bias_column
    )


def second_conv(hidden, second_ref, bias_column, rows, valid):
    mixed = jnp.dot(
        second_ref[...], jnp.where(valid, hidden, 0.0).astype(BF16), preferred_element_type=F32
    )
    total = add_shifted(mixed, (-1, 0, 1), 2 * rows)
    return jnp.where(valid[: 2 * rows], total + bias_column, 0.0)


def pull_back(cotangent, slope, first_t_ref, second_t_ref, rows, valid):
    stack = stack_shifted(cotangent, (1, 0, -1))
    back = jnp.dot(second_t_ref[:, : stack.shape[0]], stack, preferred_element_type=F32)
    back = jnp.where(valid, back * slope, 0.0).astype(BF16)
    mixed = jnp.dot(first_t_ref[...], back, preferred_element_type=F32)
    total = add_shifted(mixed, (1, 0, -1), 2 * rows)
    return jnp.where(valid[: 2 * rows], total, 0.0)


def valid_lanes(rows, width, lines):
    return lane_index((rows, width)) < lines


def column(columns_ref, place, rows):
    at = 4 * 9 * CASCADES + place
    return columns_ref[:rows, at : at + 1]


def round_bf(value):
    return value.astype(BF16).astype(F32)


def pack_kernel(coils, rows, pitch, maps_ref, image_ref, out_ref, scratch):
    scratch[...] = jnp.zeros_like(scratch)
    count = maps_ref.shape[1] // LANES
    for coil in range(coils):
        value = maps_ref[coil * rows : (coil + 1) * rows, :].astype(F32)
        write_rows(scratch, pitch, lane_chunks(value), coil * count)
    write_rows(scratch, pitch, lane_chunks(image_ref[...].astype(F32)), coils * count)
    out_ref[...] = scratch[...].astype(BF16).reshape(out_ref.shape)


def begin_kernel(
    coils,
    lines,
    rows,
    kspace_ref,
    mask_ref,
    table_ref,
    plus_ref,
    taps_ref,
    repeat_ref,
    place_ref,
    offset_ref,
    images_ref,
    first_ref,
    first_t_ref,
    second_ref,
    second_t_ref,
    columns_ref,
):
    real, imag = split_complex(lane_chunks(kspace_ref[...].astype(F32)), lines)
    mask = over_coils(mask_ref[...], coils)
    measured = jnp.concatenate([real * mask, imag * mask], axis=0)
    images = line_apply(depth_apply(measured, plus_ref), table_ref, 1.0)
    images_ref[...] = images.astype(BF16)

    tall = jnp.dot(
        repeat_ref[...],
        taps_ref[...],
        precision=lax.Precision.HIGHEST,
        preferred_element_type=F32,
    )
    columns_ref[...] = tall
    wide = jnp.dot(tall.astype(BF16), place_ref[...], preferred_element_type=F32)
    offset = offset_ref[...]
    width = offset.shape[1]
    for cascade in range(CASCADES):
        for kind, straight, turned in ((0, first_ref, first_t_ref), (1, second_t_ref, second_ref)):
            total = jnp.zeros_like(offset)
            for tap in range(3):
                start = ((kind * CASCADES + cascade) * 3 + tap) * width
                wanted = float(tap if kind == 0 else 2 - tap)
                total = total + jnp.where(offset == wanted, wide[:, start : start + width], 0.0)
            straight[cascade] = total.astype(BF16)
            turned[cascade] = total.T[: 6 * rows].astype(BF16)


def rows_kernel(
    coils,
    slots,
    lines,
    pitch,
    sent_ref,
    images_ref,
    mask_ref,
    table_ref,
    minus_ref,
    plus_ref,
    out_ref,
    maps_ref,
    arrived,
    leaving,
):
    arrived[...] = sent_ref[...].astype(F32).reshape(arrived.shape)
    count = 2 * lines // LANES
    parts = [
        split_complex(read_rows(arrived, pitch, coil * count, count, slots), lines)
        for coil in range(coils)
    ]
    maps_real = jnp.concatenate([part[0] for part in parts], axis=0)
    maps_imag = jnp.concatenate([part[1] for part in parts], axis=0)
    maps_ref[...] = jnp.concatenate([maps_real, maps_imag], axis=0).astype(BF16)
    real, imag = split_complex(read_rows(arrived, pitch, coils * count, count, slots), lines)
    mask = over_coils(mask_ref[...], 2 * coils)
    images = spread(maps_real, maps_imag, real, imag, coils)
    images = masked_normal(images, table_ref, minus_ref, plus_ref, mask)
    turned = collect(maps_real, maps_imag, images, coils)
    begun = collect(maps_real, maps_imag, images_ref[...].astype(F32), coils)
    power = coil_sum(maps_real * maps_real + maps_imag * maps_imag, coils)
    leaving[...] = jnp.zeros_like(leaving)
    values = []
    for value in (*begun, *turned, power):
        values += lane_chunks(value)
    write_rows(leaving, out_ref.shape[2], values)
    message = leaving[...].astype(BF16).reshape(slots, *out_ref.shape[2:])
    for device in range(out_ref.shape[1]):
        out_ref[:, device] = message


def unpack_sum(sent_ref, scratch):
    total = sent_ref[:, 0].astype(F32)
    for device in range(1, sent_ref.shape[1]):
        total = total + sent_ref[:, device].astype(F32)
    scratch[...] = total.reshape(scratch.shape)


def read_pair(scratch, pitch, first, count, rows):
    real = jnp.concatenate(read_rows(scratch, pitch, first, count, rows), axis=1)
    imag = jnp.concatenate(read_rows(scratch, pitch, first + count, count, rows), axis=1)
    return jnp.concatenate([real, imag], axis=0)


def first_refine_kernel(
    lines, rows, sent_ref, first_ref, second_ref, columns_ref, out_ref, model_ref, arrived, leaving
):
    unpack_sum(sent_ref, arrived)
    width = padded(lines, LANES)
    count = width // LANES
    picture = round_bf(read_pair(arrived, sent_ref.shape[2], 0, count, rows))
    hidden = hidden_state(picture, first_ref.at[0], column(columns_ref, 0, first_ref.shape[1]))
    valid = valid_lanes(hidden.shape[0], width, lines)
    hidden = hidden * jax.nn.sigmoid(hidden)
    bias = column(columns_ref, 2 * CASCADES, 2 * rows)
    model = second_conv(hidden, second_ref.at[0], bias, rows, valid)
    model_ref[...] = model.astype(BF16)
    leaving[...] = jnp.zeros_like(leaving)
    real, imag = halves(model)
    write_rows(leaving, out_ref.shape[1], lane_chunks(real) + lane_chunks(imag))
    out_ref[...] = leaving[...].astype(BF16).reshape(out_ref.shape)


def slots_kernel(
    lines,
    rows,
    sent_ref,
    model_ref,
    cotangent_ref,
    first_ref,
    first_t_ref,
    second_ref,
    second_t_ref,
    columns_ref,
    image_ref,
    spread_ref,
    arrived,
):
    unpack_sum(sent_ref, arrived)
    width = padded(lines, LANES)
    count = width // LANES
    pitch = sent_ref.shape[2]
    begun = read_pair(arrived, pitch, 0, count, rows)
    turned = read_pair(arrived, pitch, 2 * count, count, rows)
    power = jnp.concatenate(read_rows(arrived, pitch, 4 * count, count, rows), axis=1)
    power = jnp.concatenate([power, power], axis=0)
    cotangent = jnp.concatenate(
        split_complex(lane_chunks(cotangent_ref[...].astype(F32)), lines), axis=0
    )
    model = model_ref[...].astype(F32)
    tall = first_ref.shape[1]
    weight = [column(columns_ref, CASCADES + cascade, 2 * rows) for cascade in range(CASCADES)]

    share = [jnp.ones_like(weight[0])]
    for cascade in range(CASCADES):
        share.append(share[cascade] - weight[cascade] * (share[cascade] - 1.0))

    def slopes(hidden):
        gate = jax.nn.sigmoid(hidden)
        return hidden * gate, gate * (1.0 + hidden * (1.0 - gate))

    hidden = hidden_state(round_bf(begun), first_ref.at[0], column(columns_ref, 0, tall))
    valid = valid_lanes(hidden.shape[0], width, lines)
    unused, slope_first = slopes(hidden)
    picture = round_bf(share[1] * begun + power * model)
    hidden = hidden_state(picture, first_ref.at[1], column(columns_ref, 1, tall))
    active, slope_second = slopes(hidden)
    bias = column(columns_ref, 2 * CASCADES + 1, 2 * rows)
    later = round_bf(second_conv(active, second_ref.at[1], bias, rows, valid))
    image_ref[...] = share[2] * begun + power * (model + later)

    through = power * cotangent
    back_second = round_bf(
        pull_back(through, slope_second, first_t_ref.at[1], second_t_ref.at[1], rows, valid)
    )
    through = through - weight[1] * turned + power * back_second
    back_first = round_bf(
        pull_back(through, slope_first, first_t_ref.at[0], second_t_ref.at[0], rows, valid)
    )
    kept = (1.0 - weight[0], 1.0 - weight[1])
    of_cotangent = weight[1] + weight[0] * kept[1] + kept[0] * kept[1]
    of_second = weight[0] + kept[0]
    spread_ref[...] = of_cotangent * cotangent + of_second * back_second + back_first


def normal_kernel(
    coils,
    slots,
    sent_ref,
    maps_ref,
    spread_ref,
    mask_ref,
    table_ref,
    minus_ref,
    plus_ref,
    out_ref,
    arrived,
    leaving,
):
    arrived[...] = sent_ref[...].astype(F32).reshape(arrived.shape)
    count = maps_ref.shape[1] // LANES
    real, imag = halves(read_pair(arrived, sent_ref.shape[1], 0, count, slots))
    maps_real, maps_imag = halves(maps_ref[...].astype(F32))
    mask = over_coils(mask_ref[...], 2 * coils)
    images = spread(maps_real, maps_imag, real, imag, coils)
    images = masked_normal(images, table_ref, minus_ref, plus_ref, mask)
    leaving[...] = jnp.zeros_like(leaving)
    values = []
    for value in (*collect(maps_real, maps_imag, images, coils), *halves(spread_ref[...])):
        values += lane_chunks(value)
    write_rows(leaving, out_ref.shape[2], values)
    message = leaving[...].astype(BF16).reshape(slots, *out_ref.shape[2:])
    for device in range(out_ref.shape[1]):
        out_ref[:, device] = message


def end_kernel(
    coils,
    slots,
    lines,
    columns_ref,
    sent_ref,
    image_ref,
    maps_ref,
    mask_ref,
    table_ref,
    minus_ref,
    picture_ref,
    grad_ref,
    arrived,
):
    count = maps_ref.shape[1] // LANES
    pitch = sent_ref.shape[2]
    arrived[...] = sent_ref[:, 0].astype(F32).reshape(arrived.shape)
    real, imag = halves(read_pair(arrived, pitch, 2 * count, count, slots))
    maps_real, maps_imag = halves(maps_ref[...].astype(F32))
    images = spread(maps_real, maps_imag, real, imag, coils)
    spectrum = depth_apply(line_apply(images, table_ref, -1.0), minus_ref)
    spectrum = spectrum * over_coils(mask_ref[...], 2 * coils)
    chunks = join_complex(*halves(spectrum), lines)
    write_rows(grad_ref, len(chunks), chunks)

    unpack_sum(sent_ref, arrived)
    turned = read_pair(arrived, pitch, 0, count, slots)
    picture = image_ref[...] - column(columns_ref, CASCADES + 1, turned.shape[0]) * turned
    for index, chunk in enumerate(join_complex(*halves(picture), lines)):
        picture_ref[:, index * LANES : (index + 1) * LANES] = chunk


def call(kernel, name, operands, outs, scratch, flops, vmem_bytes=VMEM_BYTES):
    moved = sum(math.prod(item.shape) * item.dtype.itemsize for item in (*operands, *outs))
    return pl.pallas_call(
        kernel,
        name=name,
        out_shape=tuple(outs),
        in_specs=[pl.BlockSpec(memory_space=pltpu.VMEM) for item in operands],
        out_specs=tuple(pl.BlockSpec(memory_space=pltpu.VMEM) for item in outs),
        scratch_shapes=[pltpu.VMEM(shape, F32) for shape in scratch],
        compiler_params=pltpu.CompilerParams(vmem_limit_bytes=vmem_bytes),
        cost_estimate=pl.CostEstimate(flops=flops, bytes_accessed=moved, transcendentals=0),
    )(*operands)


def body(
    kspace, coil_maps, sampling, dc_weight, kernel_in, bias_in, kernel_out, bias_out, cotangent
):
    coils, slots = kspace.shape[:2]
    rows, two_lines = coil_maps.shape[2:]
    lines = two_lines // 2
    channels = bias_in.shape[1]
    coil_devices = lax.axis_size("coil")
    width = padded(lines, LANES)
    count = width // LANES
    planes = coils * slots
    both = ("section", "coil")

    table = jnp.asarray(line_constant(lines))
    minus = jnp.asarray(depth_constant(coils, slots, VOLUMES, -1.0))
    plus = jnp.asarray(depth_constant(coils, slots, VOLUMES, 1.0))
    repeat, place, offset = (jnp.asarray(item) for item in conv_constants(rows, channels))
    mask = sampling.astype(F32).reshape(slots, lines)
    mask = jnp.pad(mask, ((0, 0), (0, width - lines)))
    taps = jnp.concatenate(
        [
            kernel_in.transpose(2, 0, 1, 3).reshape(channels, -1),
            kernel_out.transpose(3, 0, 1, 2).reshape(channels, -1),
            bias_in.T,
            jnp.broadcast_to(dc_weight[None, :], (channels, CASCADES)),
            jnp.pad(bias_out.T, ((0, channels - bias_out.shape[1]), (0, 0))),
        ],
        axis=1,
    )
    taps = jnp.pad(taps, ((0, 0), (0, place.shape[0] - taps.shape[1])))

    def shape(*dims, kind=F32):
        return jax.ShapeDtypeStruct(dims, kind)

    line_flops = 2 * (2 * planes) * width * (2 * width)

    pitch = padded((coils + 1) * (two_lines // LANES), 16)
    (packed,) = call(
        functools.partial(pack_kernel, coils, rows, pitch),
        "pack_maps",
        (coil_maps.reshape(coils * rows, two_lines), cotangent.reshape(rows, two_lines)),
        [shape(rows, pitch, LANES, kind=BF16)],
        [(rows * pitch, LANES)],
        1000,
        PACK_VMEM_BYTES,
    )
    arrived = lax.all_to_all(packed, "section", 0, 0, tiled=True)

    tall, wide = channels * rows, offset.shape[1]
    images, first, first_t, second, second_t, columns = call(
        functools.partial(begin_kernel, coils, lines, rows),
        "measured_images",
        (kspace.reshape(planes, two_lines), mask, table, plus, taps, repeat, place, offset),
        [
            shape(2 * planes, width, kind=BF16),
            shape(CASCADES, tall, wide, kind=BF16),
            shape(CASCADES, 6 * rows, tall, kind=BF16),
            shape(CASCADES, 6 * rows, tall, kind=BF16),
            shape(CASCADES, tall, wide, kind=BF16),
            shape(tall, place.shape[0]),
        ],
        [],
        2 * line_flops,
    )

    depth_pitch = padded(5 * count, 16)
    partial, maps = call(
        functools.partial(rows_kernel, coils, slots, lines, pitch),
        "combine_rows",
        (arrived, images, mask, table, minus, plus),
        [
            shape(slots, coil_devices, depth_pitch, LANES, kind=BF16),
            shape(2 * planes, width, kind=BF16),
        ],
        [(slots * pitch, LANES), (slots * depth_pitch, LANES)],
        3 * line_flops,
    )
    partial = partial.reshape(slots * coil_devices, depth_pitch, LANES)
    partial = lax.all_to_all(partial, both, 0, 0, tiled=True)
    partial = partial.reshape(rows, coil_devices, depth_pitch, LANES)

    model_pitch = padded(2 * count, 8)
    moved, model = call(
        functools.partial(first_refine_kernel, lines, rows),
        "refine_first",
        (partial, first, second, columns),
        [shape(rows, model_pitch, LANES, kind=BF16), shape(2 * rows, width, kind=BF16)],
        [(rows * depth_pitch, LANES), (rows * model_pitch, LANES)],
        4 * tall * wide * width,
    )
    moved = lax.all_to_all(moved, "section", 0, 0, tiled=True)

    image, pulled = call(
        functools.partial(slots_kernel, lines, rows),
        "refine_and_back",
        (
            partial,
            model,
            cotangent.reshape(rows, two_lines),
            first,
            first_t,
            second,
            second_t,
            columns,
        ),
        [shape(2 * rows, width), shape(2 * rows, width)],
        [(rows * depth_pitch, LANES)],
        14 * tall * wide * width,
    )

    end_pitch = padded(4 * count, 16)
    (partial,) = call(
        functools.partial(normal_kernel, coils, slots),
        "masked_normal",
        (moved, maps, pulled, mask, table, minus, plus),
        [shape(slots, coil_devices, end_pitch, LANES, kind=BF16)],
        [(slots * model_pitch, LANES), (slots * end_pitch, LANES)],
        3 * line_flops,
    )
    partial = partial.reshape(slots * coil_devices, end_pitch, LANES)
    partial = lax.all_to_all(partial, both, 0, 0, tiled=True)
    partial = partial.reshape(rows, coil_devices, end_pitch, LANES)

    image, grad = call(
        functools.partial(end_kernel, coils, slots, lines),
        "outputs",
        (columns, partial, image, maps, mask, table, minus),
        [shape(rows, two_lines), shape(planes * (two_lines // LANES), LANES)],
        [(rows * end_pitch, LANES)],
        2 * line_flops,
    )
    return image.reshape(1, rows, two_lines), grad.reshape(coils, slots, 1, two_lines)


def solution(mesh):
    return jax.shard_map(
        body,
        mesh=mesh,
        in_specs=(
            P("coil", None, "section", None),
            P("coil", "section", None, None),
            P(),
            P(),
            P(),
            P(),
            P(),
            P(),
            P("section", None, None),
        ),
        out_specs=(P("section", None, None), P("coil", None, "section", None)),
        check_vma=False,
    )
```

```python
import functools
import math

import jax
import jax.numpy as jnp
import ml_dtypes
import numpy as np
from jax import lax
from jax.experimental import pallas as pl
from jax.experimental.pallas import tpu as pltpu
from jax.sharding import PartitionSpec as P

CASCADES = 2
VOLUMES = 2
LANES = 128
VMEM_BYTES = 48 * 1024 * 1024
LARGE_VMEM_BYTES = 60 * 1024 * 1024

F32 = jnp.float32
BF16 = jnp.bfloat16


def padded(size, unit):
    return -(-size // unit) * unit


def dft_parts(count):
    indices = np.arange(count)
    angles = (indices[:, None] * indices[None, :] % count) * (2.0 * math.pi / count)
    factor = 1.0 / math.sqrt(count)
    return np.cos(angles) * factor, np.sin(angles) * factor


def line_constant(lines):
    width = padded(lines, LANES)
    cosine, sine = dft_parts(lines)
    table = np.zeros((width, 2 * width), np.float32)
    table[:lines, :lines] = cosine
    table[:lines, width : width + lines] = sine
    return table.astype(ml_dtypes.bfloat16)


def depth_constant(coils, slots, volumes, sign):
    cosine, sine = dft_parts(slots // volumes)
    spread_over = np.eye(coils * volumes)
    real, imag = np.kron(spread_over, cosine), sign * np.kron(spread_over, sine)
    return np.block([[real, -imag], [imag, real]]).astype(np.float32).astype(ml_dtypes.bfloat16)


def conv_constants(rows, channels):
    groups = 6
    width = padded(groups * rows, LANES)
    repeat = np.kron(np.eye(channels), np.ones((rows, 1))).astype(np.float32)
    repeat = np.pad(repeat, ((0, 0), (0, padded(channels, LANES) - channels)))
    taps = CASCADES * 3
    place = np.zeros((padded(2 * taps * groups + 3 * CASCADES, LANES), 2 * taps * width), np.float32)
    for kind in range(2):
        for tap in range(taps):
            for group in range(groups):
                start = (kind * taps + tap) * width + group * rows
                place[(kind * taps + tap) * groups + group, start : start + rows] = 1.0
    offset = np.full((channels * rows, width), -9.0, np.float32)
    row = np.arange(rows)
    offset[:, : groups * rows] = np.tile(row[None, :] - row[:, None] + 1.0, (channels, groups))
    offset = np.clip(offset, -9.0, 9.0)
    return repeat, place.astype(ml_dtypes.bfloat16), offset


def lane_index(shape):
    return lax.broadcasted_iota(jnp.int32, shape, len(shape) - 1)


def split_complex(chunks, lines):
    whole, rest = divmod(lines, LANES)
    count = padded(lines, LANES) // LANES
    if rest == 0:
        return jnp.concatenate(chunks[:count], 1), jnp.concatenate(chunks[count:], 1)
    lane = lane_index(chunks[0].shape)
    real = chunks[:whole] + [jnp.where(lane < rest, chunks[whole], 0.0)]
    turned = [pltpu.roll(chunk, LANES - rest, 1) for chunk in chunks[whole:]]
    turned.append(jnp.zeros_like(turned[0]))
    imag = [jnp.where(lane < LANES - rest, turned[k], turned[k + 1]) for k in range(count)]
    imag[-1] = jnp.where(lane < rest, imag[-1], 0.0)
    return jnp.concatenate(real, 1), jnp.concatenate(imag, 1)


def lane_chunks(value):
    return [value[:, start : start + LANES] for start in range(0, value.shape[1], LANES)]


def join_complex(real, imag, lines):
    whole, rest = divmod(lines, LANES)
    real, imag = lane_chunks(real), lane_chunks(imag)
    if rest == 0:
        return real + imag
    lane = lane_index(real[0].shape)
    turned = [real[whole]] + [pltpu.roll(chunk, rest, 1) for chunk in imag]
    mixed = [jnp.where(lane < rest, turned[k], turned[k + 1]) for k in range(len(imag))]
    return (real[:whole] + mixed)[: 2 * lines // LANES]


def halves(stacked):
    half = stacked.shape[0] // 2
    return stacked[:half], stacked[half:]


def line_apply(stacked, table_ref, sign):
    mixed = jnp.dot(stacked.astype(BF16), table_ref[...], preferred_element_type=F32)
    width = table_ref.shape[1] // 2
    top, bottom = halves(mixed)
    return jnp.concatenate(
        [
            top[:, :width] - sign * bottom[:, width:],
            bottom[:, :width] + sign * top[:, width:],
        ],
        axis=0,
    )


def depth_apply(stacked, depth_ref):
    return jnp.dot(depth_ref[...], stacked.astype(BF16), preferred_element_type=F32)


def over_coils(value, coils):
    return jnp.concatenate([value] * coils, axis=0)


def coil_sum(value, coils):
    slots = value.shape[0] // coils
    total = value[:slots]
    for coil in range(1, coils):
        total = total + value[coil * slots : (coil + 1) * slots]
    return total


def over_rows(parts, coils):
    return jnp.concatenate([part for part in parts for coil in range(coils)], axis=0)


def spread(maps_real, maps_imag, real, imag):
    return jnp.concatenate(
        [maps_real * real - maps_imag * imag, maps_real * imag + maps_imag * real], axis=0
    )


def collect(maps_real, maps_imag, images):
    real, imag = halves(images)
    return maps_real * real + maps_imag * imag, maps_real * imag - maps_imag * real


def blocks(value, count):
    size = value.shape[0] // count
    return [value[index * size : (index + 1) * size] for index in range(count)]


def row_sums(value, rows, coils):
    return [coil_sum(part, coils) for part in blocks(value, rows)]


def pick(parts, index):
    chosen = parts[0]
    for place in range(1, len(parts)):
        chosen = jnp.where(index == place, parts[place], chosen)
    return chosen


def own_volume(depth):
    return lax.div(lax.axis_index("section"), jnp.int32(depth))


def masked_normal(images, table_ref, minus_ref, plus_ref, mask):
    spectrum = depth_apply(line_apply(images, table_ref, -1.0), minus_ref)
    return line_apply(depth_apply(spectrum * mask, plus_ref), table_ref, 1.0)


def write_rows(scratch, pitch, values, first=0):
    for index, value in enumerate(values):
        scratch[pl.ds(first + index, value.shape[0], stride=pitch), :] = value


def read_rows(scratch, pitch, first, count, rows):
    return [scratch[pl.ds(first + index, rows, stride=pitch), :] for index in range(count)]


def shifted(value, step):
    if step == 0:
        return value
    width = value.shape[1]
    return pltpu.roll(value, (-step) % width, 1)


def stack_shifted(value, order):
    return jnp.concatenate([shifted(value, step) for step in order], axis=0).astype(BF16)


def add_shifted(value, order, rows):
    total = None
    for index, step in enumerate(order):
        part = shifted(value[index * rows : (index + 1) * rows], step)
        total = part if total is None else total + part
    return total


def hidden_state(image, first_ref, bias_column):
    stack = stack_shifted(image, (-1, 0, 1))
    return (
        jnp.dot(first_ref[:, : stack.shape[0]], stack, preferred_element_type=F32) + bias_column
    )


def second_conv(hidden, second_ref, bias_column, rows, valid):
    mixed = jnp.dot(
        second_ref[...], jnp.where(valid, hidden, 0.0).astype(BF16), preferred_element_type=F32
    )
    total = add_shifted(mixed, (-1, 0, 1), 2 * rows)
    return jnp.where(valid[: 2 * rows], total + bias_column, 0.0)


def pull_back(cotangent, slope, first_t_ref, second_t_ref, rows, valid):
    stack = stack_shifted(cotangent, (1, 0, -1))
    back = jnp.dot(second_t_ref[:, : stack.shape[0]], stack, preferred_element_type=F32)
    back = jnp.where(valid, back * slope, 0.0).astype(BF16)
    mixed = jnp.dot(first_t_ref[...], back, preferred_element_type=F32)
    total = add_shifted(mixed, (1, 0, -1), 2 * rows)
    return jnp.where(valid[: 2 * rows], total, 0.0)


def valid_lanes(rows, width, lines):
    return lane_index((rows, width)) < lines


def column(columns_ref, place, rows):
    at = 4 * 9 * CASCADES + place
    return columns_ref[:rows, at : at + 1]


def round_bf(value):
    return value.astype(BF16).astype(F32)


def pack_kernel(coils, depth, pitch, maps_ref, image_ref, out_ref, scratch):
    rows = image_ref.shape[0]
    count = maps_ref.shape[1] // LANES
    scratch[...] = jnp.zeros_like(scratch)
    image = image_ref[...].astype(F32)
    for coil in range(coils + 1):
        value = maps_ref[coil * rows : (coil + 1) * rows, :].astype(F32) if coil < coils else image
        for place, part in enumerate(blocks(value, rows // depth)):
            first = (place * (coils + 1) + coil) * count
            write_rows(scratch, pitch, lane_chunks(part), first)
    out_ref[...] = scratch[...].astype(BF16).reshape(out_ref.shape)


def images_kernel(coils, lines, volumes, mask_ref, table_ref, plus_ref, *refs):
    depth = mask_ref.shape[0] // volumes
    volume = own_volume(depth)
    arrivals = []
    for ref in refs[:volumes]:
        parts = blocks(ref[...].astype(F32), coils * volumes)
        arrivals.append(
            jnp.concatenate(
                [pick(parts[coil * volumes : (coil + 1) * volumes], volume) for coil in range(coils)],
                axis=0,
            )
        )
    ordered = []
    for place in range(volumes):
        step = lax.rem(volume - place + volumes, jnp.int32(volumes))
        ordered.append(pick(arrivals, step))
    kspace = jnp.concatenate(ordered, axis=0)
    mask = over_coils(pick(blocks(mask_ref[...], volumes), volume), volumes * coils)
    real, imag = split_complex(lane_chunks(kspace), lines)
    measured = jnp.concatenate([real * mask, imag * mask], axis=0)
    images = line_apply(depth_apply(measured, plus_ref), table_ref, 1.0)
    refs[volumes][...] = images.astype(BF16)


def taps_kernel(
    rows,
    weight_ref,
    kernel_in_ref,
    kernel_out_ref,
    bias_in_ref,
    bias_out_ref,
    repeat_ref,
    place_ref,
    offset_ref,
    first_ref,
    first_t_ref,
    second_ref,
    second_t_ref,
    columns_ref,
    taps,
):
    taps[...] = jnp.zeros_like(taps)
    channels = kernel_in_ref.shape[2]
    at = 0
    for ref in (kernel_in_ref, kernel_out_ref):
        for index in range(ref.shape[0]):
            taps[at : at + 2, :channels] = ref[index]
            at += 2
    taps[at : at + CASCADES, :channels] = bias_in_ref[...]
    at += CASCADES
    for cascade in range(CASCADES):
        taps[at : at + 1, :] = jnp.full((1, taps.shape[1]), weight_ref[cascade], F32)
        at += 1
    taps[at : at + CASCADES, : bias_out_ref.shape[1]] = bias_out_ref[...]
    tall = lax.dot_general(
        repeat_ref[...],
        taps[...],
        (((1,), (1,)), ((), ())),
        precision=lax.Precision.HIGHEST,
        preferred_element_type=F32,
    )
    columns_ref[...] = tall
    wide = jnp.dot(tall.astype(BF16), place_ref[...], preferred_element_type=F32)
    offset = offset_ref[...]
    width = offset.shape[1]
    for cascade in range(CASCADES):
        for kind, straight, turned in ((0, first_ref, first_t_ref), (1, second_t_ref, second_ref)):
            total = jnp.zeros_like(offset)
            for tap in range(3):
                start = ((kind * CASCADES + cascade) * 3 + tap) * width
                wanted = float(tap if kind == 0 else 2 - tap)
                total = total + jnp.where(offset == wanted, wide[:, start : start + width], 0.0)
            straight[cascade] = total.astype(BF16)
            turned[cascade] = total.T[: 6 * rows].astype(BF16)


def rows_kernel(
    coils,
    lines,
    volumes,
    sent_ref,
    images_ref,
    mask_ref,
    table_ref,
    minus_ref,
    plus_ref,
    out_ref,
    maps_ref,
    *refs,
):
    handed, (arrived, leaving) = refs[: volumes - 1], refs[volumes - 1 :]
    depth, pitch = sent_ref.shape[:2]
    volume = own_volume(depth)
    arrived[...] = sent_ref[...].astype(F32).reshape(arrived.shape)
    count = 2 * lines // LANES
    parts, reals, imags = [], [], []
    for place in range(volumes):
        first = place * (coils + 1) * count
        for coil in range(coils):
            chunks = read_rows(arrived, pitch, first + coil * count, count, depth)
            parts.append(split_complex(chunks, lines))
        chunks = read_rows(arrived, pitch, first + coils * count, count, depth)
        real, imag = split_complex(chunks, lines)
        reals.append(real)
        imags.append(imag)
    maps_real = jnp.concatenate([part[0] for part in parts], axis=0)
    maps_imag = jnp.concatenate([part[1] for part in parts], axis=0)
    maps_ref[...] = jnp.concatenate([maps_real, maps_imag], axis=0).astype(BF16)
    real_parts, imag_parts = blocks(maps_real, volumes), blocks(maps_imag, volumes)
    for step, ref in enumerate(handed, 1):
        place = lax.rem(volume + step, jnp.int32(volumes))
        both = [pick(real_parts, place), pick(imag_parts, place)]
        ref[...] = jnp.concatenate(both, axis=0).astype(BF16)

    mask = over_coils(pick(blocks(mask_ref[...], volumes), volume), 2 * volumes * coils)
    images = spread(maps_real, maps_imag, over_rows(reals, coils), over_rows(imags, coils))
    images = masked_normal(images, table_ref, minus_ref, plus_ref, mask)
    found = [
        *collect(maps_real, maps_imag, images_ref[...].astype(F32)),
        *collect(maps_real, maps_imag, images),
        maps_real * maps_real + maps_imag * maps_imag,
    ]
    leaving[...] = jnp.zeros_like(leaving)
    sums = [row_sums(value, volumes, coils) for value in found]
    for place in range(volumes):
        chunks = [chunk for value in sums for chunk in lane_chunks(value[place])]
        write_rows(leaving, out_ref.shape[2], chunks, place * len(chunks))
    message = leaving[...].astype(BF16).reshape(depth, *out_ref.shape[2:])
    for device in range(out_ref.shape[1]):
        out_ref[:, device] = message


def unpack_sum(sent_ref, scratch):
    total = sent_ref[:, 0].astype(F32)
    for device in range(1, sent_ref.shape[1]):
        total = total + sent_ref[:, device].astype(F32)
    scratch[...] = total.reshape(scratch.shape)


def read_image(scratch, pitch, first, count, depth):
    return jnp.concatenate(read_rows(scratch, pitch, first, count, depth), axis=1)


def read_places(scratch, pitch, first, period, count, depth, volumes):
    parts = [
        read_image(scratch, pitch, first + place * period, count, depth) for place in range(volumes)
    ]
    return jnp.concatenate(parts, axis=0)


def read_complex(scratch, pitch, first, period, count, depth, volumes):
    real = read_places(scratch, pitch, first, period, count, depth, volumes)
    imag = read_places(scratch, pitch, first + count, period, count, depth, volumes)
    return jnp.concatenate([real, imag], axis=0)


def first_refine_kernel(
    lines,
    volumes,
    sent_ref,
    first_ref,
    second_ref,
    columns_ref,
    out_ref,
    model_ref,
    arrived,
    leaving,
):
    unpack_sum(sent_ref, arrived)
    depth, pitch = sent_ref.shape[0], sent_ref.shape[2]
    rows = depth * volumes
    width = padded(lines, LANES)
    count = width // LANES
    picture = round_bf(read_complex(arrived, pitch, 0, 5 * count, count, depth, volumes))
    hidden = hidden_state(picture, first_ref.at[0], column(columns_ref, 0, first_ref.shape[1]))
    valid = valid_lanes(hidden.shape[0], width, lines)
    hidden = hidden * jax.nn.sigmoid(hidden)
    bias = column(columns_ref, 2 * CASCADES, 2 * rows)
    model = second_conv(hidden, second_ref.at[0], bias, rows, valid)
    model_ref[...] = model.astype(BF16)
    leaving[...] = jnp.zeros_like(leaving)
    real, imag = halves(model)
    for place, pair in enumerate(zip(blocks(real, volumes), blocks(imag, volumes))):
        chunks = lane_chunks(pair[0]) + lane_chunks(pair[1])
        write_rows(leaving, out_ref.shape[1], chunks, place * len(chunks))
    out_ref[...] = leaving[...].astype(BF16).reshape(out_ref.shape)


def slots_kernel(
    lines,
    volumes,
    sent_ref,
    model_ref,
    cotangent_ref,
    first_ref,
    first_t_ref,
    second_ref,
    second_t_ref,
    columns_ref,
    image_ref,
    spread_ref,
    arrived,
):
    unpack_sum(sent_ref, arrived)
    depth, pitch = sent_ref.shape[0], sent_ref.shape[2]
    rows = depth * volumes
    width = padded(lines, LANES)
    count = width // LANES
    begun = read_complex(arrived, pitch, 0, 5 * count, count, depth, volumes)
    turned = read_complex(arrived, pitch, 2 * count, 5 * count, count, depth, volumes)
    power = read_places(arrived, pitch, 4 * count, 5 * count, count, depth, volumes)
    power = jnp.concatenate([power, power], axis=0)
    cotangent = jnp.concatenate(
        split_complex(lane_chunks(cotangent_ref[...].astype(F32)), lines), axis=0
    )
    model = model_ref[...].astype(F32)
    tall = first_ref.shape[1]
    weight = [column(columns_ref, CASCADES + cascade, 2 * rows) for cascade in range(CASCADES)]

    share = [jnp.ones_like(weight[0])]
    for cascade in range(CASCADES):
        share.append(share[cascade] - weight[cascade] * (share[cascade] - 1.0))

    def slopes(hidden):
        gate = jax.nn.sigmoid(hidden)
        return hidden * gate, gate * (1.0 + hidden * (1.0 - gate))

    hidden = hidden_state(round_bf(begun), first_ref.at[0], column(columns_ref, 0, tall))
    valid = valid_lanes(hidden.shape[0], width, lines)
    unused, slope_first = slopes(hidden)
    picture = round_bf(share[1] * begun + power * model)
    hidden = hidden_state(picture, first_ref.at[1], column(columns_ref, 1, tall))
    active, slope_second = slopes(hidden)
    bias = column(columns_ref, 2 * CASCADES + 1, 2 * rows)
    later = round_bf(second_conv(active, second_ref.at[1], bias, rows, valid))
    image_ref[...] = share[2] * begun + power * (model + later)

    through = power * cotangent
    back_second = round_bf(
        pull_back(through, slope_second, first_t_ref.at[1], second_t_ref.at[1], rows, valid)
    )
    through = through - weight[1] * turned + power * back_second
    back_first = round_bf(
        pull_back(through, slope_first, first_t_ref.at[0], second_t_ref.at[0], rows, valid)
    )
    kept = (1.0 - weight[0], 1.0 - weight[1])
    of_cotangent = weight[1] + weight[0] * kept[1] + kept[0] * kept[1]
    of_second = weight[0] + kept[0]
    spread_ref[...] = of_cotangent * cotangent + of_second * back_second + back_first


def normal_kernel(
    coils,
    lines,
    volumes,
    sent_ref,
    maps_ref,
    spread_ref,
    mask_ref,
    table_ref,
    minus_ref,
    plus_ref,
    out_ref,
    arrived,
    leaving,
):
    arrived[...] = sent_ref[...].astype(F32).reshape(arrived.shape)
    depth, pitch = sent_ref.shape[:2]
    volume = own_volume(depth)
    count = maps_ref.shape[1] // LANES
    firsts = [place * 2 * count for place in range(volumes)]
    reals = [read_image(arrived, pitch, first, count, depth) for first in firsts]
    imags = [read_image(arrived, pitch, first + count, count, depth) for first in firsts]
    maps_real, maps_imag = halves(maps_ref[...].astype(F32))
    mask = over_coils(pick(blocks(mask_ref[...], volumes), volume), 2 * volumes * coils)
    images = spread(maps_real, maps_imag, over_rows(reals, coils), over_rows(imags, coils))
    images = masked_normal(images, table_ref, minus_ref, plus_ref, mask)
    found = [row_sums(value, volumes, coils) for value in collect(maps_real, maps_imag, images)]
    leaving[...] = jnp.zeros_like(leaving)
    pitch = out_ref.shape[2]
    first = 0
    for place in range(volumes):
        chunks = join_complex(found[0][place], found[1][place], lines)
        for target in range(volumes):
            kept = [jnp.where(volume == target, chunk, 0.0) for chunk in chunks]
            write_rows(leaving, pitch, kept, target * depth * pitch + first)
        first += len(chunks)
    write_rows(leaving, pitch, join_complex(*halves(spread_ref[...]), lines), first)
    message = leaving[...].astype(BF16).reshape(out_ref.shape[0], *out_ref.shape[2:])
    for device in range(out_ref.shape[1]):
        out_ref[:, device] = message


def end_kernel(
    coils,
    lines,
    volumes,
    columns_ref,
    sent_ref,
    image_ref,
    mask_ref,
    table_ref,
    minus_ref,
    maps_ref,
    *refs,
):
    handed, (picture_ref, grad_ref, arrived) = refs[: volumes - 1], refs[volumes - 1 :]
    slots, pitch = sent_ref.shape[0], sent_ref.shape[2]
    depth = slots // volumes
    volume = own_volume(depth)
    count = 2 * lines // LANES
    own = maps_ref[...].astype(F32)
    sources = [[pick(blocks(part, volumes), volume) for part in halves(own)]]
    sources += [halves(ref[...].astype(F32)) for ref in handed]
    maps = []
    for part in range(2):
        ordered = []
        for place in range(volumes):
            step = lax.rem(volume - place + volumes, jnp.int32(volumes))
            ordered.append(blocks(pick([source[part] for source in sources], step), coils))
        maps.append(
            jnp.concatenate([ordered[v][coil] for coil in range(coils) for v in range(volumes)], 0)
        )
    arrived[...] = sent_ref[:, 0].astype(F32).reshape(arrived.shape)
    chunks = read_rows(arrived, pitch, volumes * count, count, slots)
    real, imag = split_complex(chunks, lines)
    images = spread(*maps, over_coils(real, coils), over_coils(imag, coils))
    spectrum = depth_apply(line_apply(images, table_ref, -1.0), minus_ref)
    spectrum = spectrum * over_coils(mask_ref[...], 2 * coils)
    chunks = join_complex(*halves(spectrum), lines)
    write_rows(grad_ref, len(chunks), chunks)

    unpack_sum(sent_ref, arrived)
    picture = image_ref[...]
    scale = column(columns_ref, CASCADES + 1, picture.shape[0])
    parts = [[], []]
    size = depth * pitch
    total = arrived[:size]
    for other in range(1, volumes):
        total = total + arrived[other * size : (other + 1) * size]
    arrived[:size] = total
    for place in range(volumes):
        chunks = read_rows(arrived, pitch, place * count, count, depth)
        for part, value in zip(parts, split_complex(chunks, lines)):
            part.append(value)
    picture = picture - scale * jnp.concatenate(parts[0] + parts[1], axis=0)
    for index, chunk in enumerate(join_complex(*halves(picture), lines)):
        picture_ref[:, index * LANES : (index + 1) * LANES] = chunk


def call(kernel, name, operands, outs, scratch, flops, vmem_bytes=VMEM_BYTES, scalars=0):
    spaces = [pltpu.SMEM] * scalars + [pltpu.VMEM] * (len(operands) - scalars)
    moved = sum(math.prod(item.shape) * item.dtype.itemsize for item in (*operands, *outs))
    return pl.pallas_call(
        kernel,
        name=name,
        out_shape=tuple(outs),
        in_specs=[pl.BlockSpec(memory_space=space) for space in spaces],
        out_specs=tuple(pl.BlockSpec(memory_space=pltpu.VMEM) for item in outs),
        scratch_shapes=[pltpu.VMEM(shape, F32) for shape in scratch],
        compiler_params=pltpu.CompilerParams(vmem_limit_bytes=vmem_bytes),
        cost_estimate=pl.CostEstimate(flops=flops, bytes_accessed=moved, transcendentals=0),
    )(*operands)


def body(
    kspace, coil_maps, sampling, dc_weight, kernel_in, bias_in, kernel_out, bias_out, cotangent
):
    coils, slots = kspace.shape[:2]
    rows, two_lines = coil_maps.shape[2:]
    lines = two_lines // 2
    channels = bias_in.shape[1]
    coil_devices, sections = lax.axis_size("coil"), lax.axis_size("section")
    volumes = VOLUMES
    depth = slots // volumes
    width = padded(lines, LANES)
    count, whole_count = width // LANES, two_lines // LANES
    planes = coils * slots
    both = ("section", "coil")
    near = [[group * depth + t for t in range(depth)] for group in range(volumes)]
    span = depth * coil_devices
    near_both = [[group * span + t for t in range(span)] for group in range(volumes)]

    def from_group(value, step):
        shift = step * depth
        return lax.ppermute(value, "section", [(s, (s + shift) % sections) for s in range(sections)])

    def exchange(value, axes, groups):
        return lax.all_to_all(value, axes, 0, 0, tiled=True, axis_index_groups=groups)

    table = jnp.asarray(line_constant(lines))
    minus = jnp.asarray(depth_constant(coils, slots, volumes, -1.0))
    plus = jnp.asarray(depth_constant(coils, slots, volumes, 1.0))
    repeat, place, offset = (jnp.asarray(item) for item in conv_constants(rows, channels))
    mask = sampling.astype(F32).reshape(slots, lines)
    mask = jnp.pad(mask, ((0, 0), (0, width - lines)))

    def shape(*dims, kind=F32):
        return jax.ShapeDtypeStruct(dims, kind)

    line_flops = 2 * (2 * planes) * width * (2 * width)

    pitch = padded(volumes * (coils + 1) * whole_count, 16)
    (packed,) = call(
        functools.partial(pack_kernel, coils, depth, pitch),
        "pack_maps",
        (coil_maps.reshape(coils * rows, two_lines), cotangent.reshape(rows, two_lines)),
        [shape(depth, pitch, LANES, kind=BF16)],
        [(depth * pitch, LANES)],
        1000,
        LARGE_VMEM_BYTES,
    )
    samples = kspace.reshape(planes, two_lines)
    arrivals = [samples] + [from_group(samples, step) for step in range(1, volumes)]
    arrived = exchange(packed, "section", near)

    (images,) = call(
        functools.partial(images_kernel, coils, lines, volumes),
        "measured_images",
        (mask, table, plus, *arrivals),
        [shape(2 * planes, width, kind=BF16)],
        [],
        2 * line_flops,
    )

    depth_pitch = padded(volumes * 5 * count, 16)
    partial, maps, *handed = call(
        functools.partial(rows_kernel, coils, lines, volumes),
        "combine_rows",
        (arrived, images, mask, table, minus, plus),
        [
            shape(depth, coil_devices, depth_pitch, LANES, kind=BF16),
            shape(2 * planes, width, kind=BF16),
        ]
        + [shape(2 * planes // volumes, width, kind=BF16)] * (volumes - 1),
        [(depth * pitch, LANES), (depth * depth_pitch, LANES)],
        3 * line_flops,
    )
    kernel_in, kernel_out, partial = lax.optimization_barrier((kernel_in, kernel_out, partial))
    tall, wide = channels * rows, offset.shape[1]
    first, first_t, second, second_t, columns = call(
        functools.partial(taps_kernel, rows),
        "lay_out_taps",
        (
            dc_weight,
            kernel_in.transpose(0, 1, 3, 2).reshape(-1, 2, channels),
            kernel_out.reshape(-1, 2, channels),
            bias_in,
            bias_out,
            repeat,
            place,
            offset,
        ),
        [
            shape(CASCADES, tall, wide, kind=BF16),
            shape(CASCADES, 6 * rows, tall, kind=BF16),
            shape(CASCADES, 6 * rows, tall, kind=BF16),
            shape(CASCADES, tall, wide, kind=BF16),
            shape(tall, place.shape[0]),
        ],
        [(place.shape[0], repeat.shape[1])],
        2 * tall * place.shape[0] * place.shape[1],
        LARGE_VMEM_BYTES,
        1,
    )
    partial = exchange(partial.reshape(-1, depth_pitch, LANES), both, near_both)
    partial = partial.reshape(depth, coil_devices, depth_pitch, LANES)
    handed = [from_group(value, step) for step, value in enumerate(handed, 1)]

    model_pitch = padded(volumes * 2 * count, 16)
    moved, model = call(
        functools.partial(first_refine_kernel, lines, volumes),
        "refine_first",
        (partial, first, second, columns),
        [shape(depth, model_pitch, LANES, kind=BF16), shape(2 * rows, width, kind=BF16)],
        [(depth * depth_pitch, LANES), (depth * model_pitch, LANES)],
        4 * tall * wide * width,
    )
    moved = exchange(moved, "section", near)

    image, pulled = call(
        functools.partial(slots_kernel, lines, volumes),
        "refine_and_back",
        (
            partial,
            model,
            cotangent.reshape(rows, two_lines),
            first,
            first_t,
            second,
            second_t,
            columns,
        ),
        [shape(2 * rows, width), shape(2 * rows, width)],
        [(depth * depth_pitch, LANES)],
        14 * tall * wide * width,
    )

    end_pitch = padded((volumes + 1) * whole_count, 16)
    (partial,) = call(
        functools.partial(normal_kernel, coils, lines, volumes),
        "masked_normal",
        (moved, maps, pulled, mask, table, minus, plus),
        [shape(slots, coil_devices, end_pitch, LANES, kind=BF16)],
        [(depth * model_pitch, LANES), (slots * end_pitch, LANES)],
        3 * line_flops,
    )
    partial = exchange(partial.reshape(-1, end_pitch, LANES), both, None)
    partial = partial.reshape(slots, coil_devices, end_pitch, LANES)

    image, grad = call(
        functools.partial(end_kernel, coils, lines, volumes),
        "outputs",
        (columns, partial, image, mask, table, minus, maps, *handed),
        [shape(rows, two_lines), shape(planes * whole_count, LANES)],
        [(slots * end_pitch, LANES)],
        2 * line_flops,
    )
    return image.reshape(1, rows, two_lines), grad.reshape(coils, slots, 1, two_lines)


def solution(mesh):
    return jax.shard_map(
        body,
        mesh=mesh,
        in_specs=(
            P("coil", None, "section", None),
            P("coil", "section", None, None),
            P(),
            P(),
            P(),
            P(),
            P(),
            P(),
            P("section", None, None),
        ),
        out_specs=(P("section", None, None), P("coil", None, "section", None)),
        check_vma=False,
    )
```

```python
import functools
import math

import jax
import jax.numpy as jnp
import ml_dtypes
import numpy as np
from jax import lax
from jax.experimental import pallas as pl
from jax.experimental.pallas import tpu as pltpu
from jax.sharding import PartitionSpec as P

CASCADES = 2
VOLUMES = 2
LANES = 128
VMEM_BYTES = 48 * 1024 * 1024
LARGE_VMEM_BYTES = 60 * 1024 * 1024

F32 = jnp.float32
BF16 = jnp.bfloat16


def padded(size, unit):
    return -(-size // unit) * unit


def dft_parts(count):
    indices = np.arange(count)
    angles = (indices[:, None] * indices[None, :] % count) * (2.0 * math.pi / count)
    factor = 1.0 / math.sqrt(count)
    return np.cos(angles) * factor, np.sin(angles) * factor


def line_constant(lines):
    width = padded(lines, LANES)
    cosine, sine = dft_parts(lines)
    table = np.zeros((width, 2 * width), np.float32)
    table[:lines, :lines] = cosine
    table[:lines, width : width + lines] = sine
    return table.astype(ml_dtypes.bfloat16)


def depth_constant(coils, slots, volumes, sign):
    cosine, sine = dft_parts(slots // volumes)
    spread_over = np.eye(coils * volumes)
    real, imag = np.kron(spread_over, cosine), sign * np.kron(spread_over, sine)
    return np.block([[real, -imag], [imag, real]]).astype(np.float32).astype(ml_dtypes.bfloat16)


def conv_constants(rows, channels):
    groups = 6
    width = padded(groups * rows, LANES)
    repeat = np.kron(np.eye(channels), np.ones((rows, 1))).astype(np.float32)
    repeat = np.pad(repeat, ((0, 0), (0, padded(channels, LANES) - channels)))
    taps = CASCADES * 3
    place = np.zeros((padded(2 * taps * groups + 3 * CASCADES, LANES), 2 * taps * width), np.float32)
    for kind in range(2):
        for tap in range(taps):
            for group in range(groups):
                start = (kind * taps + tap) * width + group * rows
                place[(kind * taps + tap) * groups + group, start : start + rows] = 1.0
    offset = np.full((channels * rows, width), -9.0, np.float32)
    row = np.arange(rows)
    offset[:, : groups * rows] = np.tile(row[None, :] - row[:, None] + 1.0, (channels, groups))
    offset = np.clip(offset, -9.0, 9.0)
    return repeat, place.astype(ml_dtypes.bfloat16), offset


def lane_index(shape):
    return lax.broadcasted_iota(jnp.int32, shape, len(shape) - 1)


def split_complex(chunks, lines):
    whole, rest = divmod(lines, LANES)
    count = padded(lines, LANES) // LANES
    if rest == 0:
        return jnp.concatenate(chunks[:count], 1), jnp.concatenate(chunks[count:], 1)
    lane = lane_index(chunks[0].shape)
    real = chunks[:whole] + [jnp.where(lane < rest, chunks[whole], 0.0)]
    turned = [pltpu.roll(chunk, LANES - rest, 1) for chunk in chunks[whole:]]
    turned.append(jnp.zeros_like(turned[0]))
    imag = [jnp.where(lane < LANES - rest, turned[k], turned[k + 1]) for k in range(count)]
    imag[-1] = jnp.where(lane < rest, imag[-1], 0.0)
    return jnp.concatenate(real, 1), jnp.concatenate(imag, 1)


def lane_chunks(value):
    return [value[:, start : start + LANES] for start in range(0, value.shape[1], LANES)]


def join_complex(real, imag, lines):
    whole, rest = divmod(lines, LANES)
    real, imag = lane_chunks(real), lane_chunks(imag)
    if rest == 0:
        return real + imag
    lane = lane_index(real[0].shape)
    turned = [real[whole]] + [pltpu.roll(chunk, rest, 1) for chunk in imag]
    mixed = [jnp.where(lane < rest, turned[k], turned[k + 1]) for k in range(len(imag))]
    return (real[:whole] + mixed)[: 2 * lines // LANES]


def halves(stacked):
    half = stacked.shape[0] // 2
    return stacked[:half], stacked[half:]


def line_apply(stacked, table_ref, sign):
    mixed = jnp.dot(stacked.astype(BF16), table_ref[...], preferred_element_type=F32)
    width = table_ref.shape[1] // 2
    top, bottom = halves(mixed)
    return jnp.concatenate(
        [
            top[:, :width] - sign * bottom[:, width:],
            bottom[:, :width] + sign * top[:, width:],
        ],
        axis=0,
    )


def depth_apply(stacked, depth_ref):
    return jnp.dot(depth_ref[...], stacked.astype(BF16), preferred_element_type=F32)


def over_coils(value, coils):
    return jnp.concatenate([value] * coils, axis=0)


def coil_sum(value, coils):
    slots = value.shape[0] // coils
    total = value[:slots]
    for coil in range(1, coils):
        total = total + value[coil * slots : (coil + 1) * slots]
    return total


def over_rows(parts, coils):
    return jnp.concatenate([part for part in parts for coil in range(coils)], axis=0)


def spread(maps_real, maps_imag, real, imag):
    return jnp.concatenate(
        [maps_real * real - maps_imag * imag, maps_real * imag + maps_imag * real], axis=0
    )


def collect(maps_real, maps_imag, images):
    real, imag = halves(images)
    return maps_real * real + maps_imag * imag, maps_real * imag - maps_imag * real


def blocks(value, count):
    size = value.shape[0] // count
    return [value[index * size : (index + 1) * size] for index in range(count)]


def row_sums(value, rows, coils):
    return [coil_sum(part, coils) for part in blocks(value, rows)]


def pick(parts, index):
    chosen = parts[0]
    for place in range(1, len(parts)):
        chosen = jnp.where(index == place, parts[place], chosen)
    return chosen


def own_volume(depth):
    return lax.div(lax.axis_index("section"), jnp.int32(depth))


def masked_normal(images, table_ref, minus_ref, plus_ref, mask):
    spectrum = depth_apply(line_apply(images, table_ref, -1.0), minus_ref)
    return line_apply(depth_apply(spectrum * mask, plus_ref), table_ref, 1.0)


def write_rows(scratch, pitch, values, first=0):
    for index, value in enumerate(values):
        scratch[pl.ds(first + index, value.shape[0], stride=pitch), :] = value


def read_rows(scratch, pitch, first, count, rows):
    return [scratch[pl.ds(first + index, rows, stride=pitch), :] for index in range(count)]


def shifted(value, step):
    if step == 0:
        return value
    width = value.shape[1]
    return pltpu.roll(value, (-step) % width, 1)


def stack_shifted(value, order):
    return jnp.concatenate([shifted(value, step) for step in order], axis=0).astype(BF16)


def add_shifted(value, order, rows):
    total = None
    for index, step in enumerate(order):
        part = shifted(value[index * rows : (index + 1) * rows], step)
        total = part if total is None else total + part
    return total


def hidden_state(image, first_ref, bias_column):
    stack = stack_shifted(image, (-1, 0, 1))
    return (
        jnp.dot(first_ref[:, : stack.shape[0]], stack, preferred_element_type=F32) + bias_column
    )


def second_conv(hidden, second_ref, bias_column, rows, valid):
    mixed = jnp.dot(
        second_ref[...], jnp.where(valid, hidden, 0.0).astype(BF16), preferred_element_type=F32
    )
    total = add_shifted(mixed, (-1, 0, 1), 2 * rows)
    return jnp.where(valid[: 2 * rows], total + bias_column, 0.0)


def pull_back(cotangent, slope, first_t_ref, second_t_ref, rows, valid):
    stack = stack_shifted(cotangent, (1, 0, -1))
    back = jnp.dot(second_t_ref[:, : stack.shape[0]], stack, preferred_element_type=F32)
    back = jnp.where(valid, back * slope, 0.0).astype(BF16)
    mixed = jnp.dot(first_t_ref[...], back, preferred_element_type=F32)
    total = add_shifted(mixed, (1, 0, -1), 2 * rows)
    return jnp.where(valid[: 2 * rows], total, 0.0)


def valid_lanes(rows, width, lines):
    return lane_index((rows, width)) < lines


def column(columns_ref, place, rows):
    at = 4 * 9 * CASCADES + place
    return columns_ref[:rows, at : at + 1]


def round_bf(value):
    return value.astype(BF16).astype(F32)


def choose_volume(value, coils, volumes, volume):
    parts = blocks(value, coils * volumes)
    chosen = [pick(parts[coil * volumes : (coil + 1) * volumes], volume) for coil in range(coils)]
    return jnp.concatenate(chosen, axis=0)


def pack_kernel(coils, volumes, pitch, kspace_ref, maps_ref, image_ref, out_ref, *refs):
    handed, (scratch,) = refs[:-1], refs[-1:]
    rows = image_ref.shape[0]
    depth = rows // volumes
    volume = own_volume(depth)
    kspace = kspace_ref[...].astype(F32)
    for step, ref in enumerate(handed):
        other = lax.rem(volume + step, jnp.int32(volumes))
        ref[...] = choose_volume(kspace, coils, volumes, other).astype(BF16)
    count = maps_ref.shape[1] // LANES
    scratch[...] = jnp.zeros_like(scratch)
    image = image_ref[...].astype(F32)
    for coil in range(coils + 1):
        value = maps_ref[coil * rows : (coil + 1) * rows, :].astype(F32) if coil < coils else image
        for place, part in enumerate(blocks(value, volumes)):
            first = (place * (coils + 1) + coil) * count
            write_rows(scratch, pitch, lane_chunks(part), first)
    out_ref[...] = scratch[...].astype(BF16).reshape(out_ref.shape)


def images_kernel(coils, lines, volumes, mask_ref, table_ref, plus_ref, *refs):
    depth = mask_ref.shape[0] // volumes
    volume = own_volume(depth)
    arrivals = [ref[...].astype(F32) for ref in refs[:volumes]]
    ordered = []
    for place in range(volumes):
        step = lax.rem(volume - place + volumes, jnp.int32(volumes))
        ordered.append(pick(arrivals, step))
    kspace = jnp.concatenate(ordered, axis=0)
    mask = over_coils(pick(blocks(mask_ref[...], volumes), volume), volumes * coils)
    real, imag = split_complex(lane_chunks(kspace), lines)
    measured = jnp.concatenate([real * mask, imag * mask], axis=0)
    images = line_apply(depth_apply(measured, plus_ref), table_ref, 1.0)
    refs[volumes][...] = images.astype(BF16)


def taps_kernel(
    rows,
    volumes,
    weight_ref,
    maps_ref,
    kernel_in_ref,
    kernel_out_ref,
    bias_in_ref,
    bias_out_ref,
    repeat_ref,
    place_ref,
    offset_ref,
    first_ref,
    first_t_ref,
    second_ref,
    second_t_ref,
    columns_ref,
    *refs,
):
    handed, (taps,) = refs[:-1], refs[-1:]
    volume = own_volume(rows // volumes)
    maps = blocks(maps_ref[...].astype(F32), 2 * volumes)
    for step, ref in enumerate(handed, 1):
        place = lax.rem(volume + step, jnp.int32(volumes))
        both = [pick(maps[:volumes], place), pick(maps[volumes:], place)]
        ref[...] = jnp.concatenate(both, axis=0).astype(BF16)
    taps[...] = jnp.zeros_like(taps)
    channels = kernel_in_ref.shape[2]
    at = 0
    for ref in (kernel_in_ref, kernel_out_ref):
        for index in range(ref.shape[0]):
            taps[at : at + 2, :channels] = ref[index]
            at += 2
    taps[at : at + CASCADES, :channels] = bias_in_ref[...]
    at += CASCADES
    for cascade in range(CASCADES):
        taps[at : at + 1, :] = jnp.full((1, taps.shape[1]), weight_ref[cascade], F32)
        at += 1
    taps[at : at + CASCADES, : bias_out_ref.shape[1]] = bias_out_ref[...]
    tall = lax.dot_general(
        repeat_ref[...],
        taps[...],
        (((1,), (1,)), ((), ())),
        precision=lax.Precision.HIGHEST,
        preferred_element_type=F32,
    )
    columns_ref[...] = tall
    wide = jnp.dot(tall.astype(BF16), place_ref[...], preferred_element_type=F32)
    offset = offset_ref[...]
    width = offset.shape[1]
    for cascade in range(CASCADES):
        for kind, straight, turned in ((0, first_ref, first_t_ref), (1, second_t_ref, second_ref)):
            total = jnp.zeros_like(offset)
            for tap in range(3):
                start = ((kind * CASCADES + cascade) * 3 + tap) * width
                wanted = float(tap if kind == 0 else 2 - tap)
                total = total + jnp.where(offset == wanted, wide[:, start : start + width], 0.0)
            straight[cascade] = total.astype(BF16)
            turned[cascade] = total.T[: 6 * rows].astype(BF16)


def rows_kernel(
    coils,
    lines,
    volumes,
    sent_ref,
    images_ref,
    mask_ref,
    table_ref,
    minus_ref,
    plus_ref,
    out_ref,
    maps_ref,
    arrived,
    leaving,
):
    depth, pitch = sent_ref.shape[:2]
    volume = own_volume(depth)
    arrived[...] = sent_ref[...].astype(F32).reshape(arrived.shape)
    count = 2 * lines // LANES
    parts, reals, imags = [], [], []
    for place in range(volumes):
        first = place * (coils + 1) * count
        for coil in range(coils):
            chunks = read_rows(arrived, pitch, first + coil * count, count, depth)
            parts.append(split_complex(chunks, lines))
        chunks = read_rows(arrived, pitch, first + coils * count, count, depth)
        real, imag = split_complex(chunks, lines)
        reals.append(real)
        imags.append(imag)
    maps_real = jnp.concatenate([part[0] for part in parts], axis=0)
    maps_imag = jnp.concatenate([part[1] for part in parts], axis=0)
    maps_ref[...] = jnp.concatenate([maps_real, maps_imag], axis=0).astype(BF16)

    mask = over_coils(pick(blocks(mask_ref[...], volumes), volume), 2 * volumes * coils)
    images = spread(maps_real, maps_imag, over_rows(reals, coils), over_rows(imags, coils))
    images = masked_normal(images, table_ref, minus_ref, plus_ref, mask)
    found = [
        *collect(maps_real, maps_imag, images_ref[...].astype(F32)),
        *collect(maps_real, maps_imag, images),
        maps_real * maps_real + maps_imag * maps_imag,
    ]
    leaving[...] = jnp.zeros_like(leaving)
    sums = [row_sums(value, volumes, coils) for value in found]
    for place in range(volumes):
        chunks = [chunk for value in sums for chunk in lane_chunks(value[place])]
        write_rows(leaving, out_ref.shape[2], chunks, place * len(chunks))
    message = leaving[...].astype(BF16).reshape(depth, *out_ref.shape[2:])
    for device in range(out_ref.shape[1]):
        out_ref[:, device] = message


def unpack_sum(sent_ref, scratch):
    total = sent_ref[:, 0].astype(F32)
    for device in range(1, sent_ref.shape[1]):
        total = total + sent_ref[:, device].astype(F32)
    scratch[...] = total.reshape(scratch.shape)


def read_image(scratch, pitch, first, count, depth):
    return jnp.concatenate(read_rows(scratch, pitch, first, count, depth), axis=1)


def read_places(scratch, pitch, first, period, count, depth, volumes):
    parts = [
        read_image(scratch, pitch, first + place * period, count, depth) for place in range(volumes)
    ]
    return jnp.concatenate(parts, axis=0)


def read_complex(scratch, pitch, first, period, count, depth, volumes):
    real = read_places(scratch, pitch, first, period, count, depth, volumes)
    imag = read_places(scratch, pitch, first + count, period, count, depth, volumes)
    return jnp.concatenate([real, imag], axis=0)


def first_refine_kernel(
    lines,
    volumes,
    sent_ref,
    first_ref,
    second_ref,
    columns_ref,
    out_ref,
    model_ref,
    arrived,
    leaving,
):
    unpack_sum(sent_ref, arrived)
    depth, pitch = sent_ref.shape[0], sent_ref.shape[2]
    rows = depth * volumes
    width = padded(lines, LANES)
    count = width // LANES
    picture = round_bf(read_complex(arrived, pitch, 0, 5 * count, count, depth, volumes))
    hidden = hidden_state(picture, first_ref.at[0], column(columns_ref, 0, first_ref.shape[1]))
    valid = valid_lanes(hidden.shape[0], width, lines)
    hidden = hidden * jax.nn.sigmoid(hidden)
    bias = column(columns_ref, 2 * CASCADES, 2 * rows)
    model = second_conv(hidden, second_ref.at[0], bias, rows, valid)
    model_ref[...] = model.astype(BF16)
    leaving[...] = jnp.zeros_like(leaving)
    real, imag = halves(model)
    for place, pair in enumerate(zip(blocks(real, volumes), blocks(imag, volumes))):
        chunks = lane_chunks(pair[0]) + lane_chunks(pair[1])
        write_rows(leaving, out_ref.shape[1], chunks, place * len(chunks))
    out_ref[...] = leaving[...].astype(BF16).reshape(out_ref.shape)


def slots_kernel(
    lines,
    volumes,
    sent_ref,
    model_ref,
    cotangent_ref,
    first_ref,
    first_t_ref,
    second_ref,
    second_t_ref,
    columns_ref,
    image_ref,
    spread_ref,
    arrived,
):
    unpack_sum(sent_ref, arrived)
    depth, pitch = sent_ref.shape[0], sent_ref.shape[2]
    rows = depth * volumes
    width = padded(lines, LANES)
    count = width // LANES
    begun = read_complex(arrived, pitch, 0, 5 * count, count, depth, volumes)
    turned = read_complex(arrived, pitch, 2 * count, 5 * count, count, depth, volumes)
    power = read_places(arrived, pitch, 4 * count, 5 * count, count, depth, volumes)
    power = jnp.concatenate([power, power], axis=0)
    cotangent = jnp.concatenate(
        split_complex(lane_chunks(cotangent_ref[...].astype(F32)), lines), axis=0
    )
    model = model_ref[...].astype(F32)
    tall = first_ref.shape[1]
    weight = [column(columns_ref, CASCADES + cascade, 2 * rows) for cascade in range(CASCADES)]

    share = [jnp.ones_like(weight[0])]
    for cascade in range(CASCADES):
        share.append(share[cascade] - weight[cascade] * (share[cascade] - 1.0))

    def slopes(hidden):
        gate = jax.nn.sigmoid(hidden)
        return hidden * gate, gate * (1.0 + hidden * (1.0 - gate))

    hidden = hidden_state(round_bf(begun), first_ref.at[0], column(columns_ref, 0, tall))
    valid = valid_lanes(hidden.shape[0], width, lines)
    unused, slope_first = slopes(hidden)
    picture = round_bf(share[1] * begun + power * model)
    hidden = hidden_state(picture, first_ref.at[1], column(columns_ref, 1, tall))
    active, slope_second = slopes(hidden)
    bias = column(columns_ref, 2 * CASCADES + 1, 2 * rows)
    later = round_bf(second_conv(active, second_ref.at[1], bias, rows, valid))
    image_ref[...] = share[2] * begun + power * (model + later)

    through = power * cotangent
    back_second = round_bf(
        pull_back(through, slope_second, first_t_ref.at[1], second_t_ref.at[1], rows, valid)
    )
    through = through - weight[1] * turned + power * back_second
    back_first = round_bf(
        pull_back(through, slope_first, first_t_ref.at[0], second_t_ref.at[0], rows, valid)
    )
    kept = (1.0 - weight[0], 1.0 - weight[1])
    of_cotangent = weight[1] + weight[0] * kept[1] + kept[0] * kept[1]
    of_second = weight[0] + kept[0]
    spread_ref[...] = of_cotangent * cotangent + of_second * back_second + back_first


def normal_kernel(
    coils,
    lines,
    volumes,
    sent_ref,
    maps_ref,
    spread_ref,
    mask_ref,
    table_ref,
    minus_ref,
    plus_ref,
    out_ref,
    arrived,
    leaving,
):
    arrived[...] = sent_ref[...].astype(F32).reshape(arrived.shape)
    depth, pitch = sent_ref.shape[:2]
    volume = own_volume(depth)
    count = maps_ref.shape[1] // LANES
    firsts = [place * 2 * count for place in range(volumes)]
    reals = [read_image(arrived, pitch, first, count, depth) for first in firsts]
    imags = [read_image(arrived, pitch, first + count, count, depth) for first in firsts]
    maps_real, maps_imag = halves(maps_ref[...].astype(F32))
    mask = over_coils(pick(blocks(mask_ref[...], volumes), volume), 2 * volumes * coils)
    images = spread(maps_real, maps_imag, over_rows(reals, coils), over_rows(imags, coils))
    images = masked_normal(images, table_ref, minus_ref, plus_ref, mask)
    found = [row_sums(value, volumes, coils) for value in collect(maps_real, maps_imag, images)]
    leaving[...] = jnp.zeros_like(leaving)
    pitch = out_ref.shape[2]
    first = 0
    for place in range(volumes):
        chunks = join_complex(found[0][place], found[1][place], lines)
        for target in range(volumes):
            kept = [jnp.where(volume == target, chunk, 0.0) for chunk in chunks]
            write_rows(leaving, pitch, kept, target * depth * pitch + first)
        first += len(chunks)
    write_rows(leaving, pitch, join_complex(*halves(spread_ref[...]), lines), first)
    message = leaving[...].astype(BF16).reshape(out_ref.shape[0], *out_ref.shape[2:])
    for device in range(out_ref.shape[1]):
        out_ref[:, device] = message


def end_kernel(
    coils,
    lines,
    volumes,
    columns_ref,
    sent_ref,
    image_ref,
    mask_ref,
    table_ref,
    minus_ref,
    maps_ref,
    *refs,
):
    handed, (picture_ref, grad_ref, arrived) = refs[: volumes - 1], refs[volumes - 1 :]
    slots, pitch = sent_ref.shape[0], sent_ref.shape[2]
    depth = slots // volumes
    volume = own_volume(depth)
    count = 2 * lines // LANES
    own = maps_ref[...].astype(F32)
    sources = [[pick(blocks(part, volumes), volume) for part in halves(own)]]
    sources += [halves(ref[...].astype(F32)) for ref in handed]
    maps = []
    for part in range(2):
        ordered = []
        for place in range(volumes):
            step = lax.rem(volume - place + volumes, jnp.int32(volumes))
            ordered.append(blocks(pick([source[part] for source in sources], step), coils))
        maps.append(
            jnp.concatenate([ordered[v][coil] for coil in range(coils) for v in range(volumes)], 0)
        )
    arrived[...] = sent_ref[:, 0].astype(F32).reshape(arrived.shape)
    chunks = read_rows(arrived, pitch, volumes * count, count, slots)
    real, imag = split_complex(chunks, lines)
    images = spread(*maps, over_coils(real, coils), over_coils(imag, coils))
    spectrum = depth_apply(line_apply(images, table_ref, -1.0), minus_ref)
    spectrum = spectrum * over_coils(mask_ref[...], 2 * coils)
    chunks = join_complex(*halves(spectrum), lines)
    write_rows(grad_ref, len(chunks), chunks)

    unpack_sum(sent_ref, arrived)
    picture = image_ref[...]
    scale = column(columns_ref, CASCADES + 1, picture.shape[0])
    parts = [[], []]
    size = depth * pitch
    total = arrived[:size]
    for other in range(1, volumes):
        total = total + arrived[other * size : (other + 1) * size]
    arrived[:size] = total
    for place in range(volumes):
        chunks = read_rows(arrived, pitch, place * count, count, depth)
        for part, value in zip(parts, split_complex(chunks, lines)):
            part.append(value)
    picture = picture - scale * jnp.concatenate(parts[0] + parts[1], axis=0)
    for index, chunk in enumerate(join_complex(*halves(picture), lines)):
        picture_ref[:, index * LANES : (index + 1) * LANES] = chunk


def call(kernel, name, operands, outs, scratch, flops, vmem_bytes=VMEM_BYTES, scalars=0):
    spaces = [pltpu.SMEM] * scalars + [pltpu.VMEM] * (len(operands) - scalars)
    moved = sum(math.prod(item.shape) * item.dtype.itemsize for item in (*operands, *outs))
    return pl.pallas_call(
        kernel,
        name=name,
        out_shape=tuple(outs),
        in_specs=[pl.BlockSpec(memory_space=space) for space in spaces],
        out_specs=tuple(pl.BlockSpec(memory_space=pltpu.VMEM) for item in outs),
        scratch_shapes=[pltpu.VMEM(shape, F32) for shape in scratch],
        compiler_params=pltpu.CompilerParams(vmem_limit_bytes=vmem_bytes),
        cost_estimate=pl.CostEstimate(flops=flops, bytes_accessed=moved, transcendentals=0),
    )(*operands)


def body(
    kspace, coil_maps, sampling, dc_weight, kernel_in, bias_in, kernel_out, bias_out, cotangent
):
    coils, slots = kspace.shape[:2]
    rows, two_lines = coil_maps.shape[2:]
    lines = two_lines // 2
    channels = bias_in.shape[1]
    coil_devices, sections = lax.axis_size("coil"), lax.axis_size("section")
    volumes = VOLUMES
    depth = slots // volumes
    width = padded(lines, LANES)
    count, whole_count = width // LANES, two_lines // LANES
    planes = coils * slots
    both = ("section", "coil")
    near = [[group * depth + t for t in range(depth)] for group in range(volumes)]
    span = depth * coil_devices
    near_both = [[group * span + t for t in range(span)] for group in range(volumes)]

    def from_group(value, step):
        shift = step * depth
        return lax.ppermute(value, "section", [(s, (s + shift) % sections) for s in range(sections)])

    def exchange(value, axes, groups):
        return lax.all_to_all(value, axes, 0, 0, tiled=True, axis_index_groups=groups)

    table = jnp.asarray(line_constant(lines))
    minus = jnp.asarray(depth_constant(coils, slots, volumes, -1.0))
    plus = jnp.asarray(depth_constant(coils, slots, volumes, 1.0))
    repeat, place, offset = (jnp.asarray(item) for item in conv_constants(rows, channels))
    mask = sampling.astype(F32).reshape(slots, lines)
    mask = jnp.pad(mask, ((0, 0), (0, width - lines)))

    def shape(*dims, kind=F32):
        return jax.ShapeDtypeStruct(dims, kind)

    line_flops = 2 * (2 * planes) * width * (2 * width)

    pitch = padded(volumes * (coils + 1) * whole_count, 16)
    packed, *samples = call(
        functools.partial(pack_kernel, coils, volumes, pitch),
        "pack_maps",
        (
            kspace.reshape(planes, two_lines),
            coil_maps.reshape(coils * rows, two_lines),
            cotangent.reshape(rows, two_lines),
        ),
        [shape(depth, pitch, LANES, kind=BF16)]
        + [shape(coils * depth, two_lines, kind=BF16)] * volumes,
        [(depth * pitch, LANES)],
        1000,
        LARGE_VMEM_BYTES,
    )
    arrivals = samples[:1]
    arrivals += [from_group(value, step) for step, value in enumerate(samples[1:], 1)]
    arrived = exchange(packed, "section", near)

    (images,) = call(
        functools.partial(images_kernel, coils, lines, volumes),
        "measured_images",
        (mask, table, plus, *arrivals),
        [shape(2 * planes, width, kind=BF16)],
        [],
        2 * line_flops,
    )

    depth_pitch = padded(volumes * 5 * count, 16)
    partial, maps = call(
        functools.partial(rows_kernel, coils, lines, volumes),
        "combine_rows",
        (arrived, images, mask, table, minus, plus),
        [
            shape(depth, coil_devices, depth_pitch, LANES, kind=BF16),
            shape(2 * planes, width, kind=BF16),
        ],
        [(depth * pitch, LANES), (depth * depth_pitch, LANES)],
        3 * line_flops,
    )
    kernel_in, kernel_out, partial = lax.optimization_barrier((kernel_in, kernel_out, partial))
    tall, wide = channels * rows, offset.shape[1]
    first, first_t, second, second_t, columns, *handed = call(
        functools.partial(taps_kernel, rows, volumes),
        "lay_out_taps",
        (
            dc_weight,
            maps,
            kernel_in.transpose(0, 1, 3, 2).reshape(-1, 2, channels),
            kernel_out.reshape(-1, 2, channels),
            bias_in,
            bias_out,
            repeat,
            place,
            offset,
        ),
        [
            shape(CASCADES, tall, wide, kind=BF16),
            shape(CASCADES, 6 * rows, tall, kind=BF16),
            shape(CASCADES, 6 * rows, tall, kind=BF16),
            shape(CASCADES, tall, wide, kind=BF16),
            shape(tall, place.shape[0]),
        ]
        + [shape(2 * planes // volumes, width, kind=BF16)] * (volumes - 1),
        [(place.shape[0], repeat.shape[1])],
        2 * tall * place.shape[0] * place.shape[1],
        scalars=1,
    )
    partial = exchange(partial.reshape(-1, depth_pitch, LANES), both, near_both)
    partial = partial.reshape(depth, coil_devices, depth_pitch, LANES)
    handed = [from_group(value, step) for step, value in enumerate(handed, 1)]

    model_pitch = padded(volumes * 2 * count, 16)
    moved, model = call(
        functools.partial(first_refine_kernel, lines, volumes),
        "refine_first",
        (partial, first, second, columns),
        [shape(depth, model_pitch, LANES, kind=BF16), shape(2 * rows, width, kind=BF16)],
        [(depth * depth_pitch, LANES), (depth * model_pitch, LANES)],
        4 * tall * wide * width,
    )
    moved = exchange(moved, "section", near)

    image, pulled = call(
        functools.partial(slots_kernel, lines, volumes),
        "refine_and_back",
        (
            partial,
            model,
            cotangent.reshape(rows, two_lines),
            first,
            first_t,
            second,
            second_t,
            columns,
        ),
        [shape(2 * rows, width), shape(2 * rows, width)],
        [(depth * depth_pitch, LANES)],
        14 * tall * wide * width,
    )

    moved, *handed = lax.optimization_barrier((moved, *handed))
    end_pitch = padded((volumes + 1) * whole_count, 16)
    (partial,) = call(
        functools.partial(normal_kernel, coils, lines, volumes),
        "masked_normal",
        (moved, maps, pulled, mask, table, minus, plus),
        [shape(slots, coil_devices, end_pitch, LANES, kind=BF16)],
        [(depth * model_pitch, LANES), (slots * end_pitch, LANES)],
        3 * line_flops,
    )
    partial = exchange(partial.reshape(-1, end_pitch, LANES), both, None)
    partial = partial.reshape(slots, coil_devices, end_pitch, LANES)

    image, grad = call(
        functools.partial(end_kernel, coils, lines, volumes),
        "outputs",
        (columns, partial, image, mask, table, minus, maps, *handed),
        [shape(rows, two_lines), shape(planes * whole_count, LANES)],
        [(slots * end_pitch, LANES)],
        2 * line_flops,
    )
    return image.reshape(1, rows, two_lines), grad.reshape(coils, slots, 1, two_lines)


def solution(mesh):
    return jax.shard_map(
        body,
        mesh=mesh,
        in_specs=(
            P("coil", None, "section", None),
            P("coil", "section", None, None),
            P(),
            P(),
            P(),
            P(),
            P(),
            P(),
            P("section", None, None),
        ),
        out_specs=(P("section", None, None), P("coil", None, "section", None)),
        check_vma=False,
    )
```

```python
import functools
import math

import jax
import jax.numpy as jnp
import ml_dtypes
import numpy as np
from jax import lax
from jax.experimental import pallas as pl
from jax.experimental.pallas import tpu as pltpu
from jax.sharding import PartitionSpec as P

CASCADES = 2
VOLUMES = 2
LANES = 128
VMEM_BYTES = 48 * 1024 * 1024
LARGE_VMEM_BYTES = 60 * 1024 * 1024

F32 = jnp.float32
BF16 = jnp.bfloat16


def padded(size, unit):
    return -(-size // unit) * unit


def dft_parts(count):
    indices = np.arange(count)
    angles = (indices[:, None] * indices[None, :] % count) * (2.0 * math.pi / count)
    factor = 1.0 / math.sqrt(count)
    return np.cos(angles) * factor, np.sin(angles) * factor


def line_constant(lines):
    width = padded(lines, LANES)
    cosine, sine = dft_parts(lines)
    table = np.zeros((width, 2 * width), np.float32)
    table[:lines, :lines] = cosine
    table[:lines, width : width + lines] = sine
    return table.astype(ml_dtypes.bfloat16)


def depth_constant(coils, slots, volumes, sign):
    cosine, sine = dft_parts(slots // volumes)
    spread_over = np.eye(coils * volumes)
    real, imag = np.kron(spread_over, cosine), sign * np.kron(spread_over, sine)
    return np.block([[real, -imag], [imag, real]]).astype(np.float32).astype(ml_dtypes.bfloat16)


def conv_constants(rows, channels):
    groups = 6
    width = padded(groups * rows, LANES)
    repeat = np.kron(np.eye(channels), np.ones((rows, 1))).astype(np.float32)
    repeat = np.pad(repeat, ((0, 0), (0, padded(channels, LANES) - channels)))
    taps = CASCADES * 3
    place = np.zeros((padded(2 * taps * groups + 3 * CASCADES, LANES), 2 * taps * width), np.float32)
    for kind in range(2):
        for tap in range(taps):
            for group in range(groups):
                start = (kind * taps + tap) * width + group * rows
                place[(kind * taps + tap) * groups + group, start : start + rows] = 1.0
    offset = np.full((channels * rows, width), -9.0, np.float32)
    row = np.arange(rows)
    offset[:, : groups * rows] = np.tile(row[None, :] - row[:, None] + 1.0, (channels, groups))
    offset = np.clip(offset, -9.0, 9.0)
    return repeat, place.astype(ml_dtypes.bfloat16), offset


def lane_index(shape):
    return lax.broadcasted_iota(jnp.int32, shape, len(shape) - 1)


def split_complex(chunks, lines):
    whole, rest = divmod(lines, LANES)
    count = padded(lines, LANES) // LANES
    if rest == 0:
        return jnp.concatenate(chunks[:count], 1), jnp.concatenate(chunks[count:], 1)
    lane = lane_index(chunks[0].shape)
    real = chunks[:whole] + [jnp.where(lane < rest, chunks[whole], 0.0)]
    turned = [pltpu.roll(chunk, LANES - rest, 1) for chunk in chunks[whole:]]
    turned.append(jnp.zeros_like(turned[0]))
    imag = [jnp.where(lane < LANES - rest, turned[k], turned[k + 1]) for k in range(count)]
    imag[-1] = jnp.where(lane < rest, imag[-1], 0.0)
    return jnp.concatenate(real, 1), jnp.concatenate(imag, 1)


def lane_chunks(value):
    return [value[:, start : start + LANES] for start in range(0, value.shape[1], LANES)]


def join_complex(real, imag, lines):
    whole, rest = divmod(lines, LANES)
    real, imag = lane_chunks(real), lane_chunks(imag)
    if rest == 0:
        return real + imag
    lane = lane_index(real[0].shape)
    turned = [real[whole]] + [pltpu.roll(chunk, rest, 1) for chunk in imag]
    mixed = [jnp.where(lane < rest, turned[k], turned[k + 1]) for k in range(len(imag))]
    return (real[:whole] + mixed)[: 2 * lines // LANES]


def halves(stacked):
    half = stacked.shape[0] // 2
    return stacked[:half], stacked[half:]


def line_apply(stacked, table_ref, sign):
    mixed = jnp.dot(stacked.astype(BF16), table_ref[...], preferred_element_type=F32)
    width = table_ref.shape[1] // 2
    top, bottom = halves(mixed)
    return jnp.concatenate(
        [
            top[:, :width] - sign * bottom[:, width:],
            bottom[:, :width] + sign * top[:, width:],
        ],
        axis=0,
    )


def depth_apply(stacked, depth_ref):
    return jnp.dot(depth_ref[...], stacked.astype(BF16), preferred_element_type=F32)


def over_coils(value, coils):
    return jnp.concatenate([value] * coils, axis=0)


def coil_sum(value, coils):
    slots = value.shape[0] // coils
    total = value[:slots]
    for coil in range(1, coils):
        total = total + value[coil * slots : (coil + 1) * slots]
    return total


def over_rows(parts, coils):
    return jnp.concatenate([part for part in parts for coil in range(coils)], axis=0)


def spread(maps_real, maps_imag, real, imag):
    return jnp.concatenate(
        [maps_real * real - maps_imag * imag, maps_real * imag + maps_imag * real], axis=0
    )


def collect(maps_real, maps_imag, images):
    real, imag = halves(images)
    return maps_real * real + maps_imag * imag, maps_real * imag - maps_imag * real


def blocks(value, count):
    size = value.shape[0] // count
    return [value[index * size : (index + 1) * size] for index in range(count)]


def row_sums(value, rows, coils):
    return [coil_sum(part, coils) for part in blocks(value, rows)]


def pick(parts, index):
    chosen = parts[0]
    for place in range(1, len(parts)):
        chosen = jnp.where(index == place, parts[place], chosen)
    return chosen


def own_volume(depth):
    return lax.div(lax.axis_index("section"), jnp.int32(depth))


def masked_normal(images, table_ref, minus_ref, plus_ref, mask):
    spectrum = depth_apply(line_apply(images, table_ref, -1.0), minus_ref)
    return line_apply(depth_apply(spectrum * mask, plus_ref), table_ref, 1.0)


def write_rows(scratch, pitch, values, first=0):
    for index, value in enumerate(values):
        scratch[pl.ds(first + index, value.shape[0], stride=pitch), :] = value


def read_rows(scratch, pitch, first, count, rows):
    return [scratch[pl.ds(first + index, rows, stride=pitch), :] for index in range(count)]


def shifted(value, step):
    if step == 0:
        return value
    width = value.shape[1]
    return pltpu.roll(value, (-step) % width, 1)


def stack_shifted(value, order):
    return jnp.concatenate([shifted(value, step) for step in order], axis=0).astype(BF16)


def add_shifted(value, order, rows):
    total = None
    for index, step in enumerate(order):
        part = shifted(value[index * rows : (index + 1) * rows], step)
        total = part if total is None else total + part
    return total


def hidden_state(image, first_ref, bias_column):
    stack = stack_shifted(image, (-1, 0, 1))
    return (
        jnp.dot(first_ref[:, : stack.shape[0]], stack, preferred_element_type=F32) + bias_column
    )


def second_conv(hidden, second_ref, bias_column, rows, valid):
    mixed = jnp.dot(
        second_ref[...], jnp.where(valid, hidden, 0.0).astype(BF16), preferred_element_type=F32
    )
    total = add_shifted(mixed, (-1, 0, 1), 2 * rows)
    return jnp.where(valid[: 2 * rows], total + bias_column, 0.0)


def pull_back(cotangent, slope, first_t_ref, second_t_ref, rows, valid):
    stack = stack_shifted(cotangent, (1, 0, -1))
    back = jnp.dot(second_t_ref[:, : stack.shape[0]], stack, preferred_element_type=F32)
    back = jnp.where(valid, back * slope, 0.0).astype(BF16)
    mixed = jnp.dot(first_t_ref[...], back, preferred_element_type=F32)
    total = add_shifted(mixed, (1, 0, -1), 2 * rows)
    return jnp.where(valid[: 2 * rows], total, 0.0)


def valid_lanes(rows, width, lines):
    return lane_index((rows, width)) < lines


def column(columns_ref, place, rows):
    at = 4 * 9 * CASCADES + place
    return columns_ref[:rows, at : at + 1]


def round_bf(value):
    return value.astype(BF16).astype(F32)


def choose_volume(value, coils, volumes, volume):
    parts = blocks(value, coils * volumes)
    chosen = [pick(parts[coil * volumes : (coil + 1) * volumes], volume) for coil in range(coils)]
    return jnp.concatenate(chosen, axis=0)


def pack_kernel(coils, volumes, pitch, kspace_ref, maps_ref, image_ref, out_ref, *refs):
    handed, (scratch,) = refs[:-1], refs[-1:]
    rows = image_ref.shape[0]
    depth = rows // volumes
    volume = own_volume(depth)
    kspace = kspace_ref[...].astype(F32)
    for step, ref in enumerate(handed, 1):
        other = lax.rem(volume + step, jnp.int32(volumes))
        ref[...] = choose_volume(kspace, coils, volumes, other).astype(BF16)
    count = maps_ref.shape[1] // LANES
    scratch[...] = jnp.zeros_like(scratch)
    image = image_ref[...].astype(F32)
    for coil in range(coils + 1):
        value = maps_ref[coil * rows : (coil + 1) * rows, :].astype(F32) if coil < coils else image
        for place, part in enumerate(blocks(value, volumes)):
            first = (place * (coils + 1) + coil) * count
            write_rows(scratch, pitch, lane_chunks(part), first)
    out_ref[...] = scratch[...].astype(BF16).reshape(out_ref.shape)


def taps_kernel(
    rows,
    weight_ref,
    kernel_in_ref,
    kernel_out_ref,
    bias_in_ref,
    bias_out_ref,
    repeat_ref,
    place_ref,
    offset_ref,
    first_ref,
    first_t_ref,
    second_ref,
    second_t_ref,
    columns_ref,
    taps,
):
    taps[...] = jnp.zeros_like(taps)
    channels = kernel_in_ref.shape[2]
    at = 0
    for ref in (kernel_in_ref, kernel_out_ref):
        for index in range(ref.shape[0]):
            taps[at : at + 2, :channels] = ref[index]
            at += 2
    taps[at : at + CASCADES, :channels] = bias_in_ref[...]
    at += CASCADES
    for cascade in range(CASCADES):
        taps[at : at + 1, :] = jnp.full((1, taps.shape[1]), weight_ref[cascade], F32)
        at += 1
    taps[at : at + CASCADES, : bias_out_ref.shape[1]] = bias_out_ref[...]
    tall = lax.dot_general(
        repeat_ref[...],
        taps[...],
        (((1,), (1,)), ((), ())),
        precision=lax.Precision.HIGHEST,
        preferred_element_type=F32,
    )
    columns_ref[...] = tall
    wide = jnp.dot(tall.astype(BF16), place_ref[...], preferred_element_type=F32)
    offset = offset_ref[...]
    width = offset.shape[1]
    for cascade in range(CASCADES):
        for kind, straight, turned in ((0, first_ref, first_t_ref), (1, second_t_ref, second_ref)):
            total = jnp.zeros_like(offset)
            for tap in range(3):
                start = ((kind * CASCADES + cascade) * 3 + tap) * width
                wanted = float(tap if kind == 0 else 2 - tap)
                total = total + jnp.where(offset == wanted, wide[:, start : start + width], 0.0)
            straight[cascade] = total.astype(BF16)
            turned[cascade] = total.T[: 6 * rows].astype(BF16)


def write_sums(scratch, pitch, first, values, volumes, coils):
    sums = [row_sums(value, volumes, coils) for value in values]
    period = pitch // volumes
    for place in range(volumes):
        chunks = [chunk for value in sums for chunk in lane_chunks(value[place])]
        write_rows(scratch, pitch, chunks, place * period + first)


def rows_kernel(
    coils,
    lines,
    volumes,
    sums_pitch,
    sent_ref,
    mask_ref,
    table_ref,
    minus_ref,
    plus_ref,
    maps_ref,
    sums_ref,
    *refs,
):
    handed, (arrived,) = refs[:-1], refs[-1:]
    depth, pitch = sent_ref.shape[:2]
    volume = own_volume(depth)
    arrived[...] = sent_ref[...].astype(F32).reshape(arrived.shape)
    count = 2 * lines // LANES
    parts, reals, imags = [], [], []
    for place in range(volumes):
        first = place * (coils + 1) * count
        for coil in range(coils):
            chunks = read_rows(arrived, pitch, first + coil * count, count, depth)
            parts.append(split_complex(chunks, lines))
        chunks = read_rows(arrived, pitch, first + coils * count, count, depth)
        real, imag = split_complex(chunks, lines)
        reals.append(real)
        imags.append(imag)
    maps_real = jnp.concatenate([part[0] for part in parts], axis=0)
    maps_imag = jnp.concatenate([part[1] for part in parts], axis=0)
    maps_ref[...] = jnp.concatenate([maps_real, maps_imag], axis=0).astype(BF16)
    real_parts, imag_parts = blocks(maps_real, volumes), blocks(maps_imag, volumes)
    for step, ref in enumerate(handed, 1):
        place = lax.rem(volume + step, jnp.int32(volumes))
        both = [pick(real_parts, place), pick(imag_parts, place)]
        ref[...] = jnp.concatenate(both, axis=0).astype(BF16)
    mask = over_coils(pick(blocks(mask_ref[...], volumes), volume), 2 * volumes * coils)
    images = spread(maps_real, maps_imag, over_rows(reals, coils), over_rows(imags, coils))
    images = masked_normal(images, table_ref, minus_ref, plus_ref, mask)
    sums_ref[...] = jnp.zeros_like(sums_ref)
    power = maps_real * maps_real + maps_imag * maps_imag
    found = [*collect(maps_real, maps_imag, images), power]
    first = 2 * maps_ref.shape[1] // LANES
    write_sums(sums_ref, sums_pitch, first, found, volumes, coils)


def measured_kernel(
    coils,
    lines,
    volumes,
    kspace_ref,
    mask_ref,
    table_ref,
    plus_ref,
    maps_ref,
    sums_ref,
    *refs,
):
    arrival_refs, (out_ref, leaving) = refs[: volumes - 1], refs[volumes - 1 :]
    depth, pitch = out_ref.shape[0], out_ref.shape[2]
    volume = own_volume(depth)
    arrivals = [choose_volume(kspace_ref[...].astype(F32), coils, volumes, volume)]
    arrivals += [ref[...].astype(F32) for ref in arrival_refs]
    ordered = []
    for place in range(volumes):
        step = lax.rem(volume - place + volumes, jnp.int32(volumes))
        ordered.append(pick(arrivals, step))
    mask = over_coils(pick(blocks(mask_ref[...], volumes), volume), volumes * coils)
    real, imag = split_complex(lane_chunks(jnp.concatenate(ordered, axis=0)), lines)
    measured = jnp.concatenate([real * mask, imag * mask], axis=0)
    images = line_apply(depth_apply(measured, plus_ref), table_ref, 1.0)
    maps_real, maps_imag = halves(maps_ref[...].astype(F32))
    leaving[...] = sums_ref[...]
    found = collect(maps_real, maps_imag, round_bf(images))
    write_sums(leaving, pitch, 0, found, volumes, coils)
    message = leaving[...].astype(BF16).reshape(depth, *out_ref.shape[2:])
    for device in range(out_ref.shape[1]):
        out_ref[:, device] = message


def unpack_sum(sent_ref, scratch):
    total = sent_ref[:, 0].astype(F32)
    for device in range(1, sent_ref.shape[1]):
        total = total + sent_ref[:, device].astype(F32)
    scratch[...] = total.reshape(scratch.shape)


def read_image(scratch, pitch, first, count, depth):
    return jnp.concatenate(read_rows(scratch, pitch, first, count, depth), axis=1)


def read_places(scratch, pitch, first, period, count, depth, volumes):
    parts = [
        read_image(scratch, pitch, first + place * period, count, depth) for place in range(volumes)
    ]
    return jnp.concatenate(parts, axis=0)


def read_complex(scratch, pitch, first, period, count, depth, volumes):
    real = read_places(scratch, pitch, first, period, count, depth, volumes)
    imag = read_places(scratch, pitch, first + count, period, count, depth, volumes)
    return jnp.concatenate([real, imag], axis=0)


def first_refine_kernel(
    lines,
    volumes,
    sent_ref,
    first_ref,
    second_ref,
    columns_ref,
    out_ref,
    model_ref,
    arrived,
    leaving,
):
    unpack_sum(sent_ref, arrived)
    depth, pitch = sent_ref.shape[0], sent_ref.shape[2]
    rows = depth * volumes
    width = padded(lines, LANES)
    count = width // LANES
    picture = round_bf(read_complex(arrived, pitch, 0, pitch // volumes, count, depth, volumes))
    hidden = hidden_state(picture, first_ref.at[0], column(columns_ref, 0, first_ref.shape[1]))
    valid = valid_lanes(hidden.shape[0], width, lines)
    hidden = hidden * jax.nn.sigmoid(hidden)
    bias = column(columns_ref, 2 * CASCADES, 2 * rows)
    model = second_conv(hidden, second_ref.at[0], bias, rows, valid)
    model_ref[...] = model.astype(BF16)
    leaving[...] = jnp.zeros_like(leaving)
    real, imag = halves(model)
    for place, pair in enumerate(zip(blocks(real, volumes), blocks(imag, volumes))):
        chunks = lane_chunks(pair[0]) + lane_chunks(pair[1])
        write_rows(leaving, out_ref.shape[1], chunks, place * len(chunks))
    out_ref[...] = leaving[...].astype(BF16).reshape(out_ref.shape)


def slots_kernel(
    lines,
    volumes,
    sent_ref,
    model_ref,
    cotangent_ref,
    first_ref,
    first_t_ref,
    second_ref,
    second_t_ref,
    columns_ref,
    image_ref,
    spread_ref,
    arrived,
):
    unpack_sum(sent_ref, arrived)
    depth, pitch = sent_ref.shape[0], sent_ref.shape[2]
    rows = depth * volumes
    width = padded(lines, LANES)
    count = width // LANES
    begun = read_complex(arrived, pitch, 0, pitch // volumes, count, depth, volumes)
    turned = read_complex(arrived, pitch, 2 * count, pitch // volumes, count, depth, volumes)
    power = read_places(arrived, pitch, 4 * count, pitch // volumes, count, depth, volumes)
    power = jnp.concatenate([power, power], axis=0)
    cotangent = jnp.concatenate(
        split_complex(lane_chunks(cotangent_ref[...].astype(F32)), lines), axis=0
    )
    model = model_ref[...].astype(F32)
    tall = first_ref.shape[1]
    weight = [column(columns_ref, CASCADES + cascade, 2 * rows) for cascade in range(CASCADES)]

    share = [jnp.ones_like(weight[0])]
    for cascade in range(CASCADES):
        share.append(share[cascade] - weight[cascade] * (share[cascade] - 1.0))

    def slopes(hidden):
        gate = jax.nn.sigmoid(hidden)
        return hidden * gate, gate * (1.0 + hidden * (1.0 - gate))

    hidden = hidden_state(round_bf(begun), first_ref.at[0], column(columns_ref, 0, tall))
    valid = valid_lanes(hidden.shape[0], width, lines)
    unused, slope_first = slopes(hidden)
    picture = round_bf(share[1] * begun + power * model)
    hidden = hidden_state(picture, first_ref.at[1], column(columns_ref, 1, tall))
    active, slope_second = slopes(hidden)
    bias = column(columns_ref, 2 * CASCADES + 1, 2 * rows)
    later = round_bf(second_conv(active, second_ref.at[1], bias, rows, valid))
    image_ref[...] = share[2] * begun + power * (model + later)

    through = power * cotangent
    back_second = round_bf(
        pull_back(through, slope_second, first_t_ref.at[1], second_t_ref.at[1], rows, valid)
    )
    through = through - weight[1] * turned + power * back_second
    back_first = round_bf(
        pull_back(through, slope_first, first_t_ref.at[0], second_t_ref.at[0], rows, valid)
    )
    kept = (1.0 - weight[0], 1.0 - weight[1])
    of_cotangent = weight[1] + weight[0] * kept[1] + kept[0] * kept[1]
    of_second = weight[0] + kept[0]
    spread_ref[...] = of_cotangent * cotangent + of_second * back_second + back_first


def normal_kernel(
    coils,
    lines,
    volumes,
    sent_ref,
    maps_ref,
    spread_ref,
    mask_ref,
    table_ref,
    minus_ref,
    plus_ref,
    out_ref,
    arrived,
    leaving,
):
    arrived[...] = sent_ref[...].astype(F32).reshape(arrived.shape)
    depth, pitch = sent_ref.shape[:2]
    volume = own_volume(depth)
    count = maps_ref.shape[1] // LANES
    firsts = [place * 2 * count for place in range(volumes)]
    reals = [read_image(arrived, pitch, first, count, depth) for first in firsts]
    imags = [read_image(arrived, pitch, first + count, count, depth) for first in firsts]
    maps_real, maps_imag = halves(maps_ref[...].astype(F32))
    mask = over_coils(pick(blocks(mask_ref[...], volumes), volume), 2 * volumes * coils)
    images = spread(maps_real, maps_imag, over_rows(reals, coils), over_rows(imags, coils))
    images = masked_normal(images, table_ref, minus_ref, plus_ref, mask)
    found = [row_sums(value, volumes, coils) for value in collect(maps_real, maps_imag, images)]
    leaving[...] = jnp.zeros_like(leaving)
    pitch = out_ref.shape[2]
    first = 0
    for place in range(volumes):
        chunks = join_complex(found[0][place], found[1][place], lines)
        for target in range(volumes):
            kept = [jnp.where(volume == target, chunk, 0.0) for chunk in chunks]
            write_rows(leaving, pitch, kept, target * depth * pitch + first)
        first += len(chunks)
    write_rows(leaving, pitch, join_complex(*halves(spread_ref[...]), lines), first)
    message = leaving[...].astype(BF16).reshape(out_ref.shape[0], *out_ref.shape[2:])
    for device in range(out_ref.shape[1]):
        out_ref[:, device] = message


def end_kernel(
    coils,
    lines,
    volumes,
    columns_ref,
    sent_ref,
    image_ref,
    mask_ref,
    table_ref,
    minus_ref,
    maps_ref,
    *refs,
):
    handed, (picture_ref, grad_ref, arrived) = refs[: volumes - 1], refs[volumes - 1 :]
    slots, pitch = sent_ref.shape[0], sent_ref.shape[2]
    depth = slots // volumes
    volume = own_volume(depth)
    count = 2 * lines // LANES
    own = maps_ref[...].astype(F32)
    sources = [[pick(blocks(part, volumes), volume) for part in halves(own)]]
    sources += [halves(ref[...].astype(F32)) for ref in handed]
    maps = []
    for part in range(2):
        ordered = []
        for place in range(volumes):
            step = lax.rem(volume - place + volumes, jnp.int32(volumes))
            ordered.append(blocks(pick([source[part] for source in sources], step), coils))
        maps.append(
            jnp.concatenate([ordered[v][coil] for coil in range(coils) for v in range(volumes)], 0)
        )
    arrived[...] = sent_ref[:, 0].astype(F32).reshape(arrived.shape)
    chunks = read_rows(arrived, pitch, volumes * count, count, slots)
    real, imag = split_complex(chunks, lines)
    images = spread(*maps, over_coils(real, coils), over_coils(imag, coils))
    spectrum = depth_apply(line_apply(images, table_ref, -1.0), minus_ref)
    spectrum = spectrum * over_coils(mask_ref[...], 2 * coils)
    chunks = join_complex(*halves(spectrum), lines)
    write_rows(grad_ref, len(chunks), chunks)

    unpack_sum(sent_ref, arrived)
    picture = image_ref[...]
    scale = column(columns_ref, CASCADES + 1, picture.shape[0])
    parts = [[], []]
    size = depth * pitch
    total = arrived[:size]
    for other in range(1, volumes):
        total = total + arrived[other * size : (other + 1) * size]
    arrived[:size] = total
    for place in range(volumes):
        chunks = read_rows(arrived, pitch, place * count, count, depth)
        for part, value in zip(parts, split_complex(chunks, lines)):
            part.append(value)
    picture = picture - scale * jnp.concatenate(parts[0] + parts[1], axis=0)
    for index, chunk in enumerate(join_complex(*halves(picture), lines)):
        picture_ref[:, index * LANES : (index + 1) * LANES] = chunk


def call(kernel, name, operands, outs, scratch, flops, vmem_bytes=VMEM_BYTES, scalars=0):
    spaces = [pltpu.SMEM] * scalars + [pltpu.VMEM] * (len(operands) - scalars)
    moved = sum(math.prod(item.shape) * item.dtype.itemsize for item in (*operands, *outs))
    return pl.pallas_call(
        kernel,
        name=name,
        out_shape=tuple(outs),
        in_specs=[pl.BlockSpec(memory_space=space) for space in spaces],
        out_specs=tuple(pl.BlockSpec(memory_space=pltpu.VMEM) for item in outs),
        scratch_shapes=[pltpu.VMEM(shape, F32) for shape in scratch],
        compiler_params=pltpu.CompilerParams(vmem_limit_bytes=vmem_bytes),
        cost_estimate=pl.CostEstimate(flops=flops, bytes_accessed=moved, transcendentals=0),
    )(*operands)


def body(
    kspace, coil_maps, sampling, dc_weight, kernel_in, bias_in, kernel_out, bias_out, cotangent
):
    coils, slots = kspace.shape[:2]
    rows, two_lines = coil_maps.shape[2:]
    lines = two_lines // 2
    channels = bias_in.shape[1]
    coil_devices, sections = lax.axis_size("coil"), lax.axis_size("section")
    volumes = VOLUMES
    depth = slots // volumes
    width = padded(lines, LANES)
    count, whole_count = width // LANES, two_lines // LANES
    planes = coils * slots
    both = ("section", "coil")
    near = [[group * depth + t for t in range(depth)] for group in range(volumes)]
    span = depth * coil_devices
    near_both = [[group * span + t for t in range(span)] for group in range(volumes)]

    def from_group(value, step):
        shift = step * depth
        return lax.ppermute(value, "section", [(s, (s + shift) % sections) for s in range(sections)])

    def exchange(value, axes, groups):
        return lax.all_to_all(value, axes, 0, 0, tiled=True, axis_index_groups=groups)

    table = jnp.asarray(line_constant(lines))
    minus = jnp.asarray(depth_constant(coils, slots, volumes, -1.0))
    plus = jnp.asarray(depth_constant(coils, slots, volumes, 1.0))
    repeat, place, offset = (jnp.asarray(item) for item in conv_constants(rows, channels))
    mask = sampling.astype(F32).reshape(slots, lines)
    mask = jnp.pad(mask, ((0, 0), (0, width - lines)))

    def shape(*dims, kind=F32):
        return jax.ShapeDtypeStruct(dims, kind)

    line_flops = 2 * (2 * planes) * width * (2 * width)

    pitch = padded(volumes * (coils + 1) * whole_count, 16)
    packed, *samples = call(
        functools.partial(pack_kernel, coils, volumes, pitch),
        "pack_maps",
        (
            kspace.reshape(planes, two_lines),
            coil_maps.reshape(coils * rows, two_lines),
            cotangent.reshape(rows, two_lines),
        ),
        [shape(depth, pitch, LANES, kind=BF16)]
        + [shape(coils * depth, two_lines, kind=BF16)] * (volumes - 1),
        [(depth * pitch, LANES)],
        1000,
        LARGE_VMEM_BYTES,
    )
    samples = [from_group(value, step) for step, value in enumerate(samples, 1)]
    arrived = exchange(packed, "section", near)

    tall, wide = channels * rows, offset.shape[1]
    first, first_t, second, second_t, columns = call(
        functools.partial(taps_kernel, rows),
        "lay_out_taps",
        (
            dc_weight,
            kernel_in.transpose(0, 1, 3, 2).reshape(-1, 2, channels),
            kernel_out.reshape(-1, 2, channels),
            bias_in,
            bias_out,
            repeat,
            place,
            offset,
        ),
        [
            shape(CASCADES, tall, wide, kind=BF16),
            shape(CASCADES, 6 * rows, tall, kind=BF16),
            shape(CASCADES, 6 * rows, tall, kind=BF16),
            shape(CASCADES, tall, wide, kind=BF16),
            shape(tall, place.shape[0]),
        ],
        [(place.shape[0], repeat.shape[1])],
        2 * tall * place.shape[0] * place.shape[1],
        scalars=1,
    )
    arrived, columns = lax.optimization_barrier((arrived, columns))

    depth_pitch = padded(volumes * 5 * count, 16 * volumes)
    maps, sums, *handed = call(
        functools.partial(rows_kernel, coils, lines, volumes, depth_pitch),
        "combine_rows",
        (arrived, mask, table, minus, plus),
        [shape(2 * planes, width, kind=BF16), shape(depth * depth_pitch, LANES)]
        + [shape(2 * planes // volumes, width, kind=BF16)] * (volumes - 1),
        [(depth * pitch, LANES)],
        3 * line_flops,
    )
    (partial,) = call(
        functools.partial(measured_kernel, coils, lines, volumes),
        "combine_measured",
        (kspace.reshape(planes, two_lines), mask, table, plus, maps, sums, *samples),
        [shape(depth, coil_devices, depth_pitch, LANES, kind=BF16)],
        [(depth * depth_pitch, LANES)],
        2 * line_flops,
    )
    handed = [from_group(value, step) for step, value in enumerate(handed, 1)]
    partial = exchange(partial.reshape(-1, depth_pitch, LANES), both, near_both)
    partial = partial.reshape(depth, coil_devices, depth_pitch, LANES)

    model_pitch = padded(volumes * 2 * count, 16)
    moved, model = call(
        functools.partial(first_refine_kernel, lines, volumes),
        "refine_first",
        (partial, first, second, columns),
        [shape(depth, model_pitch, LANES, kind=BF16), shape(2 * rows, width, kind=BF16)],
        [(depth * depth_pitch, LANES), (depth * model_pitch, LANES)],
        4 * tall * wide * width,
    )
    moved = exchange(moved, "section", near)

    image, pulled = call(
        functools.partial(slots_kernel, lines, volumes),
        "refine_and_back",
        (
            partial,
            model,
            cotangent.reshape(rows, two_lines),
            first,
            first_t,
            second,
            second_t,
            columns,
        ),
        [shape(2 * rows, width), shape(2 * rows, width)],
        [(depth * depth_pitch, LANES)],
        14 * tall * wide * width,
    )

    moved, *handed = lax.optimization_barrier((moved, *handed))
    end_pitch = padded((volumes + 1) * whole_count, 16)
    (partial,) = call(
        functools.partial(normal_kernel, coils, lines, volumes),
        "masked_normal",
        (moved, maps, pulled, mask, table, minus, plus),
        [shape(slots, coil_devices, end_pitch, LANES, kind=BF16)],
        [(depth * model_pitch, LANES), (slots * end_pitch, LANES)],
        3 * line_flops,
    )
    partial = exchange(partial.reshape(-1, end_pitch, LANES), both, None)
    partial = partial.reshape(slots, coil_devices, end_pitch, LANES)

    image, grad = call(
        functools.partial(end_kernel, coils, lines, volumes),
        "outputs",
        (columns, partial, image, mask, table, minus, maps, *handed),
        [shape(rows, two_lines), shape(planes * whole_count, LANES)],
        [(slots * end_pitch, LANES)],
        2 * line_flops,
    )
    return image.reshape(1, rows, two_lines), grad.reshape(coils, slots, 1, two_lines)


def solution(mesh):
    return jax.shard_map(
        body,
        mesh=mesh,
        in_specs=(
            P("coil", None, "section", None),
            P("coil", "section", None, None),
            P(),
            P(),
            P(),
            P(),
            P(),
            P(),
            P("section", None, None),
        ),
        out_specs=(P("section", None, None), P("coil", None, "section", None)),
        check_vma=False,
    )
```

```python
import functools
import math

import jax
import jax.numpy as jnp
import ml_dtypes
import numpy as np
from jax import lax
from jax.experimental import pallas as pl
from jax.experimental.pallas import tpu as pltpu
from jax.sharding import PartitionSpec as P

CASCADES = 2
VOLUMES = 2
LANES = 128
VMEM_BYTES = 48 * 1024 * 1024
FAR_PARTS = 3
LARGE_VMEM_BYTES = 60 * 1024 * 1024

F32 = jnp.float32
BF16 = jnp.bfloat16


def padded(size, unit):
    return -(-size // unit) * unit


def dft_parts(count):
    indices = np.arange(count)
    angles = (indices[:, None] * indices[None, :] % count) * (2.0 * math.pi / count)
    factor = 1.0 / math.sqrt(count)
    return np.cos(angles) * factor, np.sin(angles) * factor


def line_constant(lines):
    width = padded(lines, LANES)
    cosine, sine = dft_parts(lines)
    table = np.zeros((width, 2 * width), np.float32)
    table[:lines, :lines] = cosine
    table[:lines, width : width + lines] = sine
    return table.astype(ml_dtypes.bfloat16)


def depth_constant(coils, slots, volumes, sign):
    cosine, sine = dft_parts(slots // volumes)
    spread_over = np.eye(coils * volumes)
    real, imag = np.kron(spread_over, cosine), sign * np.kron(spread_over, sine)
    return np.block([[real, -imag], [imag, real]]).astype(np.float32).astype(ml_dtypes.bfloat16)


def conv_constants(rows, channels):
    groups = 6
    width = padded(groups * rows, LANES)
    repeat = np.kron(np.eye(channels), np.ones((rows, 1))).astype(np.float32)
    repeat = np.pad(repeat, ((0, 0), (0, padded(channels, LANES) - channels)))
    taps = CASCADES * 3
    place = np.zeros((padded(2 * taps * groups + 3 * CASCADES, LANES), 2 * taps * width), np.float32)
    for kind in range(2):
        for tap in range(taps):
            for group in range(groups):
                start = (kind * taps + tap) * width + group * rows
                place[(kind * taps + tap) * groups + group, start : start + rows] = 1.0
    offset = np.full((channels * rows, width), -9.0, np.float32)
    row = np.arange(rows)
    offset[:, : groups * rows] = np.tile(row[None, :] - row[:, None] + 1.0, (channels, groups))
    offset = np.clip(offset, -9.0, 9.0)
    return repeat, place.astype(ml_dtypes.bfloat16), offset


def lane_index(shape):
    return lax.broadcasted_iota(jnp.int32, shape, len(shape) - 1)


def split_complex(chunks, lines):
    whole, rest = divmod(lines, LANES)
    count = padded(lines, LANES) // LANES
    if rest == 0:
        return jnp.concatenate(chunks[:count], 1), jnp.concatenate(chunks[count:], 1)
    lane = lane_index(chunks[0].shape)
    real = chunks[:whole] + [jnp.where(lane < rest, chunks[whole], 0.0)]
    turned = [pltpu.roll(chunk, LANES - rest, 1) for chunk in chunks[whole:]]
    turned.append(jnp.zeros_like(turned[0]))
    imag = [jnp.where(lane < LANES - rest, turned[k], turned[k + 1]) for k in range(count)]
    imag[-1] = jnp.where(lane < rest, imag[-1], 0.0)
    return jnp.concatenate(real, 1), jnp.concatenate(imag, 1)


def lane_chunks(value):
    return [value[:, start : start + LANES] for start in range(0, value.shape[1], LANES)]


def join_complex(real, imag, lines):
    whole, rest = divmod(lines, LANES)
    real, imag = lane_chunks(real), lane_chunks(imag)
    if rest == 0:
        return real + imag
    lane = lane_index(real[0].shape)
    turned = [real[whole]] + [pltpu.roll(chunk, rest, 1) for chunk in imag]
    mixed = [jnp.where(lane < rest, turned[k], turned[k + 1]) for k in range(len(imag))]
    return (real[:whole] + mixed)[: 2 * lines // LANES]


def halves(stacked):
    half = stacked.shape[0] // 2
    return stacked[:half], stacked[half:]


def line_apply(stacked, table_ref, sign):
    mixed = jnp.dot(stacked.astype(BF16), table_ref[...], preferred_element_type=F32)
    width = table_ref.shape[1] // 2
    top, bottom = halves(mixed)
    return jnp.concatenate(
        [
            top[:, :width] - sign * bottom[:, width:],
            bottom[:, :width] + sign * top[:, width:],
        ],
        axis=0,
    )


def depth_apply(stacked, depth_ref):
    return jnp.dot(depth_ref[...], stacked.astype(BF16), preferred_element_type=F32)


def over_coils(value, coils):
    return jnp.concatenate([value] * coils, axis=0)


def coil_sum(value, coils):
    slots = value.shape[0] // coils
    total = value[:slots]
    for coil in range(1, coils):
        total = total + value[coil * slots : (coil + 1) * slots]
    return total


def over_rows(parts, coils):
    return jnp.concatenate([part for part in parts for coil in range(coils)], axis=0)


def spread(maps_real, maps_imag, real, imag):
    return jnp.concatenate(
        [maps_real * real - maps_imag * imag, maps_real * imag + maps_imag * real], axis=0
    )


def collect(maps_real, maps_imag, images):
    real, imag = halves(images)
    return maps_real * real + maps_imag * imag, maps_real * imag - maps_imag * real


def blocks(value, count):
    size = value.shape[0] // count
    return [value[index * size : (index + 1) * size] for index in range(count)]


def row_sums(value, rows, coils):
    return [coil_sum(part, coils) for part in blocks(value, rows)]


def pick(parts, index):
    chosen = parts[0]
    for place in range(1, len(parts)):
        chosen = jnp.where(index == place, parts[place], chosen)
    return chosen


def own_volume(depth):
    return lax.div(lax.axis_index("section"), jnp.int32(depth))


def masked_normal(images, table_ref, minus_ref, plus_ref, mask):
    spectrum = depth_apply(line_apply(images, table_ref, -1.0), minus_ref)
    return line_apply(depth_apply(spectrum * mask, plus_ref), table_ref, 1.0)


def write_rows(scratch, pitch, values, first=0):
    for index, value in enumerate(values):
        scratch[pl.ds(first + index, value.shape[0], stride=pitch), :] = value


def read_rows(scratch, pitch, first, count, rows):
    return [scratch[pl.ds(first + index, rows, stride=pitch), :] for index in range(count)]


def shifted(value, step):
    if step == 0:
        return value
    width = value.shape[1]
    return pltpu.roll(value, (-step) % width, 1)


def stack_shifted(value, order):
    return jnp.concatenate([shifted(value, step) for step in order], axis=0).astype(BF16)


def add_shifted(value, order, rows):
    total = None
    for index, step in enumerate(order):
        part = shifted(value[index * rows : (index + 1) * rows], step)
        total = part if total is None else total + part
    return total


def hidden_state(image, first_ref, bias_column):
    stack = stack_shifted(image, (-1, 0, 1))
    return (
        jnp.dot(first_ref[:, : stack.shape[0]], stack, preferred_element_type=F32) + bias_column
    )


def second_conv(hidden, second_ref, bias_column, rows, valid):
    mixed = jnp.dot(
        second_ref[...], jnp.where(valid, hidden, 0.0).astype(BF16), preferred_element_type=F32
    )
    total = add_shifted(mixed, (-1, 0, 1), 2 * rows)
    return jnp.where(valid[: 2 * rows], total + bias_column, 0.0)


def pull_back(cotangent, slope, first_t_ref, second_t_ref, rows, valid):
    stack = stack_shifted(cotangent, (1, 0, -1))
    back = jnp.dot(second_t_ref[:, : stack.shape[0]], stack, preferred_element_type=F32)
    back = jnp.where(valid, back * slope, 0.0).astype(BF16)
    mixed = jnp.dot(first_t_ref[...], back, preferred_element_type=F32)
    total = add_shifted(mixed, (1, 0, -1), 2 * rows)
    return jnp.where(valid[: 2 * rows], total, 0.0)


def read_mask(sampling_ref, width):
    mask = sampling_ref[...].astype(F32)
    return jnp.pad(mask, ((0, 0), (0, width - mask.shape[1])))


def valid_lanes(rows, width, lines):
    return lane_index((rows, width)) < lines


def column(columns_ref, place, rows):
    at = 4 * 9 * CASCADES + place
    return columns_ref[:rows, at : at + 1]


def round_bf(value):
    return value.astype(BF16).astype(F32)


def choose_volume(value, coils, volumes, volume):
    parts = blocks(value, coils * volumes)
    chosen = [pick(parts[coil * volumes : (coil + 1) * volumes], volume) for coil in range(coils)]
    return jnp.concatenate(chosen, axis=0)


def pack_kernel(coils, volumes, pitch, kspace_ref, maps_ref, image_ref, out_ref, *refs):
    handed, (scratch,) = refs[:-1], refs[-1:]
    rows = image_ref.shape[0]
    depth = rows // volumes
    volume = own_volume(depth)
    kspace = kspace_ref[...].astype(F32)
    for step, ref in enumerate(handed, 1):
        other = lax.rem(volume + step, jnp.int32(volumes))
        ref[...] = choose_volume(kspace, coils, volumes, other).astype(BF16)
    count = maps_ref.shape[1] // LANES
    scratch[...] = jnp.zeros_like(scratch)
    image = image_ref[...].astype(F32)
    for coil in range(coils + 1):
        value = maps_ref[coil * rows : (coil + 1) * rows, :].astype(F32) if coil < coils else image
        for place, part in enumerate(blocks(value, volumes)):
            first = (place * (coils + 1) + coil) * count
            write_rows(scratch, pitch, lane_chunks(part), first)
    out_ref[...] = scratch[...].astype(BF16).reshape(out_ref.shape)


def taps_kernel(
    rows,
    weight_ref,
    kernel_in_ref,
    kernel_out_ref,
    bias_in_ref,
    bias_out_ref,
    repeat_ref,
    place_ref,
    offset_ref,
    first_ref,
    first_t_ref,
    second_ref,
    second_t_ref,
    columns_ref,
    taps,
):
    taps[...] = jnp.zeros_like(taps)
    channels = kernel_in_ref.shape[2]
    at = 0
    for ref in (kernel_in_ref, kernel_out_ref):
        for index in range(ref.shape[0]):
            taps[at : at + 2, :channels] = ref[index]
            at += 2
    taps[at : at + CASCADES, :channels] = bias_in_ref[...]
    at += CASCADES
    for cascade in range(CASCADES):
        taps[at : at + 1, :] = jnp.full((1, taps.shape[1]), weight_ref[cascade], F32)
        at += 1
    taps[at : at + CASCADES, : bias_out_ref.shape[1]] = bias_out_ref[...]
    tall = lax.dot_general(
        repeat_ref[...],
        taps[...],
        (((1,), (1,)), ((), ())),
        precision=lax.Precision.HIGHEST,
        preferred_element_type=F32,
    )
    columns_ref[...] = tall
    wide = jnp.dot(tall.astype(BF16), place_ref[...], preferred_element_type=F32)
    offset = offset_ref[...]
    width = offset.shape[1]
    for cascade in range(CASCADES):
        for kind, straight, turned in ((0, first_ref, first_t_ref), (1, second_t_ref, second_ref)):
            total = jnp.zeros_like(offset)
            for tap in range(3):
                start = ((kind * CASCADES + cascade) * 3 + tap) * width
                wanted = float(tap if kind == 0 else 2 - tap)
                total = total + jnp.where(offset == wanted, wide[:, start : start + width], 0.0)
            straight[cascade] = total.astype(BF16)
            turned[cascade] = total.T[: 6 * rows].astype(BF16)


def line_images(kspace, mask, lines, table_ref, plus_ref):
    real, imag = split_complex(lane_chunks(kspace), lines)
    measured = jnp.concatenate([real * mask, imag * mask], axis=0)
    return line_apply(depth_apply(measured, plus_ref), table_ref, 1.0)


def far_kernel(coils, lines, volumes, kspace_ref, mask_ref, table_ref, plus_ref, out_ref):
    parts = blocks(read_mask(mask_ref, table_ref.shape[0]), volumes)
    mask = pick(parts, own_volume(parts[0].shape[0]))
    mask = over_coils(mask, coils)
    images = line_images(kspace_ref[...].astype(F32), mask, lines, table_ref, plus_ref)
    out_ref[: images.shape[0]] = images
    if out_ref.shape[0] > images.shape[0]:
        out_ref[images.shape[0] :] = jnp.zeros_like(out_ref[images.shape[0] :])


def own_kernel(coils, lines, volumes, kspace_ref, mask_ref, table_ref, plus_ref, out_ref):
    parts = blocks(read_mask(mask_ref, table_ref.shape[0]), volumes)
    volume = own_volume(parts[0].shape[0])
    kspace = choose_volume(kspace_ref[...].astype(F32), coils, volumes, volume)
    mask = over_coils(pick(parts, volume), coils)
    out_ref[...] = line_images(kspace, mask, lines, table_ref, plus_ref)


def rows_kernel(
    coils,
    lines,
    volumes,
    sent_ref,
    mask_ref,
    table_ref,
    minus_ref,
    plus_ref,
    *refs,
):
    arrival_refs, refs = refs[:volumes], refs[volumes:]
    (out_ref, maps_ref), handed, (arrived, leaving) = refs[:2], refs[2:-2], refs[-2:]
    depth, pitch = sent_ref.shape[:2]
    volume = own_volume(depth)
    mask = pick(blocks(read_mask(mask_ref, table_ref.shape[0]), volumes), volume)
    mask = over_coils(mask, volumes * coils)

    arrivals = [halves(ref[: 2 * coils * depth]) for ref in arrival_refs]
    measured = []
    for part in range(2):
        for place in range(volumes):
            step = lax.rem(volume - place + volumes, jnp.int32(volumes))
            measured.append(pick([arrival[part] for arrival in arrivals], step))
    measured = jnp.concatenate(measured, axis=0)

    arrived[...] = sent_ref[...].astype(F32).reshape(arrived.shape)
    count = 2 * lines // LANES
    parts, reals, imags = [], [], []
    for place in range(volumes):
        first = place * (coils + 1) * count
        for coil in range(coils):
            chunks = read_rows(arrived, pitch, first + coil * count, count, depth)
            parts.append(split_complex(chunks, lines))
        chunks = read_rows(arrived, pitch, first + coils * count, count, depth)
        real, imag = split_complex(chunks, lines)
        reals.append(real)
        imags.append(imag)
    maps_real = jnp.concatenate([part[0] for part in parts], axis=0)
    maps_imag = jnp.concatenate([part[1] for part in parts], axis=0)
    maps_ref[...] = jnp.concatenate([maps_real, maps_imag], axis=0).astype(BF16)
    real_parts, imag_parts = blocks(maps_real, volumes), blocks(maps_imag, volumes)
    for step, ref in enumerate(handed, 1):
        place = lax.rem(volume + step, jnp.int32(volumes))
        both = [pick(real_parts, place), pick(imag_parts, place)]
        ref[...] = jnp.concatenate(both, axis=0).astype(BF16)

    images = spread(maps_real, maps_imag, over_rows(reals, coils), over_rows(imags, coils))
    mask = jnp.concatenate([mask, mask], axis=0)
    images = masked_normal(images, table_ref, minus_ref, plus_ref, mask)
    found = [
        *collect(maps_real, maps_imag, round_bf(measured)),
        *collect(maps_real, maps_imag, images),
        maps_real * maps_real + maps_imag * maps_imag,
    ]
    leaving[...] = jnp.zeros_like(leaving)
    sums = [row_sums(value, volumes, coils) for value in found]
    pitch = out_ref.shape[2]
    for place in range(volumes):
        chunks = [chunk for value in sums for chunk in lane_chunks(value[place])]
        write_rows(leaving, pitch, chunks, place * (pitch // volumes))
    message = leaving[...].astype(BF16).reshape(depth, *out_ref.shape[2:])
    for device in range(out_ref.shape[1]):
        out_ref[:, device] = message


def unpack_sum(sent_ref, scratch):
    total = sent_ref[:, 0].astype(F32)
    for device in range(1, sent_ref.shape[1]):
        total = total + sent_ref[:, device].astype(F32)
    scratch[...] = total.reshape(scratch.shape)


def read_image(scratch, pitch, first, count, depth):
    return jnp.concatenate(read_rows(scratch, pitch, first, count, depth), axis=1)


def read_places(scratch, pitch, first, period, count, depth, volumes):
    parts = [
        read_image(scratch, pitch, first + place * period, count, depth) for place in range(volumes)
    ]
    return jnp.concatenate(parts, axis=0)


def read_complex(scratch, pitch, first, period, count, depth, volumes):
    real = read_places(scratch, pitch, first, period, count, depth, volumes)
    imag = read_places(scratch, pitch, first + count, period, count, depth, volumes)
    return jnp.concatenate([real, imag], axis=0)


def first_refine_kernel(
    lines,
    volumes,
    sent_ref,
    first_ref,
    second_ref,
    columns_ref,
    out_ref,
    model_ref,
    arrived,
    leaving,
):
    unpack_sum(sent_ref, arrived)
    depth, pitch = sent_ref.shape[0], sent_ref.shape[2]
    rows = depth * volumes
    width = padded(lines, LANES)
    count = width // LANES
    picture = round_bf(read_complex(arrived, pitch, 0, pitch // volumes, count, depth, volumes))
    hidden = hidden_state(picture, first_ref.at[0], column(columns_ref, 0, first_ref.shape[1]))
    valid = valid_lanes(hidden.shape[0], width, lines)
    hidden = hidden * jax.nn.sigmoid(hidden)
    bias = column(columns_ref, 2 * CASCADES, 2 * rows)
    model = second_conv(hidden, second_ref.at[0], bias, rows, valid)
    model_ref[...] = model.astype(BF16)
    leaving[...] = jnp.zeros_like(leaving)
    real, imag = halves(model)
    for place, pair in enumerate(zip(blocks(real, volumes), blocks(imag, volumes))):
        chunks = lane_chunks(pair[0]) + lane_chunks(pair[1])
        write_rows(leaving, out_ref.shape[1], chunks, place * len(chunks))
    out_ref[...] = leaving[...].astype(BF16).reshape(out_ref.shape)


def slots_kernel(
    lines,
    volumes,
    sent_ref,
    model_ref,
    cotangent_ref,
    first_ref,
    first_t_ref,
    second_ref,
    second_t_ref,
    columns_ref,
    image_ref,
    spread_ref,
    arrived,
):
    unpack_sum(sent_ref, arrived)
    depth, pitch = sent_ref.shape[0], sent_ref.shape[2]
    rows = depth * volumes
    width = padded(lines, LANES)
    count = width // LANES
    begun = read_complex(arrived, pitch, 0, pitch // volumes, count, depth, volumes)
    turned = read_complex(arrived, pitch, 2 * count, pitch // volumes, count, depth, volumes)
    power = read_places(arrived, pitch, 4 * count, pitch // volumes, count, depth, volumes)
    power = jnp.concatenate([power, power], axis=0)
    cotangent = jnp.concatenate(
        split_complex(lane_chunks(cotangent_ref[...].astype(F32)), lines), axis=0
    )
    model = model_ref[...].astype(F32)
    tall = first_ref.shape[1]
    weight = [column(columns_ref, CASCADES + cascade, 2 * rows) for cascade in range(CASCADES)]

    share = [jnp.ones_like(weight[0])]
    for cascade in range(CASCADES):
        share.append(share[cascade] - weight[cascade] * (share[cascade] - 1.0))

    def slopes(hidden):
        gate = jax.nn.sigmoid(hidden)
        return hidden * gate, gate * (1.0 + hidden * (1.0 - gate))

    hidden = hidden_state(round_bf(begun), first_ref.at[0], column(columns_ref, 0, tall))
    valid = valid_lanes(hidden.shape[0], width, lines)
    unused, slope_first = slopes(hidden)
    picture = round_bf(share[1] * begun + power * model)
    hidden = hidden_state(picture, first_ref.at[1], column(columns_ref, 1, tall))
    active, slope_second = slopes(hidden)
    bias = column(columns_ref, 2 * CASCADES + 1, 2 * rows)
    later = round_bf(second_conv(active, second_ref.at[1], bias, rows, valid))
    image_ref[...] = share[2] * begun + power * (model + later)

    through = power * cotangent
    back_second = round_bf(
        pull_back(through, slope_second, first_t_ref.at[1], second_t_ref.at[1], rows, valid)
    )
    through = through - weight[1] * turned + power * back_second
    back_first = round_bf(
        pull_back(through, slope_first, first_t_ref.at[0], second_t_ref.at[0], rows, valid)
    )
    kept = (1.0 - weight[0], 1.0 - weight[1])
    of_cotangent = weight[1] + weight[0] * kept[1] + kept[0] * kept[1]
    of_second = weight[0] + kept[0]
    spread_ref[...] = of_cotangent * cotangent + of_second * back_second + back_first


def normal_kernel(
    coils,
    lines,
    volumes,
    sent_ref,
    maps_ref,
    spread_ref,
    mask_ref,
    table_ref,
    minus_ref,
    plus_ref,
    out_ref,
    arrived,
    leaving,
):
    arrived[...] = sent_ref[...].astype(F32).reshape(arrived.shape)
    depth, pitch = sent_ref.shape[:2]
    volume = own_volume(depth)
    count = maps_ref.shape[1] // LANES
    firsts = [place * 2 * count for place in range(volumes)]
    reals = [read_image(arrived, pitch, first, count, depth) for first in firsts]
    imags = [read_image(arrived, pitch, first + count, count, depth) for first in firsts]
    maps_real, maps_imag = halves(maps_ref[...].astype(F32))
    mask = over_coils(pick(blocks(read_mask(mask_ref, table_ref.shape[0]), volumes), volume), 2 * volumes * coils)
    images = spread(maps_real, maps_imag, over_rows(reals, coils), over_rows(imags, coils))
    images = masked_normal(images, table_ref, minus_ref, plus_ref, mask)
    found = [row_sums(value, volumes, coils) for value in collect(maps_real, maps_imag, images)]
    leaving[...] = jnp.zeros_like(leaving)
    pitch = out_ref.shape[2]
    first = 0
    for place in range(volumes):
        chunks = join_complex(found[0][place], found[1][place], lines)
        for target in range(volumes):
            kept = [jnp.where(volume == target, chunk, 0.0) for chunk in chunks]
            write_rows(leaving, pitch, kept, target * depth * pitch + first)
        first += len(chunks)
    write_rows(leaving, pitch, join_complex(*halves(spread_ref[...]), lines), first)
    message = leaving[...].astype(BF16).reshape(out_ref.shape[0], *out_ref.shape[2:])
    for device in range(out_ref.shape[1]):
        out_ref[:, device] = message


def end_kernel(
    coils,
    lines,
    volumes,
    columns_ref,
    sent_ref,
    image_ref,
    mask_ref,
    table_ref,
    minus_ref,
    maps_ref,
    *refs,
):
    handed, (picture_ref, grad_ref, arrived) = refs[: volumes - 1], refs[volumes - 1 :]
    slots, pitch = sent_ref.shape[0], sent_ref.shape[2]
    depth = slots // volumes
    volume = own_volume(depth)
    count = 2 * lines // LANES
    own = maps_ref[...].astype(F32)
    sources = [[pick(blocks(part, volumes), volume) for part in halves(own)]]
    sources += [halves(ref[...].astype(F32)) for ref in handed]
    maps = []
    for part in range(2):
        ordered = []
        for place in range(volumes):
            step = lax.rem(volume - place + volumes, jnp.int32(volumes))
            ordered.append(blocks(pick([source[part] for source in sources], step), coils))
        maps.append(
            jnp.concatenate([ordered[v][coil] for coil in range(coils) for v in range(volumes)], 0)
        )
    arrived[...] = sent_ref[:, 0].astype(F32).reshape(arrived.shape)
    chunks = read_rows(arrived, pitch, volumes * count, count, slots)
    real, imag = split_complex(chunks, lines)
    images = spread(*maps, over_coils(real, coils), over_coils(imag, coils))
    spectrum = depth_apply(line_apply(images, table_ref, -1.0), minus_ref)
    spectrum = spectrum * over_coils(read_mask(mask_ref, table_ref.shape[0]), 2 * coils)
    chunks = join_complex(*halves(spectrum), lines)
    write_rows(grad_ref, len(chunks), chunks)

    unpack_sum(sent_ref, arrived)
    picture = image_ref[...]
    scale = column(columns_ref, CASCADES + 1, picture.shape[0])
    parts = [[], []]
    size = depth * pitch
    total = arrived[:size]
    for other in range(1, volumes):
        total = total + arrived[other * size : (other + 1) * size]
    arrived[:size] = total
    for place in range(volumes):
        chunks = read_rows(arrived, pitch, place * count, count, depth)
        for part, value in zip(parts, split_complex(chunks, lines)):
            part.append(value)
    picture = picture - scale * jnp.concatenate(parts[0] + parts[1], axis=0)
    for index, chunk in enumerate(join_complex(*halves(picture), lines)):
        picture_ref[:, index * LANES : (index + 1) * LANES] = chunk


def call(kernel, name, operands, outs, scratch, flops, vmem_bytes=VMEM_BYTES, scalars=0):
    spaces = [pltpu.SMEM] * scalars + [pltpu.VMEM] * (len(operands) - scalars)
    moved = sum(math.prod(item.shape) * item.dtype.itemsize for item in (*operands, *outs))
    return pl.pallas_call(
        kernel,
        name=name,
        out_shape=tuple(outs),
        in_specs=[pl.BlockSpec(memory_space=space) for space in spaces],
        out_specs=tuple(pl.BlockSpec(memory_space=pltpu.VMEM) for item in outs),
        scratch_shapes=[pltpu.VMEM(shape, F32) for shape in scratch],
        compiler_params=pltpu.CompilerParams(vmem_limit_bytes=vmem_bytes),
        cost_estimate=pl.CostEstimate(flops=flops, bytes_accessed=moved, transcendentals=0),
    )(*operands)


def body(
    kspace, coil_maps, sampling, dc_weight, kernel_in, bias_in, kernel_out, bias_out, cotangent
):
    coils, slots = kspace.shape[:2]
    rows, two_lines = coil_maps.shape[2:]
    lines = two_lines // 2
    channels = bias_in.shape[1]
    coil_devices, sections = lax.axis_size("coil"), lax.axis_size("section")
    volumes = VOLUMES
    depth = slots // volumes
    width = padded(lines, LANES)
    count, whole_count = width // LANES, two_lines // LANES
    planes = coils * slots
    both = ("section", "coil")
    near = [[group * depth + t for t in range(depth)] for group in range(volumes)]
    span = depth * coil_devices
    near_both = [[group * span + t for t in range(span)] for group in range(volumes)]

    def from_group(value, step, core=0):
        pairs = [(s, ((s + step * depth) % sections) ^ core) for s in range(sections)]
        return lax.ppermute(value, "section", pairs)

    def between_cores(value):
        return lax.ppermute(value, "section", [(s, s ^ 1) for s in range(sections)])

    def exchange(value, axes, groups):
        return lax.all_to_all(value, axes, 0, 0, tiled=True, axis_index_groups=groups)

    table = jnp.asarray(line_constant(lines))
    minus = jnp.asarray(depth_constant(coils, slots, volumes, -1.0))
    plus = jnp.asarray(depth_constant(coils, slots, volumes, 1.0))
    near_plus = jnp.asarray(depth_constant(coils, depth, 1, 1.0))
    repeat, place, offset = (jnp.asarray(item) for item in conv_constants(rows, channels))
    mask = sampling.reshape(slots, lines)

    def shape(*dims, kind=F32):
        return jax.ShapeDtypeStruct(dims, kind)

    line_flops = 2 * (2 * planes) * width * (2 * width)

    pitch = padded(volumes * (coils + 1) * whole_count, 16)
    packed, *samples = call(
        functools.partial(pack_kernel, coils, volumes, pitch),
        "pack_maps",
        (
            kspace.reshape(planes, two_lines),
            coil_maps.reshape(coils * rows, two_lines),
            cotangent.reshape(rows, two_lines),
        ),
        [shape(depth, pitch, LANES, kind=BF16)]
        + [shape(coils * depth, two_lines, kind=BF16)] * (volumes - 1),
        [(depth * pitch, LANES)],
        1000,
        LARGE_VMEM_BYTES,
    )
    samples = [from_group(value, step, 1) for step, value in enumerate(samples, 1)]
    tall, wide = channels * rows, offset.shape[1]
    first, first_t, second, second_t, columns = call(
        functools.partial(taps_kernel, rows),
        "lay_out_taps",
        (
            dc_weight,
            kernel_in.transpose(0, 1, 3, 2).reshape(-1, 2, channels),
            kernel_out.reshape(-1, 2, channels),
            bias_in,
            bias_out,
            repeat,
            place,
            offset,
        ),
        [
            shape(CASCADES, tall, wide, kind=BF16),
            shape(CASCADES, 6 * rows, tall, kind=BF16),
            shape(CASCADES, 6 * rows, tall, kind=BF16),
            shape(CASCADES, tall, wide, kind=BF16),
            shape(tall, place.shape[0]),
        ],
        [(place.shape[0], repeat.shape[1])],
        2 * tall * place.shape[0] * place.shape[1],
        scalars=1,
    )
    *samples, columns = lax.optimization_barrier((*samples, columns))
    (own,) = call(
        functools.partial(own_kernel, coils, lines, volumes),
        "own_images",
        (kspace.reshape(planes, two_lines), mask, table, near_plus),
        [shape(2 * coils * depth, width)],
        [],
        line_flops,
    )
    images = [own]
    for value in samples:
        (image,) = call(
            functools.partial(far_kernel, coils, lines, volumes),
            "far_images",
            (value, mask, table, near_plus),
            [shape(FAR_PARTS * coils * depth, width)],
            [],
            line_flops,
        )
        images.append(between_cores(image))
    arrived = exchange(packed, "section", near)

    depth_pitch = padded(volumes * 5 * count, 16 * volumes)
    partial, maps, *handed = call(
        functools.partial(rows_kernel, coils, lines, volumes),
        "combine_rows",
        (arrived, mask, table, minus, plus, *images),
        [
            shape(depth, coil_devices, depth_pitch, LANES, kind=BF16),
            shape(2 * planes, width, kind=BF16),
        ]
        + [shape(2 * planes // volumes, width, kind=BF16)] * (volumes - 1),
        [(depth * pitch, LANES), (depth * depth_pitch, LANES)],
        4 * line_flops,
    )
    handed = [from_group(value, step) for step, value in enumerate(handed, 1)]

    partial = exchange(partial.reshape(-1, depth_pitch, LANES), both, near_both)
    partial = partial.reshape(depth, coil_devices, depth_pitch, LANES)

    model_pitch = padded(volumes * 2 * count, 16)
    moved, model = call(
        functools.partial(first_refine_kernel, lines, volumes),
        "refine_first",
        (partial, first, second, columns),
        [shape(depth, model_pitch, LANES, kind=BF16), shape(2 * rows, width, kind=BF16)],
        [(depth * depth_pitch, LANES), (depth * model_pitch, LANES)],
        4 * tall * wide * width,
    )
    moved = exchange(moved, "section", near)

    image, pulled = call(
        functools.partial(slots_kernel, lines, volumes),
        "refine_and_back",
        (
            partial,
            model,
            cotangent.reshape(rows, two_lines),
            first,
            first_t,
            second,
            second_t,
            columns,
        ),
        [shape(2 * rows, width), shape(2 * rows, width)],
        [(depth * depth_pitch, LANES)],
        14 * tall * wide * width,
    )

    moved, *handed = lax.optimization_barrier((moved, *handed))
    end_pitch = padded((volumes + 1) * whole_count, 16)
    (partial,) = call(
        functools.partial(normal_kernel, coils, lines, volumes),
        "masked_normal",
        (moved, maps, pulled, mask, table, minus, plus),
        [shape(slots, coil_devices, end_pitch, LANES, kind=BF16)],
        [(depth * model_pitch, LANES), (slots * end_pitch, LANES)],
        3 * line_flops,
    )
    partial = exchange(partial.reshape(-1, end_pitch, LANES), both, None)
    partial = partial.reshape(slots, coil_devices, end_pitch, LANES)

    image, grad = call(
        functools.partial(end_kernel, coils, lines, volumes),
        "outputs",
        (columns, partial, image, mask, table, minus, maps, *handed),
        [shape(rows, two_lines), shape(planes * whole_count, LANES)],
        [(slots * end_pitch, LANES)],
        2 * line_flops,
    )
    return image.reshape(1, rows, two_lines), grad.reshape(coils, slots, 1, two_lines)


def solution(mesh):
    return jax.shard_map(
        body,
        mesh=mesh,
        in_specs=(
            P("coil", None, "section", None),
            P("coil", "section", None, None),
            P(),
            P(),
            P(),
            P(),
            P(),
            P(),
            P("section", None, None),
        ),
        out_specs=(P("section", None, None), P("coil", None, "section", None)),
        check_vma=False,
    )
```

```python
import functools
import math

import jax
import jax.numpy as jnp
import ml_dtypes
import numpy as np
from jax import lax
from jax.experimental import pallas as pl
from jax.experimental.pallas import tpu as pltpu
from jax.sharding import PartitionSpec as P

CASCADES = 2
VOLUMES = 2
LANES = 128
VMEM_BYTES = 48 * 1024 * 1024
FAR_PARTS = 3
LARGE_VMEM_BYTES = 60 * 1024 * 1024

F32 = jnp.float32
BF16 = jnp.bfloat16


def padded(size, unit):
    return -(-size // unit) * unit


def dft_parts(count):
    indices = np.arange(count)
    angles = (indices[:, None] * indices[None, :] % count) * (2.0 * math.pi / count)
    factor = 1.0 / math.sqrt(count)
    return np.cos(angles) * factor, np.sin(angles) * factor


def line_constant(lines):
    width = padded(lines, LANES)
    cosine, sine = dft_parts(lines)
    table = np.zeros((width, 2 * width), np.float32)
    table[:lines, :lines] = cosine
    table[:lines, width : width + lines] = sine
    return table.astype(ml_dtypes.bfloat16)


def depth_constant(coils, slots, volumes, sign):
    cosine, sine = dft_parts(slots // volumes)
    spread_over = np.eye(coils * volumes)
    real, imag = np.kron(spread_over, cosine), sign * np.kron(spread_over, sine)
    return np.block([[real, -imag], [imag, real]]).astype(np.float32).astype(ml_dtypes.bfloat16)


def conv_constants(rows, channels):
    groups = 6
    width = padded(groups * rows, LANES)
    repeat = np.kron(np.eye(channels), np.ones((rows, 1))).astype(np.float32)
    repeat = np.pad(repeat, ((0, 0), (0, padded(channels, LANES) - channels)))
    taps = CASCADES * 3
    place = np.zeros((padded(2 * taps * groups + 3 * CASCADES, LANES), 2 * taps * width), np.float32)
    for kind in range(2):
        for tap in range(taps):
            for group in range(groups):
                start = (kind * taps + tap) * width + group * rows
                place[(kind * taps + tap) * groups + group, start : start + rows] = 1.0
    offset = np.full((channels * rows, width), -9.0, np.float32)
    row = np.arange(rows)
    offset[:, : groups * rows] = np.tile(row[None, :] - row[:, None] + 1.0, (channels, groups))
    offset = np.clip(offset, -9.0, 9.0)
    return repeat, place.astype(ml_dtypes.bfloat16), offset


def lane_index(shape):
    return lax.broadcasted_iota(jnp.int32, shape, len(shape) - 1)


def split_complex(chunks, lines):
    whole, rest = divmod(lines, LANES)
    count = padded(lines, LANES) // LANES
    if rest == 0:
        return jnp.concatenate(chunks[:count], 1), jnp.concatenate(chunks[count:], 1)
    lane = lane_index(chunks[0].shape)
    real = chunks[:whole] + [jnp.where(lane < rest, chunks[whole], 0.0)]
    turned = [pltpu.roll(chunk, LANES - rest, 1) for chunk in chunks[whole:]]
    turned.append(jnp.zeros_like(turned[0]))
    imag = [jnp.where(lane < LANES - rest, turned[k], turned[k + 1]) for k in range(count)]
    imag[-1] = jnp.where(lane < rest, imag[-1], 0.0)
    return jnp.concatenate(real, 1), jnp.concatenate(imag, 1)


def lane_chunks(value):
    return [value[:, start : start + LANES] for start in range(0, value.shape[1], LANES)]


def join_complex(real, imag, lines):
    whole, rest = divmod(lines, LANES)
    real, imag = lane_chunks(real), lane_chunks(imag)
    if rest == 0:
        return real + imag
    lane = lane_index(real[0].shape)
    turned = [real[whole]] + [pltpu.roll(chunk, rest, 1) for chunk in imag]
    mixed = [jnp.where(lane < rest, turned[k], turned[k + 1]) for k in range(len(imag))]
    return (real[:whole] + mixed)[: 2 * lines // LANES]


def halves(stacked):
    half = stacked.shape[0] // 2
    return stacked[:half], stacked[half:]


def line_apply(stacked, table_ref, sign):
    mixed = jnp.dot(stacked.astype(BF16), table_ref[...], preferred_element_type=F32)
    width = table_ref.shape[1] // 2
    top, bottom = halves(mixed)
    return jnp.concatenate(
        [
            top[:, :width] - sign * bottom[:, width:],
            bottom[:, :width] + sign * top[:, width:],
        ],
        axis=0,
    )


def depth_apply(stacked, depth_ref):
    return jnp.dot(depth_ref[...], stacked.astype(BF16), preferred_element_type=F32)


def over_coils(value, coils):
    return jnp.concatenate([value] * coils, axis=0)


def coil_sum(value, coils):
    slots = value.shape[0] // coils
    total = value[:slots]
    for coil in range(1, coils):
        total = total + value[coil * slots : (coil + 1) * slots]
    return total


def over_rows(parts, coils):
    return jnp.concatenate([part for part in parts for coil in range(coils)], axis=0)


def spread(maps_real, maps_imag, real, imag):
    return jnp.concatenate(
        [maps_real * real - maps_imag * imag, maps_real * imag + maps_imag * real], axis=0
    )


def collect(maps_real, maps_imag, images):
    real, imag = halves(images)
    return maps_real * real + maps_imag * imag, maps_real * imag - maps_imag * real


def blocks(value, count):
    size = value.shape[0] // count
    return [value[index * size : (index + 1) * size] for index in range(count)]


def row_sums(value, rows, coils):
    return [coil_sum(part, coils) for part in blocks(value, rows)]


def pick(parts, index):
    chosen = parts[0]
    for place in range(1, len(parts)):
        chosen = jnp.where(index == place, parts[place], chosen)
    return chosen


def own_volume(depth):
    return lax.div(lax.axis_index("section"), jnp.int32(depth))


def masked_normal(images, table_ref, minus_ref, plus_ref, mask):
    spectrum = depth_apply(line_apply(images, table_ref, -1.0), minus_ref)
    return line_apply(depth_apply(spectrum * mask, plus_ref), table_ref, 1.0)


def write_rows(scratch, pitch, values, first=0):
    for index, value in enumerate(values):
        scratch[pl.ds(first + index, value.shape[0], stride=pitch), :] = value


def read_rows(scratch, pitch, first, count, rows):
    return [scratch[pl.ds(first + index, rows, stride=pitch), :] for index in range(count)]


def shifted(value, step):
    if step == 0:
        return value
    width = value.shape[1]
    return pltpu.roll(value, (-step) % width, 1)


def stack_shifted(value, order):
    return jnp.concatenate([shifted(value, step) for step in order], axis=0).astype(BF16)


def add_shifted(value, order, rows):
    total = None
    for index, step in enumerate(order):
        part = shifted(value[index * rows : (index + 1) * rows], step)
        total = part if total is None else total + part
    return total


def hidden_state(image, first_ref, bias_column):
    stack = stack_shifted(image, (-1, 0, 1))
    return (
        jnp.dot(first_ref[:, : stack.shape[0]], stack, preferred_element_type=F32) + bias_column
    )


def second_conv(hidden, second_ref, bias_column, rows, valid):
    mixed = jnp.dot(
        second_ref[...], jnp.where(valid, hidden, 0.0).astype(BF16), preferred_element_type=F32
    )
    total = add_shifted(mixed, (-1, 0, 1), 2 * rows)
    return jnp.where(valid[: 2 * rows], total + bias_column, 0.0)


def pull_back(cotangent, slope, first_t_ref, second_t_ref, rows, valid):
    stack = stack_shifted(cotangent, (1, 0, -1))
    back = jnp.dot(second_t_ref[:, : stack.shape[0]], stack, preferred_element_type=F32)
    back = jnp.where(valid, back * slope, 0.0).astype(BF16)
    mixed = jnp.dot(first_t_ref[...], back, preferred_element_type=F32)
    total = add_shifted(mixed, (1, 0, -1), 2 * rows)
    return jnp.where(valid[: 2 * rows], total, 0.0)


def read_mask(sampling_ref, width):
    mask = sampling_ref[...].astype(F32)
    return jnp.pad(mask, ((0, 0), (0, width - mask.shape[1])))


def valid_lanes(rows, width, lines):
    return lane_index((rows, width)) < lines


def column(columns_ref, place, rows):
    at = 4 * 9 * CASCADES + place
    return columns_ref[:rows, at : at + 1]


def round_bf(value):
    return value.astype(BF16).astype(F32)


def choose_volume(value, coils, volumes, volume):
    parts = blocks(value, coils * volumes)
    chosen = [pick(parts[coil * volumes : (coil + 1) * volumes], volume) for coil in range(coils)]
    return jnp.concatenate(chosen, axis=0)


def pack_kernel(coils, volumes, pitch, kspace_ref, maps_ref, image_ref, out_ref, *refs):
    handed, (scratch,) = refs[:-1], refs[-1:]
    rows = image_ref.shape[0]
    depth = rows // volumes
    volume = own_volume(depth)
    kspace = kspace_ref[...].astype(F32)
    for step, ref in enumerate(handed, 1):
        other = lax.rem(volume + step, jnp.int32(volumes))
        ref[...] = choose_volume(kspace, coils, volumes, other).astype(BF16)
    count = maps_ref.shape[1] // LANES
    scratch[...] = jnp.zeros_like(scratch)
    image = image_ref[...].astype(F32)
    for coil in range(coils + 1):
        value = maps_ref[coil * rows : (coil + 1) * rows, :].astype(F32) if coil < coils else image
        for place, part in enumerate(blocks(value, volumes)):
            first = (place * (coils + 1) + coil) * count
            write_rows(scratch, pitch, lane_chunks(part), first)
    out_ref[...] = scratch[...].astype(BF16).reshape(out_ref.shape)


def taps_kernel(
    rows,
    weight_ref,
    kernel_in_ref,
    kernel_out_ref,
    bias_in_ref,
    bias_out_ref,
    repeat_ref,
    place_ref,
    offset_ref,
    first_ref,
    first_t_ref,
    second_ref,
    second_t_ref,
    columns_ref,
    taps,
):
    taps[...] = jnp.zeros_like(taps)
    channels = kernel_in_ref.shape[2]
    at = 0
    for ref in (kernel_in_ref, kernel_out_ref):
        for index in range(ref.shape[0]):
            taps[at : at + 2, :channels] = ref[index]
            at += 2
    taps[at : at + CASCADES, :channels] = bias_in_ref[...]
    at += CASCADES
    for cascade in range(CASCADES):
        taps[at : at + 1, :] = jnp.full((1, taps.shape[1]), weight_ref[cascade], F32)
        at += 1
    taps[at : at + CASCADES, : bias_out_ref.shape[1]] = bias_out_ref[...]
    tall = lax.dot_general(
        repeat_ref[...],
        taps[...],
        (((1,), (1,)), ((), ())),
        precision=lax.Precision.HIGHEST,
        preferred_element_type=F32,
    )
    columns_ref[...] = tall
    wide = jnp.dot(tall.astype(BF16), place_ref[...], preferred_element_type=F32)
    offset = offset_ref[...]
    width = offset.shape[1]
    for cascade in range(CASCADES):
        for kind, straight, turned in ((0, first_ref, first_t_ref), (1, second_t_ref, second_ref)):
            total = jnp.zeros_like(offset)
            for tap in range(3):
                start = ((kind * CASCADES + cascade) * 3 + tap) * width
                wanted = float(tap if kind == 0 else 2 - tap)
                total = total + jnp.where(offset == wanted, wide[:, start : start + width], 0.0)
            straight[cascade] = total.astype(BF16)
            turned[cascade] = total.T[: 6 * rows].astype(BF16)


def line_images(kspace, mask, lines, table_ref, plus_ref):
    real, imag = split_complex(lane_chunks(kspace), lines)
    measured = jnp.concatenate([real * mask, imag * mask], axis=0)
    return line_apply(depth_apply(measured, plus_ref), table_ref, 1.0)


def far_kernel(coils, lines, volumes, kspace_ref, mask_ref, table_ref, plus_ref, out_ref):
    parts = blocks(read_mask(mask_ref, table_ref.shape[0]), volumes)
    mask = pick(parts, own_volume(parts[0].shape[0]))
    mask = over_coils(mask, coils)
    images = line_images(kspace_ref[...].astype(F32), mask, lines, table_ref, plus_ref)
    out_ref[: images.shape[0]] = images
    if out_ref.shape[0] > images.shape[0]:
        out_ref[images.shape[0] :] = jnp.zeros_like(out_ref[images.shape[0] :])


def own_kernel(coils, lines, volumes, kspace_ref, mask_ref, table_ref, plus_ref, out_ref):
    parts = blocks(read_mask(mask_ref, table_ref.shape[0]), volumes)
    volume = own_volume(parts[0].shape[0])
    kspace = choose_volume(kspace_ref[...].astype(F32), coils, volumes, volume)
    mask = over_coils(pick(parts, volume), coils)
    out_ref[...] = line_images(kspace, mask, lines, table_ref, plus_ref)


def rows_kernel(
    coils,
    lines,
    volumes,
    sent_ref,
    mask_ref,
    table_ref,
    minus_ref,
    plus_ref,
    *refs,
):
    arrival_refs, refs = refs[:volumes], refs[volumes:]
    out_ref, maps_ref, arrived, leaving = refs
    depth, pitch = sent_ref.shape[:2]
    volume = own_volume(depth)
    mask = pick(blocks(read_mask(mask_ref, table_ref.shape[0]), volumes), volume)
    mask = over_coils(mask, volumes * coils)

    arrivals = [halves(ref[: 2 * coils * depth]) for ref in arrival_refs]
    measured = []
    for part in range(2):
        for place in range(volumes):
            step = lax.rem(volume - place + volumes, jnp.int32(volumes))
            measured.append(pick([arrival[part] for arrival in arrivals], step))
    measured = jnp.concatenate(measured, axis=0)

    arrived[...] = sent_ref[...].astype(F32).reshape(arrived.shape)
    count = 2 * lines // LANES
    parts, reals, imags = [], [], []
    for place in range(volumes):
        first = place * (coils + 1) * count
        for coil in range(coils):
            chunks = read_rows(arrived, pitch, first + coil * count, count, depth)
            parts.append(split_complex(chunks, lines))
        chunks = read_rows(arrived, pitch, first + coils * count, count, depth)
        real, imag = split_complex(chunks, lines)
        reals.append(real)
        imags.append(imag)
    maps_real = jnp.concatenate([part[0] for part in parts], axis=0)
    maps_imag = jnp.concatenate([part[1] for part in parts], axis=0)
    maps_ref[...] = jnp.concatenate([maps_real, maps_imag], axis=0).astype(BF16)

    images = spread(maps_real, maps_imag, over_rows(reals, coils), over_rows(imags, coils))
    mask = jnp.concatenate([mask, mask], axis=0)
    images = masked_normal(images, table_ref, minus_ref, plus_ref, mask)
    found = [
        *collect(maps_real, maps_imag, round_bf(measured)),
        *collect(maps_real, maps_imag, images),
        maps_real * maps_real + maps_imag * maps_imag,
    ]
    leaving[...] = jnp.zeros_like(leaving)
    sums = [row_sums(value, volumes, coils) for value in found]
    pitch = out_ref.shape[2]
    for place in range(volumes):
        chunks = [chunk for value in sums for chunk in lane_chunks(value[place])]
        write_rows(leaving, pitch, chunks, place * (pitch // volumes))
    message = leaving[...].astype(BF16).reshape(depth, *out_ref.shape[2:])
    for device in range(out_ref.shape[1]):
        out_ref[:, device] = message


def unpack_sum(sent_ref, scratch):
    total = sent_ref[:, 0].astype(F32)
    for device in range(1, sent_ref.shape[1]):
        total = total + sent_ref[:, device].astype(F32)
    scratch[...] = total.reshape(scratch.shape)


def read_image(scratch, pitch, first, count, depth):
    return jnp.concatenate(read_rows(scratch, pitch, first, count, depth), axis=1)


def read_places(scratch, pitch, first, period, count, depth, volumes):
    parts = [
        read_image(scratch, pitch, first + place * period, count, depth) for place in range(volumes)
    ]
    return jnp.concatenate(parts, axis=0)


def read_complex(scratch, pitch, first, period, count, depth, volumes):
    real = read_places(scratch, pitch, first, period, count, depth, volumes)
    imag = read_places(scratch, pitch, first + count, period, count, depth, volumes)
    return jnp.concatenate([real, imag], axis=0)


def refine_kernel(
    lines,
    volumes,
    sent_ref,
    cotangent_ref,
    first_ref,
    first_t_ref,
    second_ref,
    second_t_ref,
    columns_ref,
    out_ref,
    image_ref,
    arrived,
    leaving,
):
    unpack_sum(sent_ref, arrived)
    depth, pitch = sent_ref.shape[0], sent_ref.shape[2]
    rows = depth * volumes
    width = padded(lines, LANES)
    count = width // LANES
    begun = read_complex(arrived, pitch, 0, pitch // volumes, count, depth, volumes)
    turned = read_complex(arrived, pitch, 2 * count, pitch // volumes, count, depth, volumes)
    power = read_places(arrived, pitch, 4 * count, pitch // volumes, count, depth, volumes)
    power = jnp.concatenate([power, power], axis=0)
    cotangent = jnp.concatenate(
        split_complex(lane_chunks(cotangent_ref[...].astype(F32)), lines), axis=0
    )
    tall = first_ref.shape[1]
    weight = [column(columns_ref, CASCADES + cascade, 2 * rows) for cascade in range(CASCADES)]
    bias = [column(columns_ref, 2 * CASCADES + cascade, 2 * rows) for cascade in range(CASCADES)]

    share = [jnp.ones_like(weight[0])]
    for cascade in range(CASCADES):
        share.append(share[cascade] - weight[cascade] * (share[cascade] - 1.0))

    def slopes(hidden):
        gate = jax.nn.sigmoid(hidden)
        return hidden * gate, gate * (1.0 + hidden * (1.0 - gate))

    hidden = hidden_state(round_bf(begun), first_ref.at[0], column(columns_ref, 0, tall))
    valid = valid_lanes(hidden.shape[0], width, lines)
    active, slope_first = slopes(hidden)
    model = round_bf(second_conv(active, second_ref.at[0], bias[0], rows, valid))
    picture = round_bf(share[1] * begun + power * model)
    hidden = hidden_state(picture, first_ref.at[1], column(columns_ref, 1, tall))
    active, slope_second = slopes(hidden)
    later = round_bf(second_conv(active, second_ref.at[1], bias[1], rows, valid))
    image_ref[...] = share[2] * begun + power * (model + later)

    through = power * cotangent
    back_second = round_bf(
        pull_back(through, slope_second, first_t_ref.at[1], second_t_ref.at[1], rows, valid)
    )
    through = through - weight[1] * turned + power * back_second
    back_first = round_bf(
        pull_back(through, slope_first, first_t_ref.at[0], second_t_ref.at[0], rows, valid)
    )
    kept = (1.0 - weight[0], 1.0 - weight[1])
    of_cotangent = weight[1] + weight[0] * kept[1] + kept[0] * kept[1]
    of_second = weight[0] + kept[0]
    pulled = of_cotangent * cotangent + of_second * back_second + back_first
    leaving[...] = jnp.zeros_like(leaving)
    parts = [blocks(part, volumes) for value in (model, pulled) for part in halves(value)]
    for place in range(volumes):
        chunks = [chunk for part in parts for chunk in lane_chunks(part[place])]
        write_rows(leaving, out_ref.shape[1], chunks, place * len(chunks))
    out_ref[...] = leaving[...].astype(BF16).reshape(out_ref.shape)


def normal_kernel(
    coils,
    lines,
    volumes,
    sent_ref,
    maps_ref,
    mask_ref,
    table_ref,
    minus_ref,
    plus_ref,
    out_ref,
    *refs,
):
    pulled_refs, (arrived, leaving) = refs[:volumes], refs[volumes:]
    arrived[...] = sent_ref[...].astype(F32).reshape(arrived.shape)
    depth, pitch = sent_ref.shape[:2]
    volume = own_volume(depth)
    count = maps_ref.shape[1] // LANES
    fields = [
        [
            read_image(arrived, pitch, (place * 4 + field) * count, count, depth)
            for place in range(volumes)
        ]
        for field in range(4)
    ]
    reals, imags = fields[:2]
    maps_real, maps_imag = halves(maps_ref[...].astype(F32))
    parts = [blocks(maps_real, volumes), blocks(maps_imag, volumes), *fields[2:]]
    for step, ref in enumerate(pulled_refs):
        place = lax.rem(volume + step, jnp.int32(volumes))
        chosen = [pick(part, place) for part in parts]
        ref[...] = jnp.concatenate(chosen, axis=0).astype(BF16)
    mask = over_coils(pick(blocks(read_mask(mask_ref, table_ref.shape[0]), volumes), volume), 2 * volumes * coils)
    images = spread(maps_real, maps_imag, over_rows(reals, coils), over_rows(imags, coils))
    images = masked_normal(images, table_ref, minus_ref, plus_ref, mask)
    found = [row_sums(value, volumes, coils) for value in collect(maps_real, maps_imag, images)]
    leaving[...] = jnp.zeros_like(leaving)
    for place in range(volumes):
        chunks = join_complex(found[0][place], found[1][place], lines)
        write_rows(leaving, out_ref.shape[2], chunks, place * len(chunks))
    message = leaving[...].astype(BF16).reshape(depth, *out_ref.shape[2:])
    for device in range(out_ref.shape[1]):
        out_ref[:, device] = message


def from_volumes(refs, volume, parts, volumes):
    sources = [blocks(ref, parts) for ref in refs]
    ordered = []
    for place in range(volumes):
        step = lax.rem(volume - place + volumes, jnp.int32(volumes))
        ordered.append([pick([source[part] for source in sources], step) for part in range(parts)])
    return ordered


def end_kernel(
    coils,
    lines,
    volumes,
    columns_ref,
    sent_ref,
    image_ref,
    mask_ref,
    table_ref,
    minus_ref,
    *refs,
):
    handed = [ref[...].astype(F32) for ref in refs[:volumes]]
    picture_ref, grad_ref, arrived = refs[volumes:]
    depth, pitch = sent_ref.shape[0], sent_ref.shape[2]
    volume = own_volume(depth)
    count = 2 * lines // LANES
    planes = coils * depth
    maps = [value[: 2 * planes] for value in handed]
    maps = from_volumes(maps, volume, 2 * coils, volumes)
    maps = [
        jnp.concatenate([maps[v][first + coil] for coil in range(coils) for v in range(volumes)], 0)
        for first in (0, coils)
    ]
    pulled = from_volumes([value[2 * planes :] for value in handed], volume, 2, volumes)
    real, imag = [jnp.concatenate([part[field] for part in pulled], 0) for field in range(2)]
    images = spread(*maps, over_coils(real, coils), over_coils(imag, coils))
    spectrum = depth_apply(line_apply(images, table_ref, -1.0), minus_ref)
    spectrum = spectrum * over_coils(read_mask(mask_ref, table_ref.shape[0]), 2 * coils)
    chunks = join_complex(*halves(spectrum), lines)
    write_rows(grad_ref, len(chunks), chunks)

    unpack_sum(sent_ref, arrived)
    parts = [[], []]
    for place in range(volumes):
        chunks = read_rows(arrived, pitch, place * count, count, depth)
        for part, value in zip(parts, split_complex(chunks, lines)):
            part.append(value)
    picture = image_ref[...]
    scale = column(columns_ref, CASCADES + 1, picture.shape[0])
    picture = picture - scale * jnp.concatenate(parts[0] + parts[1], axis=0)
    for index, chunk in enumerate(join_complex(*halves(picture), lines)):
        picture_ref[:, index * LANES : (index + 1) * LANES] = chunk


def call(kernel, name, operands, outs, scratch, flops, vmem_bytes=VMEM_BYTES, scalars=0):
    spaces = [pltpu.SMEM] * scalars + [pltpu.VMEM] * (len(operands) - scalars)
    moved = sum(math.prod(item.shape) * item.dtype.itemsize for item in (*operands, *outs))
    return pl.pallas_call(
        kernel,
        name=name,
        out_shape=tuple(outs),
        in_specs=[pl.BlockSpec(memory_space=space) for space in spaces],
        out_specs=tuple(pl.BlockSpec(memory_space=pltpu.VMEM) for item in outs),
        scratch_shapes=[pltpu.VMEM(shape, F32) for shape in scratch],
        compiler_params=pltpu.CompilerParams(vmem_limit_bytes=vmem_bytes),
        cost_estimate=pl.CostEstimate(flops=flops, bytes_accessed=moved, transcendentals=0),
    )(*operands)


def body(
    kspace, coil_maps, sampling, dc_weight, kernel_in, bias_in, kernel_out, bias_out, cotangent
):
    coils, slots = kspace.shape[:2]
    rows, two_lines = coil_maps.shape[2:]
    lines = two_lines // 2
    channels = bias_in.shape[1]
    coil_devices, sections = lax.axis_size("coil"), lax.axis_size("section")
    volumes = VOLUMES
    depth = slots // volumes
    width = padded(lines, LANES)
    count, whole_count = width // LANES, two_lines // LANES
    planes = coils * slots
    both = ("section", "coil")
    near = [[group * depth + t for t in range(depth)] for group in range(volumes)]
    span = depth * coil_devices
    near_both = [[group * span + t for t in range(span)] for group in range(volumes)]

    def from_group(value, step, core=0):
        pairs = [(s, ((s + step * depth) % sections) ^ core) for s in range(sections)]
        return lax.ppermute(value, "section", pairs)

    def between_cores(value):
        return lax.ppermute(value, "section", [(s, s ^ 1) for s in range(sections)])

    def exchange(value, axes, groups):
        return lax.all_to_all(value, axes, 0, 0, tiled=True, axis_index_groups=groups)

    table = jnp.asarray(line_constant(lines))
    minus = jnp.asarray(depth_constant(coils, slots, volumes, -1.0))
    plus = jnp.asarray(depth_constant(coils, slots, volumes, 1.0))
    near_plus = jnp.asarray(depth_constant(coils, depth, 1, 1.0))
    repeat, place, offset = (jnp.asarray(item) for item in conv_constants(rows, channels))
    mask = sampling.reshape(slots, lines)

    def shape(*dims, kind=F32):
        return jax.ShapeDtypeStruct(dims, kind)

    line_flops = 2 * (2 * planes) * width * (2 * width)

    pitch = padded(volumes * (coils + 1) * whole_count, 16)
    packed, *samples = call(
        functools.partial(pack_kernel, coils, volumes, pitch),
        "pack_maps",
        (
            kspace.reshape(planes, two_lines),
            coil_maps.reshape(coils * rows, two_lines),
            cotangent.reshape(rows, two_lines),
        ),
        [shape(depth, pitch, LANES, kind=BF16)]
        + [shape(coils * depth, two_lines, kind=BF16)] * (volumes - 1),
        [(depth * pitch, LANES)],
        1000,
        LARGE_VMEM_BYTES,
    )
    samples = [from_group(value, step, 1) for step, value in enumerate(samples, 1)]
    tall, wide = channels * rows, offset.shape[1]
    first, first_t, second, second_t, columns = call(
        functools.partial(taps_kernel, rows),
        "lay_out_taps",
        (
            dc_weight,
            kernel_in.transpose(0, 1, 3, 2).reshape(-1, 2, channels),
            kernel_out.reshape(-1, 2, channels),
            bias_in,
            bias_out,
            repeat,
            place,
            offset,
        ),
        [
            shape(CASCADES, tall, wide, kind=BF16),
            shape(CASCADES, 6 * rows, tall, kind=BF16),
            shape(CASCADES, 6 * rows, tall, kind=BF16),
            shape(CASCADES, tall, wide, kind=BF16),
            shape(tall, place.shape[0]),
        ],
        [(place.shape[0], repeat.shape[1])],
        2 * tall * place.shape[0] * place.shape[1],
        scalars=1,
    )
    *samples, columns = lax.optimization_barrier((*samples, columns))
    (own,) = call(
        functools.partial(own_kernel, coils, lines, volumes),
        "own_images",
        (kspace.reshape(planes, two_lines), mask, table, near_plus),
        [shape(2 * coils * depth, width)],
        [],
        line_flops,
    )
    images = [own]
    for value in samples:
        (image,) = call(
            functools.partial(far_kernel, coils, lines, volumes),
            "far_images",
            (value, mask, table, near_plus),
            [shape(FAR_PARTS * coils * depth, width)],
            [],
            line_flops,
        )
        images.append(between_cores(image))
    arrived = exchange(packed, "section", near)

    depth_pitch = padded(volumes * 5 * count, 16 * volumes)
    partial, maps = call(
        functools.partial(rows_kernel, coils, lines, volumes),
        "combine_rows",
        (arrived, mask, table, minus, plus, *images),
        [
            shape(depth, coil_devices, depth_pitch, LANES, kind=BF16),
            shape(2 * planes, width, kind=BF16),
        ],
        [(depth * pitch, LANES), (depth * depth_pitch, LANES)],
        4 * line_flops,
    )

    partial = exchange(partial.reshape(-1, depth_pitch, LANES), both, near_both)
    partial = partial.reshape(depth, coil_devices, depth_pitch, LANES)

    model_pitch = padded(volumes * 4 * count, 8)
    moved, image = call(
        functools.partial(refine_kernel, lines, volumes),
        "refine_and_back",
        (
            partial,
            cotangent.reshape(rows, two_lines),
            first,
            first_t,
            second,
            second_t,
            columns,
        ),
        [shape(depth, model_pitch, LANES, kind=BF16), shape(2 * rows, width)],
        [(depth * depth_pitch, LANES), (depth * model_pitch, LANES)],
        14 * tall * wide * width,
    )
    moved = exchange(moved, "section", near)

    end_pitch = padded(volumes * whole_count, 16)
    partial, *handed = call(
        functools.partial(normal_kernel, coils, lines, volumes),
        "masked_normal",
        (moved, maps, mask, table, minus, plus),
        [shape(depth, coil_devices, end_pitch, LANES, kind=BF16)]
        + [shape(2 * planes // volumes + 2 * depth, width, kind=BF16)] * volumes,
        [(depth * model_pitch, LANES), (depth * end_pitch, LANES)],
        3 * line_flops,
    )
    partial = exchange(partial.reshape(-1, end_pitch, LANES), both, near_both)
    partial = partial.reshape(depth, coil_devices, end_pitch, LANES)
    handed[1:] = [
        between_cores(from_group(value, step, 1)) for step, value in enumerate(handed[1:], 1)
    ]

    image, grad = call(
        functools.partial(end_kernel, coils, lines, volumes),
        "outputs",
        (columns, partial, image, mask, table, minus, *handed),
        [shape(rows, two_lines), shape(planes * whole_count, LANES)],
        [(depth * end_pitch, LANES)],
        2 * line_flops,
    )
    return image.reshape(1, rows, two_lines), grad.reshape(coils, slots, 1, two_lines)


def solution(mesh):
    return jax.shard_map(
        body,
        mesh=mesh,
        in_specs=(
            P("coil", None, "section", None),
            P("coil", "section", None, None),
            P(),
            P(),
            P(),
            P(),
            P(),
            P(),
            P("section", None, None),
        ),
        out_specs=(P("section", None, None), P("coil", None, "section", None)),
        check_vma=False,
    )
```

```python
import functools
import math

import jax
import jax.numpy as jnp
import ml_dtypes
import numpy as np
from jax import lax
from jax.experimental import pallas as pl
from jax.experimental.pallas import tpu as pltpu
from jax.sharding import PartitionSpec as P

CASCADES = 2
VOLUMES = 2
LANES = 128
VMEM_BYTES = 48 * 1024 * 1024
FAR_PARTS = 3
LARGE_VMEM_BYTES = 60 * 1024 * 1024

F32 = jnp.float32
BF16 = jnp.bfloat16


def padded(size, unit):
    return -(-size // unit) * unit


def dft_parts(count):
    indices = np.arange(count)
    angles = (indices[:, None] * indices[None, :] % count) * (2.0 * math.pi / count)
    factor = 1.0 / math.sqrt(count)
    return np.cos(angles) * factor, np.sin(angles) * factor


def line_constant(lines):
    width = padded(lines, LANES)
    cosine, sine = dft_parts(lines)
    table = np.zeros((width, 2 * width), np.float32)
    table[:lines, :lines] = cosine
    table[:lines, width : width + lines] = sine
    return table.astype(ml_dtypes.bfloat16)


def depth_constant(coils, slots, volumes, sign):
    cosine, sine = dft_parts(slots // volumes)
    spread_over = np.eye(coils * volumes)
    real, imag = np.kron(spread_over, cosine), sign * np.kron(spread_over, sine)
    return np.block([[real, -imag], [imag, real]]).astype(np.float32).astype(ml_dtypes.bfloat16)


def conv_constants(rows, channels):
    groups = 6
    width = padded(groups * rows, LANES)
    repeat = np.kron(np.eye(channels), np.ones((rows, 1))).astype(np.float32)
    repeat = np.pad(repeat, ((0, 0), (0, padded(channels, LANES) - channels)))
    taps = CASCADES * 3
    place = np.zeros((padded(2 * taps * groups + 3 * CASCADES, LANES), 2 * taps * width), np.float32)
    for kind in range(2):
        for tap in range(taps):
            for group in range(groups):
                start = (kind * taps + tap) * width + group * rows
                place[(kind * taps + tap) * groups + group, start : start + rows] = 1.0
    offset = np.full((channels * rows, width), -9.0, np.float32)
    row = np.arange(rows)
    offset[:, : groups * rows] = np.tile(row[None, :] - row[:, None] + 1.0, (channels, groups))
    offset = np.clip(offset, -9.0, 9.0)
    return repeat, place.astype(ml_dtypes.bfloat16), offset


def lane_index(shape):
    return lax.broadcasted_iota(jnp.int32, shape, len(shape) - 1)


def split_complex(chunks, lines):
    whole, rest = divmod(lines, LANES)
    count = padded(lines, LANES) // LANES
    if rest == 0:
        return jnp.concatenate(chunks[:count], 1), jnp.concatenate(chunks[count:], 1)
    lane = lane_index(chunks[0].shape)
    real = chunks[:whole] + [jnp.where(lane < rest, chunks[whole], 0.0)]
    turned = [pltpu.roll(chunk, LANES - rest, 1) for chunk in chunks[whole:]]
    turned.append(jnp.zeros_like(turned[0]))
    imag = [jnp.where(lane < LANES - rest, turned[k], turned[k + 1]) for k in range(count)]
    imag[-1] = jnp.where(lane < rest, imag[-1], 0.0)
    return jnp.concatenate(real, 1), jnp.concatenate(imag, 1)


def lane_chunks(value):
    return [value[:, start : start + LANES] for start in range(0, value.shape[1], LANES)]


def join_complex(real, imag, lines):
    whole, rest = divmod(lines, LANES)
    real, imag = lane_chunks(real), lane_chunks(imag)
    if rest == 0:
        return real + imag
    lane = lane_index(real[0].shape)
    turned = [real[whole]] + [pltpu.roll(chunk, rest, 1) for chunk in imag]
    mixed = [jnp.where(lane < rest, turned[k], turned[k + 1]) for k in range(len(imag))]
    return (real[:whole] + mixed)[: 2 * lines // LANES]


def halves(stacked):
    half = stacked.shape[0] // 2
    return stacked[:half], stacked[half:]


def line_apply(stacked, table_ref, sign):
    mixed = jnp.dot(stacked.astype(BF16), table_ref[...], preferred_element_type=F32)
    width = table_ref.shape[1] // 2
    top, bottom = halves(mixed)
    return jnp.concatenate(
        [
            top[:, :width] - sign * bottom[:, width:],
            bottom[:, :width] + sign * top[:, width:],
        ],
        axis=0,
    )


def depth_apply(stacked, depth_ref):
    return jnp.dot(depth_ref[...], stacked.astype(BF16), preferred_element_type=F32)


def over_coils(value, coils):
    return jnp.concatenate([value] * coils, axis=0)


def coil_sum(value, coils):
    slots = value.shape[0] // coils
    total = value[:slots]
    for coil in range(1, coils):
        total = total + value[coil * slots : (coil + 1) * slots]
    return total


def over_rows(parts, coils):
    return jnp.concatenate([part for part in parts for coil in range(coils)], axis=0)


def spread(maps_real, maps_imag, real, imag):
    return jnp.concatenate(
        [maps_real * real - maps_imag * imag, maps_real * imag + maps_imag * real], axis=0
    )


def collect(maps_real, maps_imag, images):
    real, imag = halves(images)
    return maps_real * real + maps_imag * imag, maps_real * imag - maps_imag * real


def blocks(value, count):
    size = value.shape[0] // count
    return [value[index * size : (index + 1) * size] for index in range(count)]


def row_sums(value, rows, coils):
    return [coil_sum(part, coils) for part in blocks(value, rows)]


def pick(parts, index):
    chosen = parts[0]
    for place in range(1, len(parts)):
        chosen = jnp.where(index == place, parts[place], chosen)
    return chosen


def own_volume(depth):
    return lax.div(lax.axis_index("section"), jnp.int32(depth))


def masked_normal(images, table_ref, minus_ref, plus_ref, mask):
    spectrum = depth_apply(line_apply(images, table_ref, -1.0), minus_ref)
    return line_apply(depth_apply(spectrum * mask, plus_ref), table_ref, 1.0)


def write_rows(scratch, pitch, values, first=0):
    for index, value in enumerate(values):
        scratch[pl.ds(first + index, value.shape[0], stride=pitch), :] = value


def read_rows(scratch, pitch, first, count, rows):
    return [scratch[pl.ds(first + index, rows, stride=pitch), :] for index in range(count)]


def shifted(value, step):
    if step == 0:
        return value
    width = value.shape[1]
    return pltpu.roll(value, (-step) % width, 1)


def stack_shifted(value, order):
    return jnp.concatenate([shifted(value, step) for step in order], axis=0).astype(BF16)


def add_shifted(value, order, rows):
    total = None
    for index, step in enumerate(order):
        part = shifted(value[index * rows : (index + 1) * rows], step)
        total = part if total is None else total + part
    return total


def hidden_state(image, first_ref, bias_column):
    stack = stack_shifted(image, (-1, 0, 1))
    return (
        jnp.dot(first_ref[:, : stack.shape[0]], stack, preferred_element_type=F32) + bias_column
    )


def second_conv(hidden, second_ref, bias_column, rows, valid):
    mixed = jnp.dot(
        second_ref[...], jnp.where(valid, hidden, 0.0).astype(BF16), preferred_element_type=F32
    )
    total = add_shifted(mixed, (-1, 0, 1), 2 * rows)
    return jnp.where(valid[: 2 * rows], total + bias_column, 0.0)


def pull_back(cotangent, slope, first_t_ref, second_t_ref, rows, valid):
    stack = stack_shifted(cotangent, (1, 0, -1))
    back = jnp.dot(second_t_ref[:, : stack.shape[0]], stack, preferred_element_type=F32)
    back = jnp.where(valid, back * slope, 0.0).astype(BF16)
    mixed = jnp.dot(first_t_ref[...], back, preferred_element_type=F32)
    total = add_shifted(mixed, (1, 0, -1), 2 * rows)
    return jnp.where(valid[: 2 * rows], total, 0.0)


def read_mask(sampling_ref, width):
    mask = sampling_ref[...].astype(F32)
    return jnp.pad(mask, ((0, 0), (0, width - mask.shape[1])))


def valid_lanes(rows, width, lines):
    return lane_index((rows, width)) < lines


def column(columns_ref, place, rows):
    at = 4 * 9 * CASCADES + place
    return columns_ref[:rows, at : at + 1]


def round_bf(value):
    return value.astype(BF16).astype(F32)


def choose_volume(value, coils, volumes, volume):
    parts = blocks(value, coils * volumes)
    chosen = [pick(parts[coil * volumes : (coil + 1) * volumes], volume) for coil in range(coils)]
    return jnp.concatenate(chosen, axis=0)


def pack_kernel(coils, volumes, pitch, kspace_ref, maps_ref, image_ref, out_ref, *refs):
    handed, (scratch,) = refs[:-1], refs[-1:]
    rows = image_ref.shape[0]
    depth = rows // volumes
    volume = own_volume(depth)
    kspace = kspace_ref[...].astype(F32)
    for step, ref in enumerate(handed, 1):
        other = lax.rem(volume + step, jnp.int32(volumes))
        ref[...] = choose_volume(kspace, coils, volumes, other).astype(BF16)
    count = maps_ref.shape[1] // LANES
    scratch[...] = jnp.zeros_like(scratch)
    image = image_ref[...].astype(F32)
    for coil in range(coils + 1):
        value = maps_ref[coil * rows : (coil + 1) * rows, :].astype(F32) if coil < coils else image
        for place, part in enumerate(blocks(value, volumes)):
            first = (place * (coils + 1) + coil) * count
            write_rows(scratch, pitch, lane_chunks(part), first)
    out_ref[...] = scratch[...].astype(BF16).reshape(out_ref.shape)


def taps_kernel(
    rows,
    weight_ref,
    kernel_in_ref,
    kernel_out_ref,
    bias_in_ref,
    bias_out_ref,
    repeat_ref,
    place_ref,
    offset_ref,
    first_ref,
    first_t_ref,
    second_ref,
    second_t_ref,
    columns_ref,
    taps,
):
    taps[...] = jnp.zeros_like(taps)
    channels = kernel_in_ref.shape[2]
    at = 0
    for ref in (kernel_in_ref, kernel_out_ref):
        for index in range(ref.shape[0]):
            taps[at : at + 2, :channels] = ref[index]
            at += 2
    taps[at : at + CASCADES, :channels] = bias_in_ref[...]
    at += CASCADES
    for cascade in range(CASCADES):
        taps[at : at + 1, :] = jnp.full((1, taps.shape[1]), weight_ref[cascade], F32)
        at += 1
    taps[at : at + CASCADES, : bias_out_ref.shape[1]] = bias_out_ref[...]
    tall = lax.dot_general(
        repeat_ref[...],
        taps[...],
        (((1,), (1,)), ((), ())),
        precision=lax.Precision.HIGHEST,
        preferred_element_type=F32,
    )
    columns_ref[...] = tall
    wide = jnp.dot(tall.astype(BF16), place_ref[...], preferred_element_type=F32)
    offset = offset_ref[...]
    width = offset.shape[1]
    for cascade in range(CASCADES):
        for kind, straight, turned in ((0, first_ref, first_t_ref), (1, second_t_ref, second_ref)):
            total = jnp.zeros_like(offset)
            for tap in range(3):
                start = ((kind * CASCADES + cascade) * 3 + tap) * width
                wanted = float(tap if kind == 0 else 2 - tap)
                total = total + jnp.where(offset == wanted, wide[:, start : start + width], 0.0)
            straight[cascade] = total.astype(BF16)
            turned[cascade] = total.T[: 6 * rows].astype(BF16)


def line_images(kspace, mask, lines, table_ref, plus_ref):
    real, imag = split_complex(lane_chunks(kspace), lines)
    measured = jnp.concatenate([real * mask, imag * mask], axis=0)
    return line_apply(depth_apply(measured, plus_ref), table_ref, 1.0)


def far_kernel(coils, lines, volumes, kspace_ref, mask_ref, table_ref, plus_ref, out_ref):
    parts = blocks(read_mask(mask_ref, table_ref.shape[0]), volumes)
    mask = pick(parts, own_volume(parts[0].shape[0]))
    mask = over_coils(mask, coils)
    images = line_images(kspace_ref[...].astype(F32), mask, lines, table_ref, plus_ref)
    out_ref[: images.shape[0]] = images
    if out_ref.shape[0] > images.shape[0]:
        out_ref[images.shape[0] :] = jnp.zeros_like(out_ref[images.shape[0] :])


def own_kernel(coils, lines, volumes, kspace_ref, mask_ref, table_ref, plus_ref, out_ref):
    parts = blocks(read_mask(mask_ref, table_ref.shape[0]), volumes)
    volume = own_volume(parts[0].shape[0])
    kspace = choose_volume(kspace_ref[...].astype(F32), coils, volumes, volume)
    mask = over_coils(pick(parts, volume), coils)
    out_ref[...] = line_images(kspace, mask, lines, table_ref, plus_ref)


def rows_kernel(
    coils,
    lines,
    volumes,
    sent_ref,
    mask_ref,
    table_ref,
    minus_ref,
    plus_ref,
    *refs,
):
    arrival_refs, refs = refs[:volumes], refs[volumes:]
    out_ref, maps_ref, arrived, leaving = refs
    depth, pitch = sent_ref.shape[:2]
    volume = own_volume(depth)
    mask = pick(blocks(read_mask(mask_ref, table_ref.shape[0]), volumes), volume)
    mask = over_coils(mask, volumes * coils)

    arrivals = [halves(ref[: 2 * coils * depth]) for ref in arrival_refs]
    measured = []
    for part in range(2):
        for place in range(volumes):
            step = lax.rem(volume - place + volumes, jnp.int32(volumes))
            measured.append(pick([arrival[part] for arrival in arrivals], step))
    measured = jnp.concatenate(measured, axis=0)

    arrived[...] = sent_ref[...].astype(F32).reshape(arrived.shape)
    count = 2 * lines // LANES
    parts, reals, imags = [], [], []
    for place in range(volumes):
        first = place * (coils + 1) * count
        for coil in range(coils):
            chunks = read_rows(arrived, pitch, first + coil * count, count, depth)
            parts.append(split_complex(chunks, lines))
        chunks = read_rows(arrived, pitch, first + coils * count, count, depth)
        real, imag = split_complex(chunks, lines)
        reals.append(real)
        imags.append(imag)
    maps_real = jnp.concatenate([part[0] for part in parts], axis=0)
    maps_imag = jnp.concatenate([part[1] for part in parts], axis=0)
    maps_ref[...] = jnp.concatenate([maps_real, maps_imag], axis=0).astype(BF16)

    images = spread(maps_real, maps_imag, over_rows(reals, coils), over_rows(imags, coils))
    mask = jnp.concatenate([mask, mask], axis=0)
    images = masked_normal(images, table_ref, minus_ref, plus_ref, mask)
    found = [
        *collect(maps_real, maps_imag, round_bf(measured)),
        *collect(maps_real, maps_imag, images),
        maps_real * maps_real + maps_imag * maps_imag,
    ]
    leaving[...] = jnp.zeros_like(leaving)
    sums = [row_sums(value, volumes, coils) for value in found]
    pitch = out_ref.shape[2]
    for place in range(volumes):
        chunks = [chunk for value in sums for chunk in lane_chunks(value[place])]
        write_rows(leaving, pitch, chunks, place * (pitch // volumes))
    message = leaving[...].astype(BF16).reshape(depth, *out_ref.shape[2:])
    for device in range(out_ref.shape[1]):
        out_ref[:, device] = message


def unpack_sum(sent_ref, scratch):
    total = sent_ref[:, 0].astype(F32)
    for device in range(1, sent_ref.shape[1]):
        total = total + sent_ref[:, device].astype(F32)
    scratch[...] = total.reshape(scratch.shape)


def read_image(scratch, pitch, first, count, depth):
    return jnp.concatenate(read_rows(scratch, pitch, first, count, depth), axis=1)


def read_places(scratch, pitch, first, period, count, depth, volumes):
    parts = [
        read_image(scratch, pitch, first + place * period, count, depth) for place in range(volumes)
    ]
    return jnp.concatenate(parts, axis=0)


def read_complex(scratch, pitch, first, period, count, depth, volumes):
    real = read_places(scratch, pitch, first, period, count, depth, volumes)
    imag = read_places(scratch, pitch, first + count, period, count, depth, volumes)
    return jnp.concatenate([real, imag], axis=0)


def refine_kernel(
    lines,
    volumes,
    sent_ref,
    cotangent_ref,
    first_ref,
    first_t_ref,
    second_ref,
    second_t_ref,
    columns_ref,
    out_ref,
    image_ref,
    arrived,
    leaving,
):
    unpack_sum(sent_ref, arrived)
    depth, pitch = sent_ref.shape[0], sent_ref.shape[2]
    rows = depth * volumes
    width = padded(lines, LANES)
    count = width // LANES
    begun = read_complex(arrived, pitch, 0, pitch // volumes, count, depth, volumes)
    turned = read_complex(arrived, pitch, 2 * count, pitch // volumes, count, depth, volumes)
    power = read_places(arrived, pitch, 4 * count, pitch // volumes, count, depth, volumes)
    power = jnp.concatenate([power, power], axis=0)
    cotangent = jnp.concatenate(
        split_complex(lane_chunks(cotangent_ref[...].astype(F32)), lines), axis=0
    )
    tall = first_ref.shape[1]
    weight = [column(columns_ref, CASCADES + cascade, 2 * rows) for cascade in range(CASCADES)]
    bias = [column(columns_ref, 2 * CASCADES + cascade, 2 * rows) for cascade in range(CASCADES)]

    share = [jnp.ones_like(weight[0])]
    for cascade in range(CASCADES):
        share.append(share[cascade] - weight[cascade] * (share[cascade] - 1.0))

    def slopes(hidden):
        gate = jax.nn.sigmoid(hidden)
        return hidden * gate, gate * (1.0 + hidden * (1.0 - gate))

    hidden = hidden_state(round_bf(begun), first_ref.at[0], column(columns_ref, 0, tall))
    valid = valid_lanes(hidden.shape[0], width, lines)
    active, slope_first = slopes(hidden)
    model = round_bf(second_conv(active, second_ref.at[0], bias[0], rows, valid))
    picture = round_bf(share[1] * begun + power * model)
    hidden = hidden_state(picture, first_ref.at[1], column(columns_ref, 1, tall))
    active, slope_second = slopes(hidden)
    later = round_bf(second_conv(active, second_ref.at[1], bias[1], rows, valid))
    image_ref[...] = share[2] * begun + power * (model + later)

    through = power * cotangent
    back_second = round_bf(
        pull_back(through, slope_second, first_t_ref.at[1], second_t_ref.at[1], rows, valid)
    )
    through = through - weight[1] * turned + power * back_second
    back_first = round_bf(
        pull_back(through, slope_first, first_t_ref.at[0], second_t_ref.at[0], rows, valid)
    )
    kept = (1.0 - weight[0], 1.0 - weight[1])
    of_cotangent = weight[1] + weight[0] * kept[1] + kept[0] * kept[1]
    of_second = weight[0] + kept[0]
    pulled = of_cotangent * cotangent + of_second * back_second + back_first
    leaving[...] = jnp.zeros_like(leaving)
    parts = [blocks(part, volumes) for value in (model, pulled) for part in halves(value)]
    for place in range(volumes):
        chunks = [chunk for part in parts for chunk in lane_chunks(part[place])]
        write_rows(leaving, out_ref.shape[1], chunks, place * len(chunks))
    out_ref[...] = leaving[...].astype(BF16).reshape(out_ref.shape)


def hand_kernel(volumes, sent_ref, maps_ref, *refs):
    outs, (arrived,) = refs[:-1], refs[-1:]
    arrived[...] = sent_ref[...].astype(F32).reshape(arrived.shape)
    depth, pitch = sent_ref.shape[:2]
    volume = own_volume(depth)
    count = maps_ref.shape[1] // LANES
    parts = [blocks(part, volumes) for part in halves(maps_ref[...].astype(F32))]
    for field in (2, 3):
        parts.append(
            [
                read_image(arrived, pitch, (place * 4 + field) * count, count, depth)
                for place in range(volumes)
            ]
        )
    for step, ref in enumerate(outs):
        place = lax.rem(volume + step, jnp.int32(volumes))
        chosen = [pick(part, place) for part in parts]
        ref[...] = jnp.concatenate(chosen, axis=0).astype(BF16)


def normal_kernel(
    coils,
    lines,
    volumes,
    sent_ref,
    maps_ref,
    mask_ref,
    table_ref,
    minus_ref,
    plus_ref,
    out_ref,
    arrived,
    leaving,
):
    arrived[...] = sent_ref[...].astype(F32).reshape(arrived.shape)
    depth, pitch = sent_ref.shape[:2]
    volume = own_volume(depth)
    count = maps_ref.shape[1] // LANES
    fields = [
        [
            read_image(arrived, pitch, (place * 4 + field) * count, count, depth)
            for place in range(volumes)
        ]
        for field in range(2)
    ]
    reals, imags = fields
    maps_real, maps_imag = halves(maps_ref[...].astype(F32))
    mask = over_coils(pick(blocks(read_mask(mask_ref, table_ref.shape[0]), volumes), volume), 2 * volumes * coils)
    images = spread(maps_real, maps_imag, over_rows(reals, coils), over_rows(imags, coils))
    images = masked_normal(images, table_ref, minus_ref, plus_ref, mask)
    found = [row_sums(value, volumes, coils) for value in collect(maps_real, maps_imag, images)]
    leaving[...] = jnp.zeros_like(leaving)
    for place in range(volumes):
        chunks = join_complex(found[0][place], found[1][place], lines)
        write_rows(leaving, out_ref.shape[2], chunks, place * len(chunks))
    message = leaving[...].astype(BF16).reshape(depth, *out_ref.shape[2:])
    for device in range(out_ref.shape[1]):
        out_ref[:, device] = message


def from_volumes(refs, volume, parts, volumes):
    sources = [blocks(ref, parts) for ref in refs]
    ordered = []
    for place in range(volumes):
        step = lax.rem(volume - place + volumes, jnp.int32(volumes))
        ordered.append([pick([source[part] for source in sources], step) for part in range(parts)])
    return ordered


def grad_kernel(
    coils,
    lines,
    volumes,
    mask_ref,
    table_ref,
    minus_ref,
    *refs,
):
    handed, (grad_ref,) = [ref[...].astype(F32) for ref in refs[:volumes]], refs[volumes:]
    depth = mask_ref.shape[0] // volumes
    volume = own_volume(depth)
    planes = coils * depth
    maps = [value[: 2 * planes] for value in handed]
    maps = from_volumes(maps, volume, 2 * coils, volumes)
    maps = [
        jnp.concatenate([maps[v][first + coil] for coil in range(coils) for v in range(volumes)], 0)
        for first in (0, coils)
    ]
    pulled = from_volumes([value[2 * planes :] for value in handed], volume, 2, volumes)
    real, imag = [jnp.concatenate([part[field] for part in pulled], 0) for field in range(2)]
    images = spread(*maps, over_coils(real, coils), over_coils(imag, coils))
    spectrum = depth_apply(line_apply(images, table_ref, -1.0), minus_ref)
    spectrum = spectrum * over_coils(read_mask(mask_ref, table_ref.shape[0]), 2 * coils)
    chunks = join_complex(*halves(spectrum), lines)
    write_rows(grad_ref, len(chunks), chunks)


def picture_kernel(lines, volumes, columns_ref, sent_ref, image_ref, picture_ref, arrived):
    depth, pitch = sent_ref.shape[0], sent_ref.shape[2]
    count = 2 * lines // LANES
    unpack_sum(sent_ref, arrived)
    parts = [[], []]
    for place in range(volumes):
        chunks = read_rows(arrived, pitch, place * count, count, depth)
        for part, value in zip(parts, split_complex(chunks, lines)):
            part.append(value)
    picture = image_ref[...]
    scale = column(columns_ref, CASCADES + 1, picture.shape[0])
    picture = picture - scale * jnp.concatenate(parts[0] + parts[1], axis=0)
    for index, chunk in enumerate(join_complex(*halves(picture), lines)):
        picture_ref[:, index * LANES : (index + 1) * LANES] = chunk


def call(kernel, name, operands, outs, scratch, flops, vmem_bytes=VMEM_BYTES, scalars=0):
    spaces = [pltpu.SMEM] * scalars + [pltpu.VMEM] * (len(operands) - scalars)
    moved = sum(math.prod(item.shape) * item.dtype.itemsize for item in (*operands, *outs))
    return pl.pallas_call(
        kernel,
        name=name,
        out_shape=tuple(outs),
        in_specs=[pl.BlockSpec(memory_space=space) for space in spaces],
        out_specs=tuple(pl.BlockSpec(memory_space=pltpu.VMEM) for item in outs),
        scratch_shapes=[pltpu.VMEM(shape, F32) for shape in scratch],
        compiler_params=pltpu.CompilerParams(vmem_limit_bytes=vmem_bytes),
        cost_estimate=pl.CostEstimate(flops=flops, bytes_accessed=moved, transcendentals=0),
    )(*operands)


def body(
    kspace, coil_maps, sampling, dc_weight, kernel_in, bias_in, kernel_out, bias_out, cotangent
):
    coils, slots = kspace.shape[:2]
    rows, two_lines = coil_maps.shape[2:]
    lines = two_lines // 2
    channels = bias_in.shape[1]
    coil_devices, sections = lax.axis_size("coil"), lax.axis_size("section")
    volumes = VOLUMES
    depth = slots // volumes
    width = padded(lines, LANES)
    count, whole_count = width // LANES, two_lines // LANES
    planes = coils * slots
    both = ("section", "coil")
    near = [[group * depth + t for t in range(depth)] for group in range(volumes)]
    span = depth * coil_devices
    near_both = [[group * span + t for t in range(span)] for group in range(volumes)]

    def from_group(value, step, core=0):
        pairs = [(s, ((s + step * depth) % sections) ^ core) for s in range(sections)]
        return lax.ppermute(value, "section", pairs)

    def between_cores(value):
        return lax.ppermute(value, "section", [(s, s ^ 1) for s in range(sections)])

    def exchange(value, axes, groups):
        return lax.all_to_all(value, axes, 0, 0, tiled=True, axis_index_groups=groups)

    table = jnp.asarray(line_constant(lines))
    minus = jnp.asarray(depth_constant(coils, slots, volumes, -1.0))
    plus = jnp.asarray(depth_constant(coils, slots, volumes, 1.0))
    near_plus = jnp.asarray(depth_constant(coils, depth, 1, 1.0))
    repeat, place, offset = (jnp.asarray(item) for item in conv_constants(rows, channels))
    mask = sampling.reshape(slots, lines)

    def shape(*dims, kind=F32):
        return jax.ShapeDtypeStruct(dims, kind)

    line_flops = 2 * (2 * planes) * width * (2 * width)

    pitch = padded(volumes * (coils + 1) * whole_count, 16)
    packed, *samples = call(
        functools.partial(pack_kernel, coils, volumes, pitch),
        "pack_maps",
        (
            kspace.reshape(planes, two_lines),
            coil_maps.reshape(coils * rows, two_lines),
            cotangent.reshape(rows, two_lines),
        ),
        [shape(depth, pitch, LANES, kind=BF16)]
        + [shape(coils * depth, two_lines, kind=BF16)] * (volumes - 1),
        [(depth * pitch, LANES)],
        1000,
        LARGE_VMEM_BYTES,
    )
    samples = [from_group(value, step, 1) for step, value in enumerate(samples, 1)]
    tall, wide = channels * rows, offset.shape[1]
    first, first_t, second, second_t, columns = call(
        functools.partial(taps_kernel, rows),
        "lay_out_taps",
        (
            dc_weight,
            kernel_in.transpose(0, 1, 3, 2).reshape(-1, 2, channels),
            kernel_out.reshape(-1, 2, channels),
            bias_in,
            bias_out,
            repeat,
            place,
            offset,
        ),
        [
            shape(CASCADES, tall, wide, kind=BF16),
            shape(CASCADES, 6 * rows, tall, kind=BF16),
            shape(CASCADES, 6 * rows, tall, kind=BF16),
            shape(CASCADES, tall, wide, kind=BF16),
            shape(tall, place.shape[0]),
        ],
        [(place.shape[0], repeat.shape[1])],
        2 * tall * place.shape[0] * place.shape[1],
        scalars=1,
    )
    *samples, columns = lax.optimization_barrier((*samples, columns))
    (own,) = call(
        functools.partial(own_kernel, coils, lines, volumes),
        "own_images",
        (kspace.reshape(planes, two_lines), mask, table, near_plus),
        [shape(2 * coils * depth, width)],
        [],
        line_flops,
    )
    images = [own]
    for value in samples:
        (image,) = call(
            functools.partial(far_kernel, coils, lines, volumes),
            "far_images",
            (value, mask, table, near_plus),
            [shape(FAR_PARTS * coils * depth, width)],
            [],
            line_flops,
        )
        images.append(between_cores(image))
    arrived = exchange(packed, "section", near)

    depth_pitch = padded(volumes * 5 * count, 16 * volumes)
    partial, maps = call(
        functools.partial(rows_kernel, coils, lines, volumes),
        "combine_rows",
        (arrived, mask, table, minus, plus, *images),
        [
            shape(depth, coil_devices, depth_pitch, LANES, kind=BF16),
            shape(2 * planes, width, kind=BF16),
        ],
        [(depth * pitch, LANES), (depth * depth_pitch, LANES)],
        4 * line_flops,
    )

    partial = exchange(partial.reshape(-1, depth_pitch, LANES), both, near_both)
    partial = partial.reshape(depth, coil_devices, depth_pitch, LANES)

    model_pitch = padded(volumes * 4 * count, 8)
    moved, image = call(
        functools.partial(refine_kernel, lines, volumes),
        "refine_and_back",
        (
            partial,
            cotangent.reshape(rows, two_lines),
            first,
            first_t,
            second,
            second_t,
            columns,
        ),
        [shape(depth, model_pitch, LANES, kind=BF16), shape(2 * rows, width)],
        [(depth * depth_pitch, LANES), (depth * model_pitch, LANES)],
        14 * tall * wide * width,
    )
    moved = exchange(moved, "section", near)

    end_pitch = padded(volumes * whole_count, 16)
    handed = call(
        functools.partial(hand_kernel, volumes),
        "hand_on",
        (moved, maps),
        [shape(2 * planes // volumes + 2 * depth, width, kind=BF16)] * volumes,
        [(depth * model_pitch, LANES)],
        1000,
    )
    handed = list(handed)
    (partial,) = call(
        functools.partial(normal_kernel, coils, lines, volumes),
        "masked_normal",
        (moved, maps, mask, table, minus, plus),
        [shape(depth, coil_devices, end_pitch, LANES, kind=BF16)],
        [(depth * model_pitch, LANES), (depth * end_pitch, LANES)],
        3 * line_flops,
    )
    partial = exchange(partial.reshape(-1, end_pitch, LANES), both, near_both)
    partial = partial.reshape(depth, coil_devices, end_pitch, LANES)
    handed[1:] = [
        from_group(value, step) for step, value in enumerate(handed[1:], 1)
    ]

    (grad,) = call(
        functools.partial(grad_kernel, coils, lines, volumes),
        "grad_kspace",
        (mask, table, minus, *handed),
        [shape(planes * whole_count, LANES)],
        [],
        line_flops,
    )
    partial, grad = lax.optimization_barrier((partial, grad))
    (image,) = call(
        functools.partial(picture_kernel, lines, volumes),
        "image_out",
        (columns, partial, image),
        [shape(rows, two_lines)],
        [(depth * end_pitch, LANES)],
        1000,
    )
    return image.reshape(1, rows, two_lines), grad.reshape(coils, slots, 1, two_lines)


def solution(mesh):
    return jax.shard_map(
        body,
        mesh=mesh,
        in_specs=(
            P("coil", None, "section", None),
            P("coil", "section", None, None),
            P(),
            P(),
            P(),
            P(),
            P(),
            P(),
            P("section", None, None),
        ),
        out_specs=(P("section", None, None), P("coil", None, "section", None)),
        check_vma=False,
    )
```

```python
import functools
import math

import jax
import jax.numpy as jnp
import ml_dtypes
import numpy as np
from jax import lax
from jax.experimental import pallas as pl
from jax.experimental.pallas import tpu as pltpu
from jax.sharding import PartitionSpec as P

CASCADES = 2
VOLUMES = 2
LANES = 128
VMEM_BYTES = 48 * 1024 * 1024
FAR_PARTS = 3
HAND_PLANES = 6
LARGE_VMEM_BYTES = 60 * 1024 * 1024

F32 = jnp.float32
BF16 = jnp.bfloat16


def padded(size, unit):
    return -(-size // unit) * unit


def dft_parts(count):
    indices = np.arange(count)
    angles = (indices[:, None] * indices[None, :] % count) * (2.0 * math.pi / count)
    factor = 1.0 / math.sqrt(count)
    return np.cos(angles) * factor, np.sin(angles) * factor


def line_constant(lines):
    width = padded(lines, LANES)
    cosine, sine = dft_parts(lines)
    table = np.zeros((width, 2 * width), np.float32)
    table[:lines, :lines] = cosine
    table[:lines, width : width + lines] = sine
    return table.astype(ml_dtypes.bfloat16)


def depth_constant(coils, slots, volumes, sign):
    cosine, sine = dft_parts(slots // volumes)
    spread_over = np.eye(coils * volumes)
    real, imag = np.kron(spread_over, cosine), sign * np.kron(spread_over, sine)
    return np.block([[real, -imag], [imag, real]]).astype(np.float32).astype(ml_dtypes.bfloat16)


def conv_constants(rows, channels):
    groups = 6
    width = padded(groups * rows, LANES)
    repeat = np.kron(np.eye(channels), np.ones((rows, 1))).astype(np.float32)
    repeat = np.pad(repeat, ((0, 0), (0, padded(channels, LANES) - channels)))
    taps = CASCADES * 3
    place = np.zeros((padded(2 * taps * groups + 3 * CASCADES, LANES), 2 * taps * width), np.float32)
    for kind in range(2):
        for tap in range(taps):
            for group in range(groups):
                start = (kind * taps + tap) * width + group * rows
                place[(kind * taps + tap) * groups + group, start : start + rows] = 1.0
    offset = np.full((channels * rows, width), -9.0, np.float32)
    row = np.arange(rows)
    offset[:, : groups * rows] = np.tile(row[None, :] - row[:, None] + 1.0, (channels, groups))
    offset = np.clip(offset, -9.0, 9.0)
    return repeat, place.astype(ml_dtypes.bfloat16), offset


def lane_index(shape):
    return lax.broadcasted_iota(jnp.int32, shape, len(shape) - 1)


def split_complex(chunks, lines):
    whole, rest = divmod(lines, LANES)
    count = padded(lines, LANES) // LANES
    if rest == 0:
        return jnp.concatenate(chunks[:count], 1), jnp.concatenate(chunks[count:], 1)
    lane = lane_index(chunks[0].shape)
    real = chunks[:whole] + [jnp.where(lane < rest, chunks[whole], 0.0)]
    turned = [pltpu.roll(chunk, LANES - rest, 1) for chunk in chunks[whole:]]
    turned.append(jnp.zeros_like(turned[0]))
    imag = [jnp.where(lane < LANES - rest, turned[k], turned[k + 1]) for k in range(count)]
    imag[-1] = jnp.where(lane < rest, imag[-1], 0.0)
    return jnp.concatenate(real, 1), jnp.concatenate(imag, 1)


def lane_chunks(value):
    return [value[:, start : start + LANES] for start in range(0, value.shape[1], LANES)]


def join_complex(real, imag, lines):
    whole, rest = divmod(lines, LANES)
    real, imag = lane_chunks(real), lane_chunks(imag)
    if rest == 0:
        return real + imag
    lane = lane_index(real[0].shape)
    turned = [real[whole]] + [pltpu.roll(chunk, rest, 1) for chunk in imag]
    mixed = [jnp.where(lane < rest, turned[k], turned[k + 1]) for k in range(len(imag))]
    return (real[:whole] + mixed)[: 2 * lines // LANES]


def halves(stacked):
    half = stacked.shape[0] // 2
    return stacked[:half], stacked[half:]


def line_apply(stacked, table_ref, sign):
    mixed = jnp.dot(stacked.astype(BF16), table_ref[...], preferred_element_type=F32)
    width = table_ref.shape[1] // 2
    top, bottom = halves(mixed)
    return jnp.concatenate(
        [
            top[:, :width] - sign * bottom[:, width:],
            bottom[:, :width] + sign * top[:, width:],
        ],
        axis=0,
    )


def depth_apply(stacked, depth_ref):
    return jnp.dot(depth_ref[...], stacked.astype(BF16), preferred_element_type=F32)


def over_coils(value, coils):
    return jnp.concatenate([value] * coils, axis=0)


def coil_sum(value, coils):
    slots = value.shape[0] // coils
    total = value[:slots]
    for coil in range(1, coils):
        total = total + value[coil * slots : (coil + 1) * slots]
    return total


def over_rows(parts, coils):
    return jnp.concatenate([part for part in parts for coil in range(coils)], axis=0)


def spread(maps_real, maps_imag, real, imag):
    return jnp.concatenate(
        [maps_real * real - maps_imag * imag, maps_real * imag + maps_imag * real], axis=0
    )


def collect(maps_real, maps_imag, images):
    real, imag = halves(images)
    return maps_real * real + maps_imag * imag, maps_real * imag - maps_imag * real


def blocks(value, count):
    size = value.shape[0] // count
    return [value[index * size : (index + 1) * size] for index in range(count)]


def row_sums(value, rows, coils):
    return [coil_sum(part, coils) for part in blocks(value, rows)]


def pick(parts, index):
    chosen = parts[0]
    for place in range(1, len(parts)):
        chosen = jnp.where(index == place, parts[place], chosen)
    return chosen


def own_volume(depth):
    return lax.div(lax.axis_index("section"), jnp.int32(depth))


def masked_normal(images, table_ref, minus_ref, plus_ref, mask):
    spectrum = depth_apply(line_apply(images, table_ref, -1.0), minus_ref)
    return line_apply(depth_apply(spectrum * mask, plus_ref), table_ref, 1.0)


def write_rows(scratch, pitch, values, first=0):
    for index, value in enumerate(values):
        scratch[pl.ds(first + index, value.shape[0], stride=pitch), :] = value


def read_rows(scratch, pitch, first, count, rows):
    return [scratch[pl.ds(first + index, rows, stride=pitch), :] for index in range(count)]


def shifted(value, step):
    if step == 0:
        return value
    width = value.shape[1]
    return pltpu.roll(value, (-step) % width, 1)


def stack_shifted(value, order):
    return jnp.concatenate([shifted(value, step) for step in order], axis=0).astype(BF16)


def add_shifted(value, order, rows):
    total = None
    for index, step in enumerate(order):
        part = shifted(value[index * rows : (index + 1) * rows], step)
        total = part if total is None else total + part
    return total


def hidden_state(image, first_ref, bias_column):
    stack = stack_shifted(image, (-1, 0, 1))
    return (
        jnp.dot(first_ref[:, : stack.shape[0]], stack, preferred_element_type=F32) + bias_column
    )


def second_conv(hidden, second_ref, bias_column, rows, valid):
    mixed = jnp.dot(
        second_ref[...], jnp.where(valid, hidden, 0.0).astype(BF16), preferred_element_type=F32
    )
    total = add_shifted(mixed, (-1, 0, 1), 2 * rows)
    return jnp.where(valid[: 2 * rows], total + bias_column, 0.0)


def pull_back(cotangent, slope, first_t_ref, second_t_ref, rows, valid):
    stack = stack_shifted(cotangent, (1, 0, -1))
    back = jnp.dot(second_t_ref[:, : stack.shape[0]], stack, preferred_element_type=F32)
    back = jnp.where(valid, back * slope, 0.0).astype(BF16)
    mixed = jnp.dot(first_t_ref[...], back, preferred_element_type=F32)
    total = add_shifted(mixed, (1, 0, -1), 2 * rows)
    return jnp.where(valid[: 2 * rows], total, 0.0)


def read_mask(sampling_ref, width):
    mask = sampling_ref[...].astype(F32)
    return jnp.pad(mask, ((0, 0), (0, width - mask.shape[1])))


def valid_lanes(rows, width, lines):
    return lane_index((rows, width)) < lines


def column(columns_ref, place, rows):
    at = 4 * 9 * CASCADES + place
    return columns_ref[:rows, at : at + 1]


def round_bf(value):
    return value.astype(BF16).astype(F32)


def choose_volume(value, coils, volumes, volume):
    parts = blocks(value, coils * volumes)
    chosen = [pick(parts[coil * volumes : (coil + 1) * volumes], volume) for coil in range(coils)]
    return jnp.concatenate(chosen, axis=0)


def pack_kernel(coils, volumes, pitch, kspace_ref, maps_ref, image_ref, out_ref, *refs):
    handed, (scratch,) = refs[:-1], refs[-1:]
    rows = image_ref.shape[0]
    depth = rows // volumes
    volume = own_volume(depth)
    kspace = kspace_ref[...].astype(F32)
    for step, ref in enumerate(handed, 1):
        other = lax.rem(volume + step, jnp.int32(volumes))
        ref[...] = choose_volume(kspace, coils, volumes, other).astype(BF16)
    count = maps_ref.shape[1] // LANES
    scratch[...] = jnp.zeros_like(scratch)
    image = image_ref[...].astype(F32)
    for coil in range(coils + 1):
        value = maps_ref[coil * rows : (coil + 1) * rows, :].astype(F32) if coil < coils else image
        for place, part in enumerate(blocks(value, volumes)):
            first = (place * (coils + 1) + coil) * count
            write_rows(scratch, pitch, lane_chunks(part), first)
    out_ref[...] = scratch[...].astype(BF16).reshape(out_ref.shape)


def taps_kernel(
    rows,
    weight_ref,
    kernel_in_ref,
    kernel_out_ref,
    bias_in_ref,
    bias_out_ref,
    repeat_ref,
    place_ref,
    offset_ref,
    first_ref,
    first_t_ref,
    second_ref,
    second_t_ref,
    columns_ref,
    taps,
):
    taps[...] = jnp.zeros_like(taps)
    channels = kernel_in_ref.shape[2]
    at = 0
    for ref in (kernel_in_ref, kernel_out_ref):
        for index in range(ref.shape[0]):
            taps[at : at + 2, :channels] = ref[index]
            at += 2
    taps[at : at + CASCADES, :channels] = bias_in_ref[...]
    at += CASCADES
    for cascade in range(CASCADES):
        taps[at : at + 1, :] = jnp.full((1, taps.shape[1]), weight_ref[cascade], F32)
        at += 1
    taps[at : at + CASCADES, : bias_out_ref.shape[1]] = bias_out_ref[...]
    tall = lax.dot_general(
        repeat_ref[...],
        taps[...],
        (((1,), (1,)), ((), ())),
        precision=lax.Precision.HIGHEST,
        preferred_element_type=F32,
    )
    columns_ref[...] = tall
    wide = jnp.dot(tall.astype(BF16), place_ref[...], preferred_element_type=F32)
    offset = offset_ref[...]
    width = offset.shape[1]
    for cascade in range(CASCADES):
        for kind, straight, turned in ((0, first_ref, first_t_ref), (1, second_t_ref, second_ref)):
            total = jnp.zeros_like(offset)
            for tap in range(3):
                start = ((kind * CASCADES + cascade) * 3 + tap) * width
                wanted = float(tap if kind == 0 else 2 - tap)
                total = total + jnp.where(offset == wanted, wide[:, start : start + width], 0.0)
            straight[cascade] = total.astype(BF16)
            turned[cascade] = total.T[: 6 * rows].astype(BF16)


def line_images(kspace, mask, lines, table_ref, plus_ref):
    real, imag = split_complex(lane_chunks(kspace), lines)
    measured = jnp.concatenate([real * mask, imag * mask], axis=0)
    return line_apply(depth_apply(measured, plus_ref), table_ref, 1.0)


def far_kernel(coils, lines, volumes, kspace_ref, mask_ref, table_ref, plus_ref, out_ref):
    parts = blocks(read_mask(mask_ref, table_ref.shape[0]), volumes)
    mask = pick(parts, own_volume(parts[0].shape[0]))
    mask = over_coils(mask, coils)
    images = line_images(kspace_ref[...].astype(F32), mask, lines, table_ref, plus_ref)
    out_ref[: images.shape[0]] = images
    if out_ref.shape[0] > images.shape[0]:
        out_ref[images.shape[0] :] = jnp.zeros_like(out_ref[images.shape[0] :])


def own_kernel(coils, lines, volumes, kspace_ref, mask_ref, table_ref, plus_ref, out_ref):
    parts = blocks(read_mask(mask_ref, table_ref.shape[0]), volumes)
    volume = own_volume(parts[0].shape[0])
    kspace = choose_volume(kspace_ref[...].astype(F32), coils, volumes, volume)
    mask = over_coils(pick(parts, volume), coils)
    out_ref[...] = line_images(kspace, mask, lines, table_ref, plus_ref)


def rows_kernel(
    coils,
    lines,
    volumes,
    sent_ref,
    mask_ref,
    table_ref,
    minus_ref,
    plus_ref,
    *refs,
):
    arrival_refs, refs = refs[:volumes], refs[volumes:]
    out_ref, maps_ref, arrived, leaving = refs
    depth, pitch = sent_ref.shape[:2]
    volume = own_volume(depth)
    mask = pick(blocks(read_mask(mask_ref, table_ref.shape[0]), volumes), volume)
    mask = over_coils(mask, volumes * coils)

    arrivals = [halves(ref[: 2 * coils * depth]) for ref in arrival_refs]
    measured = []
    for part in range(2):
        for place in range(volumes):
            step = lax.rem(volume - place + volumes, jnp.int32(volumes))
            measured.append(pick([arrival[part] for arrival in arrivals], step))
    measured = jnp.concatenate(measured, axis=0)

    arrived[...] = sent_ref[...].astype(F32).reshape(arrived.shape)
    count = 2 * lines // LANES
    parts, reals, imags = [], [], []
    for place in range(volumes):
        first = place * (coils + 1) * count
        for coil in range(coils):
            chunks = read_rows(arrived, pitch, first + coil * count, count, depth)
            parts.append(split_complex(chunks, lines))
        chunks = read_rows(arrived, pitch, first + coils * count, count, depth)
        real, imag = split_complex(chunks, lines)
        reals.append(real)
        imags.append(imag)
    maps_real = jnp.concatenate([part[0] for part in parts], axis=0)
    maps_imag = jnp.concatenate([part[1] for part in parts], axis=0)
    maps_ref[...] = jnp.concatenate([maps_real, maps_imag], axis=0).astype(BF16)

    images = spread(maps_real, maps_imag, over_rows(reals, coils), over_rows(imags, coils))
    mask = jnp.concatenate([mask, mask], axis=0)
    images = masked_normal(images, table_ref, minus_ref, plus_ref, mask)
    found = [
        *collect(maps_real, maps_imag, round_bf(measured)),
        *collect(maps_real, maps_imag, images),
        maps_real * maps_real + maps_imag * maps_imag,
    ]
    leaving[...] = jnp.zeros_like(leaving)
    sums = [row_sums(value, volumes, coils) for value in found]
    pitch = out_ref.shape[2]
    for place in range(volumes):
        chunks = [chunk for value in sums for chunk in lane_chunks(value[place])]
        write_rows(leaving, pitch, chunks, place * (pitch // volumes))
    message = leaving[...].astype(BF16).reshape(depth, *out_ref.shape[2:])
    for device in range(out_ref.shape[1]):
        out_ref[:, device] = message


def unpack_sum(sent_ref, scratch):
    total = sent_ref[:, 0].astype(F32)
    for device in range(1, sent_ref.shape[1]):
        total = total + sent_ref[:, device].astype(F32)
    scratch[...] = total.reshape(scratch.shape)


def read_image(scratch, pitch, first, count, depth):
    return jnp.concatenate(read_rows(scratch, pitch, first, count, depth), axis=1)


def read_places(scratch, pitch, first, period, count, depth, volumes):
    parts = [
        read_image(scratch, pitch, first + place * period, count, depth) for place in range(volumes)
    ]
    return jnp.concatenate(parts, axis=0)


def read_complex(scratch, pitch, first, period, count, depth, volumes):
    real = read_places(scratch, pitch, first, period, count, depth, volumes)
    imag = read_places(scratch, pitch, first + count, period, count, depth, volumes)
    return jnp.concatenate([real, imag], axis=0)


def refine_kernel(
    lines,
    volumes,
    sent_ref,
    cotangent_ref,
    first_ref,
    first_t_ref,
    second_ref,
    second_t_ref,
    columns_ref,
    out_ref,
    image_ref,
    arrived,
    leaving,
):
    unpack_sum(sent_ref, arrived)
    depth, pitch = sent_ref.shape[0], sent_ref.shape[2]
    rows = depth * volumes
    width = padded(lines, LANES)
    count = width // LANES
    begun = read_complex(arrived, pitch, 0, pitch // volumes, count, depth, volumes)
    turned = read_complex(arrived, pitch, 2 * count, pitch // volumes, count, depth, volumes)
    power = read_places(arrived, pitch, 4 * count, pitch // volumes, count, depth, volumes)
    power = jnp.concatenate([power, power], axis=0)
    cotangent = jnp.concatenate(
        split_complex(lane_chunks(cotangent_ref[...].astype(F32)), lines), axis=0
    )
    tall = first_ref.shape[1]
    weight = [column(columns_ref, CASCADES + cascade, 2 * rows) for cascade in range(CASCADES)]
    bias = [column(columns_ref, 2 * CASCADES + cascade, 2 * rows) for cascade in range(CASCADES)]

    share = [jnp.ones_like(weight[0])]
    for cascade in range(CASCADES):
        share.append(share[cascade] - weight[cascade] * (share[cascade] - 1.0))

    def slopes(hidden):
        gate = jax.nn.sigmoid(hidden)
        return hidden * gate, gate * (1.0 + hidden * (1.0 - gate))

    hidden = hidden_state(round_bf(begun), first_ref.at[0], column(columns_ref, 0, tall))
    valid = valid_lanes(hidden.shape[0], width, lines)
    active, slope_first = slopes(hidden)
    model = round_bf(second_conv(active, second_ref.at[0], bias[0], rows, valid))
    picture = round_bf(share[1] * begun + power * model)
    hidden = hidden_state(picture, first_ref.at[1], column(columns_ref, 1, tall))
    active, slope_second = slopes(hidden)
    later = round_bf(second_conv(active, second_ref.at[1], bias[1], rows, valid))
    image_ref[...] = share[2] * begun + power * (model + later)

    through = power * cotangent
    back_second = round_bf(
        pull_back(through, slope_second, first_t_ref.at[1], second_t_ref.at[1], rows, valid)
    )
    through = through - weight[1] * turned + power * back_second
    back_first = round_bf(
        pull_back(through, slope_first, first_t_ref.at[0], second_t_ref.at[0], rows, valid)
    )
    kept = (1.0 - weight[0], 1.0 - weight[1])
    of_cotangent = weight[1] + weight[0] * kept[1] + kept[0] * kept[1]
    of_second = weight[0] + kept[0]
    pulled = of_cotangent * cotangent + of_second * back_second + back_first
    leaving[...] = jnp.zeros_like(leaving)
    parts = [blocks(part, volumes) for value in (model, pulled) for part in halves(value)]
    for place in range(volumes):
        chunks = [chunk for part in parts for chunk in lane_chunks(part[place])]
        write_rows(leaving, out_ref.shape[1], chunks, place * len(chunks))
    out_ref[...] = leaving[...].astype(BF16).reshape(out_ref.shape)


def hand_kernel(volumes, sent_ref, maps_ref, *refs):
    outs, (arrived,) = refs[:-1], refs[-1:]
    arrived[...] = sent_ref[...].astype(F32).reshape(arrived.shape)
    depth, pitch = sent_ref.shape[:2]
    volume = own_volume(depth)
    count = maps_ref.shape[1] // LANES
    parts = [blocks(part, volumes) for part in halves(maps_ref[...].astype(F32))]
    for field in (2, 3):
        parts.append(
            [
                read_image(arrived, pitch, (place * 4 + field) * count, count, depth)
                for place in range(volumes)
            ]
        )
    for step, ref in enumerate(outs):
        place = lax.rem(volume + step, jnp.int32(volumes))
        chosen = [pick(part, place) for part in parts]
        ref[...] = jnp.zeros_like(ref)
        chosen = jnp.concatenate(chosen, axis=0).astype(BF16)
        ref[: chosen.shape[0]] = chosen


def normal_kernel(
    coils,
    lines,
    volumes,
    sent_ref,
    maps_ref,
    mask_ref,
    table_ref,
    minus_ref,
    plus_ref,
    out_ref,
    arrived,
    leaving,
):
    arrived[...] = sent_ref[...].astype(F32).reshape(arrived.shape)
    depth, pitch = sent_ref.shape[:2]
    volume = own_volume(depth)
    count = maps_ref.shape[1] // LANES
    fields = [
        [
            read_image(arrived, pitch, (place * 4 + field) * count, count, depth)
            for place in range(volumes)
        ]
        for field in range(2)
    ]
    reals, imags = fields
    maps_real, maps_imag = halves(maps_ref[...].astype(F32))
    mask = over_coils(pick(blocks(read_mask(mask_ref, table_ref.shape[0]), volumes), volume), 2 * volumes * coils)
    images = spread(maps_real, maps_imag, over_rows(reals, coils), over_rows(imags, coils))
    images = masked_normal(images, table_ref, minus_ref, plus_ref, mask)
    found = [row_sums(value, volumes, coils) for value in collect(maps_real, maps_imag, images)]
    leaving[...] = jnp.zeros_like(leaving)
    for place in range(volumes):
        chunks = join_complex(found[0][place], found[1][place], lines)
        write_rows(leaving, out_ref.shape[2], chunks, place * len(chunks))
    message = leaving[...].astype(BF16).reshape(depth, *out_ref.shape[2:])
    for device in range(out_ref.shape[1]):
        out_ref[:, device] = message


def from_volumes(refs, volume, parts, volumes):
    sources = [blocks(ref, parts) for ref in refs]
    ordered = []
    for place in range(volumes):
        step = lax.rem(volume - place + volumes, jnp.int32(volumes))
        ordered.append([pick([source[part] for source in sources], step) for part in range(parts)])
    return ordered


def grad_kernel(
    coils,
    lines,
    volumes,
    mask_ref,
    table_ref,
    minus_ref,
    *refs,
):
    handed, (grad_ref,) = [ref[...].astype(F32) for ref in refs[:volumes]], refs[volumes:]
    depth = mask_ref.shape[0] // volumes
    volume = own_volume(depth)
    planes = coils * depth
    maps = [value[: 2 * planes] for value in handed]
    maps = from_volumes(maps, volume, 2 * coils, volumes)
    maps = [
        jnp.concatenate([maps[v][first + coil] for coil in range(coils) for v in range(volumes)], 0)
        for first in (0, coils)
    ]
    pulled = [value[2 * planes : 2 * planes + 2 * depth] for value in handed]
    pulled = from_volumes(pulled, volume, 2, volumes)
    real, imag = [jnp.concatenate([part[field] for part in pulled], 0) for field in range(2)]
    images = spread(*maps, over_coils(real, coils), over_coils(imag, coils))
    spectrum = depth_apply(line_apply(images, table_ref, -1.0), minus_ref)
    spectrum = spectrum * over_coils(read_mask(mask_ref, table_ref.shape[0]), 2 * coils)
    chunks = join_complex(*halves(spectrum), lines)
    write_rows(grad_ref, len(chunks), chunks)


def picture_kernel(lines, volumes, columns_ref, sent_ref, image_ref, picture_ref, arrived):
    depth, pitch = sent_ref.shape[0], sent_ref.shape[2]
    count = 2 * lines // LANES
    unpack_sum(sent_ref, arrived)
    parts = [[], []]
    for place in range(volumes):
        chunks = read_rows(arrived, pitch, place * count, count, depth)
        for part, value in zip(parts, split_complex(chunks, lines)):
            part.append(value)
    picture = image_ref[...]
    scale = column(columns_ref, CASCADES + 1, picture.shape[0])
    picture = picture - scale * jnp.concatenate(parts[0] + parts[1], axis=0)
    for index, chunk in enumerate(join_complex(*halves(picture), lines)):
        picture_ref[:, index * LANES : (index + 1) * LANES] = chunk


def end_kernel(
    coils,
    lines,
    volumes,
    columns_ref,
    sent_ref,
    image_ref,
    mask_ref,
    table_ref,
    minus_ref,
    *refs,
):
    handed, (picture_ref, grad_ref, arrived) = refs[:volumes], refs[volumes:]
    grad_kernel(coils, lines, volumes, mask_ref, table_ref, minus_ref, *handed, grad_ref)
    picture_kernel(lines, volumes, columns_ref, sent_ref, image_ref, picture_ref, arrived)


def call(kernel, name, operands, outs, scratch, flops, vmem_bytes=VMEM_BYTES, scalars=0):
    spaces = [pltpu.SMEM] * scalars + [pltpu.VMEM] * (len(operands) - scalars)
    moved = sum(math.prod(item.shape) * item.dtype.itemsize for item in (*operands, *outs))
    return pl.pallas_call(
        kernel,
        name=name,
        out_shape=tuple(outs),
        in_specs=[pl.BlockSpec(memory_space=space) for space in spaces],
        out_specs=tuple(pl.BlockSpec(memory_space=pltpu.VMEM) for item in outs),
        scratch_shapes=[pltpu.VMEM(shape, F32) for shape in scratch],
        compiler_params=pltpu.CompilerParams(vmem_limit_bytes=vmem_bytes),
        cost_estimate=pl.CostEstimate(flops=flops, bytes_accessed=moved, transcendentals=0),
    )(*operands)


def body(
    kspace, coil_maps, sampling, dc_weight, kernel_in, bias_in, kernel_out, bias_out, cotangent
):
    coils, slots = kspace.shape[:2]
    rows, two_lines = coil_maps.shape[2:]
    lines = two_lines // 2
    channels = bias_in.shape[1]
    coil_devices, sections = lax.axis_size("coil"), lax.axis_size("section")
    volumes = VOLUMES
    depth = slots // volumes
    width = padded(lines, LANES)
    count, whole_count = width // LANES, two_lines // LANES
    planes = coils * slots
    both = ("section", "coil")
    near = [[group * depth + t for t in range(depth)] for group in range(volumes)]
    span = depth * coil_devices
    near_both = [[group * span + t for t in range(span)] for group in range(volumes)]

    def from_group(value, step, core=0):
        pairs = [(s, ((s + step * depth) % sections) ^ core) for s in range(sections)]
        return lax.ppermute(value, "section", pairs)

    def between_cores(value):
        return lax.ppermute(value, "section", [(s, s ^ 1) for s in range(sections)])

    def exchange(value, axes, groups):
        return lax.all_to_all(value, axes, 0, 0, tiled=True, axis_index_groups=groups)

    table = jnp.asarray(line_constant(lines))
    minus = jnp.asarray(depth_constant(coils, slots, volumes, -1.0))
    plus = jnp.asarray(depth_constant(coils, slots, volumes, 1.0))
    near_plus = jnp.asarray(depth_constant(coils, depth, 1, 1.0))
    repeat, place, offset = (jnp.asarray(item) for item in conv_constants(rows, channels))
    mask = sampling.reshape(slots, lines)

    def shape(*dims, kind=F32):
        return jax.ShapeDtypeStruct(dims, kind)

    line_flops = 2 * (2 * planes) * width * (2 * width)

    pitch = padded(volumes * (coils + 1) * whole_count, 16)
    packed, *samples = call(
        functools.partial(pack_kernel, coils, volumes, pitch),
        "pack_maps",
        (
            kspace.reshape(planes, two_lines),
            coil_maps.reshape(coils * rows, two_lines),
            cotangent.reshape(rows, two_lines),
        ),
        [shape(depth, pitch, LANES, kind=BF16)]
        + [shape(coils * depth, two_lines, kind=BF16)] * (volumes - 1),
        [(depth * pitch, LANES)],
        1000,
        LARGE_VMEM_BYTES,
    )
    samples = [from_group(value, step, 1) for step, value in enumerate(samples, 1)]
    tall, wide = channels * rows, offset.shape[1]
    first, first_t, second, second_t, columns = call(
        functools.partial(taps_kernel, rows),
        "lay_out_taps",
        (
            dc_weight,
            kernel_in.transpose(0, 1, 3, 2).reshape(-1, 2, channels),
            kernel_out.reshape(-1, 2, channels),
            bias_in,
            bias_out,
            repeat,
            place,
            offset,
        ),
        [
            shape(CASCADES, tall, wide, kind=BF16),
            shape(CASCADES, 6 * rows, tall, kind=BF16),
            shape(CASCADES, 6 * rows, tall, kind=BF16),
            shape(CASCADES, tall, wide, kind=BF16),
            shape(tall, place.shape[0]),
        ],
        [(place.shape[0], repeat.shape[1])],
        2 * tall * place.shape[0] * place.shape[1],
        scalars=1,
    )
    *samples, columns = lax.optimization_barrier((*samples, columns))
    (own,) = call(
        functools.partial(own_kernel, coils, lines, volumes),
        "own_images",
        (kspace.reshape(planes, two_lines), mask, table, near_plus),
        [shape(2 * coils * depth, width)],
        [],
        line_flops,
    )
    images = [own]
    for value in samples:
        (image,) = call(
            functools.partial(far_kernel, coils, lines, volumes),
            "far_images",
            (value, mask, table, near_plus),
            [shape(FAR_PARTS * coils * depth, width)],
            [],
            line_flops,
        )
        images.append(between_cores(image))
    arrived = exchange(packed, "section", near)

    depth_pitch = padded(volumes * 5 * count, 16 * volumes)
    partial, maps = call(
        functools.partial(rows_kernel, coils, lines, volumes),
        "combine_rows",
        (arrived, mask, table, minus, plus, *images),
        [
            shape(depth, coil_devices, depth_pitch, LANES, kind=BF16),
            shape(2 * planes, width, kind=BF16),
        ],
        [(depth * pitch, LANES), (depth * depth_pitch, LANES)],
        4 * line_flops,
    )

    partial = exchange(partial.reshape(-1, depth_pitch, LANES), both, near_both)
    partial = partial.reshape(depth, coil_devices, depth_pitch, LANES)

    model_pitch = padded(volumes * 4 * count, 8)
    moved, image = call(
        functools.partial(refine_kernel, lines, volumes),
        "refine_and_back",
        (
            partial,
            cotangent.reshape(rows, two_lines),
            first,
            first_t,
            second,
            second_t,
            columns,
        ),
        [shape(depth, model_pitch, LANES, kind=BF16), shape(2 * rows, width)],
        [(depth * depth_pitch, LANES), (depth * model_pitch, LANES)],
        14 * tall * wide * width,
    )
    moved = exchange(moved, "section", near)

    end_pitch = padded(volumes * whole_count, 16)
    handed = call(
        functools.partial(hand_kernel, volumes),
        "hand_on",
        (moved, maps),
        [shape(2 * planes // volumes + HAND_PLANES * depth, width, kind=BF16)] * volumes,
        [(depth * model_pitch, LANES)],
        1000,
    )
    handed = list(handed)
    (partial,) = call(
        functools.partial(normal_kernel, coils, lines, volumes),
        "masked_normal",
        (moved, maps, mask, table, minus, plus),
        [shape(depth, coil_devices, end_pitch, LANES, kind=BF16)],
        [(depth * model_pitch, LANES), (depth * end_pitch, LANES)],
        3 * line_flops,
    )
    partial = exchange(partial.reshape(-1, end_pitch, LANES), both, near_both)
    partial = partial.reshape(depth, coil_devices, end_pitch, LANES)
    handed[1:] = [
        from_group(value, step) for step, value in enumerate(handed[1:], 1)
    ]

    image, grad = call(
        functools.partial(end_kernel, coils, lines, volumes),
        "outputs",
        (columns, partial, image, mask, table, minus, *handed),
        [shape(rows, two_lines), shape(planes * whole_count, LANES)],
        [(depth * end_pitch, LANES)],
        2 * line_flops,
    )
    return image.reshape(1, rows, two_lines), grad.reshape(coils, slots, 1, two_lines)


def solution(mesh):
    return jax.shard_map(
        body,
        mesh=mesh,
        in_specs=(
            P("coil", None, "section", None),
            P("coil", "section", None, None),
            P(),
            P(),
            P(),
            P(),
            P(),
            P(),
            P("section", None, None),
        ),
        out_specs=(P("section", None, None), P("coil", None, "section", None)),
        check_vma=False,
    )
```

```python
import functools
import math

import jax
import jax.numpy as jnp
import ml_dtypes
import numpy as np
from jax import lax
from jax.experimental import pallas as pl
from jax.experimental.pallas import tpu as pltpu
from jax.sharding import PartitionSpec as P

CASCADES = 2
VOLUMES = 2
LANES = 128
VMEM_BYTES = 48 * 1024 * 1024
FAR_PARTS = 3
LARGE_VMEM_BYTES = 60 * 1024 * 1024

F32 = jnp.float32
BF16 = jnp.bfloat16


def padded(size, unit):
    return -(-size // unit) * unit


def dft_parts(count):
    indices = np.arange(count)
    angles = (indices[:, None] * indices[None, :] % count) * (2.0 * math.pi / count)
    factor = 1.0 / math.sqrt(count)
    return np.cos(angles) * factor, np.sin(angles) * factor


def line_constant(lines):
    width = padded(lines, LANES)
    cosine, sine = dft_parts(lines)
    table = np.zeros((width, 2 * width), np.float32)
    table[:lines, :lines] = cosine
    table[:lines, width : width + lines] = sine
    return table.astype(ml_dtypes.bfloat16)


def depth_constant(coils, slots, volumes, sign):
    cosine, sine = dft_parts(slots // volumes)
    spread_over = np.eye(coils * volumes)
    real, imag = np.kron(spread_over, cosine), sign * np.kron(spread_over, sine)
    return np.block([[real, -imag], [imag, real]]).astype(np.float32).astype(ml_dtypes.bfloat16)


def conv_constants(rows, channels):
    groups = 6
    width = padded(groups * rows, LANES)
    repeat = np.kron(np.eye(channels), np.ones((rows, 1))).astype(np.float32)
    repeat = np.pad(repeat, ((0, 0), (0, padded(channels, LANES) - channels)))
    taps = CASCADES * 3
    place = np.zeros((padded(2 * taps * groups + 3 * CASCADES, LANES), 2 * taps * width), np.float32)
    for kind in range(2):
        for tap in range(taps):
            for group in range(groups):
                start = (kind * taps + tap) * width + group * rows
                place[(kind * taps + tap) * groups + group, start : start + rows] = 1.0
    offset = np.full((channels * rows, width), -9.0, np.float32)
    row = np.arange(rows)
    offset[:, : groups * rows] = np.tile(row[None, :] - row[:, None] + 1.0, (channels, groups))
    offset = np.clip(offset, -9.0, 9.0)
    return repeat, place.astype(ml_dtypes.bfloat16), offset


def lane_index(shape):
    return lax.broadcasted_iota(jnp.int32, shape, len(shape) - 1)


def split_complex(chunks, lines):
    whole, rest = divmod(lines, LANES)
    count = padded(lines, LANES) // LANES
    if rest == 0:
        return jnp.concatenate(chunks[:count], 1), jnp.concatenate(chunks[count:], 1)
    lane = lane_index(chunks[0].shape)
    real = chunks[:whole] + [jnp.where(lane < rest, chunks[whole], 0.0)]
    turned = [pltpu.roll(chunk, LANES - rest, 1) for chunk in chunks[whole:]]
    turned.append(jnp.zeros_like(turned[0]))
    imag = [jnp.where(lane < LANES - rest, turned[k], turned[k + 1]) for k in range(count)]
    imag[-1] = jnp.where(lane < rest, imag[-1], 0.0)
    return jnp.concatenate(real, 1), jnp.concatenate(imag, 1)


def lane_chunks(value):
    return [value[:, start : start + LANES] for start in range(0, value.shape[1], LANES)]


def join_complex(real, imag, lines):
    whole, rest = divmod(lines, LANES)
    real, imag = lane_chunks(real), lane_chunks(imag)
    if rest == 0:
        return real + imag
    lane = lane_index(real[0].shape)
    turned = [real[whole]] + [pltpu.roll(chunk, rest, 1) for chunk in imag]
    mixed = [jnp.where(lane < rest, turned[k], turned[k + 1]) for k in range(len(imag))]
    return (real[:whole] + mixed)[: 2 * lines // LANES]


def halves(stacked):
    half = stacked.shape[0] // 2
    return stacked[:half], stacked[half:]


def line_apply(stacked, table_ref, sign):
    mixed = jnp.dot(stacked.astype(BF16), table_ref[...], preferred_element_type=F32)
    width = table_ref.shape[1] // 2
    top, bottom = halves(mixed)
    return jnp.concatenate(
        [
            top[:, :width] - sign * bottom[:, width:],
            bottom[:, :width] + sign * top[:, width:],
        ],
        axis=0,
    )


def depth_apply(stacked, depth_ref):
    return jnp.dot(depth_ref[...], stacked.astype(BF16), preferred_element_type=F32)


def over_coils(value, coils):
    return jnp.concatenate([value] * coils, axis=0)


def coil_sum(value, coils):
    slots = value.shape[0] // coils
    total = value[:slots]
    for coil in range(1, coils):
        total = total + value[coil * slots : (coil + 1) * slots]
    return total


def over_rows(parts, coils):
    return jnp.concatenate([part for part in parts for coil in range(coils)], axis=0)


def spread(maps_real, maps_imag, real, imag):
    return jnp.concatenate(
        [maps_real * real - maps_imag * imag, maps_real * imag + maps_imag * real], axis=0
    )


def collect(maps_real, maps_imag, images):
    real, imag = halves(images)
    return maps_real * real + maps_imag * imag, maps_real * imag - maps_imag * real


def blocks(value, count):
    size = value.shape[0] // count
    return [value[index * size : (index + 1) * size] for index in range(count)]


def row_sums(value, rows, coils):
    return [coil_sum(part, coils) for part in blocks(value, rows)]


def pick(parts, index):
    chosen = parts[0]
    for place in range(1, len(parts)):
        chosen = jnp.where(index == place, parts[place], chosen)
    return chosen


def own_volume(depth):
    return lax.div(lax.axis_index("section"), jnp.int32(depth))


def masked_normal(images, table_ref, minus_ref, plus_ref, mask):
    spectrum = depth_apply(line_apply(images, table_ref, -1.0), minus_ref)
    return line_apply(depth_apply(spectrum * mask, plus_ref), table_ref, 1.0)


def write_rows(scratch, pitch, values, first=0):
    for index, value in enumerate(values):
        scratch[pl.ds(first + index, value.shape[0], stride=pitch), :] = value


def read_rows(scratch, pitch, first, count, rows):
    return [scratch[pl.ds(first + index, rows, stride=pitch), :] for index in range(count)]


def put_messages(out_ref, scratch, places):
    pitch = scratch.shape[0] // len(places)
    for member, spots in enumerate(places):
        message = scratch[member * pitch : member * pitch + out_ref.shape[1]].astype(BF16)
        for spot in spots:
            out_ref[spot] = message


def take_messages(scratch, sent_ref, places):
    pitch = scratch.shape[0] // len(places)
    for member, spots in enumerate(places):
        total = sent_ref[spots[0]].astype(F32)
        for spot in spots[1:]:
            total = total + sent_ref[spot].astype(F32)
        scratch[member * pitch : member * pitch + sent_ref.shape[1]] = total


def shifted(value, step):
    if step == 0:
        return value
    width = value.shape[1]
    return pltpu.roll(value, (-step) % width, 1)


def stack_shifted(value, order):
    return jnp.concatenate([shifted(value, step) for step in order], axis=0).astype(BF16)


def add_shifted(value, order, rows):
    total = None
    for index, step in enumerate(order):
        part = shifted(value[index * rows : (index + 1) * rows], step)
        total = part if total is None else total + part
    return total


def hidden_state(image, first_ref, bias_column):
    stack = stack_shifted(image, (-1, 0, 1))
    return (
        jnp.dot(first_ref[:, : stack.shape[0]], stack, preferred_element_type=F32) + bias_column
    )


def second_conv(hidden, second_ref, bias_column, rows, valid):
    mixed = jnp.dot(
        second_ref[...], jnp.where(valid, hidden, 0.0).astype(BF16), preferred_element_type=F32
    )
    total = add_shifted(mixed, (-1, 0, 1), 2 * rows)
    return jnp.where(valid[: 2 * rows], total + bias_column, 0.0)


def pull_back(cotangent, slope, first_t_ref, second_t_ref, rows, valid):
    stack = stack_shifted(cotangent, (1, 0, -1))
    back = jnp.dot(second_t_ref[:, : stack.shape[0]], stack, preferred_element_type=F32)
    back = jnp.where(valid, back * slope, 0.0).astype(BF16)
    mixed = jnp.dot(first_t_ref[...], back, preferred_element_type=F32)
    total = add_shifted(mixed, (1, 0, -1), 2 * rows)
    return jnp.where(valid[: 2 * rows], total, 0.0)


def read_mask(sampling_ref, width):
    mask = sampling_ref[...].astype(F32)
    return jnp.pad(mask, ((0, 0), (0, width - mask.shape[1])))


def valid_lanes(rows, width, lines):
    return lane_index((rows, width)) < lines


def column(columns_ref, place, rows):
    at = 4 * 9 * CASCADES + place
    return columns_ref[:rows, at : at + 1]


def round_bf(value):
    return value.astype(BF16).astype(F32)


def choose_volume(value, coils, volumes, volume):
    parts = blocks(value, coils * volumes)
    chosen = [pick(parts[coil * volumes : (coil + 1) * volumes], volume) for coil in range(coils)]
    return jnp.concatenate(chosen, axis=0)


def pack_kernel(coils, volumes, pitch, places, kspace_ref, maps_ref, image_ref, out_ref, *refs):
    handed, (scratch,) = refs[:-1], refs[-1:]
    rows = image_ref.shape[0]
    depth = rows // volumes
    volume = own_volume(depth)
    kspace = kspace_ref[...].astype(F32)
    for step, ref in enumerate(handed, 1):
        other = lax.rem(volume + step, jnp.int32(volumes))
        ref[...] = choose_volume(kspace, coils, volumes, other).astype(BF16)
    count = maps_ref.shape[1] // LANES
    scratch[...] = jnp.zeros_like(scratch)
    image = image_ref[...].astype(F32)
    for coil in range(coils + 1):
        value = maps_ref[coil * rows : (coil + 1) * rows, :].astype(F32) if coil < coils else image
        for place, part in enumerate(blocks(value, volumes)):
            first = (place * (coils + 1) + coil) * count
            write_rows(scratch, pitch, lane_chunks(part), first)
    put_messages(out_ref, scratch, places)


def taps_kernel(
    rows,
    weight_ref,
    kernel_in_ref,
    kernel_out_ref,
    bias_in_ref,
    bias_out_ref,
    repeat_ref,
    place_ref,
    offset_ref,
    first_ref,
    first_t_ref,
    second_ref,
    second_t_ref,
    columns_ref,
    taps,
):
    taps[...] = jnp.zeros_like(taps)
    channels = kernel_in_ref.shape[2]
    at = 0
    for ref in (kernel_in_ref, kernel_out_ref):
        for index in range(ref.shape[0]):
            taps[at : at + 2, :channels] = ref[index]
            at += 2
    taps[at : at + CASCADES, :channels] = bias_in_ref[...]
    at += CASCADES
    for cascade in range(CASCADES):
        taps[at : at + 1, :] = jnp.full((1, taps.shape[1]), weight_ref[cascade], F32)
        at += 1
    taps[at : at + CASCADES, : bias_out_ref.shape[1]] = bias_out_ref[...]
    tall = lax.dot_general(
        repeat_ref[...],
        taps[...],
        (((1,), (1,)), ((), ())),
        precision=lax.Precision.HIGHEST,
        preferred_element_type=F32,
    )
    columns_ref[...] = tall
    wide = jnp.dot(tall.astype(BF16), place_ref[...], preferred_element_type=F32)
    offset = offset_ref[...]
    width = offset.shape[1]
    for cascade in range(CASCADES):
        for kind, straight, turned in ((0, first_ref, first_t_ref), (1, second_t_ref, second_ref)):
            total = jnp.zeros_like(offset)
            for tap in range(3):
                start = ((kind * CASCADES + cascade) * 3 + tap) * width
                wanted = float(tap if kind == 0 else 2 - tap)
                total = total + jnp.where(offset == wanted, wide[:, start : start + width], 0.0)
            straight[cascade] = total.astype(BF16)
            turned[cascade] = total.T[: 6 * rows].astype(BF16)


def line_images(kspace, mask, lines, table_ref, plus_ref):
    real, imag = split_complex(lane_chunks(kspace), lines)
    measured = jnp.concatenate([real * mask, imag * mask], axis=0)
    return line_apply(depth_apply(measured, plus_ref), table_ref, 1.0)


def far_kernel(coils, lines, volumes, kspace_ref, mask_ref, table_ref, plus_ref, out_ref):
    parts = blocks(read_mask(mask_ref, table_ref.shape[0]), volumes)
    mask = pick(parts, own_volume(parts[0].shape[0]))
    mask = over_coils(mask, coils)
    images = line_images(kspace_ref[...].astype(F32), mask, lines, table_ref, plus_ref)
    out_ref[: images.shape[0]] = images
    if out_ref.shape[0] > images.shape[0]:
        out_ref[images.shape[0] :] = jnp.zeros_like(out_ref[images.shape[0] :])


def own_kernel(coils, lines, volumes, kspace_ref, mask_ref, table_ref, plus_ref, out_ref):
    parts = blocks(read_mask(mask_ref, table_ref.shape[0]), volumes)
    volume = own_volume(parts[0].shape[0])
    kspace = choose_volume(kspace_ref[...].astype(F32), coils, volumes, volume)
    mask = over_coils(pick(parts, volume), coils)
    out_ref[...] = line_images(kspace, mask, lines, table_ref, plus_ref)


def rows_kernel(
    coils,
    lines,
    volumes,
    from_places,
    to_places,
    sent_ref,
    mask_ref,
    table_ref,
    minus_ref,
    plus_ref,
    *refs,
):
    arrival_refs, refs = refs[:volumes], refs[volumes:]
    out_ref, maps_ref, arrived, leaving = refs
    depth, pitch = sent_ref.shape[:2]
    volume = own_volume(depth)
    mask = pick(blocks(read_mask(mask_ref, table_ref.shape[0]), volumes), volume)
    mask = over_coils(mask, volumes * coils)

    arrivals = [halves(ref[: 2 * coils * depth]) for ref in arrival_refs]
    measured = []
    for part in range(2):
        for place in range(volumes):
            step = lax.rem(volume - place + volumes, jnp.int32(volumes))
            measured.append(pick([arrival[part] for arrival in arrivals], step))
    measured = jnp.concatenate(measured, axis=0)

    take_messages(arrived, sent_ref, from_places)
    count = 2 * lines // LANES
    parts, reals, imags = [], [], []
    for place in range(volumes):
        first = place * (coils + 1) * count
        for coil in range(coils):
            chunks = read_rows(arrived, pitch, first + coil * count, count, depth)
            parts.append(split_complex(chunks, lines))
        chunks = read_rows(arrived, pitch, first + coils * count, count, depth)
        real, imag = split_complex(chunks, lines)
        reals.append(real)
        imags.append(imag)
    maps_real = jnp.concatenate([part[0] for part in parts], axis=0)
    maps_imag = jnp.concatenate([part[1] for part in parts], axis=0)
    maps_ref[...] = jnp.concatenate([maps_real, maps_imag], axis=0).astype(BF16)

    images = spread(maps_real, maps_imag, over_rows(reals, coils), over_rows(imags, coils))
    mask = jnp.concatenate([mask, mask], axis=0)
    images = masked_normal(images, table_ref, minus_ref, plus_ref, mask)
    found = [
        *collect(maps_real, maps_imag, round_bf(measured)),
        *collect(maps_real, maps_imag, images),
        maps_real * maps_real + maps_imag * maps_imag,
    ]
    leaving[...] = jnp.zeros_like(leaving)
    sums = [row_sums(value, volumes, coils) for value in found]
    pitch = out_ref.shape[1]
    for place in range(volumes):
        chunks = [chunk for value in sums for chunk in lane_chunks(value[place])]
        write_rows(leaving, pitch, chunks, place * (pitch // volumes))
    put_messages(out_ref, leaving, to_places)


def read_image(scratch, pitch, first, count, depth):
    return jnp.concatenate(read_rows(scratch, pitch, first, count, depth), axis=1)


def read_places(scratch, pitch, first, period, count, depth, volumes):
    parts = [
        read_image(scratch, pitch, first + place * period, count, depth) for place in range(volumes)
    ]
    return jnp.concatenate(parts, axis=0)


def read_complex(scratch, pitch, first, period, count, depth, volumes):
    real = read_places(scratch, pitch, first, period, count, depth, volumes)
    imag = read_places(scratch, pitch, first + count, period, count, depth, volumes)
    return jnp.concatenate([real, imag], axis=0)


def refine_kernel(
    lines,
    volumes,
    from_places,
    to_places,
    sent_ref,
    cotangent_ref,
    first_ref,
    first_t_ref,
    second_ref,
    second_t_ref,
    columns_ref,
    out_ref,
    image_ref,
    arrived,
    leaving,
):
    take_messages(arrived, sent_ref, from_places)
    depth, pitch = len(from_places), sent_ref.shape[1]
    rows = depth * volumes
    width = padded(lines, LANES)
    count = width // LANES
    begun = read_complex(arrived, pitch, 0, pitch // volumes, count, depth, volumes)
    turned = read_complex(arrived, pitch, 2 * count, pitch // volumes, count, depth, volumes)
    power = read_places(arrived, pitch, 4 * count, pitch // volumes, count, depth, volumes)
    power = jnp.concatenate([power, power], axis=0)
    cotangent = jnp.concatenate(
        split_complex(lane_chunks(cotangent_ref[...].astype(F32)), lines), axis=0
    )
    tall = first_ref.shape[1]
    weight = [column(columns_ref, CASCADES + cascade, 2 * rows) for cascade in range(CASCADES)]
    bias = [column(columns_ref, 2 * CASCADES + cascade, 2 * rows) for cascade in range(CASCADES)]

    share = [jnp.ones_like(weight[0])]
    for cascade in range(CASCADES):
        share.append(share[cascade] - weight[cascade] * (share[cascade] - 1.0))

    def slopes(hidden):
        gate = jax.nn.sigmoid(hidden)
        return hidden * gate, gate * (1.0 + hidden * (1.0 - gate))

    hidden = hidden_state(round_bf(begun), first_ref.at[0], column(columns_ref, 0, tall))
    valid = valid_lanes(hidden.shape[0], width, lines)
    active, slope_first = slopes(hidden)
    model = round_bf(second_conv(active, second_ref.at[0], bias[0], rows, valid))
    picture = round_bf(share[1] * begun + power * model)
    hidden = hidden_state(picture, first_ref.at[1], column(columns_ref, 1, tall))
    active, slope_second = slopes(hidden)
    later = round_bf(second_conv(active, second_ref.at[1], bias[1], rows, valid))
    image_ref[...] = share[2] * begun + power * (model + later)

    through = power * cotangent
    back_second = round_bf(
        pull_back(through, slope_second, first_t_ref.at[1], second_t_ref.at[1], rows, valid)
    )
    through = through - weight[1] * turned + power * back_second
    back_first = round_bf(
        pull_back(through, slope_first, first_t_ref.at[0], second_t_ref.at[0], rows, valid)
    )
    kept = (1.0 - weight[0], 1.0 - weight[1])
    of_cotangent = weight[1] + weight[0] * kept[1] + kept[0] * kept[1]
    of_second = weight[0] + kept[0]
    pulled = of_cotangent * cotangent + of_second * back_second + back_first
    leaving[...] = jnp.zeros_like(leaving)
    parts = [blocks(part, volumes) for value in (model, pulled) for part in halves(value)]
    for place in range(volumes):
        chunks = [chunk for part in parts for chunk in lane_chunks(part[place])]
        write_rows(leaving, out_ref.shape[1], chunks, place * len(chunks))
    put_messages(out_ref, leaving, to_places)


def hand_kernel(lines, volumes, from_places, sent_ref, maps_ref, *refs):
    outs, (arrived,) = refs[:-1], refs[-1:]
    take_messages(arrived, sent_ref, from_places)
    depth, pitch = sent_ref.shape[:2]
    volume = own_volume(depth)
    count = maps_ref.shape[1] // LANES
    maps = [blocks(part, volumes) for part in halves(maps_ref[...].astype(F32))]
    pulled = [
        [
            read_image(arrived, pitch, (place * 4 + field) * count, count, depth)
            for place in range(volumes)
        ]
        for field in (2, 3)
    ]
    for step, ref in enumerate(outs):
        place = lax.rem(volume + step, jnp.int32(volumes))
        chosen = [jnp.concatenate([pick(a, place), pick(b, place)]) for a, b in zip(maps, pulled)]
        for index, chunk in enumerate(join_complex(*chosen, lines)):
            ref[:, index * LANES : (index + 1) * LANES] = chunk.astype(BF16)


def normal_kernel(
    coils,
    lines,
    volumes,
    from_places,
    to_places,
    sent_ref,
    maps_ref,
    mask_ref,
    table_ref,
    minus_ref,
    plus_ref,
    out_ref,
    arrived,
    leaving,
):
    take_messages(arrived, sent_ref, from_places)
    depth, pitch = sent_ref.shape[:2]
    volume = own_volume(depth)
    count = maps_ref.shape[1] // LANES
    fields = [
        [
            read_image(arrived, pitch, (place * 4 + field) * count, count, depth)
            for place in range(volumes)
        ]
        for field in range(2)
    ]
    reals, imags = fields
    maps_real, maps_imag = halves(maps_ref[...].astype(F32))
    mask = over_coils(pick(blocks(read_mask(mask_ref, table_ref.shape[0]), volumes), volume), 2 * volumes * coils)
    images = spread(maps_real, maps_imag, over_rows(reals, coils), over_rows(imags, coils))
    images = masked_normal(images, table_ref, minus_ref, plus_ref, mask)
    found = [row_sums(value, volumes, coils) for value in collect(maps_real, maps_imag, images)]
    leaving[...] = jnp.zeros_like(leaving)
    for place in range(volumes):
        chunks = join_complex(found[0][place], found[1][place], lines)
        write_rows(leaving, leaving.shape[0] // depth, chunks, place * len(chunks))
    put_messages(out_ref, leaving, to_places)


def from_volumes(refs, volume, parts, volumes):
    sources = [blocks(ref, parts) for ref in refs]
    ordered = []
    for place in range(volumes):
        step = lax.rem(volume - place + volumes, jnp.int32(volumes))
        ordered.append([pick([source[part] for source in sources], step) for part in range(parts)])
    return ordered


def grad_kernel(
    coils,
    lines,
    volumes,
    mask_ref,
    table_ref,
    minus_ref,
    *refs,
):
    handed, (grad_ref,) = refs[:volumes], refs[volumes:]
    depth = mask_ref.shape[0] // volumes
    volume = own_volume(depth)
    handed = [split_complex(lane_chunks(ref[...].astype(F32)), lines) for ref in handed]
    handed = [jnp.concatenate(parts, axis=0) for parts in handed]
    found = from_volumes(handed, volume, 2 * (coils + 1), volumes)
    maps, pulled = [], []
    for first in (0, coils + 1):
        parts = [found[v][first + coil] for coil in range(coils) for v in range(volumes)]
        maps.append(jnp.concatenate(parts, axis=0))
        pulled.append(jnp.concatenate([found[v][first + coils] for v in range(volumes)], axis=0))
    real, imag = pulled
    images = spread(*maps, over_coils(real, coils), over_coils(imag, coils))
    spectrum = depth_apply(line_apply(images, table_ref, -1.0), minus_ref)
    spectrum = spectrum * over_coils(read_mask(mask_ref, table_ref.shape[0]), 2 * coils)
    chunks = join_complex(*halves(spectrum), lines)
    write_rows(grad_ref, len(chunks), chunks)


def picture_kernel(lines, volumes, from_places, columns_ref, sent_ref, image_ref, picture_ref, arrived):
    depth = len(from_places)
    pitch = arrived.shape[0] // depth
    count = 2 * lines // LANES
    take_messages(arrived, sent_ref, from_places)
    parts = [[], []]
    for place in range(volumes):
        chunks = read_rows(arrived, pitch, place * count, count, depth)
        for part, value in zip(parts, split_complex(chunks, lines)):
            part.append(value)
    picture = image_ref[...]
    scale = column(columns_ref, CASCADES + 1, picture.shape[0])
    picture = picture - scale * jnp.concatenate(parts[0] + parts[1], axis=0)
    for index, chunk in enumerate(join_complex(*halves(picture), lines)):
        picture_ref[:, index * LANES : (index + 1) * LANES] = chunk


def end_kernel(
    coils,
    lines,
    volumes,
    from_places,
    columns_ref,
    sent_ref,
    image_ref,
    mask_ref,
    table_ref,
    minus_ref,
    *refs,
):
    handed, (picture_ref, grad_ref, arrived) = refs[:volumes], refs[volumes:]
    grad_kernel(coils, lines, volumes, mask_ref, table_ref, minus_ref, *handed, grad_ref)
    picture_kernel(
        lines, volumes, from_places, columns_ref, sent_ref, image_ref, picture_ref, arrived
    )


def call(kernel, name, operands, outs, scratch, flops, vmem_bytes=VMEM_BYTES, scalars=0):
    spaces = [pltpu.SMEM] * scalars + [pltpu.VMEM] * (len(operands) - scalars)
    moved = sum(math.prod(item.shape) * item.dtype.itemsize for item in (*operands, *outs))
    return pl.pallas_call(
        kernel,
        name=name,
        out_shape=tuple(outs),
        in_specs=[pl.BlockSpec(memory_space=space) for space in spaces],
        out_specs=tuple(pl.BlockSpec(memory_space=pltpu.VMEM) for item in outs),
        scratch_shapes=[pltpu.VMEM(shape, F32) for shape in scratch],
        compiler_params=pltpu.CompilerParams(vmem_limit_bytes=vmem_bytes),
        cost_estimate=pl.CostEstimate(flops=flops, bytes_accessed=moved, transcendentals=0),
    )(*operands)


def body(
    kspace, coil_maps, sampling, dc_weight, kernel_in, bias_in, kernel_out, bias_out, cotangent
):
    coils, slots = kspace.shape[:2]
    rows, two_lines = coil_maps.shape[2:]
    lines = two_lines // 2
    channels = bias_in.shape[1]
    coil_devices, sections = lax.axis_size("coil"), lax.axis_size("section")
    volumes = VOLUMES
    depth = slots // volumes
    width = padded(lines, LANES)
    count, whole_count = width // LANES, two_lines // LANES
    planes = coils * slots
    both = ("section", "coil")
    span = depth * coil_devices
    near_order = [depth - 1] + list(range(depth - 1))
    both_order = list(range(span))[::-1]
    near = [[group * depth + member for member in near_order] for group in range(volumes)]
    near_both = [[group * span + member for member in both_order] for group in range(volumes)]
    near_places = [[near_order.index(member)] for member in range(depth)]
    both_places = [
        [both_order.index(member * coil_devices + coil) for coil in range(coil_devices)]
        for member in range(depth)
    ]

    def from_group(value, step, core=0):
        pairs = [(s, ((s + step * depth) % sections) ^ core) for s in range(sections)]
        return lax.ppermute(value, "section", pairs)

    def between_cores(value):
        return lax.ppermute(value, "section", [(s, s ^ 1) for s in range(sections)])

    def exchange(value, axes, groups):
        return lax.all_to_all(value, axes, 0, 0, tiled=True, axis_index_groups=groups)

    table = jnp.asarray(line_constant(lines))
    minus = jnp.asarray(depth_constant(coils, slots, volumes, -1.0))
    plus = jnp.asarray(depth_constant(coils, slots, volumes, 1.0))
    near_plus = jnp.asarray(depth_constant(coils, depth, 1, 1.0))
    repeat, place, offset = (jnp.asarray(item) for item in conv_constants(rows, channels))
    mask = sampling.reshape(slots, lines)

    def shape(*dims, kind=F32):
        return jax.ShapeDtypeStruct(dims, kind)

    line_flops = 2 * (2 * planes) * width * (2 * width)

    pitch = padded(volumes * (coils + 1) * whole_count, 16)
    packed, *samples = call(
        functools.partial(pack_kernel, coils, volumes, pitch, near_places),
        "pack_maps",
        (
            kspace.reshape(planes, two_lines),
            coil_maps.reshape(coils * rows, two_lines),
            cotangent.reshape(rows, two_lines),
        ),
        [shape(depth, pitch, LANES, kind=BF16)]
        + [shape(coils * depth, two_lines, kind=BF16)] * (volumes - 1),
        [(depth * pitch, LANES)],
        1000,
        LARGE_VMEM_BYTES,
    )
    samples = [from_group(value, step, 1) for step, value in enumerate(samples, 1)]
    tall, wide = channels * rows, offset.shape[1]
    first, first_t, second, second_t, columns = call(
        functools.partial(taps_kernel, rows),
        "lay_out_taps",
        (
            dc_weight,
            kernel_in.transpose(0, 1, 3, 2).reshape(-1, 2, channels),
            kernel_out.reshape(-1, 2, channels),
            bias_in,
            bias_out,
            repeat,
            place,
            offset,
        ),
        [
            shape(CASCADES, tall, wide, kind=BF16),
            shape(CASCADES, 6 * rows, tall, kind=BF16),
            shape(CASCADES, 6 * rows, tall, kind=BF16),
            shape(CASCADES, tall, wide, kind=BF16),
            shape(tall, place.shape[0]),
        ],
        [(place.shape[0], repeat.shape[1])],
        2 * tall * place.shape[0] * place.shape[1],
        scalars=1,
    )
    *samples, columns = lax.optimization_barrier((*samples, columns))
    (own,) = call(
        functools.partial(own_kernel, coils, lines, volumes),
        "own_images",
        (kspace.reshape(planes, two_lines), mask, table, near_plus),
        [shape(2 * coils * depth, width)],
        [],
        line_flops,
    )
    images = [own]
    for value in samples:
        (image,) = call(
            functools.partial(far_kernel, coils, lines, volumes),
            "far_images",
            (value, mask, table, near_plus),
            [shape(FAR_PARTS * coils * depth, width)],
            [],
            line_flops,
        )
        images.append(between_cores(image))
    arrived = exchange(packed, "section", near)

    depth_pitch = padded(volumes * 5 * count, 16 * volumes)
    partial, maps = call(
        functools.partial(rows_kernel, coils, lines, volumes, near_places, both_places),
        "combine_rows",
        (arrived, mask, table, minus, plus, *images),
        [
            shape(span, depth_pitch, LANES, kind=BF16),
            shape(2 * planes, width, kind=BF16),
        ],
        [(depth * pitch, LANES), (depth * depth_pitch, LANES)],
        4 * line_flops,
    )

    partial = exchange(partial, both, near_both)

    model_pitch = padded(volumes * 4 * count, 8)
    moved, image = call(
        functools.partial(refine_kernel, lines, volumes, both_places, near_places),
        "refine_and_back",
        (
            partial,
            cotangent.reshape(rows, two_lines),
            first,
            first_t,
            second,
            second_t,
            columns,
        ),
        [shape(depth, model_pitch, LANES, kind=BF16), shape(2 * rows, width)],
        [(depth * depth_pitch, LANES), (depth * model_pitch, LANES)],
        14 * tall * wide * width,
    )
    moved = exchange(moved, "section", near)

    end_lines = volumes * whole_count
    end_pitch = padded(end_lines, 16)
    handed = call(
        functools.partial(hand_kernel, lines, volumes, near_places),
        "hand_on",
        (moved, maps),
        [shape((coils + 1) * depth, two_lines, kind=BF16)] * volumes,
        [(depth * model_pitch, LANES)],
        1000,
    )
    handed = list(handed)
    (partial,) = call(
        functools.partial(normal_kernel, coils, lines, volumes, near_places, both_places),
        "masked_normal",
        (moved, maps, mask, table, minus, plus),
        [shape(span, end_lines, LANES, kind=BF16)],
        [(depth * model_pitch, LANES), (depth * end_pitch, LANES)],
        3 * line_flops,
    )
    partial = exchange(partial, both, near_both)
    handed[1:] = [
        from_group(value, step) for step, value in enumerate(handed[1:], 1)
    ]

    image, grad = call(
        functools.partial(end_kernel, coils, lines, volumes, both_places),
        "outputs",
        (columns, partial, image, mask, table, minus, *handed),
        [shape(rows, two_lines), shape(planes * whole_count, LANES)],
        [(depth * end_pitch, LANES)],
        2 * line_flops,
    )
    return image.reshape(1, rows, two_lines), grad.reshape(coils, slots, 1, two_lines)


def solution(mesh):
    return jax.shard_map(
        body,
        mesh=mesh,
        in_specs=(
            P("coil", None, "section", None),
            P("coil", "section", None, None),
            P(),
            P(),
            P(),
            P(),
            P(),
            P(),
            P("section", None, None),
        ),
        out_specs=(P("section", None, None), P("coil", None, "section", None)),
        check_vma=False,
    )
```

```python
import functools
import math

import jax
import jax.numpy as jnp
import ml_dtypes
import numpy as np
from jax import lax
from jax.experimental import pallas as pl
from jax.experimental.pallas import tpu as pltpu
from jax.sharding import PartitionSpec as P

CASCADES = 2
VOLUMES = 2
LANES = 128
VMEM_BYTES = 48 * 1024 * 1024
FAR_PARTS = 3
LARGE_VMEM_BYTES = 60 * 1024 * 1024

F32 = jnp.float32
BF16 = jnp.bfloat16


def padded(size, unit):
    return -(-size // unit) * unit


def dft_parts(count):
    indices = np.arange(count)
    angles = (indices[:, None] * indices[None, :] % count) * (2.0 * math.pi / count)
    factor = 1.0 / math.sqrt(count)
    return np.cos(angles) * factor, np.sin(angles) * factor


def line_constant(lines):
    width = padded(lines, LANES)
    cosine, sine = dft_parts(lines)
    table = np.zeros((width, 2 * width), np.float32)
    table[:lines, :lines] = cosine
    table[:lines, width : width + lines] = sine
    return table.astype(ml_dtypes.bfloat16)


def depth_constant(coils, slots, volumes, sign):
    cosine, sine = dft_parts(slots // volumes)
    spread_over = np.eye(coils * volumes)
    real, imag = np.kron(spread_over, cosine), sign * np.kron(spread_over, sine)
    return np.block([[real, -imag], [imag, real]]).astype(np.float32).astype(ml_dtypes.bfloat16)


def conv_constants(rows, channels):
    groups = 6
    width = padded(groups * rows, LANES)
    repeat = np.kron(np.eye(channels), np.ones((rows, 1))).astype(np.float32)
    repeat = np.pad(repeat, ((0, 0), (0, padded(channels, LANES) - channels)))
    taps = CASCADES * 3
    place = np.zeros((padded(2 * taps * groups + 3 * CASCADES, LANES), 2 * taps * width), np.float32)
    for kind in range(2):
        for tap in range(taps):
            for group in range(groups):
                start = (kind * taps + tap) * width + group * rows
                place[(kind * taps + tap) * groups + group, start : start + rows] = 1.0
    offset = np.full((channels * rows, width), -9.0, np.float32)
    row = np.arange(rows)
    offset[:, : groups * rows] = np.tile(row[None, :] - row[:, None] + 1.0, (channels, groups))
    offset = np.clip(offset, -9.0, 9.0)
    return repeat, place.astype(ml_dtypes.bfloat16), offset


def lane_index(shape):
    return lax.broadcasted_iota(jnp.int32, shape, len(shape) - 1)


def split_complex(chunks, lines):
    whole, rest = divmod(lines, LANES)
    count = padded(lines, LANES) // LANES
    if rest == 0:
        return jnp.concatenate(chunks[:count], 1), jnp.concatenate(chunks[count:], 1)
    lane = lane_index(chunks[0].shape)
    real = chunks[:whole] + [jnp.where(lane < rest, chunks[whole], 0.0)]
    turned = [pltpu.roll(chunk, LANES - rest, 1) for chunk in chunks[whole:]]
    turned.append(jnp.zeros_like(turned[0]))
    imag = [jnp.where(lane < LANES - rest, turned[k], turned[k + 1]) for k in range(count)]
    imag[-1] = jnp.where(lane < rest, imag[-1], 0.0)
    return jnp.concatenate(real, 1), jnp.concatenate(imag, 1)


def lane_chunks(value):
    return [value[:, start : start + LANES] for start in range(0, value.shape[1], LANES)]


def join_complex(real, imag, lines):
    whole, rest = divmod(lines, LANES)
    real, imag = lane_chunks(real), lane_chunks(imag)
    if rest == 0:
        return real + imag
    lane = lane_index(real[0].shape)
    turned = [real[whole]] + [pltpu.roll(chunk, rest, 1) for chunk in imag]
    mixed = [jnp.where(lane < rest, turned[k], turned[k + 1]) for k in range(len(imag))]
    return (real[:whole] + mixed)[: 2 * lines // LANES]


def halves(stacked):
    half = stacked.shape[0] // 2
    return stacked[:half], stacked[half:]


def line_apply(stacked, table_ref, sign):
    mixed = jnp.dot(stacked.astype(BF16), table_ref[...], preferred_element_type=F32)
    width = table_ref.shape[1] // 2
    top, bottom = halves(mixed)
    return jnp.concatenate(
        [
            top[:, :width] - sign * bottom[:, width:],
            bottom[:, :width] + sign * top[:, width:],
        ],
        axis=0,
    )


def depth_apply(stacked, depth_ref):
    return jnp.dot(depth_ref[...], stacked.astype(BF16), preferred_element_type=F32)


def over_coils(value, coils):
    return jnp.concatenate([value] * coils, axis=0)


def coil_sum(value, coils):
    slots = value.shape[0] // coils
    total = value[:slots]
    for coil in range(1, coils):
        total = total + value[coil * slots : (coil + 1) * slots]
    return total


def over_rows(parts, coils):
    return jnp.concatenate([part for part in parts for coil in range(coils)], axis=0)


def spread(maps_real, maps_imag, real, imag):
    return jnp.concatenate(
        [maps_real * real - maps_imag * imag, maps_real * imag + maps_imag * real], axis=0
    )


def collect(maps_real, maps_imag, images):
    real, imag = halves(images)
    return maps_real * real + maps_imag * imag, maps_real * imag - maps_imag * real


def blocks(value, count):
    size = value.shape[0] // count
    return [value[index * size : (index + 1) * size] for index in range(count)]


def row_sums(value, rows, coils):
    return [coil_sum(part, coils) for part in blocks(value, rows)]


def pick(parts, index):
    chosen = parts[0]
    for place in range(1, len(parts)):
        chosen = jnp.where(index == place, parts[place], chosen)
    return chosen


def own_volume(depth):
    return lax.div(lax.axis_index("section"), jnp.int32(depth))


def masked_normal(images, table_ref, minus_ref, plus_ref, mask):
    spectrum = depth_apply(line_apply(images, table_ref, -1.0), minus_ref)
    return line_apply(depth_apply(spectrum * mask, plus_ref), table_ref, 1.0)


def write_rows(scratch, pitch, values, first=0):
    for index, value in enumerate(values):
        scratch[pl.ds(first + index, value.shape[0], stride=pitch), :] = value


def read_rows(scratch, pitch, first, count, rows):
    return [scratch[pl.ds(first + index, rows, stride=pitch), :] for index in range(count)]


def put_messages(out_ref, scratch, places):
    pitch = scratch.shape[0] // len(places)
    for member, spots in enumerate(places):
        message = scratch[member * pitch : member * pitch + out_ref.shape[1]].astype(BF16)
        for spot in spots:
            out_ref[spot] = message


def take_messages(scratch, sent_ref, places):
    pitch = scratch.shape[0] // len(places)
    for member, spots in enumerate(places):
        total = sent_ref[spots[0]].astype(F32)
        for spot in spots[1:]:
            total = total + sent_ref[spot].astype(F32)
        scratch[member * pitch : member * pitch + sent_ref.shape[1]] = total


def shifted(value, step):
    if step == 0:
        return value
    width = value.shape[1]
    return pltpu.roll(value, (-step) % width, 1)


def stack_shifted(value, order):
    return jnp.concatenate([shifted(value, step) for step in order], axis=0).astype(BF16)


def add_shifted(value, order, rows):
    total = None
    for index, step in enumerate(order):
        part = shifted(value[index * rows : (index + 1) * rows], step)
        total = part if total is None else total + part
    return total


def hidden_state(image, first_ref, bias_column):
    stack = stack_shifted(image, (-1, 0, 1))
    return (
        jnp.dot(first_ref[:, : stack.shape[0]], stack, preferred_element_type=F32) + bias_column
    )


def second_conv(hidden, second_ref, bias_column, rows, valid):
    mixed = jnp.dot(
        second_ref[...], jnp.where(valid, hidden, 0.0).astype(BF16), preferred_element_type=F32
    )
    total = add_shifted(mixed, (-1, 0, 1), 2 * rows)
    return jnp.where(valid[: 2 * rows], total + bias_column, 0.0)


def pull_back(cotangent, slope, first_t_ref, second_t_ref, rows, valid):
    stack = stack_shifted(cotangent, (1, 0, -1))
    back = jnp.dot(second_t_ref[:, : stack.shape[0]], stack, preferred_element_type=F32)
    back = jnp.where(valid, back * slope, 0.0).astype(BF16)
    mixed = jnp.dot(first_t_ref[...], back, preferred_element_type=F32)
    total = add_shifted(mixed, (1, 0, -1), 2 * rows)
    return jnp.where(valid[: 2 * rows], total, 0.0)


def read_mask(sampling_ref, width):
    mask = sampling_ref[...].astype(F32)
    return jnp.pad(mask, ((0, 0), (0, width - mask.shape[1])))


def valid_lanes(rows, width, lines):
    return lane_index((rows, width)) < lines


def column(columns_ref, place, rows):
    at = 4 * 9 * CASCADES + place
    return columns_ref[:rows, at : at + 1]


def round_bf(value):
    return value.astype(BF16).astype(F32)


def choose_volume(value, coils, volumes, volume):
    parts = blocks(value, coils * volumes)
    chosen = [pick(parts[coil * volumes : (coil + 1) * volumes], volume) for coil in range(coils)]
    return jnp.concatenate(chosen, axis=0)


def pack_kernel(coils, volumes, pitch, places, kspace_ref, maps_ref, image_ref, out_ref, *refs):
    handed, (scratch,) = refs[:-1], refs[-1:]
    rows = image_ref.shape[0]
    depth = rows // volumes
    volume = own_volume(depth)
    kspace = kspace_ref[...].astype(F32)
    for step, ref in enumerate(handed, 1):
        other = lax.rem(volume + step, jnp.int32(volumes))
        ref[...] = choose_volume(kspace, coils, volumes, other).astype(BF16)
    count = maps_ref.shape[1] // LANES
    scratch[...] = jnp.zeros_like(scratch)
    image = image_ref[...].astype(F32)
    for coil in range(coils + 1):
        value = maps_ref[coil * rows : (coil + 1) * rows, :].astype(F32) if coil < coils else image
        for place, part in enumerate(blocks(value, volumes)):
            first = (place * (coils + 1) + coil) * count
            write_rows(scratch, pitch, lane_chunks(part), first)
    put_messages(out_ref, scratch, places)


def taps_kernel(
    rows,
    weight_ref,
    kernel_in_ref,
    kernel_out_ref,
    bias_in_ref,
    bias_out_ref,
    repeat_ref,
    place_ref,
    offset_ref,
    first_ref,
    first_t_ref,
    second_ref,
    second_t_ref,
    columns_ref,
    taps,
):
    taps[...] = jnp.zeros_like(taps)
    channels = kernel_in_ref.shape[2]
    at = 0
    for ref in (kernel_in_ref, kernel_out_ref):
        for index in range(ref.shape[0]):
            taps[at : at + 2, :channels] = ref[index]
            at += 2
    taps[at : at + CASCADES, :channels] = bias_in_ref[...]
    at += CASCADES
    for cascade in range(CASCADES):
        taps[at : at + 1, :] = jnp.full((1, taps.shape[1]), weight_ref[cascade], F32)
        at += 1
    taps[at : at + CASCADES, : bias_out_ref.shape[1]] = bias_out_ref[...]
    tall = lax.dot_general(
        repeat_ref[...],
        taps[...],
        (((1,), (1,)), ((), ())),
        precision=lax.Precision.HIGHEST,
        preferred_element_type=F32,
    )
    columns_ref[...] = tall
    wide = jnp.dot(tall.astype(BF16), place_ref[...], preferred_element_type=F32)
    offset = offset_ref[...]
    width = offset.shape[1]
    for cascade in range(CASCADES):
        for kind, straight, turned in ((0, first_ref, first_t_ref), (1, second_t_ref, second_ref)):
            total = jnp.zeros_like(offset)
            for tap in range(3):
                start = ((kind * CASCADES + cascade) * 3 + tap) * width
                wanted = float(tap if kind == 0 else 2 - tap)
                total = total + jnp.where(offset == wanted, wide[:, start : start + width], 0.0)
            straight[cascade] = total.astype(BF16)
            turned[cascade] = total.T[: 6 * rows].astype(BF16)


def line_images(kspace, mask, lines, table_ref, plus_ref):
    real, imag = split_complex(lane_chunks(kspace), lines)
    measured = jnp.concatenate([real * mask, imag * mask], axis=0)
    return line_apply(depth_apply(measured, plus_ref), table_ref, 1.0)


def far_kernel(coils, lines, volumes, kspace_ref, mask_ref, table_ref, plus_ref, out_ref):
    parts = blocks(read_mask(mask_ref, table_ref.shape[0]), volumes)
    mask = pick(parts, own_volume(parts[0].shape[0]))
    mask = over_coils(mask, coils)
    images = line_images(kspace_ref[...].astype(F32), mask, lines, table_ref, plus_ref)
    out_ref[: images.shape[0]] = images
    if out_ref.shape[0] > images.shape[0]:
        out_ref[images.shape[0] :] = jnp.zeros_like(out_ref[images.shape[0] :])


def own_kernel(coils, lines, volumes, kspace_ref, mask_ref, table_ref, plus_ref, out_ref):
    parts = blocks(read_mask(mask_ref, table_ref.shape[0]), volumes)
    volume = own_volume(parts[0].shape[0])
    kspace = choose_volume(kspace_ref[...].astype(F32), coils, volumes, volume)
    mask = over_coils(pick(parts, volume), coils)
    out_ref[...] = line_images(kspace, mask, lines, table_ref, plus_ref)


def rows_kernel(
    coils,
    lines,
    volumes,
    from_places,
    to_places,
    sent_ref,
    mask_ref,
    table_ref,
    minus_ref,
    plus_ref,
    *refs,
):
    arrival_refs, refs = refs[:volumes], refs[volumes:]
    out_ref, maps_ref, arrived, leaving = refs
    depth = sent_ref.shape[0]
    pitch = arrived.shape[0] // depth
    volume = own_volume(depth)
    mask = pick(blocks(read_mask(mask_ref, table_ref.shape[0]), volumes), volume)
    mask = over_coils(mask, volumes * coils)

    arrivals = [halves(ref[: 2 * coils * depth]) for ref in arrival_refs]
    measured = []
    for part in range(2):
        for place in range(volumes):
            step = lax.rem(volume - place + volumes, jnp.int32(volumes))
            measured.append(pick([arrival[part] for arrival in arrivals], step))
    measured = jnp.concatenate(measured, axis=0)

    take_messages(arrived, sent_ref, from_places)
    count = 2 * lines // LANES
    parts, reals, imags = [], [], []
    for place in range(volumes):
        first = place * (coils + 1) * count
        for coil in range(coils):
            chunks = read_rows(arrived, pitch, first + coil * count, count, depth)
            parts.append(split_complex(chunks, lines))
        chunks = read_rows(arrived, pitch, first + coils * count, count, depth)
        real, imag = split_complex(chunks, lines)
        reals.append(real)
        imags.append(imag)
    maps_real = jnp.concatenate([part[0] for part in parts], axis=0)
    maps_imag = jnp.concatenate([part[1] for part in parts], axis=0)
    maps_ref[...] = jnp.concatenate([maps_real, maps_imag], axis=0).astype(BF16)

    images = spread(maps_real, maps_imag, over_rows(reals, coils), over_rows(imags, coils))
    mask = jnp.concatenate([mask, mask], axis=0)
    images = masked_normal(images, table_ref, minus_ref, plus_ref, mask)
    found = [
        *collect(maps_real, maps_imag, round_bf(measured)),
        *collect(maps_real, maps_imag, images),
        maps_real * maps_real + maps_imag * maps_imag,
    ]
    leaving[...] = jnp.zeros_like(leaving)
    sums = [row_sums(value, volumes, coils) for value in found]
    pitch = leaving.shape[0] // depth
    for place in range(volumes):
        chunks = [chunk for value in sums for chunk in lane_chunks(value[place])]
        write_rows(leaving, pitch, chunks, place * len(chunks))
    put_messages(out_ref, leaving, to_places)


def read_image(scratch, pitch, first, count, depth):
    return jnp.concatenate(read_rows(scratch, pitch, first, count, depth), axis=1)


def read_places(scratch, pitch, first, period, count, depth, volumes):
    parts = [
        read_image(scratch, pitch, first + place * period, count, depth) for place in range(volumes)
    ]
    return jnp.concatenate(parts, axis=0)


def read_complex(scratch, pitch, first, period, count, depth, volumes):
    real = read_places(scratch, pitch, first, period, count, depth, volumes)
    imag = read_places(scratch, pitch, first + count, period, count, depth, volumes)
    return jnp.concatenate([real, imag], axis=0)


def refine_kernel(
    lines,
    volumes,
    from_places,
    to_places,
    sent_ref,
    cotangent_ref,
    first_ref,
    first_t_ref,
    second_ref,
    second_t_ref,
    columns_ref,
    out_ref,
    image_ref,
    arrived,
    leaving,
):
    take_messages(arrived, sent_ref, from_places)
    depth = len(from_places)
    pitch = arrived.shape[0] // depth
    rows = depth * volumes
    width = padded(lines, LANES)
    count = width // LANES
    begun = read_complex(arrived, pitch, 0, 5 * count, count, depth, volumes)
    turned = read_complex(arrived, pitch, 2 * count, 5 * count, count, depth, volumes)
    power = read_places(arrived, pitch, 4 * count, 5 * count, count, depth, volumes)
    power = jnp.concatenate([power, power], axis=0)
    cotangent = jnp.concatenate(
        split_complex(lane_chunks(cotangent_ref[...].astype(F32)), lines), axis=0
    )
    tall = first_ref.shape[1]
    weight = [column(columns_ref, CASCADES + cascade, 2 * rows) for cascade in range(CASCADES)]
    bias = [column(columns_ref, 2 * CASCADES + cascade, 2 * rows) for cascade in range(CASCADES)]

    share = [jnp.ones_like(weight[0])]
    for cascade in range(CASCADES):
        share.append(share[cascade] - weight[cascade] * (share[cascade] - 1.0))

    def slopes(hidden):
        gate = jax.nn.sigmoid(hidden)
        return hidden * gate, gate * (1.0 + hidden * (1.0 - gate))

    hidden = hidden_state(round_bf(begun), first_ref.at[0], column(columns_ref, 0, tall))
    valid = valid_lanes(hidden.shape[0], width, lines)
    active, slope_first = slopes(hidden)
    model = round_bf(second_conv(active, second_ref.at[0], bias[0], rows, valid))
    picture = round_bf(share[1] * begun + power * model)
    hidden = hidden_state(picture, first_ref.at[1], column(columns_ref, 1, tall))
    active, slope_second = slopes(hidden)
    later = round_bf(second_conv(active, second_ref.at[1], bias[1], rows, valid))
    image_ref[...] = share[2] * begun + power * (model + later)

    through = power * cotangent
    back_second = round_bf(
        pull_back(through, slope_second, first_t_ref.at[1], second_t_ref.at[1], rows, valid)
    )
    through = through - weight[1] * turned + power * back_second
    back_first = round_bf(
        pull_back(through, slope_first, first_t_ref.at[0], second_t_ref.at[0], rows, valid)
    )
    kept = (1.0 - weight[0], 1.0 - weight[1])
    of_cotangent = weight[1] + weight[0] * kept[1] + kept[0] * kept[1]
    of_second = weight[0] + kept[0]
    pulled = of_cotangent * cotangent + of_second * back_second + back_first
    leaving[...] = jnp.zeros_like(leaving)
    parts = [blocks(part, volumes) for value in (model, pulled) for part in halves(value)]
    for place in range(volumes):
        chunks = [chunk for part in parts for chunk in lane_chunks(part[place])]
        write_rows(leaving, out_ref.shape[1], chunks, place * len(chunks))
    put_messages(out_ref, leaving, to_places)


def hand_kernel(lines, volumes, from_places, sent_ref, maps_ref, *refs):
    outs, (arrived,) = refs[:-1], refs[-1:]
    take_messages(arrived, sent_ref, from_places)
    depth, pitch = sent_ref.shape[:2]
    volume = own_volume(depth)
    count = maps_ref.shape[1] // LANES
    maps = [blocks(part, volumes) for part in halves(maps_ref[...].astype(F32))]
    pulled = [
        [
            read_image(arrived, pitch, (place * 4 + field) * count, count, depth)
            for place in range(volumes)
        ]
        for field in (2, 3)
    ]
    for step, ref in enumerate(outs):
        place = lax.rem(volume + step, jnp.int32(volumes))
        chosen = [jnp.concatenate([pick(a, place), pick(b, place)]) for a, b in zip(maps, pulled)]
        for index, chunk in enumerate(join_complex(*chosen, lines)):
            ref[:, index * LANES : (index + 1) * LANES] = chunk.astype(BF16)


def normal_kernel(
    coils,
    lines,
    volumes,
    from_places,
    to_places,
    sent_ref,
    maps_ref,
    mask_ref,
    table_ref,
    minus_ref,
    plus_ref,
    out_ref,
    arrived,
    leaving,
):
    take_messages(arrived, sent_ref, from_places)
    depth, pitch = sent_ref.shape[:2]
    volume = own_volume(depth)
    count = maps_ref.shape[1] // LANES
    fields = [
        [
            read_image(arrived, pitch, (place * 4 + field) * count, count, depth)
            for place in range(volumes)
        ]
        for field in range(2)
    ]
    reals, imags = fields
    maps_real, maps_imag = halves(maps_ref[...].astype(F32))
    mask = over_coils(pick(blocks(read_mask(mask_ref, table_ref.shape[0]), volumes), volume), 2 * volumes * coils)
    images = spread(maps_real, maps_imag, over_rows(reals, coils), over_rows(imags, coils))
    images = masked_normal(images, table_ref, minus_ref, plus_ref, mask)
    found = [row_sums(value, volumes, coils) for value in collect(maps_real, maps_imag, images)]
    leaving[...] = jnp.zeros_like(leaving)
    for place in range(volumes):
        chunks = join_complex(found[0][place], found[1][place], lines)
        write_rows(leaving, leaving.shape[0] // depth, chunks, place * len(chunks))
    put_messages(out_ref, leaving, to_places)


def from_volumes(refs, volume, parts, volumes):
    sources = [blocks(ref, parts) for ref in refs]
    ordered = []
    for place in range(volumes):
        step = lax.rem(volume - place + volumes, jnp.int32(volumes))
        ordered.append([pick([source[part] for source in sources], step) for part in range(parts)])
    return ordered


def grad_kernel(
    coils,
    lines,
    volumes,
    mask_ref,
    table_ref,
    minus_ref,
    *refs,
):
    handed, (grad_ref,) = refs[:volumes], refs[volumes:]
    depth = mask_ref.shape[0] // volumes
    volume = own_volume(depth)
    handed = [split_complex(lane_chunks(ref[...].astype(F32)), lines) for ref in handed]
    handed = [jnp.concatenate(parts, axis=0) for parts in handed]
    found = from_volumes(handed, volume, 2 * (coils + 1), volumes)
    maps, pulled = [], []
    for first in (0, coils + 1):
        parts = [found[v][first + coil] for coil in range(coils) for v in range(volumes)]
        maps.append(jnp.concatenate(parts, axis=0))
        pulled.append(jnp.concatenate([found[v][first + coils] for v in range(volumes)], axis=0))
    real, imag = pulled
    images = spread(*maps, over_coils(real, coils), over_coils(imag, coils))
    spectrum = depth_apply(line_apply(images, table_ref, -1.0), minus_ref)
    spectrum = spectrum * over_coils(read_mask(mask_ref, table_ref.shape[0]), 2 * coils)
    chunks = join_complex(*halves(spectrum), lines)
    write_rows(grad_ref, len(chunks), chunks)


def picture_kernel(lines, volumes, from_places, columns_ref, sent_ref, image_ref, picture_ref, arrived):
    depth = len(from_places)
    pitch = arrived.shape[0] // depth
    count = 2 * lines // LANES
    take_messages(arrived, sent_ref, from_places)
    parts = [[], []]
    for place in range(volumes):
        chunks = read_rows(arrived, pitch, place * count, count, depth)
        for part, value in zip(parts, split_complex(chunks, lines)):
            part.append(value)
    picture = image_ref[...]
    scale = column(columns_ref, CASCADES + 1, picture.shape[0])
    picture = picture - scale * jnp.concatenate(parts[0] + parts[1], axis=0)
    for index, chunk in enumerate(join_complex(*halves(picture), lines)):
        picture_ref[:, index * LANES : (index + 1) * LANES] = chunk


def end_kernel(
    coils,
    lines,
    volumes,
    from_places,
    columns_ref,
    sent_ref,
    image_ref,
    mask_ref,
    table_ref,
    minus_ref,
    *refs,
):
    handed, (picture_ref, grad_ref, arrived) = refs[:volumes], refs[volumes:]
    grad_kernel(coils, lines, volumes, mask_ref, table_ref, minus_ref, *handed, grad_ref)
    picture_kernel(
        lines, volumes, from_places, columns_ref, sent_ref, image_ref, picture_ref, arrived
    )


def call(kernel, name, operands, outs, scratch, flops, vmem_bytes=VMEM_BYTES, scalars=0):
    spaces = [pltpu.SMEM] * scalars + [pltpu.VMEM] * (len(operands) - scalars)
    moved = sum(math.prod(item.shape) * item.dtype.itemsize for item in (*operands, *outs))
    return pl.pallas_call(
        kernel,
        name=name,
        out_shape=tuple(outs),
        in_specs=[pl.BlockSpec(memory_space=space) for space in spaces],
        out_specs=tuple(pl.BlockSpec(memory_space=pltpu.VMEM) for item in outs),
        scratch_shapes=[pltpu.VMEM(shape, F32) for shape in scratch],
        compiler_params=pltpu.CompilerParams(vmem_limit_bytes=vmem_bytes),
        cost_estimate=pl.CostEstimate(flops=flops, bytes_accessed=moved, transcendentals=0),
    )(*operands)


def body(
    kspace, coil_maps, sampling, dc_weight, kernel_in, bias_in, kernel_out, bias_out, cotangent
):
    coils, slots = kspace.shape[:2]
    rows, two_lines = coil_maps.shape[2:]
    lines = two_lines // 2
    channels = bias_in.shape[1]
    coil_devices, sections = lax.axis_size("coil"), lax.axis_size("section")
    volumes = VOLUMES
    depth = slots // volumes
    width = padded(lines, LANES)
    count, whole_count = width // LANES, two_lines // LANES
    planes = coils * slots
    both = ("section", "coil")
    span = depth * coil_devices
    near_order = [depth - 1] + list(range(depth - 1))
    both_order = list(range(span))[::-1]
    near = [[group * depth + member for member in near_order] for group in range(volumes)]
    near_both = [[group * span + member for member in both_order] for group in range(volumes)]
    near_places = [[near_order.index(member)] for member in range(depth)]
    both_places = [
        [both_order.index(member * coil_devices + coil) for coil in range(coil_devices)]
        for member in range(depth)
    ]

    def from_group(value, step, core=0):
        pairs = [(s, ((s + step * depth) % sections) ^ core) for s in range(sections)]
        return lax.ppermute(value, "section", pairs)

    def between_cores(value):
        return lax.ppermute(value, "section", [(s, s) for s in range(sections)])

    def exchange(value, axes, groups):
        return lax.all_to_all(value, axes, 0, 0, tiled=True, axis_index_groups=groups)

    table = jnp.asarray(line_constant(lines))
    minus = jnp.asarray(depth_constant(coils, slots, volumes, -1.0))
    plus = jnp.asarray(depth_constant(coils, slots, volumes, 1.0))
    near_plus = jnp.asarray(depth_constant(coils, depth, 1, 1.0))
    repeat, place, offset = (jnp.asarray(item) for item in conv_constants(rows, channels))
    mask = sampling.reshape(slots, lines)

    def shape(*dims, kind=F32):
        return jax.ShapeDtypeStruct(dims, kind)

    line_flops = 2 * (2 * planes) * width * (2 * width)

    maps_lines = volumes * (coils + 1) * whole_count
    pitch = padded(maps_lines, 8)
    packed, *samples = call(
        functools.partial(pack_kernel, coils, volumes, pitch, near_places),
        "pack_maps",
        (
            kspace.reshape(planes, two_lines),
            coil_maps.reshape(coils * rows, two_lines),
            cotangent.reshape(rows, two_lines),
        ),
        [shape(depth, maps_lines, LANES, kind=BF16)]
        + [shape(coils * depth, two_lines, kind=BF16)] * (volumes - 1),
        [(depth * pitch, LANES)],
        1000,
        LARGE_VMEM_BYTES,
    )
    samples = [from_group(value, step) for step, value in enumerate(samples, 1)]
    tall, wide = channels * rows, offset.shape[1]
    first, first_t, second, second_t, columns = call(
        functools.partial(taps_kernel, rows),
        "lay_out_taps",
        (
            dc_weight,
            kernel_in.transpose(0, 1, 3, 2).reshape(-1, 2, channels),
            kernel_out.reshape(-1, 2, channels),
            bias_in,
            bias_out,
            repeat,
            place,
            offset,
        ),
        [
            shape(CASCADES, tall, wide, kind=BF16),
            shape(CASCADES, 6 * rows, tall, kind=BF16),
            shape(CASCADES, 6 * rows, tall, kind=BF16),
            shape(CASCADES, tall, wide, kind=BF16),
            shape(tall, place.shape[0]),
        ],
        [(place.shape[0], repeat.shape[1])],
        2 * tall * place.shape[0] * place.shape[1],
        scalars=1,
    )
    *samples, columns = lax.optimization_barrier((*samples, columns))
    (own,) = call(
        functools.partial(own_kernel, coils, lines, volumes),
        "own_images",
        (kspace.reshape(planes, two_lines), mask, table, near_plus),
        [shape(2 * coils * depth, width)],
        [],
        line_flops,
    )
    images = [own]
    for value in samples:
        (image,) = call(
            functools.partial(far_kernel, coils, lines, volumes),
            "far_images",
            (value, mask, table, near_plus),
            [shape(FAR_PARTS * coils * depth, width)],
            [],
            line_flops,
        )
        images.append(between_cores(image))
    arrived = exchange(packed, "section", near)

    sums_lines = volumes * 5 * count
    depth_pitch = padded(sums_lines, 8)
    partial, maps = call(
        functools.partial(rows_kernel, coils, lines, volumes, near_places, both_places),
        "combine_rows",
        (arrived, mask, table, minus, plus, *images),
        [
            shape(span, sums_lines, LANES, kind=BF16),
            shape(2 * planes, width, kind=BF16),
        ],
        [(depth * pitch, LANES), (depth * depth_pitch, LANES)],
        4 * line_flops,
    )

    partial = exchange(partial, both, near_both)

    model_pitch = padded(volumes * 4 * count, 8)
    moved, image = call(
        functools.partial(refine_kernel, lines, volumes, both_places, near_places),
        "refine_and_back",
        (
            partial,
            cotangent.reshape(rows, two_lines),
            first,
            first_t,
            second,
            second_t,
            columns,
        ),
        [shape(depth, model_pitch, LANES, kind=BF16), shape(2 * rows, width)],
        [(depth * depth_pitch, LANES), (depth * model_pitch, LANES)],
        14 * tall * wide * width,
    )
    moved = exchange(moved, "section", near)

    end_lines = volumes * whole_count
    end_pitch = padded(end_lines, 16)
    handed = call(
        functools.partial(hand_kernel, lines, volumes, near_places),
        "hand_on",
        (moved, maps),
        [shape((coils + 1) * depth, two_lines, kind=BF16)] * volumes,
        [(depth * model_pitch, LANES)],
        1000,
    )
    handed = list(handed)
    (partial,) = call(
        functools.partial(normal_kernel, coils, lines, volumes, near_places, both_places),
        "masked_normal",
        (moved, maps, mask, table, minus, plus),
        [shape(span, end_lines, LANES, kind=BF16)],
        [(depth * model_pitch, LANES), (depth * end_pitch, LANES)],
        3 * line_flops,
    )
    partial = exchange(partial, both, near_both)
    handed[1:] = [
        from_group(value, step) for step, value in enumerate(handed[1:], 1)
    ]

    image, grad = call(
        functools.partial(end_kernel, coils, lines, volumes, both_places),
        "outputs",
        (columns, partial, image, mask, table, minus, *handed),
        [shape(rows, two_lines), shape(planes * whole_count, LANES)],
        [(depth * end_pitch, LANES)],
        2 * line_flops,
    )
    return image.reshape(1, rows, two_lines), grad.reshape(coils, slots, 1, two_lines)


def solution(mesh):
    return jax.shard_map(
        body,
        mesh=mesh,
        in_specs=(
            P("coil", None, "section", None),
            P("coil", "section", None, None),
            P(),
            P(),
            P(),
            P(),
            P(),
            P(),
            P("section", None, None),
        ),
        out_specs=(P("section", None, None), P("coil", None, "section", None)),
        check_vma=False,
    )
```

```python
import functools
import math

import jax
import jax.numpy as jnp
import ml_dtypes
import numpy as np
from jax import lax
from jax.experimental import pallas as pl
from jax.experimental.pallas import tpu as pltpu
from jax.sharding import PartitionSpec as P

CASCADES = 2
VOLUMES = 2
LANES = 128
VMEM_BYTES = 48 * 1024 * 1024
FAR_PARTS = 3
LARGE_VMEM_BYTES = 60 * 1024 * 1024

F32 = jnp.float32
BF16 = jnp.bfloat16


def padded(size, unit):
    return -(-size // unit) * unit


def dft_parts(count):
    indices = np.arange(count)
    angles = (indices[:, None] * indices[None, :] % count) * (2.0 * math.pi / count)
    factor = 1.0 / math.sqrt(count)
    return np.cos(angles) * factor, np.sin(angles) * factor


def line_constant(lines):
    width = padded(lines, LANES)
    cosine, sine = dft_parts(lines)
    table = np.zeros((width, 2 * width), np.float32)
    table[:lines, :lines] = cosine
    table[:lines, width : width + lines] = sine
    return table.astype(ml_dtypes.bfloat16)


def depth_constant(coils, slots, volumes, sign):
    cosine, sine = dft_parts(slots // volumes)
    spread_over = np.eye(coils * volumes)
    real, imag = np.kron(spread_over, cosine), sign * np.kron(spread_over, sine)
    return np.block([[real, -imag], [imag, real]]).astype(np.float32).astype(ml_dtypes.bfloat16)


def conv_constants(rows, channels):
    groups = 6
    width = padded(groups * rows, LANES)
    repeat = np.kron(np.eye(channels), np.ones((rows, 1))).astype(np.float32)
    repeat = np.pad(repeat, ((0, 0), (0, padded(channels, LANES) - channels)))
    taps = CASCADES * 3
    place = np.zeros((padded(2 * taps * groups + 3 * CASCADES, LANES), 2 * taps * width), np.float32)
    for kind in range(2):
        for tap in range(taps):
            for group in range(groups):
                start = (kind * taps + tap) * width + group * rows
                place[(kind * taps + tap) * groups + group, start : start + rows] = 1.0
    offset = np.full((channels * rows, width), -9.0, np.float32)
    row = np.arange(rows)
    offset[:, : groups * rows] = np.tile(row[None, :] - row[:, None] + 1.0, (channels, groups))
    offset = np.clip(offset, -9.0, 9.0)
    return repeat, place.astype(ml_dtypes.bfloat16), offset


def lane_index(shape):
    return lax.broadcasted_iota(jnp.int32, shape, len(shape) - 1)


def split_complex(chunks, lines):
    whole, rest = divmod(lines, LANES)
    count = padded(lines, LANES) // LANES
    if rest == 0:
        return jnp.concatenate(chunks[:count], 1), jnp.concatenate(chunks[count:], 1)
    lane = lane_index(chunks[0].shape)
    real = chunks[:whole] + [jnp.where(lane < rest, chunks[whole], 0.0)]
    turned = [pltpu.roll(chunk, LANES - rest, 1) for chunk in chunks[whole:]]
    turned.append(jnp.zeros_like(turned[0]))
    imag = [jnp.where(lane < LANES - rest, turned[k], turned[k + 1]) for k in range(count)]
    imag[-1] = jnp.where(lane < rest, imag[-1], 0.0)
    return jnp.concatenate(real, 1), jnp.concatenate(imag, 1)


def lane_chunks(value):
    return [value[:, start : start + LANES] for start in range(0, value.shape[1], LANES)]


def join_complex(real, imag, lines):
    whole, rest = divmod(lines, LANES)
    real, imag = lane_chunks(real), lane_chunks(imag)
    if rest == 0:
        return real + imag
    lane = lane_index(real[0].shape)
    turned = [real[whole]] + [pltpu.roll(chunk, rest, 1) for chunk in imag]
    mixed = [jnp.where(lane < rest, turned[k], turned[k + 1]) for k in range(len(imag))]
    return (real[:whole] + mixed)[: 2 * lines // LANES]


def halves(stacked):
    half = stacked.shape[0] // 2
    return stacked[:half], stacked[half:]


def line_apply(stacked, table_ref, sign):
    mixed = jnp.dot(stacked.astype(BF16), table_ref[...], preferred_element_type=F32)
    width = table_ref.shape[1] // 2
    top, bottom = halves(mixed)
    return jnp.concatenate(
        [
            top[:, :width] - sign * bottom[:, width:],
            bottom[:, :width] + sign * top[:, width:],
        ],
        axis=0,
    )


def depth_apply(stacked, depth_ref):
    return jnp.dot(depth_ref[...], stacked.astype(BF16), preferred_element_type=F32)


def over_coils(value, coils):
    return jnp.concatenate([value] * coils, axis=0)


def coil_sum(value, coils):
    slots = value.shape[0] // coils
    total = value[:slots]
    for coil in range(1, coils):
        total = total + value[coil * slots : (coil + 1) * slots]
    return total


def over_rows(parts, coils):
    return jnp.concatenate([part for part in parts for coil in range(coils)], axis=0)


def spread(maps_real, maps_imag, real, imag):
    return jnp.concatenate(
        [maps_real * real - maps_imag * imag, maps_real * imag + maps_imag * real], axis=0
    )


def collect(maps_real, maps_imag, images):
    real, imag = halves(images)
    return maps_real * real + maps_imag * imag, maps_real * imag - maps_imag * real


def blocks(value, count):
    size = value.shape[0] // count
    return [value[index * size : (index + 1) * size] for index in range(count)]


def row_sums(value, rows, coils):
    return [coil_sum(part, coils) for part in blocks(value, rows)]


def pick(parts, index):
    chosen = parts[0]
    for place in range(1, len(parts)):
        chosen = jnp.where(index == place, parts[place], chosen)
    return chosen


def own_volume(depth):
    return lax.div(lax.axis_index("section"), jnp.int32(depth))


def masked_normal(images, table_ref, minus_ref, plus_ref, mask):
    spectrum = depth_apply(line_apply(images, table_ref, -1.0), minus_ref)
    return line_apply(depth_apply(spectrum * mask, plus_ref), table_ref, 1.0)


def write_rows(scratch, pitch, values, first=0):
    for index, value in enumerate(values):
        scratch[pl.ds(first + index, value.shape[0], stride=pitch), :] = value


def read_rows(scratch, pitch, first, count, rows):
    return [scratch[pl.ds(first + index, rows, stride=pitch), :] for index in range(count)]


def put_messages(out_ref, scratch, places):
    pitch = scratch.shape[0] // len(places)
    for member, spots in enumerate(places):
        message = scratch[member * pitch : member * pitch + out_ref.shape[1]].astype(BF16)
        for spot in spots:
            out_ref[spot] = message


def take_messages(scratch, sent_ref, places):
    pitch = scratch.shape[0] // len(places)
    for member, spots in enumerate(places):
        total = sent_ref[spots[0]].astype(F32)
        for spot in spots[1:]:
            total = total + sent_ref[spot].astype(F32)
        scratch[member * pitch : member * pitch + sent_ref.shape[1]] = total


def shifted(value, step):
    if step == 0:
        return value
    width = value.shape[1]
    return pltpu.roll(value, (-step) % width, 1)


def stack_shifted(value, order):
    return jnp.concatenate([shifted(value, step) for step in order], axis=0).astype(BF16)


def add_shifted(value, order, rows):
    total = None
    for index, step in enumerate(order):
        part = shifted(value[index * rows : (index + 1) * rows], step)
        total = part if total is None else total + part
    return total


def hidden_state(image, first_ref, bias_column):
    stack = stack_shifted(image, (-1, 0, 1))
    return (
        jnp.dot(first_ref[:, : stack.shape[0]], stack, preferred_element_type=F32) + bias_column
    )


def second_conv(hidden, second_ref, bias_column, rows, valid):
    mixed = jnp.dot(
        second_ref[...], jnp.where(valid, hidden, 0.0).astype(BF16), preferred_element_type=F32
    )
    total = add_shifted(mixed, (-1, 0, 1), 2 * rows)
    return jnp.where(valid[: 2 * rows], total + bias_column, 0.0)


def pull_back(cotangent, slope, first_t_ref, second_t_ref, rows, valid):
    stack = stack_shifted(cotangent, (1, 0, -1))
    back = jnp.dot(second_t_ref[:, : stack.shape[0]], stack, preferred_element_type=F32)
    back = jnp.where(valid, back * slope, 0.0).astype(BF16)
    mixed = jnp.dot(first_t_ref[...], back, preferred_element_type=F32)
    total = add_shifted(mixed, (1, 0, -1), 2 * rows)
    return jnp.where(valid[: 2 * rows], total, 0.0)


def read_mask(sampling_ref, width):
    mask = sampling_ref[...].astype(F32)
    return jnp.pad(mask, ((0, 0), (0, width - mask.shape[1])))


def valid_lanes(rows, width, lines):
    return lane_index((rows, width)) < lines


def column(columns_ref, place, rows):
    at = 4 * 9 * CASCADES + place
    return columns_ref[:rows, at : at + 1]


def round_bf(value):
    return value.astype(BF16).astype(F32)


def choose_volume(value, coils, volumes, volume):
    parts = blocks(value, coils * volumes)
    chosen = [pick(parts[coil * volumes : (coil + 1) * volumes], volume) for coil in range(coils)]
    return jnp.concatenate(chosen, axis=0)


def pack_kernel(coils, volumes, pitch, places, kspace_ref, maps_ref, image_ref, out_ref, *refs):
    handed, (scratch,) = refs[:-1], refs[-1:]
    rows = image_ref.shape[0]
    depth = rows // volumes
    volume = own_volume(depth)
    kspace = kspace_ref[...].astype(F32)
    for step, ref in enumerate(handed, 1):
        other = lax.rem(volume + step, jnp.int32(volumes))
        ref[...] = choose_volume(kspace, coils, volumes, other).astype(BF16)
    count = maps_ref.shape[1] // LANES
    scratch[...] = jnp.zeros_like(scratch)
    image = image_ref[...].astype(F32)
    for coil in range(coils + 1):
        value = maps_ref[coil * rows : (coil + 1) * rows, :].astype(F32) if coil < coils else image
        for place, part in enumerate(blocks(value, volumes)):
            first = (place * (coils + 1) + coil) * count
            write_rows(scratch, pitch, lane_chunks(part), first)
    put_messages(out_ref, scratch, places)


def taps_kernel(
    rows,
    weight_ref,
    kernel_in_ref,
    kernel_out_ref,
    bias_in_ref,
    bias_out_ref,
    repeat_ref,
    place_ref,
    offset_ref,
    first_ref,
    first_t_ref,
    second_ref,
    second_t_ref,
    columns_ref,
    taps,
):
    taps[...] = jnp.zeros_like(taps)
    channels = kernel_in_ref.shape[2]
    at = 0
    for ref in (kernel_in_ref, kernel_out_ref):
        for index in range(ref.shape[0]):
            taps[at : at + 2, :channels] = ref[index]
            at += 2
    taps[at : at + CASCADES, :channels] = bias_in_ref[...]
    at += CASCADES
    for cascade in range(CASCADES):
        taps[at : at + 1, :] = jnp.full((1, taps.shape[1]), weight_ref[cascade], F32)
        at += 1
    taps[at : at + CASCADES, : bias_out_ref.shape[1]] = bias_out_ref[...]
    tall = lax.dot_general(
        repeat_ref[...],
        taps[...],
        (((1,), (1,)), ((), ())),
        precision=lax.Precision.HIGHEST,
        preferred_element_type=F32,
    )
    columns_ref[...] = tall
    wide = jnp.dot(tall.astype(BF16), place_ref[...], preferred_element_type=F32)
    offset = offset_ref[...]
    width = offset.shape[1]
    for cascade in range(CASCADES):
        for kind, straight, turned in ((0, first_ref, first_t_ref), (1, second_t_ref, second_ref)):
            total = jnp.zeros_like(offset)
            for tap in range(3):
                start = ((kind * CASCADES + cascade) * 3 + tap) * width
                wanted = float(tap if kind == 0 else 2 - tap)
                total = total + jnp.where(offset == wanted, wide[:, start : start + width], 0.0)
            straight[cascade] = total.astype(BF16)
            turned[cascade] = total.T[: 6 * rows].astype(BF16)


def line_images(kspace, mask, lines, table_ref, plus_ref):
    real, imag = split_complex(lane_chunks(kspace), lines)
    measured = jnp.concatenate([real * mask, imag * mask], axis=0)
    return line_apply(depth_apply(measured, plus_ref), table_ref, 1.0)


def far_kernel(coils, lines, volumes, kspace_ref, mask_ref, table_ref, plus_ref, out_ref):
    parts = blocks(read_mask(mask_ref, table_ref.shape[0]), volumes)
    mask = pick(parts, own_volume(parts[0].shape[0]))
    mask = over_coils(mask, coils)
    images = line_images(kspace_ref[...].astype(F32), mask, lines, table_ref, plus_ref)
    out_ref[: images.shape[0]] = images
    if out_ref.shape[0] > images.shape[0]:
        out_ref[images.shape[0] :] = jnp.zeros_like(out_ref[images.shape[0] :])


def rows_kernel(
    coils,
    lines,
    volumes,
    from_places,
    to_places,
    sent_ref,
    kspace_ref,
    mask_ref,
    table_ref,
    minus_ref,
    plus_ref,
    near_ref,
    *refs,
):
    arrival_refs, refs = refs[: volumes - 1], refs[volumes - 1 :]
    out_ref, maps_ref, arrived, leaving = refs
    depth = sent_ref.shape[0]
    pitch = arrived.shape[0] // depth
    volume = own_volume(depth)
    mask = pick(blocks(read_mask(mask_ref, table_ref.shape[0]), volumes), volume)
    mask = over_coils(mask, volumes * coils)

    own = choose_volume(kspace_ref[...].astype(F32), coils, volumes, volume)
    own = line_images(own, mask[: coils * depth], lines, table_ref, near_ref)
    arrivals = [halves(own)] + [halves(ref[: 2 * coils * depth]) for ref in arrival_refs]
    measured = []
    for part in range(2):
        for place in range(volumes):
            step = lax.rem(volume - place + volumes, jnp.int32(volumes))
            measured.append(pick([arrival[part] for arrival in arrivals], step))
    measured = jnp.concatenate(measured, axis=0)

    take_messages(arrived, sent_ref, from_places)
    count = 2 * lines // LANES
    parts, reals, imags = [], [], []
    for place in range(volumes):
        first = place * (coils + 1) * count
        for coil in range(coils):
            chunks = read_rows(arrived, pitch, first + coil * count, count, depth)
            parts.append(split_complex(chunks, lines))
        chunks = read_rows(arrived, pitch, first + coils * count, count, depth)
        real, imag = split_complex(chunks, lines)
        reals.append(real)
        imags.append(imag)
    maps_real = jnp.concatenate([part[0] for part in parts], axis=0)
    maps_imag = jnp.concatenate([part[1] for part in parts], axis=0)
    maps_ref[...] = jnp.concatenate([maps_real, maps_imag], axis=0).astype(BF16)

    images = spread(maps_real, maps_imag, over_rows(reals, coils), over_rows(imags, coils))
    mask = jnp.concatenate([mask, mask], axis=0)
    images = masked_normal(images, table_ref, minus_ref, plus_ref, mask)
    found = [
        *collect(maps_real, maps_imag, round_bf(measured)),
        *collect(maps_real, maps_imag, images),
        maps_real * maps_real + maps_imag * maps_imag,
    ]
    leaving[...] = jnp.zeros_like(leaving)
    sums = [row_sums(value, volumes, coils) for value in found]
    pitch = leaving.shape[0] // depth
    for place in range(volumes):
        chunks = [chunk for value in sums for chunk in lane_chunks(value[place])]
        write_rows(leaving, pitch, chunks, place * len(chunks))
    put_messages(out_ref, leaving, to_places)


def read_image(scratch, pitch, first, count, depth):
    return jnp.concatenate(read_rows(scratch, pitch, first, count, depth), axis=1)


def read_places(scratch, pitch, first, period, count, depth, volumes):
    parts = [
        read_image(scratch, pitch, first + place * period, count, depth) for place in range(volumes)
    ]
    return jnp.concatenate(parts, axis=0)


def read_complex(scratch, pitch, first, period, count, depth, volumes):
    real = read_places(scratch, pitch, first, period, count, depth, volumes)
    imag = read_places(scratch, pitch, first + count, period, count, depth, volumes)
    return jnp.concatenate([real, imag], axis=0)


def refine_kernel(
    lines,
    volumes,
    from_places,
    to_places,
    sent_ref,
    cotangent_ref,
    first_ref,
    first_t_ref,
    second_ref,
    second_t_ref,
    columns_ref,
    out_ref,
    image_ref,
    arrived,
    leaving,
):
    take_messages(arrived, sent_ref, from_places)
    depth = len(from_places)
    pitch = arrived.shape[0] // depth
    rows = depth * volumes
    width = padded(lines, LANES)
    count = width // LANES
    begun = read_complex(arrived, pitch, 0, 5 * count, count, depth, volumes)
    turned = read_complex(arrived, pitch, 2 * count, 5 * count, count, depth, volumes)
    power = read_places(arrived, pitch, 4 * count, 5 * count, count, depth, volumes)
    power = jnp.concatenate([power, power], axis=0)
    cotangent = jnp.concatenate(
        split_complex(lane_chunks(cotangent_ref[...].astype(F32)), lines), axis=0
    )
    tall = first_ref.shape[1]
    weight = [column(columns_ref, CASCADES + cascade, 2 * rows) for cascade in range(CASCADES)]
    bias = [column(columns_ref, 2 * CASCADES + cascade, 2 * rows) for cascade in range(CASCADES)]

    share = [jnp.ones_like(weight[0])]
    for cascade in range(CASCADES):
        share.append(share[cascade] - weight[cascade] * (share[cascade] - 1.0))

    def slopes(hidden):
        gate = jax.nn.sigmoid(hidden)
        return hidden * gate, gate * (1.0 + hidden * (1.0 - gate))

    hidden = hidden_state(round_bf(begun), first_ref.at[0], column(columns_ref, 0, tall))
    valid = valid_lanes(hidden.shape[0], width, lines)
    active, slope_first = slopes(hidden)
    model = round_bf(second_conv(active, second_ref.at[0], bias[0], rows, valid))
    picture = round_bf(share[1] * begun + power * model)
    hidden = hidden_state(picture, first_ref.at[1], column(columns_ref, 1, tall))
    active, slope_second = slopes(hidden)
    later = round_bf(second_conv(active, second_ref.at[1], bias[1], rows, valid))
    image_ref[...] = share[2] * begun + power * (model + later)

    through = power * cotangent
    back_second = round_bf(
        pull_back(through, slope_second, first_t_ref.at[1], second_t_ref.at[1], rows, valid)
    )
    through = through - weight[1] * turned + power * back_second
    back_first = round_bf(
        pull_back(through, slope_first, first_t_ref.at[0], second_t_ref.at[0], rows, valid)
    )
    kept = (1.0 - weight[0], 1.0 - weight[1])
    of_cotangent = weight[1] + weight[0] * kept[1] + kept[0] * kept[1]
    of_second = weight[0] + kept[0]
    pulled = of_cotangent * cotangent + of_second * back_second + back_first
    leaving[...] = jnp.zeros_like(leaving)
    parts = [blocks(part, volumes) for value in (model, pulled) for part in halves(value)]
    for place in range(volumes):
        chunks = [chunk for part in parts for chunk in lane_chunks(part[place])]
        write_rows(leaving, out_ref.shape[1], chunks, place * len(chunks))
    put_messages(out_ref, leaving, to_places)


def hand_kernel(lines, volumes, from_places, sent_ref, maps_ref, *refs):
    outs, (arrived,) = refs[:-1], refs[-1:]
    take_messages(arrived, sent_ref, from_places)
    depth, pitch = sent_ref.shape[:2]
    volume = own_volume(depth)
    count = maps_ref.shape[1] // LANES
    maps = [blocks(part, volumes) for part in halves(maps_ref[...].astype(F32))]
    pulled = [
        [
            read_image(arrived, pitch, (place * 4 + field) * count, count, depth)
            for place in range(volumes)
        ]
        for field in (2, 3)
    ]
    for step, ref in enumerate(outs):
        place = lax.rem(volume + step, jnp.int32(volumes))
        chosen = [jnp.concatenate([pick(a, place), pick(b, place)]) for a, b in zip(maps, pulled)]
        for index, chunk in enumerate(join_complex(*chosen, lines)):
            ref[:, index * LANES : (index + 1) * LANES] = chunk.astype(BF16)


def normal_kernel(
    coils,
    lines,
    volumes,
    from_places,
    to_places,
    sent_ref,
    maps_ref,
    mask_ref,
    table_ref,
    minus_ref,
    plus_ref,
    out_ref,
    arrived,
    leaving,
):
    take_messages(arrived, sent_ref, from_places)
    depth, pitch = sent_ref.shape[:2]
    volume = own_volume(depth)
    count = maps_ref.shape[1] // LANES
    fields = [
        [
            read_image(arrived, pitch, (place * 4 + field) * count, count, depth)
            for place in range(volumes)
        ]
        for field in range(2)
    ]
    reals, imags = fields
    maps_real, maps_imag = halves(maps_ref[...].astype(F32))
    mask = over_coils(pick(blocks(read_mask(mask_ref, table_ref.shape[0]), volumes), volume), 2 * volumes * coils)
    images = spread(maps_real, maps_imag, over_rows(reals, coils), over_rows(imags, coils))
    images = masked_normal(images, table_ref, minus_ref, plus_ref, mask)
    found = [row_sums(value, volumes, coils) for value in collect(maps_real, maps_imag, images)]
    leaving[...] = jnp.zeros_like(leaving)
    for place in range(volumes):
        chunks = join_complex(found[0][place], found[1][place], lines)
        write_rows(leaving, leaving.shape[0] // depth, chunks, place * len(chunks))
    put_messages(out_ref, leaving, to_places)


def from_volumes(refs, volume, parts, volumes):
    sources = [blocks(ref, parts) for ref in refs]
    ordered = []
    for place in range(volumes):
        step = lax.rem(volume - place + volumes, jnp.int32(volumes))
        ordered.append([pick([source[part] for source in sources], step) for part in range(parts)])
    return ordered


def grad_kernel(
    coils,
    lines,
    volumes,
    mask_ref,
    table_ref,
    minus_ref,
    *refs,
):
    handed, (grad_ref,) = refs[:volumes], refs[volumes:]
    depth = mask_ref.shape[0] // volumes
    volume = own_volume(depth)
    handed = [split_complex(lane_chunks(ref[...].astype(F32)), lines) for ref in handed]
    handed = [jnp.concatenate(parts, axis=0) for parts in handed]
    found = from_volumes(handed, volume, 2 * (coils + 1), volumes)
    maps, pulled = [], []
    for first in (0, coils + 1):
        parts = [found[v][first + coil] for coil in range(coils) for v in range(volumes)]
        maps.append(jnp.concatenate(parts, axis=0))
        pulled.append(jnp.concatenate([found[v][first + coils] for v in range(volumes)], axis=0))
    real, imag = pulled
    images = spread(*maps, over_coils(real, coils), over_coils(imag, coils))
    spectrum = depth_apply(line_apply(images, table_ref, -1.0), minus_ref)
    spectrum = spectrum * over_coils(read_mask(mask_ref, table_ref.shape[0]), 2 * coils)
    chunks = join_complex(*halves(spectrum), lines)
    write_rows(grad_ref, len(chunks), chunks)


def picture_kernel(lines, volumes, from_places, columns_ref, sent_ref, image_ref, picture_ref, arrived):
    depth = len(from_places)
    pitch = arrived.shape[0] // depth
    count = 2 * lines // LANES
    take_messages(arrived, sent_ref, from_places)
    parts = [[], []]
    for place in range(volumes):
        chunks = read_rows(arrived, pitch, place * count, count, depth)
        for part, value in zip(parts, split_complex(chunks, lines)):
            part.append(value)
    picture = image_ref[...]
    scale = column(columns_ref, CASCADES + 1, picture.shape[0])
    picture = picture - scale * jnp.concatenate(parts[0] + parts[1], axis=0)
    for index, chunk in enumerate(join_complex(*halves(picture), lines)):
        picture_ref[:, index * LANES : (index + 1) * LANES] = chunk


def end_kernel(
    coils,
    lines,
    volumes,
    from_places,
    columns_ref,
    sent_ref,
    image_ref,
    mask_ref,
    table_ref,
    minus_ref,
    *refs,
):
    handed, (picture_ref, grad_ref, arrived) = refs[:volumes], refs[volumes:]
    grad_kernel(coils, lines, volumes, mask_ref, table_ref, minus_ref, *handed, grad_ref)
    picture_kernel(
        lines, volumes, from_places, columns_ref, sent_ref, image_ref, picture_ref, arrived
    )


def call(kernel, name, operands, outs, scratch, flops, vmem_bytes=VMEM_BYTES, scalars=0):
    spaces = [pltpu.SMEM] * scalars + [pltpu.VMEM] * (len(operands) - scalars)
    moved = sum(math.prod(item.shape) * item.dtype.itemsize for item in (*operands, *outs))
    return pl.pallas_call(
        kernel,
        name=name,
        out_shape=tuple(outs),
        in_specs=[pl.BlockSpec(memory_space=space) for space in spaces],
        out_specs=tuple(pl.BlockSpec(memory_space=pltpu.VMEM) for item in outs),
        scratch_shapes=[pltpu.VMEM(shape, F32) for shape in scratch],
        compiler_params=pltpu.CompilerParams(vmem_limit_bytes=vmem_bytes),
        cost_estimate=pl.CostEstimate(flops=flops, bytes_accessed=moved, transcendentals=0),
    )(*operands)


def body(
    kspace, coil_maps, sampling, dc_weight, kernel_in, bias_in, kernel_out, bias_out, cotangent
):
    coils, slots = kspace.shape[:2]
    rows, two_lines = coil_maps.shape[2:]
    lines = two_lines // 2
    channels = bias_in.shape[1]
    coil_devices, sections = lax.axis_size("coil"), lax.axis_size("section")
    volumes = VOLUMES
    depth = slots // volumes
    width = padded(lines, LANES)
    count, whole_count = width // LANES, two_lines // LANES
    planes = coils * slots
    both = ("section", "coil")
    span = depth * coil_devices
    near_order = [depth - 1] + list(range(depth - 1))
    both_order = list(range(span))[::-1]
    near = [[group * depth + member for member in near_order] for group in range(volumes)]
    near_both = [[group * span + member for member in both_order] for group in range(volumes)]
    near_places = [[near_order.index(member)] for member in range(depth)]
    both_places = [
        [both_order.index(member * coil_devices + coil) for coil in range(coil_devices)]
        for member in range(depth)
    ]

    def from_group(value, step, core=0):
        pairs = [(s, ((s + step * depth) % sections) ^ core) for s in range(sections)]
        return lax.ppermute(value, "section", pairs)

    def between_cores(value):
        return lax.ppermute(value, "section", [(s, s) for s in range(sections)])

    def exchange(value, axes, groups):
        return lax.all_to_all(value, axes, 0, 0, tiled=True, axis_index_groups=groups)

    table = jnp.asarray(line_constant(lines))
    minus = jnp.asarray(depth_constant(coils, slots, volumes, -1.0))
    plus = jnp.asarray(depth_constant(coils, slots, volumes, 1.0))
    near_plus = jnp.asarray(depth_constant(coils, depth, 1, 1.0))
    repeat, place, offset = (jnp.asarray(item) for item in conv_constants(rows, channels))
    mask = sampling.reshape(slots, lines)

    def shape(*dims, kind=F32):
        return jax.ShapeDtypeStruct(dims, kind)

    line_flops = 2 * (2 * planes) * width * (2 * width)

    maps_lines = volumes * (coils + 1) * whole_count
    pitch = padded(maps_lines, 8)
    packed, *samples = call(
        functools.partial(pack_kernel, coils, volumes, pitch, near_places),
        "pack_maps",
        (
            kspace.reshape(planes, two_lines),
            coil_maps.reshape(coils * rows, two_lines),
            cotangent.reshape(rows, two_lines),
        ),
        [shape(depth, maps_lines, LANES, kind=BF16)]
        + [shape(coils * depth, two_lines, kind=BF16)] * (volumes - 1),
        [(depth * pitch, LANES)],
        1000,
        LARGE_VMEM_BYTES,
    )
    samples = [from_group(value, step) for step, value in enumerate(samples, 1)]
    tall, wide = channels * rows, offset.shape[1]
    first, first_t, second, second_t, columns = call(
        functools.partial(taps_kernel, rows),
        "lay_out_taps",
        (
            dc_weight,
            kernel_in.transpose(0, 1, 3, 2).reshape(-1, 2, channels),
            kernel_out.reshape(-1, 2, channels),
            bias_in,
            bias_out,
            repeat,
            place,
            offset,
        ),
        [
            shape(CASCADES, tall, wide, kind=BF16),
            shape(CASCADES, 6 * rows, tall, kind=BF16),
            shape(CASCADES, 6 * rows, tall, kind=BF16),
            shape(CASCADES, tall, wide, kind=BF16),
            shape(tall, place.shape[0]),
        ],
        [(place.shape[0], repeat.shape[1])],
        2 * tall * place.shape[0] * place.shape[1],
        scalars=1,
    )
    *samples, columns = lax.optimization_barrier((*samples, columns))
    images = []
    for value in samples:
        (image,) = call(
            functools.partial(far_kernel, coils, lines, volumes),
            "far_images",
            (value, mask, table, near_plus),
            [shape(FAR_PARTS * coils * depth, width)],
            [],
            line_flops,
        )
        images.append(between_cores(image))
    arrived = exchange(packed, "section", near)

    sums_lines = volumes * 5 * count
    depth_pitch = padded(sums_lines, 8)
    partial, maps = call(
        functools.partial(rows_kernel, coils, lines, volumes, near_places, both_places),
        "combine_rows",
        (arrived, kspace.reshape(planes, two_lines), mask, table, minus, plus, near_plus, *images),
        [
            shape(span, sums_lines, LANES, kind=BF16),
            shape(2 * planes, width, kind=BF16),
        ],
        [(depth * pitch, LANES), (depth * depth_pitch, LANES)],
        4 * line_flops,
    )

    partial = exchange(partial, both, near_both)

    model_pitch = padded(volumes * 4 * count, 8)
    moved, image = call(
        functools.partial(refine_kernel, lines, volumes, both_places, near_places),
        "refine_and_back",
        (
            partial,
            cotangent.reshape(rows, two_lines),
            first,
            first_t,
            second,
            second_t,
            columns,
        ),
        [shape(depth, model_pitch, LANES, kind=BF16), shape(2 * rows, width)],
        [(depth * depth_pitch, LANES), (depth * model_pitch, LANES)],
        14 * tall * wide * width,
    )
    moved = exchange(moved, "section", near)

    end_lines = volumes * whole_count
    end_pitch = padded(end_lines, 16)
    handed = call(
        functools.partial(hand_kernel, lines, volumes, near_places),
        "hand_on",
        (moved, maps),
        [shape((coils + 1) * depth, two_lines, kind=BF16)] * volumes,
        [(depth * model_pitch, LANES)],
        1000,
    )
    handed = list(handed)
    (partial,) = call(
        functools.partial(normal_kernel, coils, lines, volumes, near_places, both_places),
        "masked_normal",
        (moved, maps, mask, table, minus, plus),
        [shape(span, end_lines, LANES, kind=BF16)],
        [(depth * model_pitch, LANES), (depth * end_pitch, LANES)],
        3 * line_flops,
    )
    partial = exchange(partial, both, near_both)
    handed[1:] = [
        from_group(value, step) for step, value in enumerate(handed[1:], 1)
    ]

    image, grad = call(
        functools.partial(end_kernel, coils, lines, volumes, both_places),
        "outputs",
        (columns, partial, image, mask, table, minus, *handed),
        [shape(rows, two_lines), shape(planes * whole_count, LANES)],
        [(depth * end_pitch, LANES)],
        2 * line_flops,
    )
    return image.reshape(1, rows, two_lines), grad.reshape(coils, slots, 1, two_lines)


def solution(mesh):
    return jax.shard_map(
        body,
        mesh=mesh,
        in_specs=(
            P("coil", None, "section", None),
            P("coil", "section", None, None),
            P(),
            P(),
            P(),
            P(),
            P(),
            P(),
            P("section", None, None),
        ),
        out_specs=(P("section", None, None), P("coil", None, "section", None)),
        check_vma=False,
    )
```

```python
import functools
import math

import jax
import jax.numpy as jnp
import ml_dtypes
import numpy as np
from jax import lax
from jax.experimental import pallas as pl
from jax.experimental.pallas import tpu as pltpu
from jax.sharding import PartitionSpec as P

CASCADES = 2
VOLUMES = 2
LANES = 128
VMEM_BYTES = 48 * 1024 * 1024
FAR_PARTS = 3
LARGE_VMEM_BYTES = 60 * 1024 * 1024

F32 = jnp.float32
BF16 = jnp.bfloat16


def padded(size, unit):
    return -(-size // unit) * unit


def dft_parts(count):
    indices = np.arange(count)
    angles = (indices[:, None] * indices[None, :] % count) * (2.0 * math.pi / count)
    factor = 1.0 / math.sqrt(count)
    return np.cos(angles) * factor, np.sin(angles) * factor


def line_constant(lines):
    width = padded(lines, LANES)
    cosine, sine = dft_parts(lines)
    table = np.zeros((width, 2 * width), np.float32)
    table[:lines, :lines] = cosine
    table[:lines, width : width + lines] = sine
    return table.astype(ml_dtypes.bfloat16)


def depth_constant(coils, slots, volumes, sign):
    cosine, sine = dft_parts(slots // volumes)
    spread_over = np.eye(coils * volumes)
    real, imag = np.kron(spread_over, cosine), sign * np.kron(spread_over, sine)
    return np.block([[real, -imag], [imag, real]]).astype(np.float32).astype(ml_dtypes.bfloat16)


def conv_constants(rows, channels):
    groups = 6
    width = padded(groups * rows, LANES)
    repeat = np.kron(np.eye(channels), np.ones((rows, 1))).astype(np.float32)
    repeat = np.pad(repeat, ((0, 0), (0, padded(channels, LANES) - channels)))
    taps = CASCADES * 3
    place = np.zeros((padded(2 * taps * groups + 3 * CASCADES, LANES), 2 * taps * width), np.float32)
    for kind in range(2):
        for tap in range(taps):
            for group in range(groups):
                start = (kind * taps + tap) * width + group * rows
                place[(kind * taps + tap) * groups + group, start : start + rows] = 1.0
    offset = np.full((channels * rows, width), -9.0, np.float32)
    row = np.arange(rows)
    offset[:, : groups * rows] = np.tile(row[None, :] - row[:, None] + 1.0, (channels, groups))
    offset = np.clip(offset, -9.0, 9.0)
    return repeat, place.astype(ml_dtypes.bfloat16), offset


def lane_index(shape):
    return lax.broadcasted_iota(jnp.int32, shape, len(shape) - 1)


def split_complex(chunks, lines):
    whole, rest = divmod(lines, LANES)
    count = padded(lines, LANES) // LANES
    if rest == 0:
        return jnp.concatenate(chunks[:count], 1), jnp.concatenate(chunks[count:], 1)
    lane = lane_index(chunks[0].shape)
    real = chunks[:whole] + [jnp.where(lane < rest, chunks[whole], 0.0)]
    turned = [pltpu.roll(chunk, LANES - rest, 1) for chunk in chunks[whole:]]
    turned.append(jnp.zeros_like(turned[0]))
    imag = [jnp.where(lane < LANES - rest, turned[k], turned[k + 1]) for k in range(count)]
    imag[-1] = jnp.where(lane < rest, imag[-1], 0.0)
    return jnp.concatenate(real, 1), jnp.concatenate(imag, 1)


def lane_chunks(value):
    return [value[:, start : start + LANES] for start in range(0, value.shape[1], LANES)]


def join_complex(real, imag, lines):
    whole, rest = divmod(lines, LANES)
    real, imag = lane_chunks(real), lane_chunks(imag)
    if rest == 0:
        return real + imag
    lane = lane_index(real[0].shape)
    turned = [real[whole]] + [pltpu.roll(chunk, rest, 1) for chunk in imag]
    mixed = [jnp.where(lane < rest, turned[k], turned[k + 1]) for k in range(len(imag))]
    return (real[:whole] + mixed)[: 2 * lines // LANES]


def halves(stacked):
    half = stacked.shape[0] // 2
    return stacked[:half], stacked[half:]


def line_apply(stacked, table_ref, sign):
    mixed = jnp.dot(stacked.astype(BF16), table_ref[...], preferred_element_type=F32)
    width = table_ref.shape[1] // 2
    top, bottom = halves(mixed)
    return jnp.concatenate(
        [
            top[:, :width] - sign * bottom[:, width:],
            bottom[:, :width] + sign * top[:, width:],
        ],
        axis=0,
    )


def depth_apply(stacked, depth_ref):
    return jnp.dot(depth_ref[...], stacked.astype(BF16), preferred_element_type=F32)


def over_coils(value, coils):
    return jnp.concatenate([value] * coils, axis=0)


def coil_sum(value, coils):
    slots = value.shape[0] // coils
    total = value[:slots]
    for coil in range(1, coils):
        total = total + value[coil * slots : (coil + 1) * slots]
    return total


def over_rows(parts, coils):
    return jnp.concatenate([part for part in parts for coil in range(coils)], axis=0)


def spread(maps_real, maps_imag, real, imag):
    return jnp.concatenate(
        [maps_real * real - maps_imag * imag, maps_real * imag + maps_imag * real], axis=0
    )


def collect(maps_real, maps_imag, images):
    real, imag = halves(images)
    return maps_real * real + maps_imag * imag, maps_real * imag - maps_imag * real


def blocks(value, count):
    size = value.shape[0] // count
    return [value[index * size : (index + 1) * size] for index in range(count)]


def row_sums(value, rows, coils):
    return [coil_sum(part, coils) for part in blocks(value, rows)]


def pick(parts, index):
    chosen = parts[0]
    for place in range(1, len(parts)):
        chosen = jnp.where(index == place, parts[place], chosen)
    return chosen


def own_volume(depth):
    return lax.div(lax.axis_index("section"), jnp.int32(depth))


def masked_normal(images, table_ref, minus_ref, plus_ref, mask):
    spectrum = depth_apply(line_apply(images, table_ref, -1.0), minus_ref)
    return line_apply(depth_apply(spectrum * mask, plus_ref), table_ref, 1.0)


def write_rows(scratch, pitch, values, first=0):
    for index, value in enumerate(values):
        scratch[pl.ds(first + index, value.shape[0], stride=pitch), :] = value


def read_rows(scratch, pitch, first, count, rows):
    return [scratch[pl.ds(first + index, rows, stride=pitch), :] for index in range(count)]


def put_messages(out_ref, scratch, places):
    pitch = scratch.shape[0] // len(places)
    for member, spots in enumerate(places):
        message = scratch[member * pitch : member * pitch + out_ref.shape[1]].astype(BF16)
        for spot in spots:
            out_ref[spot] = message


def take_messages(scratch, sent_ref, places):
    pitch = scratch.shape[0] // len(places)
    for member, spots in enumerate(places):
        total = sent_ref[spots[0]].astype(F32)
        for spot in spots[1:]:
            total = total + sent_ref[spot].astype(F32)
        scratch[member * pitch : member * pitch + sent_ref.shape[1]] = total


def shifted(value, step):
    if step == 0:
        return value
    width = value.shape[1]
    return pltpu.roll(value, (-step) % width, 1)


def stack_shifted(value, order):
    return jnp.concatenate([shifted(value, step) for step in order], axis=0).astype(BF16)


def add_shifted(value, order, rows):
    total = None
    for index, step in enumerate(order):
        part = shifted(value[index * rows : (index + 1) * rows], step)
        total = part if total is None else total + part
    return total


def hidden_state(image, first_ref, bias_column):
    stack = stack_shifted(image, (-1, 0, 1))
    return (
        jnp.dot(first_ref[:, : stack.shape[0]], stack, preferred_element_type=F32) + bias_column
    )


def second_conv(hidden, second_ref, bias_column, rows, valid):
    mixed = jnp.dot(
        second_ref[...], jnp.where(valid, hidden, 0.0).astype(BF16), preferred_element_type=F32
    )
    total = add_shifted(mixed, (-1, 0, 1), 2 * rows)
    return jnp.where(valid[: 2 * rows], total + bias_column, 0.0)


def pull_back(cotangent, slope, first_t_ref, second_t_ref, rows, valid):
    stack = stack_shifted(cotangent, (1, 0, -1))
    back = jnp.dot(second_t_ref[:, : stack.shape[0]], stack, preferred_element_type=F32)
    back = jnp.where(valid, back * slope, 0.0).astype(BF16)
    mixed = jnp.dot(first_t_ref[...], back, preferred_element_type=F32)
    total = add_shifted(mixed, (1, 0, -1), 2 * rows)
    return jnp.where(valid[: 2 * rows], total, 0.0)


def read_mask(sampling_ref, width):
    mask = sampling_ref[...].astype(F32)
    return jnp.pad(mask, ((0, 0), (0, width - mask.shape[1])))


def valid_lanes(rows, width, lines):
    return lane_index((rows, width)) < lines


def column(columns_ref, place, rows):
    at = 4 * 9 * CASCADES + place
    return columns_ref[:rows, at : at + 1]


def round_bf(value):
    return value.astype(BF16).astype(F32)


def choose_volume(value, coils, volumes, volume):
    parts = blocks(value, coils * volumes)
    chosen = [pick(parts[coil * volumes : (coil + 1) * volumes], volume) for coil in range(coils)]
    return jnp.concatenate(chosen, axis=0)


def pack_kernel(coils, volumes, pitch, places, kspace_ref, maps_ref, image_ref, out_ref, *refs):
    handed, (scratch,) = refs[:-1], refs[-1:]
    rows = image_ref.shape[0]
    depth = rows // volumes
    volume = own_volume(depth)
    kspace = kspace_ref[...].astype(F32)
    for step, ref in enumerate(handed, 1):
        other = lax.rem(volume + step, jnp.int32(volumes))
        ref[...] = choose_volume(kspace, coils, volumes, other).astype(BF16)
    count = maps_ref.shape[1] // LANES
    image = image_ref[...].astype(F32)
    for coil in range(coils + 1):
        value = maps_ref[coil * rows : (coil + 1) * rows, :].astype(F32) if coil < coils else image
        for place, part in enumerate(blocks(value, volumes)):
            first = (place * (coils + 1) + coil) * count
            write_rows(scratch, pitch, lane_chunks(part), first)
    put_messages(out_ref, scratch, places)


def taps_kernel(
    rows,
    weight_ref,
    kernel_in_ref,
    kernel_out_ref,
    bias_in_ref,
    bias_out_ref,
    repeat_ref,
    place_ref,
    offset_ref,
    first_ref,
    first_t_ref,
    second_ref,
    second_t_ref,
    columns_ref,
    taps,
):
    taps[...] = jnp.zeros_like(taps)
    channels = kernel_in_ref.shape[2]
    at = 0
    for ref in (kernel_in_ref, kernel_out_ref):
        for index in range(ref.shape[0]):
            taps[at : at + 2, :channels] = ref[index]
            at += 2
    taps[at : at + CASCADES, :channels] = bias_in_ref[...]
    at += CASCADES
    for cascade in range(CASCADES):
        taps[at : at + 1, :] = jnp.full((1, taps.shape[1]), weight_ref[cascade], F32)
        at += 1
    taps[at : at + CASCADES, : bias_out_ref.shape[1]] = bias_out_ref[...]
    tall = lax.dot_general(
        repeat_ref[...],
        taps[...],
        (((1,), (1,)), ((), ())),
        precision=lax.Precision.HIGHEST,
        preferred_element_type=F32,
    )
    columns_ref[...] = tall
    wide = jnp.dot(tall.astype(BF16), place_ref[...], preferred_element_type=F32)
    offset = offset_ref[...]
    width = offset.shape[1]
    for cascade in range(CASCADES):
        for kind, straight, turned in ((0, first_ref, first_t_ref), (1, second_t_ref, second_ref)):
            total = jnp.zeros_like(offset)
            for tap in range(3):
                start = ((kind * CASCADES + cascade) * 3 + tap) * width
                wanted = float(tap if kind == 0 else 2 - tap)
                total = total + jnp.where(offset == wanted, wide[:, start : start + width], 0.0)
            straight[cascade] = total.astype(BF16)
            turned[cascade] = total.T[: 6 * rows].astype(BF16)


def line_images(kspace, mask, lines, table_ref, plus_ref):
    real, imag = split_complex(lane_chunks(kspace), lines)
    measured = jnp.concatenate([real * mask, imag * mask], axis=0)
    return line_apply(depth_apply(measured, plus_ref), table_ref, 1.0)


def far_kernel(coils, lines, volumes, kspace_ref, mask_ref, table_ref, plus_ref, out_ref):
    parts = blocks(read_mask(mask_ref, table_ref.shape[0]), volumes)
    mask = pick(parts, own_volume(parts[0].shape[0]))
    mask = over_coils(mask, coils)
    images = line_images(kspace_ref[...].astype(F32), mask, lines, table_ref, plus_ref)
    out_ref[: images.shape[0]] = images
    if out_ref.shape[0] > images.shape[0]:
        out_ref[images.shape[0] :] = jnp.zeros_like(out_ref[images.shape[0] :])


def rows_kernel(
    coils,
    lines,
    volumes,
    from_places,
    to_places,
    sent_ref,
    kspace_ref,
    mask_ref,
    table_ref,
    minus_ref,
    plus_ref,
    near_ref,
    *refs,
):
    arrival_refs, refs = refs[: volumes - 1], refs[volumes - 1 :]
    out_ref, maps_ref, arrived, leaving = refs
    depth = sent_ref.shape[0]
    pitch = arrived.shape[0] // depth
    volume = own_volume(depth)
    mask = pick(blocks(read_mask(mask_ref, table_ref.shape[0]), volumes), volume)
    mask = over_coils(mask, volumes * coils)

    own = choose_volume(kspace_ref[...].astype(F32), coils, volumes, volume)
    own = line_images(own, mask[: coils * depth], lines, table_ref, near_ref)
    arrivals = [halves(own)] + [halves(ref[: 2 * coils * depth]) for ref in arrival_refs]
    measured = []
    for part in range(2):
        for place in range(volumes):
            step = lax.rem(volume - place + volumes, jnp.int32(volumes))
            measured.append(pick([arrival[part] for arrival in arrivals], step))
    measured = jnp.concatenate(measured, axis=0)

    take_messages(arrived, sent_ref, from_places)
    count = 2 * lines // LANES
    parts, reals, imags = [], [], []
    for place in range(volumes):
        first = place * (coils + 1) * count
        for coil in range(coils):
            chunks = read_rows(arrived, pitch, first + coil * count, count, depth)
            parts.append(split_complex(chunks, lines))
        chunks = read_rows(arrived, pitch, first + coils * count, count, depth)
        real, imag = split_complex(chunks, lines)
        reals.append(real)
        imags.append(imag)
    maps_real = jnp.concatenate([part[0] for part in parts], axis=0)
    maps_imag = jnp.concatenate([part[1] for part in parts], axis=0)
    maps_ref[...] = jnp.concatenate([maps_real, maps_imag], axis=0).astype(BF16)

    images = spread(maps_real, maps_imag, over_rows(reals, coils), over_rows(imags, coils))
    mask = jnp.concatenate([mask, mask], axis=0)
    images = masked_normal(images, table_ref, minus_ref, plus_ref, mask)
    found = [
        *collect(maps_real, maps_imag, round_bf(measured)),
        *collect(maps_real, maps_imag, images),
        maps_real * maps_real + maps_imag * maps_imag,
    ]
    sums = [row_sums(value, volumes, coils) for value in found]
    pitch = leaving.shape[0] // depth
    for place in range(volumes):
        chunks = [chunk for value in sums for chunk in lane_chunks(value[place])]
        write_rows(leaving, pitch, chunks, place * len(chunks))
    put_messages(out_ref, leaving, to_places)


def read_image(scratch, pitch, first, count, depth):
    return jnp.concatenate(read_rows(scratch, pitch, first, count, depth), axis=1)


def read_places(scratch, pitch, first, period, count, depth, volumes):
    parts = [
        read_image(scratch, pitch, first + place * period, count, depth) for place in range(volumes)
    ]
    return jnp.concatenate(parts, axis=0)


def read_complex(scratch, pitch, first, period, count, depth, volumes):
    real = read_places(scratch, pitch, first, period, count, depth, volumes)
    imag = read_places(scratch, pitch, first + count, period, count, depth, volumes)
    return jnp.concatenate([real, imag], axis=0)


def refine_kernel(
    lines,
    volumes,
    from_places,
    to_places,
    sent_ref,
    cotangent_ref,
    first_ref,
    first_t_ref,
    second_ref,
    second_t_ref,
    columns_ref,
    out_ref,
    image_ref,
    arrived,
    leaving,
):
    take_messages(arrived, sent_ref, from_places)
    depth = len(from_places)
    pitch = arrived.shape[0] // depth
    rows = depth * volumes
    width = padded(lines, LANES)
    count = width // LANES
    begun = read_complex(arrived, pitch, 0, 5 * count, count, depth, volumes)
    turned = read_complex(arrived, pitch, 2 * count, 5 * count, count, depth, volumes)
    power = read_places(arrived, pitch, 4 * count, 5 * count, count, depth, volumes)
    power = jnp.concatenate([power, power], axis=0)
    cotangent = jnp.concatenate(
        split_complex(lane_chunks(cotangent_ref[...].astype(F32)), lines), axis=0
    )
    tall = first_ref.shape[1]
    weight = [column(columns_ref, CASCADES + cascade, 2 * rows) for cascade in range(CASCADES)]
    bias = [column(columns_ref, 2 * CASCADES + cascade, 2 * rows) for cascade in range(CASCADES)]

    share = [jnp.ones_like(weight[0])]
    for cascade in range(CASCADES):
        share.append(share[cascade] - weight[cascade] * (share[cascade] - 1.0))

    def slopes(hidden):
        gate = jax.nn.sigmoid(hidden)
        return hidden * gate, gate * (1.0 + hidden * (1.0 - gate))

    hidden = hidden_state(round_bf(begun), first_ref.at[0], column(columns_ref, 0, tall))
    valid = valid_lanes(hidden.shape[0], width, lines)
    active, slope_first = slopes(hidden)
    model = round_bf(second_conv(active, second_ref.at[0], bias[0], rows, valid))
    picture = round_bf(share[1] * begun + power * model)
    hidden = hidden_state(picture, first_ref.at[1], column(columns_ref, 1, tall))
    active, slope_second = slopes(hidden)
    later = round_bf(second_conv(active, second_ref.at[1], bias[1], rows, valid))
    image_ref[...] = share[2] * begun + power * (model + later)

    through = power * cotangent
    back_second = round_bf(
        pull_back(through, slope_second, first_t_ref.at[1], second_t_ref.at[1], rows, valid)
    )
    through = through - weight[1] * turned + power * back_second
    back_first = round_bf(
        pull_back(through, slope_first, first_t_ref.at[0], second_t_ref.at[0], rows, valid)
    )
    kept = (1.0 - weight[0], 1.0 - weight[1])
    of_cotangent = weight[1] + weight[0] * kept[1] + kept[0] * kept[1]
    of_second = weight[0] + kept[0]
    pulled = of_cotangent * cotangent + of_second * back_second + back_first
    parts = [blocks(part, volumes) for value in (model, pulled) for part in halves(value)]
    for place in range(volumes):
        chunks = [chunk for part in parts for chunk in lane_chunks(part[place])]
        write_rows(leaving, out_ref.shape[1], chunks, place * len(chunks))
    put_messages(out_ref, leaving, to_places)


def hand_kernel(lines, volumes, from_places, sent_ref, maps_ref, *refs):
    outs, (arrived,) = refs[:-1], refs[-1:]
    take_messages(arrived, sent_ref, from_places)
    depth = sent_ref.shape[0]
    pitch = arrived.shape[0] // depth
    volume = own_volume(depth)
    count = maps_ref.shape[1] // LANES
    maps = [blocks(part, volumes) for part in halves(maps_ref[...].astype(F32))]
    pulled = [
        [
            read_image(arrived, pitch, (place * 4 + field) * count, count, depth)
            for place in range(volumes)
        ]
        for field in (2, 3)
    ]
    for step, ref in enumerate(outs):
        place = lax.rem(volume + step, jnp.int32(volumes))
        chosen = [jnp.concatenate([pick(a, place), pick(b, place)]) for a, b in zip(maps, pulled)]
        for index, chunk in enumerate(join_complex(*chosen, lines)):
            ref[:, index * LANES : (index + 1) * LANES] = chunk.astype(BF16)


def normal_kernel(
    coils,
    lines,
    volumes,
    from_places,
    to_places,
    sent_ref,
    maps_ref,
    mask_ref,
    table_ref,
    minus_ref,
    plus_ref,
    out_ref,
    arrived,
    leaving,
):
    take_messages(arrived, sent_ref, from_places)
    depth = sent_ref.shape[0]
    pitch = arrived.shape[0] // depth
    volume = own_volume(depth)
    count = maps_ref.shape[1] // LANES
    fields = [
        [
            read_image(arrived, pitch, (place * 4 + field) * count, count, depth)
            for place in range(volumes)
        ]
        for field in range(2)
    ]
    reals, imags = fields
    maps_real, maps_imag = halves(maps_ref[...].astype(F32))
    mask = over_coils(pick(blocks(read_mask(mask_ref, table_ref.shape[0]), volumes), volume), 2 * volumes * coils)
    images = spread(maps_real, maps_imag, over_rows(reals, coils), over_rows(imags, coils))
    images = masked_normal(images, table_ref, minus_ref, plus_ref, mask)
    found = [row_sums(value, volumes, coils) for value in collect(maps_real, maps_imag, images)]
    for place in range(volumes):
        chunks = join_complex(found[0][place], found[1][place], lines)
        write_rows(leaving, leaving.shape[0] // depth, chunks, place * len(chunks))
    put_messages(out_ref, leaving, to_places)


def from_volumes(refs, volume, parts, volumes):
    sources = [blocks(ref, parts) for ref in refs]
    ordered = []
    for place in range(volumes):
        step = lax.rem(volume - place + volumes, jnp.int32(volumes))
        ordered.append([pick([source[part] for source in sources], step) for part in range(parts)])
    return ordered


def grad_kernel(
    coils,
    lines,
    volumes,
    mask_ref,
    table_ref,
    minus_ref,
    *refs,
):
    handed, (grad_ref,) = refs[:volumes], refs[volumes:]
    depth = mask_ref.shape[0] // volumes
    volume = own_volume(depth)
    handed = [split_complex(lane_chunks(ref[...].astype(F32)), lines) for ref in handed]
    handed = [jnp.concatenate(parts, axis=0) for parts in handed]
    found = from_volumes(handed, volume, 2 * (coils + 1), volumes)
    maps, pulled = [], []
    for first in (0, coils + 1):
        parts = [found[v][first + coil] for coil in range(coils) for v in range(volumes)]
        maps.append(jnp.concatenate(parts, axis=0))
        pulled.append(jnp.concatenate([found[v][first + coils] for v in range(volumes)], axis=0))
    real, imag = pulled
    images = spread(*maps, over_coils(real, coils), over_coils(imag, coils))
    spectrum = depth_apply(line_apply(images, table_ref, -1.0), minus_ref)
    spectrum = spectrum * over_coils(read_mask(mask_ref, table_ref.shape[0]), 2 * coils)
    chunks = join_complex(*halves(spectrum), lines)
    write_rows(grad_ref, len(chunks), chunks)


def picture_kernel(lines, volumes, from_places, columns_ref, sent_ref, image_ref, picture_ref, arrived):
    depth = len(from_places)
    pitch = arrived.shape[0] // depth
    count = 2 * lines // LANES
    take_messages(arrived, sent_ref, from_places)
    parts = [[], []]
    for place in range(volumes):
        chunks = read_rows(arrived, pitch, place * count, count, depth)
        for part, value in zip(parts, split_complex(chunks, lines)):
            part.append(value)
    picture = image_ref[...]
    scale = column(columns_ref, CASCADES + 1, picture.shape[0])
    picture = picture - scale * jnp.concatenate(parts[0] + parts[1], axis=0)
    for index, chunk in enumerate(join_complex(*halves(picture), lines)):
        picture_ref[:, index * LANES : (index + 1) * LANES] = chunk


def end_kernel(
    coils,
    lines,
    volumes,
    from_places,
    columns_ref,
    sent_ref,
    image_ref,
    mask_ref,
    table_ref,
    minus_ref,
    *refs,
):
    handed, (picture_ref, grad_ref, arrived) = refs[:volumes], refs[volumes:]
    grad_kernel(coils, lines, volumes, mask_ref, table_ref, minus_ref, *handed, grad_ref)
    picture_kernel(
        lines, volumes, from_places, columns_ref, sent_ref, image_ref, picture_ref, arrived
    )


def call(kernel, name, operands, outs, scratch, flops, vmem_bytes=VMEM_BYTES, scalars=0):
    spaces = [pltpu.SMEM] * scalars + [pltpu.VMEM] * (len(operands) - scalars)
    moved = sum(math.prod(item.shape) * item.dtype.itemsize for item in (*operands, *outs))
    return pl.pallas_call(
        kernel,
        name=name,
        out_shape=tuple(outs),
        in_specs=[pl.BlockSpec(memory_space=space) for space in spaces],
        out_specs=tuple(pl.BlockSpec(memory_space=pltpu.VMEM) for item in outs),
        scratch_shapes=[pltpu.VMEM(shape, F32) for shape in scratch],
        compiler_params=pltpu.CompilerParams(vmem_limit_bytes=vmem_bytes),
        cost_estimate=pl.CostEstimate(flops=flops, bytes_accessed=moved, transcendentals=0),
    )(*operands)


def body(
    kspace, coil_maps, sampling, dc_weight, kernel_in, bias_in, kernel_out, bias_out, cotangent
):
    coils, slots = kspace.shape[:2]
    rows, two_lines = coil_maps.shape[2:]
    lines = two_lines // 2
    channels = bias_in.shape[1]
    coil_devices, sections = lax.axis_size("coil"), lax.axis_size("section")
    volumes = VOLUMES
    depth = slots // volumes
    width = padded(lines, LANES)
    count, whole_count = width // LANES, two_lines // LANES
    planes = coils * slots
    both = ("section", "coil")
    span = depth * coil_devices
    near_order = [depth - 1] + list(range(depth - 1))
    both_order = list(range(span))[::-1]
    near = [[group * depth + member for member in near_order] for group in range(volumes)]
    near_both = [[group * span + member for member in both_order] for group in range(volumes)]
    near_places = [[near_order.index(member)] for member in range(depth)]
    both_places = [
        [both_order.index(member * coil_devices + coil) for coil in range(coil_devices)]
        for member in range(depth)
    ]

    def from_group(value, step, core=0):
        pairs = [(s, ((s + step * depth) % sections) ^ core) for s in range(sections)]
        return lax.ppermute(value, "section", pairs)

    def between_cores(value):
        return lax.ppermute(value, "section", [(s, s) for s in range(sections)])

    def exchange(value, axes, groups):
        return lax.all_to_all(value, axes, 0, 0, tiled=True, axis_index_groups=groups)

    table = jnp.asarray(line_constant(lines))
    minus = jnp.asarray(depth_constant(coils, slots, volumes, -1.0))
    plus = jnp.asarray(depth_constant(coils, slots, volumes, 1.0))
    near_plus = jnp.asarray(depth_constant(coils, depth, 1, 1.0))
    repeat, place, offset = (jnp.asarray(item) for item in conv_constants(rows, channels))
    mask = sampling.reshape(slots, lines)

    def shape(*dims, kind=F32):
        return jax.ShapeDtypeStruct(dims, kind)

    line_flops = 2 * (2 * planes) * width * (2 * width)

    maps_lines = volumes * (coils + 1) * whole_count
    pitch = padded(maps_lines, 8)
    packed, *samples = call(
        functools.partial(pack_kernel, coils, volumes, pitch, near_places),
        "pack_maps",
        (
            kspace.reshape(planes, two_lines),
            coil_maps.reshape(coils * rows, two_lines),
            cotangent.reshape(rows, two_lines),
        ),
        [shape(depth, maps_lines, LANES, kind=BF16)]
        + [shape(coils * depth, two_lines, kind=BF16)] * (volumes - 1),
        [(depth * pitch, LANES)],
        1000,
        LARGE_VMEM_BYTES,
    )
    samples = [from_group(value, step) for step, value in enumerate(samples, 1)]
    tall, wide = channels * rows, offset.shape[1]
    first, first_t, second, second_t, columns = call(
        functools.partial(taps_kernel, rows),
        "lay_out_taps",
        (
            dc_weight,
            kernel_in.transpose(0, 1, 3, 2).reshape(-1, 2, channels),
            kernel_out.reshape(-1, 2, channels),
            bias_in,
            bias_out,
            repeat,
            place,
            offset,
        ),
        [
            shape(CASCADES, tall, wide, kind=BF16),
            shape(CASCADES, 6 * rows, tall, kind=BF16),
            shape(CASCADES, 6 * rows, tall, kind=BF16),
            shape(CASCADES, tall, wide, kind=BF16),
            shape(tall, place.shape[0]),
        ],
        [(place.shape[0], repeat.shape[1])],
        2 * tall * place.shape[0] * place.shape[1],
        scalars=1,
    )
    *samples, columns = lax.optimization_barrier((*samples, columns))
    images = []
    for value in samples:
        (image,) = call(
            functools.partial(far_kernel, coils, lines, volumes),
            "far_images",
            (value, mask, table, near_plus),
            [shape(FAR_PARTS * coils * depth, width)],
            [],
            line_flops,
        )
        images.append(between_cores(image))
    arrived = exchange(packed, "section", near)

    sums_lines = volumes * 5 * count
    depth_pitch = padded(sums_lines, 8)
    partial, maps = call(
        functools.partial(rows_kernel, coils, lines, volumes, near_places, both_places),
        "combine_rows",
        (arrived, kspace.reshape(planes, two_lines), mask, table, minus, plus, near_plus, *images),
        [
            shape(span, sums_lines, LANES, kind=BF16),
            shape(2 * planes, width, kind=BF16),
        ],
        [(depth * pitch, LANES), (depth * depth_pitch, LANES)],
        4 * line_flops,
    )

    partial = exchange(partial, both, near_both)

    model_lines = volumes * 4 * count
    model_pitch = padded(model_lines, 8)
    moved, image = call(
        functools.partial(refine_kernel, lines, volumes, both_places, near_places),
        "refine_and_back",
        (
            partial,
            cotangent.reshape(rows, two_lines),
            first,
            first_t,
            second,
            second_t,
            columns,
        ),
        [shape(depth, model_lines, LANES, kind=BF16), shape(2 * rows, width)],
        [(depth * depth_pitch, LANES), (depth * model_pitch, LANES)],
        14 * tall * wide * width,
    )
    moved = exchange(moved, "section", near)

    end_lines = volumes * whole_count
    end_pitch = padded(end_lines, 16)
    handed = call(
        functools.partial(hand_kernel, lines, volumes, near_places),
        "hand_on",
        (moved, maps),
        [shape((coils + 1) * depth, two_lines, kind=BF16)] * volumes,
        [(depth * model_pitch, LANES)],
        1000,
    )
    handed = list(handed)
    (partial,) = call(
        functools.partial(normal_kernel, coils, lines, volumes, near_places, both_places),
        "masked_normal",
        (moved, maps, mask, table, minus, plus),
        [shape(span, end_lines, LANES, kind=BF16)],
        [(depth * model_pitch, LANES), (depth * end_pitch, LANES)],
        3 * line_flops,
    )
    partial = exchange(partial, both, near_both)
    handed[1:] = [
        from_group(value, step) for step, value in enumerate(handed[1:], 1)
    ]

    image, grad = call(
        functools.partial(end_kernel, coils, lines, volumes, both_places),
        "outputs",
        (columns, partial, image, mask, table, minus, *handed),
        [shape(rows, two_lines), shape(planes * whole_count, LANES)],
        [(depth * end_pitch, LANES)],
        2 * line_flops,
    )
    return image.reshape(1, rows, two_lines), grad.reshape(coils, slots, 1, two_lines)


def solution(mesh):
    return jax.shard_map(
        body,
        mesh=mesh,
        in_specs=(
            P("coil", None, "section", None),
            P("coil", "section", None, None),
            P(),
            P(),
            P(),
            P(),
            P(),
            P(),
            P("section", None, None),
        ),
        out_specs=(P("section", None, None), P("coil", None, "section", None)),
        check_vma=False,
    )
```

```python
import functools
import math

import jax
import jax.numpy as jnp
import ml_dtypes
import numpy as np
from jax import lax
from jax.experimental import pallas as pl
from jax.experimental.pallas import tpu as pltpu
from jax.sharding import PartitionSpec as P

CASCADES = 2
VOLUMES = 2
LANES = 128
VMEM_BYTES = 48 * 1024 * 1024
FAR_PARTS = 3
LARGE_VMEM_BYTES = 60 * 1024 * 1024

F32 = jnp.float32
BF16 = jnp.bfloat16


def padded(size, unit):
    return -(-size // unit) * unit


def dft_parts(count):
    indices = np.arange(count)
    angles = (indices[:, None] * indices[None, :] % count) * (2.0 * math.pi / count)
    factor = 1.0 / math.sqrt(count)
    return np.cos(angles) * factor, np.sin(angles) * factor


def line_constant(lines):
    width = padded(lines, LANES)
    cosine, sine = dft_parts(lines)
    table = np.zeros((width, 2 * width), np.float32)
    table[:lines, :lines] = cosine
    table[:lines, width : width + lines] = sine
    return table.astype(ml_dtypes.bfloat16)


def depth_constant(coils, slots, volumes, sign):
    cosine, sine = dft_parts(slots // volumes)
    spread_over = np.eye(coils * volumes)
    real, imag = np.kron(spread_over, cosine), sign * np.kron(spread_over, sine)
    return np.block([[real, -imag], [imag, real]]).astype(np.float32).astype(ml_dtypes.bfloat16)


def conv_constants(rows, channels):
    groups = 6
    width = padded(groups * rows, LANES)
    repeat = np.kron(np.eye(channels), np.ones((rows, 1))).astype(np.float32)
    repeat = np.pad(repeat, ((0, 0), (0, padded(channels, LANES) - channels)))
    taps = CASCADES * 3
    place = np.zeros((padded(2 * taps * groups + 3 * CASCADES, LANES), 2 * taps * width), np.float32)
    for kind in range(2):
        for tap in range(taps):
            for group in range(groups):
                start = (kind * taps + tap) * width + group * rows
                place[(kind * taps + tap) * groups + group, start : start + rows] = 1.0
    offset = np.full((channels * rows, width), -9.0, np.float32)
    row = np.arange(rows)
    offset[:, : groups * rows] = np.tile(row[None, :] - row[:, None] + 1.0, (channels, groups))
    offset = np.clip(offset, -9.0, 9.0)
    return repeat, place.astype(ml_dtypes.bfloat16), offset


def lane_index(shape):
    return lax.broadcasted_iota(jnp.int32, shape, len(shape) - 1)


def split_complex(chunks, lines):
    whole, rest = divmod(lines, LANES)
    count = padded(lines, LANES) // LANES
    if rest == 0:
        return jnp.concatenate(chunks[:count], 1), jnp.concatenate(chunks[count:], 1)
    lane = lane_index(chunks[0].shape)
    real = chunks[:whole] + [jnp.where(lane < rest, chunks[whole], 0.0)]
    turned = [pltpu.roll(chunk, LANES - rest, 1) for chunk in chunks[whole:]]
    turned.append(jnp.zeros_like(turned[0]))
    imag = [jnp.where(lane < LANES - rest, turned[k], turned[k + 1]) for k in range(count)]
    imag[-1] = jnp.where(lane < rest, imag[-1], 0.0)
    return jnp.concatenate(real, 1), jnp.concatenate(imag, 1)


def lane_chunks(value):
    return [value[:, start : start + LANES] for start in range(0, value.shape[1], LANES)]


def join_complex(real, imag, lines):
    whole, rest = divmod(lines, LANES)
    real, imag = lane_chunks(real), lane_chunks(imag)
    if rest == 0:
        return real + imag
    lane = lane_index(real[0].shape)
    turned = [real[whole]] + [pltpu.roll(chunk, rest, 1) for chunk in imag]
    mixed = [jnp.where(lane < rest, turned[k], turned[k + 1]) for k in range(len(imag))]
    return (real[:whole] + mixed)[: 2 * lines // LANES]


def halves(stacked):
    half = stacked.shape[0] // 2
    return stacked[:half], stacked[half:]


def line_apply(stacked, table_ref, sign):
    mixed = jnp.dot(stacked.astype(BF16), table_ref[...], preferred_element_type=F32)
    width = table_ref.shape[1] // 2
    top, bottom = halves(mixed)
    return jnp.concatenate(
        [
            top[:, :width] - sign * bottom[:, width:],
            bottom[:, :width] + sign * top[:, width:],
        ],
        axis=0,
    )


def depth_apply(stacked, depth_ref):
    return jnp.dot(depth_ref[...], stacked.astype(BF16), preferred_element_type=F32)


def over_coils(value, coils):
    return jnp.concatenate([value] * coils, axis=0)


def coil_sum(value, coils):
    slots = value.shape[0] // coils
    total = value[:slots]
    for coil in range(1, coils):
        total = total + value[coil * slots : (coil + 1) * slots]
    return total


def over_rows(parts, coils):
    return jnp.concatenate([part for part in parts for coil in range(coils)], axis=0)


def spread(maps_real, maps_imag, real, imag):
    return jnp.concatenate(
        [maps_real * real - maps_imag * imag, maps_real * imag + maps_imag * real], axis=0
    )


def collect(maps_real, maps_imag, images):
    real, imag = halves(images)
    return maps_real * real + maps_imag * imag, maps_real * imag - maps_imag * real


def blocks(value, count):
    size = value.shape[0] // count
    return [value[index * size : (index + 1) * size] for index in range(count)]


def row_sums(value, rows, coils):
    return [coil_sum(part, coils) for part in blocks(value, rows)]


def pick(parts, index):
    chosen = parts[0]
    for place in range(1, len(parts)):
        chosen = jnp.where(index == place, parts[place], chosen)
    return chosen


def own_volume(depth):
    return lax.div(lax.axis_index("section"), jnp.int32(depth))


def masked_normal(images, table_ref, minus_ref, plus_ref, mask):
    spectrum = depth_apply(line_apply(images, table_ref, -1.0), minus_ref)
    return line_apply(depth_apply(spectrum * mask, plus_ref), table_ref, 1.0)


def write_rows(scratch, pitch, values, first=0):
    for index, value in enumerate(values):
        scratch[pl.ds(first + index, value.shape[0], stride=pitch), :] = value


def read_rows(scratch, pitch, first, count, rows):
    return [scratch[pl.ds(first + index, rows, stride=pitch), :] for index in range(count)]


def put_messages(out_ref, scratch, places):
    pitch = scratch.shape[0] // len(places)
    for member, spots in enumerate(places):
        message = scratch[member * pitch : member * pitch + out_ref.shape[1]].astype(BF16)
        for spot in spots:
            out_ref[spot] = message


def take_messages(scratch, sent_ref, places):
    pitch = scratch.shape[0] // len(places)
    for member, spots in enumerate(places):
        total = sent_ref[spots[0]].astype(F32)
        for spot in spots[1:]:
            total = total + sent_ref[spot].astype(F32)
        scratch[member * pitch : member * pitch + sent_ref.shape[1]] = total


def shifted(value, step):
    if step == 0:
        return value
    width = value.shape[1]
    return pltpu.roll(value, (-step) % width, 1)


def stack_shifted(value, order):
    return jnp.concatenate([shifted(value, step) for step in order], axis=0).astype(BF16)


def add_shifted(value, order, rows):
    total = None
    for index, step in enumerate(order):
        part = shifted(value[index * rows : (index + 1) * rows], step)
        total = part if total is None else total + part
    return total


def hidden_state(image, first_ref, bias_column):
    stack = stack_shifted(image, (-1, 0, 1))
    return (
        jnp.dot(first_ref[:, : stack.shape[0]], stack, preferred_element_type=F32) + bias_column
    )


def second_conv(hidden, second_ref, bias_column, rows, valid):
    mixed = jnp.dot(
        second_ref[...], jnp.where(valid, hidden, 0.0).astype(BF16), preferred_element_type=F32
    )
    total = add_shifted(mixed, (-1, 0, 1), 2 * rows)
    return jnp.where(valid[: 2 * rows], total + bias_column, 0.0)


def pull_back(cotangent, slope, first_t_ref, second_t_ref, rows, valid):
    stack = stack_shifted(cotangent, (1, 0, -1))
    back = jnp.dot(second_t_ref[:, : stack.shape[0]], stack, preferred_element_type=F32)
    back = jnp.where(valid, back * slope, 0.0).astype(BF16)
    mixed = jnp.dot(first_t_ref[...], back, preferred_element_type=F32)
    total = add_shifted(mixed, (1, 0, -1), 2 * rows)
    return jnp.where(valid[: 2 * rows], total, 0.0)


def read_mask(sampling_ref, width):
    mask = sampling_ref[...].astype(F32)
    return jnp.pad(mask, ((0, 0), (0, width - mask.shape[1])))


def valid_lanes(rows, width, lines):
    return lane_index((rows, width)) < lines


def column(columns_ref, place, rows):
    at = 4 * 9 * CASCADES + place
    return columns_ref[:rows, at : at + 1]


def round_bf(value):
    return value.astype(BF16).astype(F32)


def choose_volume(value, coils, volumes, volume):
    parts = blocks(value, coils * volumes)
    chosen = [pick(parts[coil * volumes : (coil + 1) * volumes], volume) for coil in range(coils)]
    return jnp.concatenate(chosen, axis=0)


def pack_kernel(coils, volumes, pitch, places, kspace_ref, maps_ref, image_ref, out_ref, *refs):
    handed, (scratch,) = refs[:-1], refs[-1:]
    rows = image_ref.shape[0]
    depth = rows // volumes
    volume = own_volume(depth)
    kspace = kspace_ref[...].astype(F32)
    for step, ref in enumerate(handed, 1):
        other = lax.rem(volume + step, jnp.int32(volumes))
        ref[...] = choose_volume(kspace, coils, volumes, other).astype(BF16)
    count = maps_ref.shape[1] // LANES
    image = image_ref[...].astype(F32)
    for coil in range(coils + 1):
        value = maps_ref[coil * rows : (coil + 1) * rows, :].astype(F32) if coil < coils else image
        for place, part in enumerate(blocks(value, volumes)):
            first = (place * (coils + 1) + coil) * count
            write_rows(scratch, pitch, lane_chunks(part), first)
    put_messages(out_ref, scratch, places)


def taps_kernel(
    rows,
    weight_ref,
    kernel_in_ref,
    kernel_out_ref,
    bias_in_ref,
    bias_out_ref,
    repeat_ref,
    place_ref,
    offset_ref,
    first_ref,
    first_t_ref,
    second_ref,
    second_t_ref,
    columns_ref,
    taps,
):
    taps[...] = jnp.zeros_like(taps)
    channels = kernel_in_ref.shape[2]
    at = 0
    for ref in (kernel_in_ref, kernel_out_ref):
        for index in range(ref.shape[0]):
            taps[at : at + 2, :channels] = ref[index]
            at += 2
    taps[at : at + CASCADES, :channels] = bias_in_ref[...]
    at += CASCADES
    for cascade in range(CASCADES):
        taps[at : at + 1, :] = jnp.full((1, taps.shape[1]), weight_ref[cascade], F32)
        at += 1
    taps[at : at + CASCADES, : bias_out_ref.shape[1]] = bias_out_ref[...]
    tall = lax.dot_general(
        repeat_ref[...],
        taps[...],
        (((1,), (1,)), ((), ())),
        precision=lax.Precision.HIGHEST,
        preferred_element_type=F32,
    )
    columns_ref[...] = tall
    wide = jnp.dot(tall.astype(BF16), place_ref[...], preferred_element_type=F32)
    offset = offset_ref[...]
    width = offset.shape[1]
    for cascade in range(CASCADES):
        for kind, straight, turned in ((0, first_ref, first_t_ref), (1, second_t_ref, second_ref)):
            total = jnp.zeros_like(offset)
            for tap in range(3):
                start = ((kind * CASCADES + cascade) * 3 + tap) * width
                wanted = float(tap if kind == 0 else 2 - tap)
                total = total + jnp.where(offset == wanted, wide[:, start : start + width], 0.0)
            straight[cascade] = total.astype(BF16)
            turned[cascade] = total.T[: 6 * rows].astype(BF16)


def line_images(kspace, mask, lines, table_ref, plus_ref):
    real, imag = split_complex(lane_chunks(kspace), lines)
    measured = jnp.concatenate([real * mask, imag * mask], axis=0)
    return line_apply(depth_apply(measured, plus_ref), table_ref, 1.0)


def far_kernel(coils, lines, volumes, kspace_ref, mask_ref, table_ref, plus_ref, out_ref):
    parts = blocks(read_mask(mask_ref, table_ref.shape[0]), volumes)
    mask = pick(parts, own_volume(parts[0].shape[0]))
    mask = over_coils(mask, coils)
    images = line_images(kspace_ref[...].astype(F32), mask, lines, table_ref, plus_ref)
    out_ref[: images.shape[0]] = images
    if out_ref.shape[0] > images.shape[0]:
        out_ref[images.shape[0] :] = jnp.zeros_like(out_ref[images.shape[0] :])


def rows_kernel(
    coils,
    lines,
    volumes,
    from_places,
    to_places,
    sent_ref,
    kspace_ref,
    mask_ref,
    table_ref,
    minus_ref,
    plus_ref,
    near_ref,
    *refs,
):
    arrival_refs, refs = refs[: volumes - 1], refs[volumes - 1 :]
    out_ref, maps_ref, arrived, leaving = refs
    depth = sent_ref.shape[0]
    pitch = arrived.shape[0] // depth
    volume = own_volume(depth)
    mask = pick(blocks(read_mask(mask_ref, table_ref.shape[0]), volumes), volume)
    mask = over_coils(mask, volumes * coils)

    own = choose_volume(kspace_ref[...].astype(F32), coils, volumes, volume)
    own = line_images(own, mask[: coils * depth], lines, table_ref, near_ref)
    arrivals = [halves(own)] + [halves(ref[: 2 * coils * depth]) for ref in arrival_refs]
    measured = []
    for part in range(2):
        for place in range(volumes):
            step = lax.rem(volume - place + volumes, jnp.int32(volumes))
            measured.append(pick([arrival[part] for arrival in arrivals], step))
    measured = jnp.concatenate(measured, axis=0)

    take_messages(arrived, sent_ref, from_places)
    count = 2 * lines // LANES
    parts, reals, imags = [], [], []
    for place in range(volumes):
        first = place * (coils + 1) * count
        for coil in range(coils):
            chunks = read_rows(arrived, pitch, first + coil * count, count, depth)
            parts.append(split_complex(chunks, lines))
        chunks = read_rows(arrived, pitch, first + coils * count, count, depth)
        real, imag = split_complex(chunks, lines)
        reals.append(real)
        imags.append(imag)
    maps_real = jnp.concatenate([part[0] for part in parts], axis=0)
    maps_imag = jnp.concatenate([part[1] for part in parts], axis=0)
    maps_ref[...] = jnp.concatenate([maps_real, maps_imag], axis=0).astype(BF16)

    images = spread(maps_real, maps_imag, over_rows(reals, coils), over_rows(imags, coils))
    mask = jnp.concatenate([mask, mask], axis=0)
    images = masked_normal(images, table_ref, minus_ref, plus_ref, mask)
    found = [
        *collect(maps_real, maps_imag, round_bf(measured)),
        *collect(maps_real, maps_imag, images),
        maps_real * maps_real + maps_imag * maps_imag,
    ]
    sums = [row_sums(value, volumes, coils) for value in found]
    pitch = leaving.shape[0] // depth
    for place in range(volumes):
        chunks = [chunk for value in sums for chunk in lane_chunks(value[place])]
        write_rows(leaving, pitch, chunks, place * len(chunks))
    put_messages(out_ref, leaving, to_places)


def read_image(scratch, pitch, first, count, depth):
    return jnp.concatenate(read_rows(scratch, pitch, first, count, depth), axis=1)


def read_places(scratch, pitch, first, period, count, depth, volumes):
    parts = [
        read_image(scratch, pitch, first + place * period, count, depth) for place in range(volumes)
    ]
    return jnp.concatenate(parts, axis=0)


def read_complex(scratch, pitch, first, period, count, depth, volumes):
    real = read_places(scratch, pitch, first, period, count, depth, volumes)
    imag = read_places(scratch, pitch, first + count, period, count, depth, volumes)
    return jnp.concatenate([real, imag], axis=0)


def refine_kernel(
    lines,
    volumes,
    from_places,
    to_places,
    sent_ref,
    cotangent_ref,
    first_ref,
    first_t_ref,
    second_ref,
    second_t_ref,
    columns_ref,
    out_ref,
    image_ref,
    arrived,
    leaving,
):
    take_messages(arrived, sent_ref, from_places)
    depth = len(from_places)
    pitch = arrived.shape[0] // depth
    rows = depth * volumes
    width = padded(lines, LANES)
    count = width // LANES
    begun = read_complex(arrived, pitch, 0, 5 * count, count, depth, volumes)
    turned = read_complex(arrived, pitch, 2 * count, 5 * count, count, depth, volumes)
    power = read_places(arrived, pitch, 4 * count, 5 * count, count, depth, volumes)
    power = jnp.concatenate([power, power], axis=0)
    cotangent = jnp.concatenate(
        split_complex(lane_chunks(cotangent_ref[...].astype(F32)), lines), axis=0
    )
    tall = first_ref.shape[1]
    weight = [column(columns_ref, CASCADES + cascade, 2 * rows) for cascade in range(CASCADES)]
    bias = [column(columns_ref, 2 * CASCADES + cascade, 2 * rows) for cascade in range(CASCADES)]

    share = [jnp.ones_like(weight[0])]
    for cascade in range(CASCADES):
        share.append(share[cascade] - weight[cascade] * (share[cascade] - 1.0))

    def slopes(hidden):
        gate = jax.nn.sigmoid(hidden)
        return hidden * gate, gate * (1.0 + hidden * (1.0 - gate))

    hidden = hidden_state(round_bf(begun), first_ref.at[0], column(columns_ref, 0, tall))
    valid = valid_lanes(hidden.shape[0], width, lines)
    active, slope_first = slopes(hidden)
    model = round_bf(second_conv(active, second_ref.at[0], bias[0], rows, valid))
    picture = round_bf(share[1] * begun + power * model)
    hidden = hidden_state(picture, first_ref.at[1], column(columns_ref, 1, tall))
    active, slope_second = slopes(hidden)
    later = round_bf(second_conv(active, second_ref.at[1], bias[1], rows, valid))
    image_ref[...] = share[2] * begun + power * (model + later)

    through = power * cotangent
    back_second = round_bf(
        pull_back(through, slope_second, first_t_ref.at[1], second_t_ref.at[1], rows, valid)
    )
    through = through - weight[1] * turned + power * back_second
    back_first = round_bf(
        pull_back(through, slope_first, first_t_ref.at[0], second_t_ref.at[0], rows, valid)
    )
    kept = (1.0 - weight[0], 1.0 - weight[1])
    of_cotangent = weight[1] + weight[0] * kept[1] + kept[0] * kept[1]
    of_second = weight[0] + kept[0]
    pulled = of_cotangent * cotangent + of_second * back_second + back_first
    parts = [blocks(part, volumes) for value in (model, pulled) for part in halves(value)]
    for place in range(volumes):
        chunks = [chunk for part in parts for chunk in lane_chunks(part[place])]
        write_rows(leaving, out_ref.shape[1], chunks, place * len(chunks))
    put_messages(out_ref, leaving, to_places)


def hand_kernel(lines, volumes, from_places, sent_ref, maps_ref, *refs):
    outs, (arrived,) = refs[:-1], refs[-1:]
    take_messages(arrived, sent_ref, from_places)
    depth = sent_ref.shape[0]
    pitch = arrived.shape[0] // depth
    volume = own_volume(depth)
    count = maps_ref.shape[1] // LANES
    maps = [blocks(part, volumes) for part in halves(maps_ref[...].astype(F32))]
    pulled = [
        [
            read_image(arrived, pitch, (place * 4 + field) * count, count, depth)
            for place in range(volumes)
        ]
        for field in (2, 3)
    ]
    for step, ref in enumerate(outs):
        place = lax.rem(volume + step, jnp.int32(volumes))
        chosen = [jnp.concatenate([pick(a, place), pick(b, place)]) for a, b in zip(maps, pulled)]
        if step == 0:
            ref[...] = jnp.concatenate(chosen, axis=0).astype(BF16)
            continue
        for index, chunk in enumerate(join_complex(*chosen, lines)):
            ref[:, index * LANES : (index + 1) * LANES] = chunk.astype(BF16)


def normal_kernel(
    coils,
    lines,
    volumes,
    from_places,
    to_places,
    sent_ref,
    maps_ref,
    mask_ref,
    table_ref,
    minus_ref,
    plus_ref,
    out_ref,
    arrived,
    leaving,
):
    take_messages(arrived, sent_ref, from_places)
    depth = sent_ref.shape[0]
    pitch = arrived.shape[0] // depth
    volume = own_volume(depth)
    count = maps_ref.shape[1] // LANES
    fields = [
        [
            read_image(arrived, pitch, (place * 4 + field) * count, count, depth)
            for place in range(volumes)
        ]
        for field in range(2)
    ]
    reals, imags = fields
    maps_real, maps_imag = halves(maps_ref[...].astype(F32))
    mask = over_coils(pick(blocks(read_mask(mask_ref, table_ref.shape[0]), volumes), volume), 2 * volumes * coils)
    images = spread(maps_real, maps_imag, over_rows(reals, coils), over_rows(imags, coils))
    images = masked_normal(images, table_ref, minus_ref, plus_ref, mask)
    found = [row_sums(value, volumes, coils) for value in collect(maps_real, maps_imag, images)]
    for place in range(volumes):
        chunks = join_complex(found[0][place], found[1][place], lines)
        write_rows(leaving, leaving.shape[0] // depth, chunks, place * len(chunks))
    put_messages(out_ref, leaving, to_places)


def from_volumes(refs, volume, parts, volumes):
    sources = [blocks(ref, parts) for ref in refs]
    ordered = []
    for place in range(volumes):
        step = lax.rem(volume - place + volumes, jnp.int32(volumes))
        ordered.append([pick([source[part] for source in sources], step) for part in range(parts)])
    return ordered


def grad_kernel(
    coils,
    lines,
    volumes,
    mask_ref,
    table_ref,
    minus_ref,
    *refs,
):
    handed, (grad_ref,) = refs[:volumes], refs[volumes:]
    depth = mask_ref.shape[0] // volumes
    volume = own_volume(depth)
    own, *handed = [ref[...].astype(F32) for ref in handed]
    handed = [split_complex(lane_chunks(value), lines) for value in handed]
    handed = [own] + [jnp.concatenate(parts, axis=0) for parts in handed]
    found = from_volumes(handed, volume, 2 * (coils + 1), volumes)
    maps, pulled = [], []
    for first in (0, coils + 1):
        parts = [found[v][first + coil] for coil in range(coils) for v in range(volumes)]
        maps.append(jnp.concatenate(parts, axis=0))
        pulled.append(jnp.concatenate([found[v][first + coils] for v in range(volumes)], axis=0))
    real, imag = pulled
    images = spread(*maps, over_coils(real, coils), over_coils(imag, coils))
    spectrum = depth_apply(line_apply(images, table_ref, -1.0), minus_ref)
    spectrum = spectrum * over_coils(read_mask(mask_ref, table_ref.shape[0]), 2 * coils)
    chunks = join_complex(*halves(spectrum), lines)
    write_rows(grad_ref, len(chunks), chunks)


def picture_kernel(lines, volumes, from_places, columns_ref, sent_ref, image_ref, picture_ref, arrived):
    depth = len(from_places)
    pitch = arrived.shape[0] // depth
    count = 2 * lines // LANES
    take_messages(arrived, sent_ref, from_places)
    parts = [[], []]
    for place in range(volumes):
        chunks = read_rows(arrived, pitch, place * count, count, depth)
        for part, value in zip(parts, split_complex(chunks, lines)):
            part.append(value)
    picture = image_ref[...]
    scale = column(columns_ref, CASCADES + 1, picture.shape[0])
    picture = picture - scale * jnp.concatenate(parts[0] + parts[1], axis=0)
    for index, chunk in enumerate(join_complex(*halves(picture), lines)):
        picture_ref[:, index * LANES : (index + 1) * LANES] = chunk


def end_kernel(
    coils,
    lines,
    volumes,
    from_places,
    columns_ref,
    sent_ref,
    image_ref,
    mask_ref,
    table_ref,
    minus_ref,
    *refs,
):
    handed, (picture_ref, grad_ref, arrived) = refs[:volumes], refs[volumes:]
    grad_kernel(coils, lines, volumes, mask_ref, table_ref, minus_ref, *handed, grad_ref)
    picture_kernel(
        lines, volumes, from_places, columns_ref, sent_ref, image_ref, picture_ref, arrived
    )


def call(kernel, name, operands, outs, scratch, flops, vmem_bytes=VMEM_BYTES, scalars=0):
    spaces = [pltpu.SMEM] * scalars + [pltpu.VMEM] * (len(operands) - scalars)
    moved = sum(math.prod(item.shape) * item.dtype.itemsize for item in (*operands, *outs))
    return pl.pallas_call(
        kernel,
        name=name,
        out_shape=tuple(outs),
        in_specs=[pl.BlockSpec(memory_space=space) for space in spaces],
        out_specs=tuple(pl.BlockSpec(memory_space=pltpu.VMEM) for item in outs),
        scratch_shapes=[pltpu.VMEM(shape, F32) for shape in scratch],
        compiler_params=pltpu.CompilerParams(vmem_limit_bytes=vmem_bytes),
        cost_estimate=pl.CostEstimate(flops=flops, bytes_accessed=moved, transcendentals=0),
    )(*operands)


def body(
    kspace, coil_maps, sampling, dc_weight, kernel_in, bias_in, kernel_out, bias_out, cotangent
):
    coils, slots = kspace.shape[:2]
    rows, two_lines = coil_maps.shape[2:]
    lines = two_lines // 2
    channels = bias_in.shape[1]
    coil_devices, sections = lax.axis_size("coil"), lax.axis_size("section")
    volumes = VOLUMES
    depth = slots // volumes
    width = padded(lines, LANES)
    count, whole_count = width // LANES, two_lines // LANES
    planes = coils * slots
    both = ("section", "coil")
    span = depth * coil_devices
    near_order = [depth - 1] + list(range(depth - 1))
    both_order = list(range(span))[::-1]
    near = [[group * depth + member for member in near_order] for group in range(volumes)]
    near_both = [[group * span + member for member in both_order] for group in range(volumes)]
    near_places = [[near_order.index(member)] for member in range(depth)]
    both_places = [
        [both_order.index(member * coil_devices + coil) for coil in range(coil_devices)]
        for member in range(depth)
    ]

    def from_group(value, step, core=0):
        pairs = [(s, ((s + step * depth) % sections) ^ core) for s in range(sections)]
        return lax.ppermute(value, "section", pairs)

    def between_cores(value):
        return lax.ppermute(value, "section", [(s, s) for s in range(sections)])

    def exchange(value, axes, groups):
        return lax.all_to_all(value, axes, 0, 0, tiled=True, axis_index_groups=groups)

    table = jnp.asarray(line_constant(lines))
    minus = jnp.asarray(depth_constant(coils, slots, volumes, -1.0))
    plus = jnp.asarray(depth_constant(coils, slots, volumes, 1.0))
    near_plus = jnp.asarray(depth_constant(coils, depth, 1, 1.0))
    repeat, place, offset = (jnp.asarray(item) for item in conv_constants(rows, channels))
    mask = sampling.reshape(slots, lines)

    def shape(*dims, kind=F32):
        return jax.ShapeDtypeStruct(dims, kind)

    line_flops = 2 * (2 * planes) * width * (2 * width)

    maps_lines = volumes * (coils + 1) * whole_count
    pitch = padded(maps_lines, 8)
    packed, *samples = call(
        functools.partial(pack_kernel, coils, volumes, pitch, near_places),
        "pack_maps",
        (
            kspace.reshape(planes, two_lines),
            coil_maps.reshape(coils * rows, two_lines),
            cotangent.reshape(rows, two_lines),
        ),
        [shape(depth, maps_lines, LANES, kind=BF16)]
        + [shape(coils * depth, two_lines, kind=BF16)] * (volumes - 1),
        [(depth * pitch, LANES)],
        1000,
        LARGE_VMEM_BYTES,
    )
    samples = [from_group(value, step) for step, value in enumerate(samples, 1)]
    tall, wide = channels * rows, offset.shape[1]
    first, first_t, second, second_t, columns = call(
        functools.partial(taps_kernel, rows),
        "lay_out_taps",
        (
            dc_weight,
            kernel_in.transpose(0, 1, 3, 2).reshape(-1, 2, channels),
            kernel_out.reshape(-1, 2, channels),
            bias_in,
            bias_out,
            repeat,
            place,
            offset,
        ),
        [
            shape(CASCADES, tall, wide, kind=BF16),
            shape(CASCADES, 6 * rows, tall, kind=BF16),
            shape(CASCADES, 6 * rows, tall, kind=BF16),
            shape(CASCADES, tall, wide, kind=BF16),
            shape(tall, place.shape[0]),
        ],
        [(place.shape[0], repeat.shape[1])],
        2 * tall * place.shape[0] * place.shape[1],
        scalars=1,
    )
    *samples, columns = lax.optimization_barrier((*samples, columns))
    images = []
    for value in samples:
        (image,) = call(
            functools.partial(far_kernel, coils, lines, volumes),
            "far_images",
            (value, mask, table, near_plus),
            [shape(FAR_PARTS * coils * depth, width)],
            [],
            line_flops,
        )
        images.append(between_cores(image))
    arrived = exchange(packed, "section", near)

    sums_lines = volumes * 5 * count
    depth_pitch = padded(sums_lines, 8)
    partial, maps = call(
        functools.partial(rows_kernel, coils, lines, volumes, near_places, both_places),
        "combine_rows",
        (arrived, kspace.reshape(planes, two_lines), mask, table, minus, plus, near_plus, *images),
        [
            shape(span, sums_lines, LANES, kind=BF16),
            shape(2 * planes, width, kind=BF16),
        ],
        [(depth * pitch, LANES), (depth * depth_pitch, LANES)],
        4 * line_flops,
    )

    partial = exchange(partial, both, near_both)

    model_lines = volumes * 4 * count
    model_pitch = padded(model_lines, 8)
    moved, image = call(
        functools.partial(refine_kernel, lines, volumes, both_places, near_places),
        "refine_and_back",
        (
            partial,
            cotangent.reshape(rows, two_lines),
            first,
            first_t,
            second,
            second_t,
            columns,
        ),
        [shape(depth, model_lines, LANES, kind=BF16), shape(2 * rows, width)],
        [(depth * depth_pitch, LANES), (depth * model_pitch, LANES)],
        14 * tall * wide * width,
    )
    moved = exchange(moved, "section", near)

    end_lines = volumes * whole_count
    end_pitch = padded(end_lines, 16)
    handed = call(
        functools.partial(hand_kernel, lines, volumes, near_places),
        "hand_on",
        (moved, maps),
        [shape(2 * (coils + 1) * depth, width, kind=BF16)]
        + [shape((coils + 1) * depth, two_lines, kind=BF16)] * (volumes - 1),
        [(depth * model_pitch, LANES)],
        1000,
    )
    handed = list(handed)
    (partial,) = call(
        functools.partial(normal_kernel, coils, lines, volumes, near_places, both_places),
        "masked_normal",
        (moved, maps, mask, table, minus, plus),
        [shape(span, end_lines, LANES, kind=BF16)],
        [(depth * model_pitch, LANES), (depth * end_pitch, LANES)],
        3 * line_flops,
    )
    partial = exchange(partial, both, near_both)
    handed[1:] = [
        from_group(value, step) for step, value in enumerate(handed[1:], 1)
    ]

    image, grad = call(
        functools.partial(end_kernel, coils, lines, volumes, both_places),
        "outputs",
        (columns, partial, image, mask, table, minus, *handed),
        [shape(rows, two_lines), shape(planes * whole_count, LANES)],
        [(depth * end_pitch, LANES)],
        2 * line_flops,
    )
    return image.reshape(1, rows, two_lines), grad.reshape(coils, slots, 1, two_lines)


def solution(mesh):
    return jax.shard_map(
        body,
        mesh=mesh,
        in_specs=(
            P("coil", None, "section", None),
            P("coil", "section", None, None),
            P(),
            P(),
            P(),
            P(),
            P(),
            P(),
            P("section", None, None),
        ),
        out_specs=(P("section", None, None), P("coil", None, "section", None)),
        check_vma=False,
    )
```

```python
import functools
import math

import jax
import jax.numpy as jnp
import ml_dtypes
import numpy as np
from jax import lax
from jax.experimental import pallas as pl
from jax.experimental.pallas import tpu as pltpu
from jax.sharding import PartitionSpec as P

CASCADES = 2
VOLUMES = 2
LANES = 128
VMEM_BYTES = 48 * 1024 * 1024
FAR_PARTS = 3
LARGE_VMEM_BYTES = 60 * 1024 * 1024

F32 = jnp.float32
BF16 = jnp.bfloat16


def padded(size, unit):
    return -(-size // unit) * unit


def dft_parts(count):
    indices = np.arange(count)
    angles = (indices[:, None] * indices[None, :] % count) * (2.0 * math.pi / count)
    factor = 1.0 / math.sqrt(count)
    return np.cos(angles) * factor, np.sin(angles) * factor


def line_constant(lines):
    width = padded(lines, LANES)
    cosine, sine = dft_parts(lines)
    table = np.zeros((width, 2 * width), np.float32)
    table[:lines, :lines] = cosine
    table[:lines, width : width + lines] = sine
    return table.astype(ml_dtypes.bfloat16)


def depth_constant(coils, slots, volumes, sign):
    cosine, sine = dft_parts(slots // volumes)
    spread_over = np.eye(coils * volumes)
    real, imag = np.kron(spread_over, cosine), sign * np.kron(spread_over, sine)
    return np.block([[real, -imag], [imag, real]]).astype(np.float32).astype(ml_dtypes.bfloat16)


def conv_constants(rows, channels):
    groups = 6
    width = padded(groups * rows, LANES)
    repeat = np.kron(np.eye(channels), np.ones((rows, 1))).astype(np.float32)
    repeat = np.pad(repeat, ((0, 0), (0, padded(channels, LANES) - channels)))
    taps = CASCADES * 3
    place = np.zeros((padded(2 * taps * groups + 3 * CASCADES, LANES), 2 * taps * width), np.float32)
    for kind in range(2):
        for tap in range(taps):
            for group in range(groups):
                start = (kind * taps + tap) * width + group * rows
                place[(kind * taps + tap) * groups + group, start : start + rows] = 1.0
    offset = np.full((channels * rows, width), -9.0, np.float32)
    row = np.arange(rows)
    offset[:, : groups * rows] = np.tile(row[None, :] - row[:, None] + 1.0, (channels, groups))
    offset = np.clip(offset, -9.0, 9.0)
    return repeat, place.astype(ml_dtypes.bfloat16), offset


def lane_index(shape):
    return lax.broadcasted_iota(jnp.int32, shape, len(shape) - 1)


def split_complex(chunks, lines):
    whole, rest = divmod(lines, LANES)
    count = padded(lines, LANES) // LANES
    if rest == 0:
        return jnp.concatenate(chunks[:count], 1), jnp.concatenate(chunks[count:], 1)
    lane = lane_index(chunks[0].shape)
    real = chunks[:whole] + [jnp.where(lane < rest, chunks[whole], 0.0)]
    turned = [pltpu.roll(chunk, LANES - rest, 1) for chunk in chunks[whole:]]
    turned.append(jnp.zeros_like(turned[0]))
    imag = [jnp.where(lane < LANES - rest, turned[k], turned[k + 1]) for k in range(count)]
    imag[-1] = jnp.where(lane < rest, imag[-1], 0.0)
    return jnp.concatenate(real, 1), jnp.concatenate(imag, 1)


def lane_chunks(value):
    return [value[:, start : start + LANES] for start in range(0, value.shape[1], LANES)]


def join_complex(real, imag, lines):
    whole, rest = divmod(lines, LANES)
    real, imag = lane_chunks(real), lane_chunks(imag)
    if rest == 0:
        return real + imag
    lane = lane_index(real[0].shape)
    turned = [real[whole]] + [pltpu.roll(chunk, rest, 1) for chunk in imag]
    mixed = [jnp.where(lane < rest, turned[k], turned[k + 1]) for k in range(len(imag))]
    return (real[:whole] + mixed)[: 2 * lines // LANES]


def halves(stacked):
    half = stacked.shape[0] // 2
    return stacked[:half], stacked[half:]


def line_apply(stacked, table_ref, sign):
    mixed = jnp.dot(stacked.astype(BF16), table_ref[...], preferred_element_type=F32)
    width = table_ref.shape[1] // 2
    top, bottom = halves(mixed)
    return jnp.concatenate(
        [
            top[:, :width] - sign * bottom[:, width:],
            bottom[:, :width] + sign * top[:, width:],
        ],
        axis=0,
    )


def depth_apply(stacked, depth_ref):
    return jnp.dot(depth_ref[...], stacked.astype(BF16), preferred_element_type=F32)


def over_coils(value, coils):
    return jnp.concatenate([value] * coils, axis=0)


def coil_sum(value, coils):
    slots = value.shape[0] // coils
    total = value[:slots]
    for coil in range(1, coils):
        total = total + value[coil * slots : (coil + 1) * slots]
    return total


def over_rows(parts, coils):
    return jnp.concatenate([part for part in parts for coil in range(coils)], axis=0)


def spread(maps_real, maps_imag, real, imag):
    return jnp.concatenate(
        [maps_real * real - maps_imag * imag, maps_real * imag + maps_imag * real], axis=0
    )


def collect(maps_real, maps_imag, images):
    real, imag = halves(images)
    return maps_real * real + maps_imag * imag, maps_real * imag - maps_imag * real


def blocks(value, count):
    size = value.shape[0] // count
    return [value[index * size : (index + 1) * size] for index in range(count)]


def row_sums(value, rows, coils):
    return [coil_sum(part, coils) for part in blocks(value, rows)]


def pick(parts, index):
    chosen = parts[0]
    for place in range(1, len(parts)):
        chosen = jnp.where(index == place, parts[place], chosen)
    return chosen


def own_volume(depth):
    return lax.div(lax.axis_index("section"), jnp.int32(depth))


def masked_normal(images, table_ref, minus_ref, plus_ref, mask):
    spectrum = depth_apply(line_apply(images, table_ref, -1.0), minus_ref)
    return line_apply(depth_apply(spectrum * mask, plus_ref), table_ref, 1.0)


def write_rows(scratch, pitch, values, first=0):
    for index, value in enumerate(values):
        scratch[pl.ds(first + index, value.shape[0], stride=pitch), :] = value


def read_rows(scratch, pitch, first, count, rows):
    return [scratch[pl.ds(first + index, rows, stride=pitch), :] for index in range(count)]


def put_messages(out_ref, scratch, places):
    pitch = scratch.shape[0] // len(places)
    for member, spots in enumerate(places):
        message = scratch[member * pitch : member * pitch + out_ref.shape[1]].astype(BF16)
        for spot in spots:
            out_ref[spot] = message


def take_messages(scratch, sent_ref, places):
    pitch = scratch.shape[0] // len(places)
    for member, spots in enumerate(places):
        total = sent_ref[spots[0]].astype(F32)
        for spot in spots[1:]:
            total = total + sent_ref[spot].astype(F32)
        scratch[member * pitch : member * pitch + sent_ref.shape[1]] = total


def shifted(value, step):
    if step == 0:
        return value
    width = value.shape[1]
    return pltpu.roll(value, (-step) % width, 1)


def stack_shifted(value, order):
    return jnp.concatenate([shifted(value, step) for step in order], axis=0).astype(BF16)


def add_shifted(value, order, rows):
    total = None
    for index, step in enumerate(order):
        part = shifted(value[index * rows : (index + 1) * rows], step)
        total = part if total is None else total + part
    return total


def hidden_state(image, first_ref, bias_column):
    stack = stack_shifted(image, (-1, 0, 1))
    return (
        jnp.dot(first_ref[:, : stack.shape[0]], stack, preferred_element_type=F32) + bias_column
    )


def second_conv(hidden, second_ref, bias_column, rows, valid):
    mixed = jnp.dot(
        second_ref[...], jnp.where(valid, hidden, 0.0).astype(BF16), preferred_element_type=F32
    )
    total = add_shifted(mixed, (-1, 0, 1), 2 * rows)
    return jnp.where(valid[: 2 * rows], total + bias_column, 0.0)


def pull_back(cotangent, slope, first_t_ref, second_t_ref, rows, valid):
    stack = stack_shifted(cotangent, (1, 0, -1))
    back = jnp.dot(second_t_ref[:, : stack.shape[0]], stack, preferred_element_type=F32)
    back = jnp.where(valid, back * slope, 0.0).astype(BF16)
    mixed = jnp.dot(first_t_ref[...], back, preferred_element_type=F32)
    total = add_shifted(mixed, (1, 0, -1), 2 * rows)
    return jnp.where(valid[: 2 * rows], total, 0.0)


def read_mask(sampling_ref, width):
    mask = sampling_ref[...].astype(F32)
    return jnp.pad(mask, ((0, 0), (0, width - mask.shape[1])))


def valid_lanes(rows, width, lines):
    return lane_index((rows, width)) < lines


def column(columns_ref, place, rows):
    at = 4 * 9 * CASCADES + place
    return columns_ref[:rows, at : at + 1]


def round_bf(value):
    return value.astype(BF16).astype(F32)


def choose_volume(value, coils, volumes, volume):
    parts = blocks(value, coils * volumes)
    chosen = [pick(parts[coil * volumes : (coil + 1) * volumes], volume) for coil in range(coils)]
    return jnp.concatenate(chosen, axis=0)


def pack_kernel(coils, volumes, pitch, places, kspace_ref, maps_ref, image_ref, out_ref, *refs):
    handed, (scratch,) = refs[:-1], refs[-1:]
    rows = image_ref.shape[0]
    depth = rows // volumes
    volume = own_volume(depth)
    kspace = kspace_ref[...].astype(F32)
    for step, ref in enumerate(handed, 1):
        other = lax.rem(volume + step, jnp.int32(volumes))
        ref[...] = choose_volume(kspace, coils, volumes, other).astype(BF16)
    count = maps_ref.shape[1] // LANES
    scratch[...] = jnp.zeros_like(scratch)
    image = image_ref[...].astype(F32)
    for coil in range(coils + 1):
        value = maps_ref[coil * rows : (coil + 1) * rows, :].astype(F32) if coil < coils else image
        for place, part in enumerate(blocks(value, volumes)):
            first = (place * (coils + 1) + coil) * count
            write_rows(scratch, pitch, lane_chunks(part), first)
    put_messages(out_ref, scratch, places)


def taps_kernel(
    rows,
    weight_ref,
    kernel_in_ref,
    kernel_out_ref,
    bias_in_ref,
    bias_out_ref,
    repeat_ref,
    place_ref,
    offset_ref,
    first_ref,
    first_t_ref,
    second_ref,
    second_t_ref,
    columns_ref,
    taps,
):
    taps[...] = jnp.zeros_like(taps)
    channels = kernel_in_ref.shape[2]
    at = 0
    for ref in (kernel_in_ref, kernel_out_ref):
        for index in range(ref.shape[0]):
            taps[at : at + 2, :channels] = ref[index]
            at += 2
    taps[at : at + CASCADES, :channels] = bias_in_ref[...]
    at += CASCADES
    for cascade in range(CASCADES):
        taps[at : at + 1, :] = jnp.full((1, taps.shape[1]), weight_ref[cascade], F32)
        at += 1
    taps[at : at + CASCADES, : bias_out_ref.shape[1]] = bias_out_ref[...]
    tall = lax.dot_general(
        repeat_ref[...],
        taps[...],
        (((1,), (1,)), ((), ())),
        precision=lax.Precision.HIGHEST,
        preferred_element_type=F32,
    )
    columns_ref[...] = tall
    wide = jnp.dot(tall.astype(BF16), place_ref[...], preferred_element_type=F32)
    offset = offset_ref[...]
    width = offset.shape[1]
    for cascade in range(CASCADES):
        for kind, straight, turned in ((0, first_ref, first_t_ref), (1, second_t_ref, second_ref)):
            total = jnp.zeros_like(offset)
            for tap in range(3):
                start = ((kind * CASCADES + cascade) * 3 + tap) * width
                wanted = float(tap if kind == 0 else 2 - tap)
                total = total + jnp.where(offset == wanted, wide[:, start : start + width], 0.0)
            straight[cascade] = total.astype(BF16)
            turned[cascade] = total.T[: 6 * rows].astype(BF16)


def line_images(kspace, mask, lines, table_ref, plus_ref):
    real, imag = split_complex(lane_chunks(kspace), lines)
    measured = jnp.concatenate([real * mask, imag * mask], axis=0)
    return line_apply(depth_apply(measured, plus_ref), table_ref, 1.0)


def far_kernel(coils, lines, volumes, kspace_ref, mask_ref, table_ref, plus_ref, out_ref):
    parts = blocks(read_mask(mask_ref, table_ref.shape[0]), volumes)
    mask = pick(parts, own_volume(parts[0].shape[0]))
    mask = over_coils(mask, coils)
    images = line_images(kspace_ref[...].astype(F32), mask, lines, table_ref, plus_ref)
    out_ref[: images.shape[0]] = images
    if out_ref.shape[0] > images.shape[0]:
        out_ref[images.shape[0] :] = jnp.zeros_like(out_ref[images.shape[0] :])


def rows_kernel(
    coils,
    lines,
    volumes,
    from_places,
    to_places,
    sent_ref,
    kspace_ref,
    mask_ref,
    table_ref,
    minus_ref,
    plus_ref,
    near_ref,
    *refs,
):
    arrival_refs, refs = refs[: volumes - 1], refs[volumes - 1 :]
    out_ref, maps_ref, arrived, leaving = refs
    depth = sent_ref.shape[0]
    pitch = arrived.shape[0] // depth
    volume = own_volume(depth)
    mask = pick(blocks(read_mask(mask_ref, table_ref.shape[0]), volumes), volume)
    mask = over_coils(mask, volumes * coils)

    own = choose_volume(kspace_ref[...].astype(F32), coils, volumes, volume)
    own = line_images(own, mask[: coils * depth], lines, table_ref, near_ref)
    arrivals = [halves(own)] + [halves(ref[: 2 * coils * depth]) for ref in arrival_refs]
    measured = []
    for part in range(2):
        for place in range(volumes):
            step = lax.rem(volume - place + volumes, jnp.int32(volumes))
            measured.append(pick([arrival[part] for arrival in arrivals], step))
    measured = jnp.concatenate(measured, axis=0)

    take_messages(arrived, sent_ref, from_places)
    count = 2 * lines // LANES
    parts, reals, imags = [], [], []
    for place in range(volumes):
        first = place * (coils + 1) * count
        for coil in range(coils):
            chunks = read_rows(arrived, pitch, first + coil * count, count, depth)
            parts.append(split_complex(chunks, lines))
        chunks = read_rows(arrived, pitch, first + coils * count, count, depth)
        real, imag = split_complex(chunks, lines)
        reals.append(real)
        imags.append(imag)
    maps_real = jnp.concatenate([part[0] for part in parts], axis=0)
    maps_imag = jnp.concatenate([part[1] for part in parts], axis=0)
    maps_ref[...] = jnp.concatenate([maps_real, maps_imag], axis=0).astype(BF16)

    images = spread(maps_real, maps_imag, over_rows(reals, coils), over_rows(imags, coils))
    mask = jnp.concatenate([mask, mask], axis=0)
    images = masked_normal(images, table_ref, minus_ref, plus_ref, mask)
    found = [
        *collect(maps_real, maps_imag, round_bf(measured)),
        *collect(maps_real, maps_imag, images),
        maps_real * maps_real + maps_imag * maps_imag,
    ]
    leaving[...] = jnp.zeros_like(leaving)
    sums = [row_sums(value, volumes, coils) for value in found]
    pitch = leaving.shape[0] // depth
    for place in range(volumes):
        chunks = [chunk for value in sums for chunk in lane_chunks(value[place])]
        write_rows(leaving, pitch, chunks, place * len(chunks))
    put_messages(out_ref, leaving, to_places)


def read_image(scratch, pitch, first, count, depth):
    return jnp.concatenate(read_rows(scratch, pitch, first, count, depth), axis=1)


def read_places(scratch, pitch, first, period, count, depth, volumes):
    parts = [
        read_image(scratch, pitch, first + place * period, count, depth) for place in range(volumes)
    ]
    return jnp.concatenate(parts, axis=0)


def read_complex(scratch, pitch, first, period, count, depth, volumes):
    real = read_places(scratch, pitch, first, period, count, depth, volumes)
    imag = read_places(scratch, pitch, first + count, period, count, depth, volumes)
    return jnp.concatenate([real, imag], axis=0)


def refine_kernel(
    lines,
    volumes,
    from_places,
    to_places,
    sent_ref,
    cotangent_ref,
    first_ref,
    first_t_ref,
    second_ref,
    second_t_ref,
    columns_ref,
    out_ref,
    image_ref,
    arrived,
    leaving,
):
    take_messages(arrived, sent_ref, from_places)
    depth = len(from_places)
    pitch = arrived.shape[0] // depth
    rows = depth * volumes
    width = padded(lines, LANES)
    count = width // LANES
    begun = read_complex(arrived, pitch, 0, 5 * count, count, depth, volumes)
    turned = read_complex(arrived, pitch, 2 * count, 5 * count, count, depth, volumes)
    power = read_places(arrived, pitch, 4 * count, 5 * count, count, depth, volumes)
    power = jnp.concatenate([power, power], axis=0)
    cotangent = jnp.concatenate(
        split_complex(lane_chunks(cotangent_ref[...].astype(F32)), lines), axis=0
    )
    tall = first_ref.shape[1]
    weight = [column(columns_ref, CASCADES + cascade, 2 * rows) for cascade in range(CASCADES)]
    bias = [column(columns_ref, 2 * CASCADES + cascade, 2 * rows) for cascade in range(CASCADES)]

    share = [jnp.ones_like(weight[0])]
    for cascade in range(CASCADES):
        share.append(share[cascade] - weight[cascade] * (share[cascade] - 1.0))

    def slopes(hidden):
        gate = jax.nn.sigmoid(hidden)
        return hidden * gate, gate * (1.0 + hidden * (1.0 - gate))

    hidden = hidden_state(round_bf(begun), first_ref.at[0], column(columns_ref, 0, tall))
    valid = valid_lanes(hidden.shape[0], width, lines)
    active, slope_first = slopes(hidden)
    model = round_bf(second_conv(active, second_ref.at[0], bias[0], rows, valid))
    picture = round_bf(share[1] * begun + power * model)
    hidden = hidden_state(picture, first_ref.at[1], column(columns_ref, 1, tall))
    active, slope_second = slopes(hidden)
    later = round_bf(second_conv(active, second_ref.at[1], bias[1], rows, valid))
    image_ref[...] = share[2] * begun + power * (model + later)

    through = power * cotangent
    back_second = round_bf(
        pull_back(through, slope_second, first_t_ref.at[1], second_t_ref.at[1], rows, valid)
    )
    through = through - weight[1] * turned + power * back_second
    back_first = round_bf(
        pull_back(through, slope_first, first_t_ref.at[0], second_t_ref.at[0], rows, valid)
    )
    kept = (1.0 - weight[0], 1.0 - weight[1])
    of_cotangent = weight[1] + weight[0] * kept[1] + kept[0] * kept[1]
    of_second = weight[0] + kept[0]
    pulled = of_cotangent * cotangent + of_second * back_second + back_first
    leaving[...] = jnp.zeros_like(leaving)
    parts = [blocks(part, volumes) for value in (model, pulled) for part in halves(value)]
    for place in range(volumes):
        chunks = [chunk for part in parts for chunk in lane_chunks(part[place])]
        write_rows(leaving, out_ref.shape[1], chunks, place * len(chunks))
    put_messages(out_ref, leaving, to_places)


def hand_kernel(lines, volumes, from_places, sent_ref, maps_ref, *refs):
    outs, (arrived,) = refs[:-1], refs[-1:]
    take_messages(arrived, sent_ref, from_places)
    depth, pitch = sent_ref.shape[:2]
    volume = own_volume(depth)
    count = maps_ref.shape[1] // LANES
    maps = [blocks(part, volumes) for part in halves(maps_ref[...].astype(F32))]
    pulled = [
        [
            read_image(arrived, pitch, (place * 4 + field) * count, count, depth)
            for place in range(volumes)
        ]
        for field in (2, 3)
    ]
    for step, ref in enumerate(outs):
        place = lax.rem(volume + step, jnp.int32(volumes))
        chosen = [jnp.concatenate([pick(a, place), pick(b, place)]) for a, b in zip(maps, pulled)]
        for index, chunk in enumerate(join_complex(*chosen, lines)):
            ref[:, index * LANES : (index + 1) * LANES] = chunk.astype(BF16)


def normal_kernel(
    coils,
    lines,
    volumes,
    from_places,
    to_places,
    sent_ref,
    maps_ref,
    mask_ref,
    table_ref,
    minus_ref,
    plus_ref,
    out_ref,
    arrived,
    leaving,
):
    take_messages(arrived, sent_ref, from_places)
    depth, pitch = sent_ref.shape[:2]
    volume = own_volume(depth)
    count = maps_ref.shape[1] // LANES
    fields = [
        [
            read_image(arrived, pitch, (place * 4 + field) * count, count, depth)
            for place in range(volumes)
        ]
        for field in range(2)
    ]
    reals, imags = fields
    maps_real, maps_imag = halves(maps_ref[...].astype(F32))
    mask = over_coils(pick(blocks(read_mask(mask_ref, table_ref.shape[0]), volumes), volume), 2 * volumes * coils)
    images = spread(maps_real, maps_imag, over_rows(reals, coils), over_rows(imags, coils))
    images = masked_normal(images, table_ref, minus_ref, plus_ref, mask)
    found = [row_sums(value, volumes, coils) for value in collect(maps_real, maps_imag, images)]
    leaving[...] = jnp.zeros_like(leaving)
    for place in range(volumes):
        chunks = join_complex(found[0][place], found[1][place], lines)
        write_rows(leaving, leaving.shape[0] // depth, chunks, place * len(chunks))
    put_messages(out_ref, leaving, to_places)


def from_volumes(refs, volume, parts, volumes):
    sources = [blocks(ref, parts) for ref in refs]
    ordered = []
    for place in range(volumes):
        step = lax.rem(volume - place + volumes, jnp.int32(volumes))
        ordered.append([pick([source[part] for source in sources], step) for part in range(parts)])
    return ordered


def grad_kernel(
    coils,
    lines,
    volumes,
    mask_ref,
    table_ref,
    minus_ref,
    *refs,
):
    handed, (grad_ref,) = refs[:volumes], refs[volumes:]
    depth = mask_ref.shape[0] // volumes
    volume = own_volume(depth)
    handed = [split_complex(lane_chunks(ref[...].astype(F32)), lines) for ref in handed]
    handed = [jnp.concatenate(parts, axis=0) for parts in handed]
    found = from_volumes(handed, volume, 2 * (coils + 1), volumes)
    maps, pulled = [], []
    for first in (0, coils + 1):
        parts = [found[v][first + coil] for coil in range(coils) for v in range(volumes)]
        maps.append(jnp.concatenate(parts, axis=0))
        pulled.append(jnp.concatenate([found[v][first + coils] for v in range(volumes)], axis=0))
    real, imag = pulled
    images = spread(*maps, over_coils(real, coils), over_coils(imag, coils))
    spectrum = depth_apply(line_apply(images, table_ref, -1.0), minus_ref)
    spectrum = spectrum * over_coils(read_mask(mask_ref, table_ref.shape[0]), 2 * coils)
    chunks = join_complex(*halves(spectrum), lines)
    write_rows(grad_ref, len(chunks), chunks)


def picture_kernel(lines, volumes, from_places, columns_ref, sent_ref, image_ref, picture_ref, arrived):
    depth = len(from_places)
    pitch = arrived.shape[0] // depth
    count = 2 * lines // LANES
    take_messages(arrived, sent_ref, from_places)
    parts = [[], []]
    for place in range(volumes):
        chunks = read_rows(arrived, pitch, place * count, count, depth)
        for part, value in zip(parts, split_complex(chunks, lines)):
            part.append(value)
    picture = image_ref[...]
    scale = column(columns_ref, CASCADES + 1, picture.shape[0])
    picture = picture - scale * jnp.concatenate(parts[0] + parts[1], axis=0)
    for index, chunk in enumerate(join_complex(*halves(picture), lines)):
        picture_ref[:, index * LANES : (index + 1) * LANES] = chunk


def end_kernel(
    coils,
    lines,
    volumes,
    from_places,
    columns_ref,
    sent_ref,
    image_ref,
    mask_ref,
    table_ref,
    minus_ref,
    *refs,
):
    handed, (picture_ref, grad_ref, arrived) = refs[:volumes], refs[volumes:]
    grad_kernel(coils, lines, volumes, mask_ref, table_ref, minus_ref, *handed, grad_ref)
    picture_kernel(
        lines, volumes, from_places, columns_ref, sent_ref, image_ref, picture_ref, arrived
    )


def call(kernel, name, operands, outs, scratch, flops, vmem_bytes=VMEM_BYTES, scalars=0):
    spaces = [pltpu.SMEM] * scalars + [pltpu.VMEM] * (len(operands) - scalars)
    moved = sum(math.prod(item.shape) * item.dtype.itemsize for item in (*operands, *outs))
    return pl.pallas_call(
        kernel,
        name=name,
        out_shape=tuple(outs),
        in_specs=[pl.BlockSpec(memory_space=space) for space in spaces],
        out_specs=tuple(pl.BlockSpec(memory_space=pltpu.VMEM) for item in outs),
        scratch_shapes=[pltpu.VMEM(shape, F32) for shape in scratch],
        compiler_params=pltpu.CompilerParams(vmem_limit_bytes=vmem_bytes),
        cost_estimate=pl.CostEstimate(flops=flops, bytes_accessed=moved, transcendentals=0),
    )(*operands)


def body(
    kspace, coil_maps, sampling, dc_weight, kernel_in, bias_in, kernel_out, bias_out, cotangent
):
    coils, slots = kspace.shape[:2]
    rows, two_lines = coil_maps.shape[2:]
    lines = two_lines // 2
    channels = bias_in.shape[1]
    coil_devices, sections = lax.axis_size("coil"), lax.axis_size("section")
    volumes = VOLUMES
    depth = slots // volumes
    width = padded(lines, LANES)
    count, whole_count = width // LANES, two_lines // LANES
    planes = coils * slots
    both = ("section", "coil")
    span = depth * coil_devices
    near_order = [depth - 1] + list(range(depth - 1))
    both_order = [m for m in range(span)[::-1] if m // coil_devices % 2] + [m for m in range(span)[::-1] if not m // coil_devices % 2]
    near = [[group * depth + member for member in near_order] for group in range(volumes)]
    near_both = [[group * span + member for member in both_order] for group in range(volumes)]
    near_places = [[near_order.index(member)] for member in range(depth)]
    both_places = [
        [both_order.index(member * coil_devices + coil) for coil in range(coil_devices)]
        for member in range(depth)
    ]

    def from_group(value, step, core=0):
        pairs = [(s, ((s + step * depth) % sections) ^ core) for s in range(sections)]
        return lax.ppermute(value, "section", pairs)

    def between_cores(value):
        return lax.ppermute(value, "section", [(s, s) for s in range(sections)])

    def exchange(value, axes, groups):
        return lax.all_to_all(value, axes, 0, 0, tiled=True, axis_index_groups=groups)

    table = jnp.asarray(line_constant(lines))
    minus = jnp.asarray(depth_constant(coils, slots, volumes, -1.0))
    plus = jnp.asarray(depth_constant(coils, slots, volumes, 1.0))
    near_plus = jnp.asarray(depth_constant(coils, depth, 1, 1.0))
    repeat, place, offset = (jnp.asarray(item) for item in conv_constants(rows, channels))
    mask = sampling.reshape(slots, lines)

    def shape(*dims, kind=F32):
        return jax.ShapeDtypeStruct(dims, kind)

    line_flops = 2 * (2 * planes) * width * (2 * width)

    maps_lines = volumes * (coils + 1) * whole_count
    pitch = padded(maps_lines, 8)
    packed, *samples = call(
        functools.partial(pack_kernel, coils, volumes, pitch, near_places),
        "pack_maps",
        (
            kspace.reshape(planes, two_lines),
            coil_maps.reshape(coils * rows, two_lines),
            cotangent.reshape(rows, two_lines),
        ),
        [shape(depth, maps_lines, LANES, kind=BF16)]
        + [shape(coils * depth, two_lines, kind=BF16)] * (volumes - 1),
        [(depth * pitch, LANES)],
        1000,
        LARGE_VMEM_BYTES,
    )
    samples = [from_group(value, step) for step, value in enumerate(samples, 1)]
    tall, wide = channels * rows, offset.shape[1]
    first, first_t, second, second_t, columns = call(
        functools.partial(taps_kernel, rows),
        "lay_out_taps",
        (
            dc_weight,
            kernel_in.transpose(0, 1, 3, 2).reshape(-1, 2, channels),
            kernel_out.reshape(-1, 2, channels),
            bias_in,
            bias_out,
            repeat,
            place,
            offset,
        ),
        [
            shape(CASCADES, tall, wide, kind=BF16),
            shape(CASCADES, 6 * rows, tall, kind=BF16),
            shape(CASCADES, 6 * rows, tall, kind=BF16),
            shape(CASCADES, tall, wide, kind=BF16),
            shape(tall, place.shape[0]),
        ],
        [(place.shape[0], repeat.shape[1])],
        2 * tall * place.shape[0] * place.shape[1],
        scalars=1,
    )
    *samples, columns = lax.optimization_barrier((*samples, columns))
    images = []
    for value in samples:
        (image,) = call(
            functools.partial(far_kernel, coils, lines, volumes),
            "far_images",
            (value, mask, table, near_plus),
            [shape(FAR_PARTS * coils * depth, width)],
            [],
            line_flops,
        )
        images.append(between_cores(image))
    arrived = exchange(packed, "section", near)

    sums_lines = volumes * 5 * count
    depth_pitch = padded(sums_lines, 8)
    partial, maps = call(
        functools.partial(rows_kernel, coils, lines, volumes, near_places, both_places),
        "combine_rows",
        (arrived, kspace.reshape(planes, two_lines), mask, table, minus, plus, near_plus, *images),
        [
            shape(span, sums_lines, LANES, kind=BF16),
            shape(2 * planes, width, kind=BF16),
        ],
        [(depth * pitch, LANES), (depth * depth_pitch, LANES)],
        4 * line_flops,
    )

    partial = exchange(partial, both, near_both)

    model_pitch = padded(volumes * 4 * count, 8)
    moved, image = call(
        functools.partial(refine_kernel, lines, volumes, both_places, near_places),
        "refine_and_back",
        (
            partial,
            cotangent.reshape(rows, two_lines),
            first,
            first_t,
            second,
            second_t,
            columns,
        ),
        [shape(depth, model_pitch, LANES, kind=BF16), shape(2 * rows, width)],
        [(depth * depth_pitch, LANES), (depth * model_pitch, LANES)],
        14 * tall * wide * width,
    )
    moved = exchange(moved, "section", near)

    end_lines = volumes * whole_count
    end_pitch = padded(end_lines, 16)
    handed = call(
        functools.partial(hand_kernel, lines, volumes, near_places),
        "hand_on",
        (moved, maps),
        [shape((coils + 1) * depth, two_lines, kind=BF16)] * volumes,
        [(depth * model_pitch, LANES)],
        1000,
    )
    handed = list(handed)
    (partial,) = call(
        functools.partial(normal_kernel, coils, lines, volumes, near_places, both_places),
        "masked_normal",
        (moved, maps, mask, table, minus, plus),
        [shape(span, end_lines, LANES, kind=BF16)],
        [(depth * model_pitch, LANES), (depth * end_pitch, LANES)],
        3 * line_flops,
    )
    partial = exchange(partial, both, near_both)
    handed[1:] = [
        from_group(value, step) for step, value in enumerate(handed[1:], 1)
    ]

    image, grad = call(
        functools.partial(end_kernel, coils, lines, volumes, both_places),
        "outputs",
        (columns, partial, image, mask, table, minus, *handed),
        [shape(rows, two_lines), shape(planes * whole_count, LANES)],
        [(depth * end_pitch, LANES)],
        2 * line_flops,
    )
    return image.reshape(1, rows, two_lines), grad.reshape(coils, slots, 1, two_lines)


def solution(mesh):
    return jax.shard_map(
        body,
        mesh=mesh,
        in_specs=(
            P("coil", None, "section", None),
            P("coil", "section", None, None),
            P(),
            P(),
            P(),
            P(),
            P(),
            P(),
            P("section", None, None),
        ),
        out_specs=(P("section", None, None), P("coil", None, "section", None)),
        check_vma=False,
    )
```
